32 devices in a mesh: dp: 16 (over z, y, x), mp: 2 (over core).
Axes of the slice: x: 2, y: 2, z: 4, core: 2. Of those that a mesh axis runs over, the one named last changes fastest.
Arguments:
- out_grad: bfloat16 [2048, 4096], P('dp'), may hold values from -40 to 40
- gate_pre: bfloat16 [2048, 5120], P('dp', 'mp'), may hold values from -6 to 6
- up_pre: bfloat16 [2048, 5120], P('dp', 'mp'), may hold values from -40 to 40
- down_weight: bfloat16 [4096, 5120], P('dp', 'mp'), may hold values from -0.078125 to 0.078125
- row_moment: float32 [4096], P('dp'), may hold values from 0.05 to 0.5
- col_moment: float32 [5120], P('mp'), may hold values from 0.05 to 0.5
Outputs:
- update: float32 [4096, 5120], P('dp', 'mp')
- row_moment_new: float32 [4096], P('dp')
- col_moment_new: float32 [5120], P('mp')
- row_mean: float32 [], replicated
- gate_grad: bfloat16 [2048, 5120], P('dp', 'mp')
- up_grad: bfloat16 [2048, 5120], P('dp', 'mp')
The draws below stay inside these ranges and needn't reach their ends.
All inputs are finite; a program needn't handle non-finite values.
Results may differ from the reference program's by a relative error of at most 0.0034.
Values may be sent and summed in bfloat16 or wider, within the bound.
No kernel may reach another device: no remote copies, remote signals or barrier semaphores. Data moves between devices by JAX's collectives and lax.ppermute only.
A program may use at most 128 MiB of HBM per device.

```python
import math
import jax
import jax.numpy as jnp
from jax import lax

D = 4096
FF = 5120
TRAIN_STEP = 3
TOKENS = 2048


def scale_grid(key, height, breadth, smallest, largest, rising):
    key_cols, key_rows = jax.random.split(key, 2)
    col_scale = jnp.exp(jax.random.uniform(key_cols, (1, breadth), jnp.float32, math.log(smallest), math.log(largest)))
    position = jnp.arange(breadth, dtype=jnp.float32)[None, :] / breadth - 0.5
    col_scale = col_scale * jnp.exp(position * math.log(rising))
    row_scale = jnp.exp(jax.random.uniform(key_rows, (height, 1), jnp.float32, math.log(0.5), math.log(2.0)))
    return col_scale * row_scale


def hot_masks(key):
    key = jax.random.fold_in(key, 5)
    key_tokens, key_features, key_units = jax.random.split(key, 3)
    token_hot = jax.random.randint(key_tokens, (TOKENS, 1), 0, 4) == 0
    feature_hot = jax.random.randint(key_features, (1, D), 0, 2) == 0
    unit_hot = jax.random.randint(key_units, (1, FF), 0, 2) == 0
    return (token_hot, feature_hot, unit_hot)


def draw_out_grad(key, part):
    token_hot, feature_hot, unit_hot = hot_masks(key)
    boost = jnp.where(jnp.logical_and(token_hot, feature_hot), 6.0, 1.0).astype(jnp.float32)
    key = jax.random.fold_in(key, 11)
    key_entries, key_scale = jax.random.split(key, 2)
    entries = jax.random.normal(key_entries, (TOKENS, D), jnp.float32)
    return jnp.clip(entries * scale_grid(key_scale, TOKENS, D, 0.32, 3.2, 3.0) * boost, -40.0, 40.0).astype(jnp.bfloat16)


def draw_up_pre(key, part):
    token_hot, feature_hot, unit_hot = hot_masks(key)
    boost = jnp.where(jnp.logical_and(token_hot, unit_hot), 6.0, 1.0).astype(jnp.float32)
    key = jax.random.fold_in(key, 23)
    key_entries, key_scale = jax.random.split(key, 2)
    entries = jax.random.normal(key_entries, (TOKENS, FF), jnp.float32)
    return jnp.clip(entries * scale_grid(key_scale, TOKENS, FF, 0.32, 3.2, 1.0) * boost, -40.0, 40.0).astype(jnp.bfloat16)


def steps_of(own_key, extent, shards, low, high):
    factor_of = 1.0
    for dim, blocks in shards:
        steps = jax.random.uniform(jax.random.fold_in(jax.random.fold_in(own_key, 6), dim), (blocks,), jnp.float32, low / len(shards), high / len(shards))
        factor_of = factor_of * jnp.repeat(jnp.exp(steps), extent[dim] // blocks).reshape((-1,) + (1,) * (len(extent) - 1 - dim))
    return factor_of


def scatter_about(key, extent, deviation, limit, cuts=(), kind=jnp.bfloat16):
    values = jax.random.normal(key, extent, jnp.float32) * deviation
    if len(cuts) > 0:
        values = steps_of(key, extent, cuts, -0.22, 0.18) * values
    return jnp.clip(values, min=-limit, max=limit).astype(kind)


def setup_inputs(seed: int = 0) -> dict:
    key_list = jax.random.split(jax.random.key(seed), 7)
    out_grad = draw_out_grad(jax.random.fold_in(key_list[6], 71), 0)
    gate_pre = scatter_about(key_list[1], (TOKENS, FF), 1.0, 6.0, ((0, 16), (1, 2)))
    up_pre = draw_up_pre(jax.random.fold_in(key_list[6], 71), 0)
    down_weight = scatter_about(key_list[3], (D, FF), FF ** -0.5, 0.078125, ((0, 16), (1, 2)))
    row_moment = jnp.clip(jnp.exp(math.log(0.5) - 2.3025851 * jax.random.uniform(key_list[4], (D,), jnp.float32) ** steps_of(key_list[4], (D,), ((0, 16),), -0.2, 0.2)), 0.05, 0.5)
    col_moment = jnp.clip(jnp.exp(math.log(0.5) - 2.3025851 * jax.random.uniform(key_list[5], (FF,), jnp.float32) ** steps_of(key_list[5], (FF,), ((0, 2),), -0.2, 0.2)), 0.05, 0.5)
    return {"out_grad": out_grad, "gate_pre": gate_pre, "up_pre": up_pre, "down_weight": down_weight, "row_moment": row_moment, "col_moment": col_moment}


def gelu_parts(values):
    factor = math.sqrt(2.0 / math.pi)
    inner = factor * (values + 0.044715 * values * values * values)
    tangent = jnp.tanh(inner)
    activated = 0.5 * values * (1.0 + tangent)
    derivative = 0.5 * (1.0 + tangent) + 0.5 * values * (1.0 - tangent * tangent) * factor * (1.0 + 3.0 * 0.044715 * values * values)
    return (activated, derivative)

def reference(out_grad, gate_pre, up_pre, down_weight, row_moment, col_moment):
    gate_value = gate_pre.astype(jnp.float32)
    up_value = up_pre.astype(jnp.float32)
    activated, derivative = gelu_parts(gate_value)
    hidden = (activated * up_value).astype(jnp.bfloat16)
    hidden_grad = jnp.dot(out_grad, down_weight, preferred_element_type=jnp.float32)
    gate_grad = (hidden_grad * up_value * derivative).astype(jnp.bfloat16)
    up_grad = (hidden_grad * activated).astype(jnp.bfloat16)
    grad = jnp.dot(out_grad.T, hidden, preferred_element_type=jnp.float32) * (1.0 / math.sqrt(TOKENS))
    decay = 1.0 - TRAIN_STEP ** (-0.8)
    squares = grad * grad + 1e-30
    row_moment_new = decay * row_moment + (1.0 - decay) * lax.optimization_barrier(jnp.mean(squares, axis=1))
    col_moment_new = decay * col_moment + (1.0 - decay) * lax.optimization_barrier(jnp.mean(squares, axis=0))
    row_mean = jnp.mean(row_moment_new)
    unclipped = grad / jnp.sqrt(row_moment_new[:, None] * col_moment_new[None, :] / row_mean)
    clip_norm = jnp.sqrt(jnp.mean(unclipped * unclipped))
    update = unclipped / jnp.maximum(1.0, clip_norm)
    return (update, row_moment_new, col_moment_new, row_mean, gate_grad, up_grad)
```

```python
import math

import jax
import jax.numpy as jnp
from jax import lax
from jax.sharding import PartitionSpec as P

TRAIN_STEP = 3
INNER_BITS = 2


def gelu_parts(values):
    factor = math.sqrt(2.0 / math.pi)
    inner = factor * (values + 0.044715 * values * values * values)
    tangent = jnp.tanh(inner)
    activated = 0.5 * values * (1.0 + tangent)
    derivative = 0.5 * (1.0 + tangent) + 0.5 * values * (1.0 - tangent * tangent) * factor * (
        1.0 + 3.0 * 0.044715 * values * values
    )
    return (activated, derivative)


def flip(value, bits):
    size = lax.axis_size("dp")
    return lax.ppermute(value, "dp", [(i, i ^ bits) for i in range(size)])


def gather(block, bits):
    half = block.shape[1] // 2
    if len(bits) == 2:
        first = flip(block, bits[0])
        second = flip(block, bits[1])
        left = [block[:, :half], first[:, :half], second[:, :half], flip(first[:, :half], bits[1])]
        right = [block[:, half:], first[:, half:], second[:, half:], flip(second[:, half:], bits[0])]
        return left, right
    blocks = [block]
    for bit in bits:
        blocks = blocks + [flip(b, bit) for b in blocks]
    return [b[:, :half] for b in blocks], [b[:, half:] for b in blocks]


def scatter(part, bits):
    def send(value, bit):
        return flip(value.astype(jnp.bfloat16), bit).astype(jnp.float32)

    if len(bits) == 2:
        low, high = bits
        left3 = send(part(3, 0), low)
        right3 = send(part(3, 1), high)
        left1 = send(part(1, 0), low)
        right2 = send(part(2, 1), high)
        left2 = send(part(2, 0) + left3, high)
        right1 = send(part(1, 1) + right3, low)
        return part(0, 0) + left1 + left2, part(0, 1) + right2 + right1
    sides = []
    for side in range(2):
        values = [part(j, side) for j in range(2 ** len(bits))]
        for level in reversed(range(len(bits))):
            count = 2**level
            values = [values[j] + send(values[j + count], bits[level]) for j in range(count)]
        sides.append(values[0])
    return tuple(sides)


def group_sum(value, bits):
    for at in range(0, len(bits), 2):
        pair = bits[at : at + 2]
        if len(pair) == 2:
            first, second = flip(value, pair[0]), flip(value, pair[1])
            value = (value + first) + (second + flip(value, pair[0] | pair[1]))
        else:
            value = value + flip(value, pair[0])
    return value


def local(out_grad, gate_pre, up_pre, down_weight, row_moment, col_moment):
    size = lax.axis_size("dp")
    me = lax.axis_index("dp")
    rows, units = down_weight.shape
    tokens = out_grad.shape[0]
    half = units // 2
    all_bits = [1 << b for b in range(size.bit_length() - 1)]
    inner_bits, outer_bits = all_bits[:INNER_BITS], all_bits[INNER_BITS:]
    inner, outer = 2 ** len(inner_bits), 2 ** len(outer_bits)

    gate_value = gate_pre.astype(jnp.float32)
    up_value = up_pre.astype(jnp.float32)
    activated, derivative = gelu_parts(gate_value)
    hidden = (activated * up_value).astype(jnp.bfloat16)

    by_block = out_grad.reshape(tokens, size, rows).transpose(1, 0, 2)

    def features_of(k):
        picks = [lax.dynamic_index_in_dim(by_block, me ^ (k * inner + j), 0, keepdims=False) for j in range(inner)]
        return jnp.concatenate(picks, axis=1)

    shares = [features_of(0)] + [flip(features_of(k), k * inner) for k in range(1, outer)]
    share = jnp.concatenate(shares, axis=0)

    hidden_sides = gather(hidden, outer_bits)
    hidden_sides = [jnp.concatenate(side, axis=0) for side in hidden_sides]
    weight_sides = gather(down_weight, inner_bits)
    weight_sides = [jnp.concatenate(side, axis=0) for side in weight_sides]

    def grad_part(j, side):
        return lax.dot_general(
            share[:, j * rows : (j + 1) * rows],
            hidden_sides[side],
            (((0,), (0,)), ((), ())),
            preferred_element_type=jnp.float32,
        )

    def hidden_grad_part(k, side):
        return jnp.dot(shares[k], weight_sides[side], preferred_element_type=jnp.float32)

    product = jnp.concatenate(scatter(grad_part, inner_bits), axis=1)
    hidden_grad = jnp.concatenate(scatter(hidden_grad_part, outer_bits), axis=1)

    gate_grad = (hidden_grad * up_value * derivative).astype(jnp.bfloat16)
    up_grad = (hidden_grad * activated).astype(jnp.bfloat16)

    grad = product * (1.0 / math.sqrt(tokens * size))
    decay = 1.0 - TRAIN_STEP ** (-0.8)
    total_rows = rows * size
    total_units = units * lax.axis_size("mp")
    powers = grad * grad
    squares = powers + 1e-30
    row_sum = lax.psum(jnp.sum(squares, axis=1), "mp")
    row_moment_new = decay * row_moment + (1.0 - decay) * (row_sum / total_units)
    col_part = jnp.sum(squares, axis=0)
    scaled_part = jnp.sum(powers / row_moment_new[:, None], axis=0)
    total_part = jnp.broadcast_to(jnp.sum(row_moment_new), (128,))
    sums = group_sum(jnp.concatenate([col_part, scaled_part, total_part]), all_bits)
    col_moment_new = decay * col_moment + (1.0 - decay) * (sums[:units] / total_rows)
    row_mean = sums[2 * units] / total_rows
    square_sum = row_mean * lax.psum(jnp.sum(sums[units : 2 * units] / col_moment_new), "mp")
    clip_norm = jnp.sqrt(square_sum / (total_rows * total_units))
    row_factor = jnp.sqrt(row_mean / row_moment_new) / jnp.maximum(1.0, clip_norm)
    col_factor = 1.0 / jnp.sqrt(col_moment_new)
    update = grad * row_factor[:, None] * col_factor[None, :]
    return (update, row_moment_new, col_moment_new, row_mean, gate_grad, up_grad)


def solution(mesh):
    in_specs = (P("dp", None), P("dp", "mp"), P("dp", "mp"), P("dp", "mp"), P("dp"), P("mp"))
    out_specs = (P("dp", "mp"), P("dp"), P("mp"), P(), P("dp", "mp"), P("dp", "mp"))
    return jax.shard_map(local, mesh=mesh, in_specs=in_specs, out_specs=out_specs, check_vma=False)
```

```python
import math

import jax
import jax.numpy as jnp
from jax import lax
from jax.sharding import PartitionSpec as P

TRAIN_STEP = 3
INNER_BITS = 2


def gelu_parts(values):
    factor = math.sqrt(2.0 / math.pi)
    inner = factor * (values + 0.044715 * values * values * values)
    tangent = jnp.tanh(inner)
    activated = 0.5 * values * (1.0 + tangent)
    derivative = 0.5 * (1.0 + tangent) + 0.5 * values * (1.0 - tangent * tangent) * factor * (
        1.0 + 3.0 * 0.044715 * values * values
    )
    return (activated, derivative)


def flip(value, bits):
    size = lax.axis_size("dp")
    return lax.ppermute(value, "dp", [(i, i ^ bits) for i in range(size)])


def gather(block, bits):
    half = block.shape[1] // 2
    if len(bits) == 2:
        first = flip(block, bits[0])
        second = flip(block, bits[1])
        left = [block[:, :half], first[:, :half], second[:, :half], flip(first[:, :half], bits[1])]
        right = [block[:, half:], first[:, half:], second[:, half:], flip(second[:, half:], bits[0])]
        return left, right
    blocks = [block]
    for bit in bits:
        blocks = blocks + [flip(b, bit) for b in blocks]
    return [b[:, :half] for b in blocks], [b[:, half:] for b in blocks]


def scatter(part, bits):
    def send(value, bit):
        return flip(value.astype(jnp.bfloat16), bit).astype(jnp.float32)

    if len(bits) == 2:
        low, high = bits
        left3 = send(part(3, 0), low)
        right3 = send(part(3, 1), high)
        left1 = send(part(1, 0), low)
        right2 = send(part(2, 1), high)
        left2 = send(part(2, 0) + left3, high)
        right1 = send(part(1, 1) + right3, low)
        return part(0, 0) + left1 + left2, part(0, 1) + right2 + right1
    sides = []
    for side in range(2):
        values = [part(j, side) for j in range(2 ** len(bits))]
        for level in reversed(range(len(bits))):
            count = 2**level
            values = [values[j] + send(values[j + count], bits[level]) for j in range(count)]
        sides.append(values[0])
    return tuple(sides)


def group_sum(value, bits):
    for at in range(0, len(bits), 2):
        pair = bits[at : at + 2]
        if len(pair) == 2:
            first, second = flip(value, pair[0]), flip(value, pair[1])
            value = (value + first) + (second + flip(value, pair[0] | pair[1]))
        else:
            value = value + flip(value, pair[0])
    return value


def local(out_grad, gate_pre, up_pre, down_weight, row_moment, col_moment):
    size = lax.axis_size("dp")
    me = lax.axis_index("dp")
    rows, units = down_weight.shape
    tokens = out_grad.shape[0]
    half = units // 2
    all_bits = [1 << b for b in range(size.bit_length() - 1)]
    inner_bits, outer_bits = all_bits[:INNER_BITS], all_bits[INNER_BITS:]
    inner, outer = 2 ** len(inner_bits), 2 ** len(outer_bits)

    activated, _ = gelu_parts(gate_pre.astype(jnp.float32))
    hidden = (activated * up_pre.astype(jnp.float32)).astype(jnp.bfloat16)

    by_block = out_grad.reshape(tokens, size, rows).transpose(1, 0, 2)

    def features_of(k):
        picks = [lax.dynamic_index_in_dim(by_block, me ^ (k * inner + j), 0, keepdims=False) for j in range(inner)]
        return jnp.concatenate(picks, axis=1)

    shares = [features_of(0)] + [flip(features_of(k), k * inner) for k in range(1, outer)]
    share = jnp.concatenate(shares, axis=0)

    hidden_sides = gather(hidden, outer_bits)
    hidden_sides = [jnp.concatenate(side, axis=0) for side in hidden_sides]
    weight_sides = gather(down_weight, inner_bits)
    weight_sides = [jnp.concatenate(side, axis=0) for side in weight_sides]

    def grad_part(j, side):
        return lax.dot_general(
            share[:, j * rows : (j + 1) * rows],
            hidden_sides[side],
            (((0,), (0,)), ((), ())),
            preferred_element_type=jnp.float32,
        )

    def hidden_grad_part(k, side):
        return jnp.dot(shares[k], weight_sides[side], preferred_element_type=jnp.float32)

    product = jnp.concatenate(scatter(grad_part, inner_bits), axis=1)
    hidden_grad = jnp.concatenate(scatter(hidden_grad_part, outer_bits), axis=1)

    gate_late, up_late, hidden_grad = lax.optimization_barrier((gate_pre, up_pre, hidden_grad))
    activated, derivative = gelu_parts(gate_late.astype(jnp.float32))
    gate_grad = (hidden_grad * up_late.astype(jnp.float32) * derivative).astype(jnp.bfloat16)
    up_grad = (hidden_grad * activated).astype(jnp.bfloat16)

    grad = product * (1.0 / math.sqrt(tokens * size))
    decay = 1.0 - TRAIN_STEP ** (-0.8)
    total_rows = rows * size
    total_units = units * lax.axis_size("mp")
    powers = grad * grad
    squares = powers + 1e-30
    row_sum = lax.psum(jnp.sum(squares, axis=1), "mp")
    row_moment_new = decay * row_moment + (1.0 - decay) * (row_sum / total_units)
    col_part = jnp.sum(squares, axis=0)
    scaled_part = jnp.sum(powers / row_moment_new[:, None], axis=0)
    total_part = jnp.broadcast_to(jnp.sum(row_moment_new), (128,))
    sums = group_sum(jnp.concatenate([col_part, scaled_part, total_part]), all_bits)
    col_moment_new = decay * col_moment + (1.0 - decay) * (sums[:units] / total_rows)
    row_mean = sums[2 * units] / total_rows
    square_sum = row_mean * lax.psum(jnp.sum(sums[units : 2 * units] / col_moment_new), "mp")
    clip_norm = jnp.sqrt(square_sum / (total_rows * total_units))
    row_factor = jnp.sqrt(row_mean / row_moment_new) / jnp.maximum(1.0, clip_norm)
    col_factor = 1.0 / jnp.sqrt(col_moment_new)
    update = grad * row_factor[:, None] * col_factor[None, :]
    return (update, row_moment_new, col_moment_new, row_mean, gate_grad, up_grad)


def solution(mesh):
    in_specs = (P("dp", None), P("dp", "mp"), P("dp", "mp"), P("dp", "mp"), P("dp"), P("mp"))
    out_specs = (P("dp", "mp"), P("dp"), P("mp"), P(), P("dp", "mp"), P("dp", "mp"))
    return jax.shard_map(local, mesh=mesh, in_specs=in_specs, out_specs=out_specs, check_vma=False)
```

```python
import math

import jax
import jax.numpy as jnp
from jax import lax
from jax.experimental import pallas as pl
from jax.experimental.pallas import tpu as pltpu
from jax.sharding import PartitionSpec as P

TRAIN_STEP = 3
INNER_BITS = 2


def gelu_parts(values):
    factor = math.sqrt(2.0 / math.pi)
    inner = factor * (values + 0.044715 * values * values * values)
    tangent = jnp.tanh(inner)
    activated = 0.5 * values * (1.0 + tangent)
    derivative = 0.5 * (1.0 + tangent) + 0.5 * values * (1.0 - tangent * tangent) * factor * (
        1.0 + 3.0 * 0.044715 * values * values
    )
    return (activated, derivative)


def flip(value, bits, axis="dp"):
    size = lax.axis_size(axis)
    return lax.ppermute(value, axis, [(i, i ^ bits) for i in range(size)])


def first_messages(block, bits):
    return [flip(block, bit) for bit in bits]


def gathered(block, messages, bits):
    half = block.shape[1] // 2
    if len(bits) == 2:
        first, second = messages
        left = [block[:, :half], first[:, :half], second[:, :half], flip(first[:, :half], bits[1])]
        right = [block[:, half:], first[:, half:], second[:, half:], flip(second[:, half:], bits[0])]
        return left, right
    blocks = [block]
    for bit in bits:
        blocks = blocks + [flip(b, bit) for b in blocks]
    return [b[:, :half] for b in blocks], [b[:, half:] for b in blocks]


def arrange(out_grad, me, core, size, inner, halves):
    tokens, width = out_grad.shape
    rows = width // size
    outer = size // inner
    part = tokens // halves

    def kernel(place, source, own, *others):
        for k in range(outer):
            for j in range(inner):
                at = pl.multiple_of((place[0] ^ (k * inner + j)) * rows, rows)
                columns = pl.ds(j * rows, rows)
                if k == 0:
                    own[:, columns] = source[:, pl.ds(at, rows)]
                else:
                    start = pl.multiple_of(place[1] * part, part)
                    others[k - 1][:, columns] = source[pl.ds(start, part), pl.ds(at, rows)]

    result = pl.pallas_call(
        kernel,
        out_shape=[jax.ShapeDtypeStruct((tokens, inner * rows), out_grad.dtype)]
        + [jax.ShapeDtypeStruct((part, inner * rows), out_grad.dtype)] * (outer - 1),
        in_specs=[pl.BlockSpec(memory_space=pltpu.SMEM), pl.BlockSpec(memory_space=pltpu.VMEM)],
        out_specs=[pl.BlockSpec(memory_space=pltpu.VMEM)] * outer,
        compiler_params=pltpu.CompilerParams(vmem_limit_bytes=16 << 20),
        cost_estimate=pl.CostEstimate(flops=0, bytes_accessed=4 * tokens * width, transcendentals=0),
    )(jnp.stack([me, core]).astype(jnp.int32), out_grad)
    return result[0], result[1:]


def arrange_plain(out_grad, me, size, inner):
    tokens, width = out_grad.shape
    by_block = out_grad.reshape(tokens, size, width // size).transpose(1, 0, 2)

    def features_of(k):
        picks = [lax.dynamic_index_in_dim(by_block, me ^ (k * inner + j), 0, keepdims=False) for j in range(inner)]
        return jnp.concatenate(picks, axis=1)

    return features_of(0), [features_of(k) for k in range(1, size // inner)]


def scatter(part, bits):
    def send(value, bit):
        return flip(value.astype(jnp.bfloat16), bit).astype(jnp.float32)

    if len(bits) == 2:
        low, high = bits
        left3 = send(part(3, 0), low)
        right3 = send(part(3, 1), high)
        left1 = send(part(1, 0), low)
        right2 = send(part(2, 1), high)
        left2 = send(part(2, 0) + left3, high)
        right1 = send(part(1, 1) + right3, low)
        return part(0, 0) + left1 + left2, part(0, 1) + right2 + right1
    sides = []
    for side in range(2):
        values = [part(j, side) for j in range(2 ** len(bits))]
        for level in reversed(range(len(bits))):
            count = 2**level
            values = [values[j] + send(values[j + count], bits[level]) for j in range(count)]
        sides.append(values[0])
    return tuple(sides)


def group_sum(value, bits):
    for at in range(0, len(bits), 2):
        pair = bits[at : at + 2]
        if len(pair) == 2:
            first, second = flip(value, pair[0]), flip(value, pair[1])
            value = (value + first) + (second + flip(value, pair[0] | pair[1]))
        else:
            value = value + flip(value, pair[0])
    return value


def local(out_grad, gate_pre, up_pre, down_weight, row_moment, col_moment):
    size = lax.axis_size("dp")
    me = lax.axis_index("dp")
    rows, units = down_weight.shape
    tokens = out_grad.shape[0]
    half = units // 2
    all_bits = [1 << b for b in range(size.bit_length() - 1)]
    inner_bits, outer_bits = all_bits[:INNER_BITS], all_bits[INNER_BITS:]
    inner, outer = 2 ** len(inner_bits), 2 ** len(outer_bits)

    activated, _ = gelu_parts(gate_pre.astype(jnp.float32))
    hidden = (activated * up_pre.astype(jnp.float32)).astype(jnp.bfloat16)

    core = lax.axis_index("mp")
    split = lax.axis_size("mp") == 2 and tokens % 32 == 0 and rows % 128 == 0
    weight_messages = first_messages(down_weight, inner_bits)
    hidden_messages = first_messages(hidden, outer_bits)
    if rows % 128 == 0:
        own_share, others = arrange(out_grad, me, core, size, inner, 2 if split else 1)
    else:
        own_share, others = arrange_plain(out_grad, me, size, inner)
    arrived = [flip(value, (k + 1) * inner) for k, value in enumerate(others)]
    weight_messages, hidden_messages, arrived = lax.optimization_barrier((weight_messages, hidden_messages, arrived))
    weight_sides = gathered(down_weight, weight_messages, inner_bits)
    hidden_sides = gathered(hidden, hidden_messages, outer_bits)
    if split:
        swapped = [flip(value, 1, "mp") for value in arrived]
        shares = [own_share] + [
            jnp.concatenate([jnp.where(core == 0, a, b), jnp.where(core == 0, b, a)], axis=0)
            for a, b in zip(arrived, swapped)
        ]
    else:
        shares = [own_share] + arrived
    share = jnp.concatenate(shares, axis=0)
    share, weight_sides, hidden_sides = lax.optimization_barrier((share, weight_sides, hidden_sides))
    shares = [share[k * tokens : (k + 1) * tokens] for k in range(outer)]
    hidden_sides = [jnp.concatenate(side, axis=0) for side in hidden_sides]
    weight_sides = [jnp.concatenate(side, axis=0) for side in weight_sides]

    def grad_part(j, side):
        return lax.dot_general(
            share[:, j * rows : (j + 1) * rows],
            hidden_sides[side],
            (((0,), (0,)), ((), ())),
            preferred_element_type=jnp.float32,
        )

    def hidden_grad_part(k, side):
        return jnp.dot(shares[k], weight_sides[side], preferred_element_type=jnp.float32)

    product = jnp.concatenate(scatter(grad_part, inner_bits), axis=1)
    hidden_grad = jnp.concatenate(scatter(hidden_grad_part, outer_bits), axis=1)

    gate_late, up_late, hidden_grad = lax.optimization_barrier((gate_pre, up_pre, hidden_grad))
    activated, derivative = gelu_parts(gate_late.astype(jnp.float32))
    gate_grad = (hidden_grad * up_late.astype(jnp.float32) * derivative).astype(jnp.bfloat16)
    up_grad = (hidden_grad * activated).astype(jnp.bfloat16)

    grad = product * (1.0 / math.sqrt(tokens * size))
    decay = 1.0 - TRAIN_STEP ** (-0.8)
    total_rows = rows * size
    total_units = units * lax.axis_size("mp")
    powers = grad * grad
    squares = powers + 1e-30
    row_sum = lax.psum(jnp.sum(squares, axis=1), "mp")
    row_moment_new = decay * row_moment + (1.0 - decay) * (row_sum / total_units)
    col_part = jnp.sum(squares, axis=0)
    scaled_part = jnp.sum(powers / row_moment_new[:, None], axis=0)
    total_part = jnp.broadcast_to(jnp.sum(row_moment_new), (128,))
    sums = group_sum(jnp.concatenate([col_part, scaled_part, total_part]), all_bits)
    col_moment_new = decay * col_moment + (1.0 - decay) * (sums[:units] / total_rows)
    row_mean = sums[2 * units] / total_rows
    square_sum = row_mean * lax.psum(jnp.sum(sums[units : 2 * units] / col_moment_new), "mp")
    clip_norm = jnp.sqrt(square_sum / (total_rows * total_units))
    row_factor = jnp.sqrt(row_mean / row_moment_new) / jnp.maximum(1.0, clip_norm)
    col_factor = 1.0 / jnp.sqrt(col_moment_new)
    update = grad * row_factor[:, None] * col_factor[None, :]
    return (update, row_moment_new, col_moment_new, row_mean, gate_grad, up_grad)


def solution(mesh):
    in_specs = (P("dp", None), P("dp", "mp"), P("dp", "mp"), P("dp", "mp"), P("dp"), P("mp"))
    out_specs = (P("dp", "mp"), P("dp"), P("mp"), P(), P("dp", "mp"), P("dp", "mp"))
    return jax.shard_map(local, mesh=mesh, in_specs=in_specs, out_specs=out_specs, check_vma=False)
```

```python
import math

import jax
import jax.numpy as jnp
from jax import lax
from jax.experimental import pallas as pl
from jax.experimental.pallas import tpu as pltpu
from jax.sharding import PartitionSpec as P

TRAIN_STEP = 3
INNER_BITS = 2
PIECES = ((0, 0), (0, 1), (1, 0), (3, 0), (2, 1), (3, 1), (2, 0), (1, 1))


def gelu_parts(values):
    factor = math.sqrt(2.0 / math.pi)
    inner = factor * (values + 0.044715 * values * values * values)
    tangent = jnp.tanh(inner)
    activated = 0.5 * values * (1.0 + tangent)
    derivative = 0.5 * (1.0 + tangent) + 0.5 * values * (1.0 - tangent * tangent) * factor * (
        1.0 + 3.0 * 0.044715 * values * values
    )
    return (activated, derivative)


def flip(value, bits, axis="dp"):
    size = lax.axis_size(axis)
    return lax.ppermute(value, axis, [(i, i ^ bits) for i in range(size)])


def group_sum(value, bits):
    for at in range(0, len(bits), 2):
        pair = bits[at : at + 2]
        if len(pair) == 2:
            first, second = flip(value, pair[0]), flip(value, pair[1])
            value = (value + first) + (second + flip(value, pair[0] | pair[1]))
        else:
            value = value + flip(value, pair[0])
    return value


def general_products(out_grad, gate_pre, up_pre, down_weight, inner_bits, outer_bits):
    size = lax.axis_size("dp")
    me = lax.axis_index("dp")
    tokens, rows = out_grad.shape[0], down_weight.shape[0]
    inner = 2 ** len(inner_bits)
    activated, _ = gelu_parts(gate_pre.astype(jnp.float32))
    hidden = (activated * up_pre.astype(jnp.float32)).astype(jnp.bfloat16)
    by_block = out_grad.reshape(tokens, size, rows).transpose(1, 0, 2)

    def features_of(k):
        picks = [lax.dynamic_index_in_dim(by_block, me ^ (k * inner + j), 0, keepdims=False) for j in range(inner)]
        return jnp.concatenate(picks, axis=1)

    def gather(block, bits):
        blocks = [block]
        for bit in bits:
            blocks = blocks + [flip(b, bit) for b in blocks]
        return jnp.concatenate(blocks, axis=0)

    def scatter(values, bits):
        for level in reversed(range(len(bits))):
            count = 2**level
            values = [
                values[j] + flip(values[j + count].astype(jnp.bfloat16), bits[level]).astype(jnp.float32)
                for j in range(count)
            ]
        return values[0]

    shares = [features_of(0)] + [flip(features_of(k), k * inner) for k in range(1, size // inner)]
    share = jnp.concatenate(shares, axis=0)
    hidden_all = gather(hidden, outer_bits)
    weight_all = gather(down_weight, inner_bits)
    product = scatter(
        [
            lax.dot_general(
                share[:, j * rows : (j + 1) * rows],
                hidden_all,
                (((0,), (0,)), ((), ())),
                preferred_element_type=jnp.float32,
            )
            for j in range(inner)
        ],
        inner_bits,
    )
    hidden_grad = scatter(
        [jnp.dot(x, weight_all, preferred_element_type=jnp.float32) for x in shares],
        outer_bits,
    )
    return product, hidden_grad


def first_stage(out_grad, gate_pre, up_pre, place, rows):
    tokens, units = gate_pre.shape
    quarter = rows // 2
    share_width = 4 * rows
    step = 32

    def kernel(place, source, gate, up, own, hidden, message1, message2, message3):
        me, core = place[0], place[1]

        def column(k, block, half):
            at = (me ^ (4 * k + block)) * rows + half * quarter
            return pl.ds(pl.multiple_of(at, quarter), quarter)

        for p, (block, half) in enumerate(PIECES):
            own[:, p * quarter : (p + 1) * quarter] = source[:, column(0, block, half)]
        for k, target, base in ((1, message1, units), (2, message2, units), (3, message3, 0)):
            for p in range(4):
                block = jnp.where(core == 0, PIECES[p][0], PIECES[p + 4][0])
                half = jnp.where(core == 0, PIECES[p][1], PIECES[p + 4][1])
                target[:, base + p * quarter : base + (p + 1) * quarter] = source[:, column(k, block, half)]

        @pl.loop(0, tokens // step)
        def _(i):
            here = pl.ds(pl.multiple_of(i * step, step), step)
            activated, _ = gelu_parts(gate[here, :].astype(jnp.float32))
            value = (activated * up[here, :].astype(jnp.float32)).astype(jnp.bfloat16)
            hidden[here, :] = value
            message1[here, :units] = value
            message2[here, :units] = value

    wide = jax.ShapeDtypeStruct((tokens, units + share_width // 2), jnp.bfloat16)
    vmem = pl.BlockSpec(memory_space=pltpu.VMEM)
    return pl.pallas_call(
        kernel,
        out_shape=[
            jax.ShapeDtypeStruct((tokens, share_width), jnp.bfloat16),
            jax.ShapeDtypeStruct((tokens, units), jnp.bfloat16),
            wide,
            wide,
            jax.ShapeDtypeStruct((tokens, share_width // 2), jnp.bfloat16),
        ],
        in_specs=[pl.BlockSpec(memory_space=pltpu.SMEM), vmem, vmem, vmem],
        out_specs=[vmem] * 5,
        compiler_params=pltpu.CompilerParams(vmem_limit_bytes=24 << 20),
        cost_estimate=pl.CostEstimate(
            flops=20 * tokens * units, bytes_accessed=16 * tokens * units, transcendentals=tokens * units
        ),
    )(place, out_grad, gate_pre, up_pre)


def staged_products(out_grad, gate_pre, up_pre, down_weight):
    x_bit, y_bit, z_bit, w_bit = 1, 2, 4, 8
    me, core = lax.axis_index("dp"), lax.axis_index("mp")
    tokens, units = gate_pre.shape
    rows = down_weight.shape[0]
    q, t = rows // 2, tokens // 2
    place = jnp.stack([me, core]).astype(jnp.int32)
    own, hidden, message1, message2, message3 = first_stage(out_grad, gate_pre, up_pre, place, rows)

    weight1, weight2 = flip(down_weight, x_bit), flip(down_weight, y_bit)
    message1, message2, message3 = flip(message1, z_bit), flip(message2, w_bit), flip(message3, z_bit | w_bit)
    weight1, weight2, message1, message2, message3 = lax.optimization_barrier(
        (weight1, weight2, message1, message2, message3)
    )

    hidden3a = flip(message1[:t, :units], w_bit)
    hidden3b = flip(message2[t:, :units], z_bit)
    weight3a = flip(weight1[:q], y_bit)
    weight3b = flip(weight2[q:], x_bit)
    mine = jnp.concatenate([message1[:, units:], message2[:, units:], message3], axis=1)
    theirs = flip(mine, 1, "mp")
    hidden3a, hidden3b, weight3a, weight3b, theirs = lax.optimization_barrier(
        (hidden3a, hidden3b, weight3a, weight3b, theirs)
    )

    def features(k):
        a, b = mine[:, (k - 1) * 2 * rows : k * 2 * rows], theirs[:, (k - 1) * 2 * rows : k * 2 * rows]
        return jnp.concatenate([jnp.where(core == 0, a, b), jnp.where(core == 0, b, a)], axis=1)

    peers = [own] + [features(k) for k in range(1, 4)]
    share = jnp.concatenate([peers[k][h * t : (h + 1) * t] for k, h in PIECES], axis=0)
    hidden_all = jnp.concatenate(
        [hidden, message1[:t, :units], hidden3a, message2[t:, :units], hidden3b, message2[:t, :units], message1[t:, :units]],
        axis=0,
    )
    weight_all = jnp.concatenate(
        [down_weight, weight1[:q], weight3a, weight2[q:], weight3b, weight2[:q], weight1[q:]], axis=0
    )

    def grad_rows(begin, end):
        return lax.dot_general(
            share[:, begin * q : end * q], hidden_all, (((0,), (0,)), ((), ())), preferred_element_type=jnp.float32
        )

    def hidden_grad_rows(begin, end):
        return jnp.dot(share[begin * t : end * t], weight_all, preferred_element_type=jnp.float32)

    def scatter(part, size, low, high):
        from_low = flip(part(2, 4).astype(jnp.bfloat16), low)
        from_high = flip(part(4, 6).astype(jnp.bfloat16), high)
        last_a = flip((part(6, 7) + from_low[size:].astype(jnp.float32)).astype(jnp.bfloat16), high)
        last_b = flip((part(7, 8) + from_high[size:].astype(jnp.float32)).astype(jnp.bfloat16), low)
        kept = jnp.concatenate([from_low[:size], from_high[:size]], axis=0).astype(jnp.float32)
        last = jnp.concatenate([last_a, last_b], axis=0).astype(jnp.float32)
        return part(0, 2) + kept + last

    product = scatter(grad_rows, q, x_bit, y_bit)
    hidden_grad = scatter(hidden_grad_rows, t, z_bit, w_bit)
    return product, hidden_grad


def local(out_grad, gate_pre, up_pre, down_weight, row_moment, col_moment):
    size = lax.axis_size("dp")
    rows, units = down_weight.shape
    tokens = out_grad.shape[0]
    all_bits = [1 << b for b in range(size.bit_length() - 1)]
    staged = size == 16 and lax.axis_size("mp") == 2 and rows % 256 == 0 and tokens % 32 == 0 and units % 128 == 0
    if staged:
        product, hidden_grad = staged_products(out_grad, gate_pre, up_pre, down_weight)
    else:
        product, hidden_grad = general_products(
            out_grad, gate_pre, up_pre, down_weight, all_bits[:INNER_BITS], all_bits[INNER_BITS:]
        )

    gate_late, up_late, hidden_grad = lax.optimization_barrier((gate_pre, up_pre, hidden_grad))
    activated, derivative = gelu_parts(gate_late.astype(jnp.float32))
    gate_grad = (hidden_grad * up_late.astype(jnp.float32) * derivative).astype(jnp.bfloat16)
    up_grad = (hidden_grad * activated).astype(jnp.bfloat16)

    grad = product * (1.0 / math.sqrt(tokens * size))
    decay = 1.0 - TRAIN_STEP ** (-0.8)
    total_rows = rows * size
    total_units = units * lax.axis_size("mp")
    powers = grad * grad
    squares = powers + 1e-30
    row_sum = lax.psum(jnp.sum(squares, axis=1), "mp")
    row_moment_new = decay * row_moment + (1.0 - decay) * (row_sum / total_units)
    col_part = jnp.sum(squares, axis=0)
    scaled_part = jnp.sum(powers / row_moment_new[:, None], axis=0)
    total_part = jnp.broadcast_to(jnp.sum(row_moment_new), (128,))
    sums = group_sum(jnp.concatenate([col_part, scaled_part, total_part]), all_bits)
    col_moment_new = decay * col_moment + (1.0 - decay) * (sums[:units] / total_rows)
    row_mean = sums[2 * units] / total_rows
    square_sum = row_mean * lax.psum(jnp.sum(sums[units : 2 * units] / col_moment_new), "mp")
    clip_norm = jnp.sqrt(square_sum / (total_rows * total_units))
    row_factor = jnp.sqrt(row_mean / row_moment_new) / jnp.maximum(1.0, clip_norm)
    col_factor = 1.0 / jnp.sqrt(col_moment_new)
    update = grad * row_factor[:, None] * col_factor[None, :]
    return (update, row_moment_new, col_moment_new, row_mean, gate_grad, up_grad)


def solution(mesh):
    in_specs = (P("dp", None), P("dp", "mp"), P("dp", "mp"), P("dp", "mp"), P("dp"), P("mp"))
    out_specs = (P("dp", "mp"), P("dp"), P("mp"), P(), P("dp", "mp"), P("dp", "mp"))
    return jax.shard_map(local, mesh=mesh, in_specs=in_specs, out_specs=out_specs, check_vma=False)
```

```python
import math

import jax
import jax.numpy as jnp
from jax import lax
from jax.experimental import pallas as pl
from jax.experimental.pallas import tpu as pltpu
from jax.sharding import PartitionSpec as P

TRAIN_STEP = 3
INNER_BITS = 2
PIECES = ((0, 0), (0, 1), (1, 0), (3, 0), (2, 1), (3, 1), (2, 0), (1, 1))


def gelu_parts(values):
    factor = math.sqrt(2.0 / math.pi)
    inner = factor * (values + 0.044715 * values * values * values)
    tangent = jnp.tanh(inner)
    activated = 0.5 * values * (1.0 + tangent)
    derivative = 0.5 * (1.0 + tangent) + 0.5 * values * (1.0 - tangent * tangent) * factor * (
        1.0 + 3.0 * 0.044715 * values * values
    )
    return (activated, derivative)


def flip(value, bits, axis="dp"):
    size = lax.axis_size(axis)
    return lax.ppermute(value, axis, [(i, i ^ bits) for i in range(size)])


def group_sum(value, bits):
    for bit in bits:
        value = value + flip(value, bit)
    return value


def general_products(out_grad, gate_pre, up_pre, down_weight, inner_bits, outer_bits):
    size = lax.axis_size("dp")
    me = lax.axis_index("dp")
    tokens, rows = out_grad.shape[0], down_weight.shape[0]
    inner = 2 ** len(inner_bits)
    activated, _ = gelu_parts(gate_pre.astype(jnp.float32))
    hidden = (activated * up_pre.astype(jnp.float32)).astype(jnp.bfloat16)
    by_block = out_grad.reshape(tokens, size, rows).transpose(1, 0, 2)

    def features_of(k):
        picks = [lax.dynamic_index_in_dim(by_block, me ^ (k * inner + j), 0, keepdims=False) for j in range(inner)]
        return jnp.concatenate(picks, axis=1)

    def gather(block, bits):
        blocks = [block]
        for bit in bits:
            blocks = blocks + [flip(b, bit) for b in blocks]
        return jnp.concatenate(blocks, axis=0)

    def scatter(values, bits):
        for level in reversed(range(len(bits))):
            count = 2**level
            values = [
                values[j] + flip(values[j + count].astype(jnp.bfloat16), bits[level]).astype(jnp.float32)
                for j in range(count)
            ]
        return values[0]

    shares = [features_of(0)] + [flip(features_of(k), k * inner) for k in range(1, size // inner)]
    share = jnp.concatenate(shares, axis=0)
    hidden_all = gather(hidden, outer_bits)
    weight_all = gather(down_weight, inner_bits)
    product = scatter(
        [
            lax.dot_general(
                share[:, j * rows : (j + 1) * rows],
                hidden_all,
                (((0,), (0,)), ((), ())),
                preferred_element_type=jnp.float32,
            )
            for j in range(inner)
        ],
        inner_bits,
    )
    hidden_grad = scatter(
        [jnp.dot(x, weight_all, preferred_element_type=jnp.float32) for x in shares],
        outer_bits,
    )
    return product, hidden_grad


def first_stage(out_grad, gate_pre, up_pre, place, rows):
    tokens, units = gate_pre.shape
    quarter = rows // 2
    share_width = 4 * rows
    step = 32

    def kernel(place, source, gate, up, own, hidden, message1, message2, message3):
        me, core = place[0], place[1]

        def column(k, block, half):
            at = (me ^ (4 * k + block)) * rows + half * quarter
            return pl.ds(pl.multiple_of(at, quarter), quarter)

        for p, (block, half) in enumerate(PIECES):
            own[:, p * quarter : (p + 1) * quarter] = source[:, column(0, block, half)]
        for k, target, base in ((1, message1, units), (2, message2, units), (3, message3, 0)):
            for p in range(4):
                block = jnp.where(core == 0, PIECES[p][0], PIECES[p + 4][0])
                half = jnp.where(core == 0, PIECES[p][1], PIECES[p + 4][1])
                target[:, base + p * quarter : base + (p + 1) * quarter] = source[:, column(k, block, half)]

        @pl.loop(0, tokens // step)
        def _(i):
            here = pl.ds(pl.multiple_of(i * step, step), step)
            activated, _ = gelu_parts(gate[here, :].astype(jnp.float32))
            value = (activated * up[here, :].astype(jnp.float32)).astype(jnp.bfloat16)
            hidden[here, :] = value
            message1[here, :units] = value
            message2[here, :units] = value

    wide = jax.ShapeDtypeStruct((tokens, units + share_width // 2), jnp.bfloat16)
    vmem = pl.BlockSpec(memory_space=pltpu.VMEM)
    return pl.pallas_call(
        kernel,
        out_shape=[
            jax.ShapeDtypeStruct((tokens, share_width), jnp.bfloat16),
            jax.ShapeDtypeStruct((tokens, units), jnp.bfloat16),
            wide,
            wide,
            jax.ShapeDtypeStruct((tokens, share_width // 2), jnp.bfloat16),
        ],
        in_specs=[pl.BlockSpec(memory_space=pltpu.SMEM), vmem, vmem, vmem],
        out_specs=[vmem] * 5,
        compiler_params=pltpu.CompilerParams(vmem_limit_bytes=24 << 20),
        cost_estimate=pl.CostEstimate(
            flops=20 * tokens * units, bytes_accessed=16 * tokens * units, transcendentals=tokens * units
        ),
    )(place, out_grad, gate_pre, up_pre)


def cut(sources, parts):
    def kernel(*refs):
        ins, outs, sems = refs[: len(sources)], refs[len(sources) : -1], refs[-1]
        copies = [
            pltpu.make_async_copy(ins[i].at[pl.ds(*rows), pl.ds(*columns)], outs[n], sems.at[n])
            for n, (i, rows, columns) in enumerate(parts)
        ]
        for copy in copies:
            copy.start()
        for copy in copies:
            copy.wait()

    shapes = [jax.ShapeDtypeStruct((rows[1], columns[1]), sources[i].dtype) for i, rows, columns in parts]
    return pl.pallas_call(
        kernel,
        out_shape=shapes,
        in_specs=[pl.BlockSpec(memory_space=pl.ANY)] * len(sources),
        out_specs=[pl.BlockSpec(memory_space=pl.ANY)] * len(parts),
        scratch_shapes=[pltpu.SemaphoreType.DMA((len(parts),))],
        compiler_params=pltpu.CompilerParams(vmem_limit_bytes=4 << 20),
        cost_estimate=pl.CostEstimate(
            flops=0, bytes_accessed=sum(4 * r[1] * c[1] for _, r, c in parts), transcendentals=0
        ),
    )(*sources)


def product(share, pieces, layout, outputs, over_rows, tile):
    units = min(piece.shape[1] for piece in pieces)
    depth = sum(rows for _, _, rows in layout)

    def kernel(*refs):
        share_ref, ins = refs[0], refs[1 : 1 + len(pieces)]
        outs, stack = refs[1 + len(pieces) : -1], refs[-1]
        at = 0
        for piece, first, rows in layout:
            stack[at : at + rows, :] = ins[piece][first : first + rows, :]
            at += rows
        for (begin, end, kind), out in zip(outputs, outs):
            if over_rows:
                value = lax.dot_general(
                    share_ref[:, begin:end], stack[...], (((0,), (0,)), ((), ())), preferred_element_type=jnp.float32
                )
            else:
                value = jnp.dot(share_ref[begin:end, :], stack[...], preferred_element_type=jnp.float32)
            out[...] = value.astype(kind)

    total = sum(end - begin for begin, end, _ in outputs)
    return pl.pallas_call(
        kernel,
        grid=(units // tile,),
        out_shape=[jax.ShapeDtypeStruct((end - begin, units), kind) for begin, end, kind in outputs],
        in_specs=[pl.BlockSpec(share.shape, lambda i: (0, 0))]
        + [pl.BlockSpec((piece.shape[0], tile), lambda i: (0, i)) for piece in pieces],
        out_specs=[pl.BlockSpec((end - begin, tile), lambda i: (0, i)) for begin, end, _ in outputs],
        scratch_shapes=[pltpu.VMEM((depth, tile), jnp.bfloat16)],
        compiler_params=pltpu.CompilerParams(vmem_limit_bytes=24 << 20),
        cost_estimate=pl.CostEstimate(
            flops=2 * total * depth * units,
            bytes_accessed=2 * (depth + 2 * total) * units + 2 * share.size,
            transcendentals=0,
        ),
    )(share, *pieces)


def staged_products(out_grad, gate_pre, up_pre, down_weight):
    x_bit, y_bit, z_bit, w_bit = 1, 2, 4, 8
    me, core = lax.axis_index("dp"), lax.axis_index("mp")
    tokens, units = gate_pre.shape
    rows = down_weight.shape[0]
    q, t = rows // 2, tokens // 2
    place = jnp.stack([me, core]).astype(jnp.int32)
    own, hidden, message1, message2, message3 = first_stage(out_grad, gate_pre, up_pre, place, rows)

    down_weight, message1 = lax.optimization_barrier((down_weight, message1))
    message1, message2, message3 = flip(message1, z_bit), flip(message2, w_bit), flip(message3, z_bit | w_bit)
    weight1, weight2 = flip(down_weight, x_bit), flip(down_weight, y_bit)
    whole, top, bottom = (0, units), (0, q), (q, q)
    to_y, to_x = cut([weight1, weight2], [(0, top, whole), (1, bottom, whole)])
    weight3a, weight3b = flip(to_y, y_bit), flip(to_x, x_bit)

    message1, message2, message3, _, _ = lax.optimization_barrier((message1, message2, message3, weight1, weight2))
    extra = (units, 2 * rows)
    to_w, to_z, mine1, mine2 = cut(
        [message1, message2], [(0, (0, t), whole), (1, (t, t), whole), (0, (0, tokens), extra), (1, (0, tokens), extra)]
    )
    hidden3a, hidden3b = flip(to_w, w_bit), flip(to_z, z_bit)
    mine = jnp.concatenate([mine1, mine2, message3], axis=1)
    theirs = flip(mine, 1, "mp")

    def features(k):
        a, b = mine[:, (k - 1) * 2 * rows : k * 2 * rows], theirs[:, (k - 1) * 2 * rows : k * 2 * rows]
        return jnp.concatenate([jnp.where(core == 0, a, b), jnp.where(core == 0, b, a)], axis=1)

    peers = [own] + [features(k) for k in range(1, 4)]
    share = jnp.concatenate([peers[k][h * t : (h + 1) * t] for k, h in PIECES], axis=0)

    def layout(size):
        return [(0, 0, 2 * size), (1, 0, size), (3, 0, size), (2, size, size), (4, 0, size), (2, 0, size), (1, size, size)]

    def scatter(pieces, depth, size, low, high, over_rows):
        tile = 512
        send, keep = jnp.bfloat16, jnp.float32
        low_part, high_part = product(
            share, pieces, layout(depth), [(2 * size, 4 * size, send), (4 * size, 6 * size, send)], over_rows, tile
        )
        from_low, from_high = flip(low_part, low), flip(high_part, high)
        own_part, a_part, b_part = product(
            share,
            pieces,
            layout(depth),
            [(0, 2 * size, keep), (6 * size, 7 * size, keep), (7 * size, 8 * size, keep)],
            over_rows,
            tile,
        )
        last_a = flip((a_part + from_low[size:].astype(keep)).astype(send), high)
        last_b = flip((b_part + from_high[size:].astype(keep)).astype(send), low)
        kept = own_part + jnp.concatenate([from_low[:size], from_high[:size]], axis=0).astype(keep)
        return kept + jnp.concatenate([last_a, last_b], axis=0).astype(keep), low_part

    grad, sent = scatter([hidden, message1, message2, hidden3a, hidden3b], t, q, x_bit, y_bit, True)
    weight3a, weight3b, _ = lax.optimization_barrier((weight3a, weight3b, sent))
    hidden_grad, _ = scatter([down_weight, weight1, weight2, weight3a, weight3b], q, t, z_bit, w_bit, False)
    return grad, hidden_grad


def local(out_grad, gate_pre, up_pre, down_weight, row_moment, col_moment):
    size = lax.axis_size("dp")
    rows, units = down_weight.shape
    tokens = out_grad.shape[0]
    all_bits = [1 << b for b in range(size.bit_length() - 1)]
    staged = size == 16 and lax.axis_size("mp") == 2 and rows % 256 == 0 and tokens % 32 == 0 and units % 512 == 0
    if staged:
        product, hidden_grad = staged_products(out_grad, gate_pre, up_pre, down_weight)
    else:
        product, hidden_grad = general_products(
            out_grad, gate_pre, up_pre, down_weight, all_bits[:INNER_BITS], all_bits[INNER_BITS:]
        )

    activated, derivative = gelu_parts(gate_pre.astype(jnp.float32))
    gate_grad = (hidden_grad * up_pre.astype(jnp.float32) * derivative).astype(jnp.bfloat16)
    up_grad = (hidden_grad * activated).astype(jnp.bfloat16)

    grad = product * (1.0 / math.sqrt(tokens * size))
    decay = 1.0 - TRAIN_STEP ** (-0.8)
    total_rows = rows * size
    total_units = units * lax.axis_size("mp")
    powers = grad * grad
    squares = powers + 1e-30
    row_sum = lax.psum(jnp.sum(squares, axis=1), "mp")
    row_moment_new = decay * row_moment + (1.0 - decay) * (row_sum / total_units)
    col_part = jnp.sum(squares, axis=0)
    scaled_part = jnp.sum(powers / row_moment_new[:, None], axis=0)
    total_part = jnp.broadcast_to(jnp.sum(row_moment_new), (128,))
    sums = group_sum(jnp.concatenate([col_part, scaled_part, total_part]), all_bits)
    col_moment_new = decay * col_moment + (1.0 - decay) * (sums[:units] / total_rows)
    row_mean = sums[2 * units] / total_rows
    square_sum = row_mean * lax.psum(jnp.sum(sums[units : 2 * units] / col_moment_new), "mp")
    clip_norm = jnp.sqrt(square_sum / (total_rows * total_units))
    row_factor = jnp.sqrt(row_mean / row_moment_new) / jnp.maximum(1.0, clip_norm)
    col_factor = 1.0 / jnp.sqrt(col_moment_new)
    update = grad * row_factor[:, None] * col_factor[None, :]
    return (update, row_moment_new, col_moment_new, row_mean, gate_grad, up_grad)


def solution(mesh):
    in_specs = (P("dp", None), P("dp", "mp"), P("dp", "mp"), P("dp", "mp"), P("dp"), P("mp"))
    out_specs = (P("dp", "mp"), P("dp"), P("mp"), P(), P("dp", "mp"), P("dp", "mp"))
    return jax.shard_map(local, mesh=mesh, in_specs=in_specs, out_specs=out_specs, check_vma=False)
```

```python
import math

import jax
import jax.numpy as jnp
from jax import lax
from jax.experimental import pallas as pl
from jax.experimental.pallas import tpu as pltpu
from jax.sharding import PartitionSpec as P

TRAIN_STEP = 3
INNER_BITS = 2
PIECES = ((0, 0), (0, 1), (1, 0), (3, 0), (2, 1), (3, 1), (2, 0), (1, 1))


def gelu_parts(values):
    factor = math.sqrt(2.0 / math.pi)
    inner = factor * (values + 0.044715 * values * values * values)
    tangent = jnp.tanh(inner)
    activated = 0.5 * values * (1.0 + tangent)
    derivative = 0.5 * (1.0 + tangent) + 0.5 * values * (1.0 - tangent * tangent) * factor * (
        1.0 + 3.0 * 0.044715 * values * values
    )
    return (activated, derivative)


def flip(value, bits, axis="dp"):
    size = lax.axis_size(axis)
    return lax.ppermute(value, axis, [(i, i ^ bits) for i in range(size)])


def group_sum(value, bits):
    size = lax.axis_size("dp")
    for bit in bits:
        pairs = [[i, i | bit] for i in range(size) if not i & bit]
        value = lax.psum(value, "dp", axis_index_groups=pairs)
    return value


def general_products(out_grad, gate_pre, up_pre, down_weight, inner_bits, outer_bits):
    size = lax.axis_size("dp")
    me = lax.axis_index("dp")
    tokens, rows = out_grad.shape[0], down_weight.shape[0]
    inner = 2 ** len(inner_bits)
    activated, _ = gelu_parts(gate_pre.astype(jnp.float32))
    hidden = (activated * up_pre.astype(jnp.float32)).astype(jnp.bfloat16)
    by_block = out_grad.reshape(tokens, size, rows).transpose(1, 0, 2)

    def features_of(k):
        picks = [lax.dynamic_index_in_dim(by_block, me ^ (k * inner + j), 0, keepdims=False) for j in range(inner)]
        return jnp.concatenate(picks, axis=1)

    def gather(block, bits):
        blocks = [block]
        for bit in bits:
            blocks = blocks + [flip(b, bit) for b in blocks]
        return jnp.concatenate(blocks, axis=0)

    def scatter(values, bits):
        for level in reversed(range(len(bits))):
            count = 2**level
            values = [
                values[j] + flip(values[j + count].astype(jnp.bfloat16), bits[level]).astype(jnp.float32)
                for j in range(count)
            ]
        return values[0]

    shares = [features_of(0)] + [flip(features_of(k), k * inner) for k in range(1, size // inner)]
    share = jnp.concatenate(shares, axis=0)
    hidden_all = gather(hidden, outer_bits)
    weight_all = gather(down_weight, inner_bits)
    product = scatter(
        [
            lax.dot_general(
                share[:, j * rows : (j + 1) * rows],
                hidden_all,
                (((0,), (0,)), ((), ())),
                preferred_element_type=jnp.float32,
            )
            for j in range(inner)
        ],
        inner_bits,
    )
    hidden_grad = scatter(
        [jnp.dot(x, weight_all, preferred_element_type=jnp.float32) for x in shares],
        outer_bits,
    )
    return product, hidden_grad


def first_stage(out_grad, gate_pre, up_pre, place, rows):
    tokens, units = gate_pre.shape
    quarter = rows // 2
    share_width = 4 * rows
    step = 32

    def kernel(place, source_hbm, gate_hbm, up_hbm, own, hidden, message1, message2, message3, source, gate, up, sems):
        copies = [
            pltpu.make_async_copy(there, here, sems.at[n])
            for n, (there, here) in enumerate(((gate_hbm, gate), (up_hbm, up), (source_hbm, source)))
        ]
        for copy in copies:
            copy.start()
        me, core = place[0], place[1]

        def column(k, block, half):
            at = (me ^ (4 * k + block)) * rows + half * quarter
            return pl.ds(pl.multiple_of(at, quarter), quarter)

        copies[0].wait()
        copies[1].wait()

        @pl.loop(0, tokens // step)
        def _(i):
            here = pl.ds(pl.multiple_of(i * step, step), step)
            activated, _ = gelu_parts(gate[here, :].astype(jnp.float32))
            value = (activated * up[here, :].astype(jnp.float32)).astype(jnp.bfloat16)
            hidden[here, :] = value
            message1[here, :units] = value
            message2[here, :units] = value

        copies[2].wait()
        for p, (block, half) in enumerate(PIECES):
            own[:, p * quarter : (p + 1) * quarter] = source[:, column(0, block, half)]
        for k, target, base in ((1, message1, units), (2, message2, units), (3, message3, 0)):
            for p in range(4):
                block = jnp.where(core == 0, PIECES[p][0], PIECES[p + 4][0])
                half = jnp.where(core == 0, PIECES[p][1], PIECES[p + 4][1])
                target[:, base + p * quarter : base + (p + 1) * quarter] = source[:, column(k, block, half)]

    wide = jax.ShapeDtypeStruct((tokens, units + share_width // 2), jnp.bfloat16)
    vmem = pl.BlockSpec(memory_space=pltpu.VMEM)
    return pl.pallas_call(
        kernel,
        out_shape=[
            jax.ShapeDtypeStruct((tokens, share_width), jnp.bfloat16),
            jax.ShapeDtypeStruct((tokens, units), jnp.bfloat16),
            wide,
            wide,
            jax.ShapeDtypeStruct((tokens, share_width // 2), jnp.bfloat16),
        ],
        in_specs=[pl.BlockSpec(memory_space=pltpu.SMEM)] + [pl.BlockSpec(memory_space=pltpu.HBM)] * 3,
        out_specs=[vmem] * 5,
        scratch_shapes=[
            pltpu.VMEM(out_grad.shape, jnp.bfloat16),
            pltpu.VMEM(gate_pre.shape, jnp.bfloat16),
            pltpu.VMEM(up_pre.shape, jnp.bfloat16),
            pltpu.SemaphoreType.DMA((3,)),
        ],
        compiler_params=pltpu.CompilerParams(vmem_limit_bytes=16 << 20),
        cost_estimate=pl.CostEstimate(
            flops=20 * tokens * units, bytes_accessed=16 * tokens * units, transcendentals=tokens * units
        ),
    )(place, out_grad, gate_pre, up_pre)


def cut(sources, parts, shapes):
    def kernel(*refs):
        ins, outs, sems = refs[: len(sources)], refs[len(sources) : -1], refs[-1]
        copies = [
            pltpu.make_async_copy(
                ins[i].at[pl.ds(*rows), pl.ds(*columns)], outs[o].at[:, pl.ds(at, columns[1])], sems.at[n]
            )
            for n, (i, rows, columns, o, at) in enumerate(parts)
        ]
        for copy in copies:
            copy.start()
        for copy in copies:
            copy.wait()

    return pl.pallas_call(
        kernel,
        out_shape=[jax.ShapeDtypeStruct(shape, jnp.bfloat16) for shape in shapes],
        in_specs=[pl.BlockSpec(memory_space=pltpu.HBM)] * len(sources),
        out_specs=[pl.BlockSpec(memory_space=pltpu.HBM)] * len(shapes),
        scratch_shapes=[pltpu.SemaphoreType.DMA((len(parts),))],
        compiler_params=pltpu.CompilerParams(vmem_limit_bytes=4 << 20),
        cost_estimate=pl.CostEstimate(
            flops=0, bytes_accessed=sum(4 * math.prod(shape) for shape in shapes), transcendentals=0
        ),
    )(*sources)


def product(share, pieces, layout, outputs, over_rows, tile):
    units = min(piece.shape[1] for piece in pieces)
    depth = sum(rows for _, _, rows in layout)

    def kernel(*refs):
        share_ref, ins = refs[0], refs[1 : 1 + len(pieces)]
        outs, stack = refs[1 + len(pieces) : -1], refs[-1]
        at = 0
        for piece, first, rows in layout:
            stack[at : at + rows, :] = ins[piece][first : first + rows, :]
            at += rows
        for (begin, end, kind), out in zip(outputs, outs):
            if over_rows:
                value = lax.dot_general(
                    share_ref[:, begin:end], stack[...], (((0,), (0,)), ((), ())), preferred_element_type=jnp.float32
                )
            else:
                value = jnp.dot(share_ref[begin:end, :], stack[...], preferred_element_type=jnp.float32)
            out[...] = value.astype(kind)

    total = sum(end - begin for begin, end, _ in outputs)
    return pl.pallas_call(
        kernel,
        grid=(units // tile,),
        out_shape=[jax.ShapeDtypeStruct((end - begin, units), kind) for begin, end, kind in outputs],
        in_specs=[pl.BlockSpec(share.shape, lambda i: (0, 0))]
        + [pl.BlockSpec((piece.shape[0], tile), lambda i: (0, i)) for piece in pieces],
        out_specs=[pl.BlockSpec((end - begin, tile), lambda i: (0, i)) for begin, end, _ in outputs],
        scratch_shapes=[pltpu.VMEM((depth, tile), jnp.bfloat16)],
        compiler_params=pltpu.CompilerParams(vmem_limit_bytes=24 << 20),
        cost_estimate=pl.CostEstimate(
            flops=2 * total * depth * units,
            bytes_accessed=2 * (depth + 2 * total) * units + 2 * share.size,
            transcendentals=0,
        ),
    )(share, *pieces)


def staged_products(out_grad, gate_pre, up_pre, down_weight):
    x_bit, y_bit, z_bit, w_bit = 1, 2, 4, 8
    me, core = lax.axis_index("dp"), lax.axis_index("mp")
    tokens, units = gate_pre.shape
    rows = down_weight.shape[0]
    q, t = rows // 2, tokens // 2
    place = jnp.stack([me, core]).astype(jnp.int32)
    own, hidden, message1, message2, message3 = first_stage(out_grad, gate_pre, up_pre, place, rows)

    down_weight, message1 = lax.optimization_barrier((down_weight, message1))
    message1, message2, message3 = flip(message1, z_bit), flip(message2, w_bit), flip(message3, z_bit | w_bit)
    weight1, weight2 = flip(down_weight, x_bit), flip(down_weight, y_bit)
    whole = (0, units)
    to_y, to_x = cut([weight1, weight2], [(0, (0, q), whole, 0, 0), (1, (q, q), whole, 1, 0)], [(q, units)] * 2)
    weight3a, weight3b = flip(to_y, y_bit), flip(to_x, x_bit)

    message1, message2, message3, _, _ = lax.optimization_barrier((message1, message2, message3, to_y, to_x))
    extra, every = (units, 2 * rows), (0, tokens)
    to_w, to_z, mine = cut(
        [message1, message2, message3],
        [
            (0, (0, t), whole, 0, 0),
            (1, (t, t), whole, 1, 0),
            (0, every, extra, 2, 0),
            (1, every, extra, 2, 2 * rows),
            (2, every, (0, 2 * rows), 2, 4 * rows),
        ],
        [(t, units), (t, units), (tokens, 6 * rows)],
    )
    theirs = flip(mine, 1, "mp")
    hidden3a, hidden3b = flip(to_w, w_bit), flip(to_z, z_bit)

    def features(k):
        a, b = mine[:, (k - 1) * 2 * rows : k * 2 * rows], theirs[:, (k - 1) * 2 * rows : k * 2 * rows]
        return jnp.concatenate([jnp.where(core == 0, a, b), jnp.where(core == 0, b, a)], axis=1)

    peers = [own] + [features(k) for k in range(1, 4)]
    share = jnp.concatenate([peers[k][h * t : (h + 1) * t] for k, h in PIECES], axis=0)

    def layout(size):
        return [(0, 0, 2 * size), (1, 0, size), (3, 0, size), (2, size, size), (4, 0, size), (2, 0, size), (1, size, size)]

    def send_parts(pieces, depth, size, over_rows):
        kind = jnp.bfloat16
        return product(
            share, pieces, layout(depth), [(2 * size, 4 * size, kind), (4 * size, 6 * size, kind)], over_rows, 512
        )

    def keep_parts(pieces, depth, size, over_rows):
        kind = jnp.float32
        bounds = [(0, 2 * size, kind), (6 * size, 7 * size, kind), (7 * size, 8 * size, kind)]
        return product(share, pieces, layout(depth), bounds, over_rows, 512)

    def finish(parts, from_low, from_high, size, low, high):
        send, keep = jnp.bfloat16, jnp.float32
        own_part, a_part, b_part = parts
        last_a = flip((a_part + from_low[size:].astype(keep)).astype(send), high)
        last_b = flip((b_part + from_high[size:].astype(keep)).astype(send), low)
        kept = own_part + jnp.concatenate([from_low[:size], from_high[:size]], axis=0).astype(keep)
        return kept + jnp.concatenate([last_a, last_b], axis=0).astype(keep)

    weights = [down_weight, weight1, weight2, weight3a, weight3b]
    to_z, to_w = send_parts(weights, q, t, False)
    from_z, from_w = flip(to_z, z_bit), flip(to_w, w_bit)
    hidden3a, hidden3b, _ = lax.optimization_barrier((hidden3a, hidden3b, to_z))
    hiddens = [hidden, message1, message2, hidden3a, hidden3b]
    to_x, to_y = send_parts(hiddens, t, q, True)
    from_x, from_y = flip(to_x, x_bit), flip(to_y, y_bit)
    share, weight3a, weight3b, _ = lax.optimization_barrier((share, weight3a, weight3b, to_x))
    weights = [down_weight, weight1, weight2, weight3a, weight3b]
    grad = finish(keep_parts(hiddens, t, q, True), from_x, from_y, q, x_bit, y_bit)
    hidden_grad = finish(keep_parts(weights, q, t, False), from_z, from_w, t, z_bit, w_bit)
    return grad, hidden_grad


def local(out_grad, gate_pre, up_pre, down_weight, row_moment, col_moment):
    size = lax.axis_size("dp")
    rows, units = down_weight.shape
    tokens = out_grad.shape[0]
    all_bits = [1 << b for b in range(size.bit_length() - 1)]
    staged = size == 16 and lax.axis_size("mp") == 2 and rows % 256 == 0 and tokens % 32 == 0 and units % 512 == 0
    if staged:
        product, hidden_grad = staged_products(out_grad, gate_pre, up_pre, down_weight)
    else:
        product, hidden_grad = general_products(
            out_grad, gate_pre, up_pre, down_weight, all_bits[:INNER_BITS], all_bits[INNER_BITS:]
        )

    activated, derivative = gelu_parts(gate_pre.astype(jnp.float32))
    gate_grad = (hidden_grad * up_pre.astype(jnp.float32) * derivative).astype(jnp.bfloat16)
    up_grad = (hidden_grad * activated).astype(jnp.bfloat16)

    grad = product * (1.0 / math.sqrt(tokens * size))
    decay = 1.0 - TRAIN_STEP ** (-0.8)
    total_rows = rows * size
    total_units = units * lax.axis_size("mp")
    powers = grad * grad
    squares = powers + 1e-30
    row_sum = lax.psum(jnp.sum(squares, axis=1), "mp")
    row_moment_new = decay * row_moment + (1.0 - decay) * (row_sum / total_units)
    col_part = jnp.sum(squares, axis=0)
    scaled_part = jnp.sum(powers / row_moment_new[:, None], axis=0)
    total_part = jnp.broadcast_to(jnp.sum(row_moment_new), (128,))
    sums = group_sum(jnp.concatenate([col_part, scaled_part, total_part]), all_bits)
    col_moment_new = decay * col_moment + (1.0 - decay) * (sums[:units] / total_rows)
    row_mean = sums[2 * units] / total_rows
    ratios = jnp.sum((sums[units : 2 * units] / col_moment_new).reshape(-1, 128), axis=0)
    square_sum = row_mean * jnp.sum(lax.psum(ratios, "mp"))
    clip_norm = jnp.sqrt(square_sum / (total_rows * total_units))
    row_factor = jnp.sqrt(row_mean / row_moment_new) / jnp.maximum(1.0, clip_norm)
    col_factor = 1.0 / jnp.sqrt(col_moment_new)
    update = grad * row_factor[:, None] * col_factor[None, :]
    return (update, row_moment_new, col_moment_new, row_mean, gate_grad, up_grad)


def solution(mesh):
    in_specs = (P("dp", None), P("dp", "mp"), P("dp", "mp"), P("dp", "mp"), P("dp"), P("mp"))
    out_specs = (P("dp", "mp"), P("dp"), P("mp"), P(), P("dp", "mp"), P("dp", "mp"))
    return jax.shard_map(local, mesh=mesh, in_specs=in_specs, out_specs=out_specs, check_vma=False)
```

```python
import math

import jax
import jax.numpy as jnp
from jax import lax
from jax.experimental import pallas as pl
from jax.experimental.pallas import tpu as pltpu
from jax.sharding import PartitionSpec as P

TRAIN_STEP = 3
INNER_BITS = 2
EAGER = pl.CostEstimate(flops=0, bytes_accessed=0, transcendentals=0)
PIECES = ((0, 0), (0, 1), (1, 0), (3, 0), (2, 1), (3, 1), (2, 0), (1, 1))


def gelu_parts(values):
    factor = math.sqrt(2.0 / math.pi)
    inner = factor * (values + 0.044715 * values * values * values)
    tangent = jnp.tanh(inner)
    activated = 0.5 * values * (1.0 + tangent)
    derivative = 0.5 * (1.0 + tangent) + 0.5 * values * (1.0 - tangent * tangent) * factor * (
        1.0 + 3.0 * 0.044715 * values * values
    )
    return (activated, derivative)


def flip(value, bits, axis="dp"):
    size = lax.axis_size(axis)
    return lax.ppermute(value, axis, [(i, i ^ bits) for i in range(size)])


def group_sum(value, bits):
    for at in range(0, len(bits), 2):
        pair = bits[at : at + 2]
        if len(pair) == 2:
            first, second = flip(value, pair[0]), flip(value, pair[1])
            value = (value + first) + (second + flip(value, pair[0] | pair[1]))
        else:
            value = value + flip(value, pair[0])
    return value


def general_products(out_grad, gate_pre, up_pre, down_weight, inner_bits, outer_bits):
    size = lax.axis_size("dp")
    me = lax.axis_index("dp")
    tokens, rows = out_grad.shape[0], down_weight.shape[0]
    inner = 2 ** len(inner_bits)
    activated, _ = gelu_parts(gate_pre.astype(jnp.float32))
    hidden = (activated * up_pre.astype(jnp.float32)).astype(jnp.bfloat16)
    by_block = out_grad.reshape(tokens, size, rows).transpose(1, 0, 2)

    def features_of(k):
        picks = [lax.dynamic_index_in_dim(by_block, me ^ (k * inner + j), 0, keepdims=False) for j in range(inner)]
        return jnp.concatenate(picks, axis=1)

    def gather(block, bits):
        blocks = [block]
        for bit in bits:
            blocks = blocks + [flip(b, bit) for b in blocks]
        return jnp.concatenate(blocks, axis=0)

    def scatter(values, bits):
        for level in reversed(range(len(bits))):
            count = 2**level
            values = [
                values[j] + flip(values[j + count].astype(jnp.bfloat16), bits[level]).astype(jnp.float32)
                for j in range(count)
            ]
        return values[0]

    shares = [features_of(0)] + [flip(features_of(k), k * inner) for k in range(1, size // inner)]
    share = jnp.concatenate(shares, axis=0)
    hidden_all = gather(hidden, outer_bits)
    weight_all = gather(down_weight, inner_bits)
    product = scatter(
        [
            lax.dot_general(
                share[:, j * rows : (j + 1) * rows],
                hidden_all,
                (((0,), (0,)), ((), ())),
                preferred_element_type=jnp.float32,
            )
            for j in range(inner)
        ],
        inner_bits,
    )
    hidden_grad = scatter(
        [jnp.dot(x, weight_all, preferred_element_type=jnp.float32) for x in shares],
        outer_bits,
    )
    return product, hidden_grad


def first_stage(out_grad, gate_pre, up_pre, place, rows):
    tokens, units = gate_pre.shape
    quarter = rows // 2
    share_width = 4 * rows
    step = 32

    def kernel(place, source_hbm, gate_hbm, up_hbm, own, hidden, message1, message2, message3, source, gate, up, sems):
        copies = [
            pltpu.make_async_copy(there, here, sems.at[n])
            for n, (there, here) in enumerate(((gate_hbm, gate), (up_hbm, up), (source_hbm, source)))
        ]
        for copy in copies:
            copy.start()
        me, core = place[0], place[1]

        def column(k, block, half):
            at = (me ^ (4 * k + block)) * rows + half * quarter
            return pl.ds(pl.multiple_of(at, quarter), quarter)

        copies[0].wait()
        copies[1].wait()

        @pl.loop(0, tokens // step)
        def _(i):
            here = pl.ds(pl.multiple_of(i * step, step), step)
            activated, _ = gelu_parts(gate[here, :].astype(jnp.float32))
            value = (activated * up[here, :].astype(jnp.float32)).astype(jnp.bfloat16)
            hidden[here, :] = value
            message1[here, :units] = value
            message2[here, :units] = value

        copies[2].wait()
        for p, (block, half) in enumerate(PIECES):
            own[:, p * quarter : (p + 1) * quarter] = source[:, column(0, block, half)]
        for k, target, base in ((1, message1, units), (2, message2, units), (3, message3, 0)):
            for p in range(4):
                block = jnp.where(core == 0, PIECES[p][0], PIECES[p + 4][0])
                half = jnp.where(core == 0, PIECES[p][1], PIECES[p + 4][1])
                target[:, base + p * quarter : base + (p + 1) * quarter] = source[:, column(k, block, half)]

    wide = jax.ShapeDtypeStruct((tokens, units + share_width // 2), jnp.bfloat16)
    vmem = pl.BlockSpec(memory_space=pltpu.VMEM)
    return pl.pallas_call(
        kernel,
        out_shape=[
            jax.ShapeDtypeStruct((tokens, share_width), jnp.bfloat16),
            jax.ShapeDtypeStruct((tokens, units), jnp.bfloat16),
            wide,
            wide,
            jax.ShapeDtypeStruct((tokens, share_width // 2), jnp.bfloat16),
        ],
        in_specs=[pl.BlockSpec(memory_space=pltpu.SMEM)] + [pl.BlockSpec(memory_space=pltpu.HBM)] * 3,
        out_specs=[vmem] * 5,
        scratch_shapes=[
            pltpu.VMEM(out_grad.shape, jnp.bfloat16),
            pltpu.VMEM(gate_pre.shape, jnp.bfloat16),
            pltpu.VMEM(up_pre.shape, jnp.bfloat16),
            pltpu.SemaphoreType.DMA((3,)),
        ],
        compiler_params=pltpu.CompilerParams(vmem_limit_bytes=56 << 20),
        cost_estimate=EAGER,
    )(place, out_grad, gate_pre, up_pre)


def cut(sources, parts, shapes):
    def kernel(*refs):
        ins, outs, sems = refs[: len(sources)], refs[len(sources) : -1], refs[-1]
        copies = [
            pltpu.make_async_copy(
                ins[i].at[pl.ds(*rows), pl.ds(*columns)], outs[o].at[:, pl.ds(at, columns[1])], sems.at[n]
            )
            for n, (i, rows, columns, o, at) in enumerate(parts)
        ]
        for copy in copies:
            copy.start()
        for copy in copies:
            copy.wait()

    return pl.pallas_call(
        kernel,
        out_shape=[jax.ShapeDtypeStruct(shape, jnp.bfloat16) for shape in shapes],
        in_specs=[pl.BlockSpec(memory_space=pltpu.HBM)] * len(sources),
        out_specs=[pl.BlockSpec(memory_space=pltpu.HBM)] * len(shapes),
        scratch_shapes=[pltpu.SemaphoreType.DMA((len(parts),))],
        compiler_params=pltpu.CompilerParams(vmem_limit_bytes=1 << 20),
        cost_estimate=EAGER,
    )(*sources)


def products(share, groups, tile):
    units = min(piece.shape[1] for piece in groups[0][0])
    pieces = [piece for group in groups for piece in group[0]]
    depths = [sum(rows for _, _, rows in group[1]) for group in groups]
    bounds = [output for group in groups for output in group[2]]

    def kernel(*refs):
        share_ref, ins = refs[0], refs[1 : 1 + len(pieces)]
        outs, stacks = refs[1 + len(pieces) : -len(groups)], refs[-len(groups) :]
        n = o = 0
        for (own, layout, outputs, over_rows), stack in zip(groups, stacks):
            at = 0
            for piece, first, rows in layout:
                stack[at : at + rows, :] = ins[n + piece][first : first + rows, :]
                at += rows
            for begin, end, kind in outputs:
                if over_rows:
                    value = lax.dot_general(
                        share_ref[:, begin:end],
                        stack[...],
                        (((0,), (0,)), ((), ())),
                        preferred_element_type=jnp.float32,
                    )
                else:
                    value = jnp.dot(share_ref[begin:end, :], stack[...], preferred_element_type=jnp.float32)
                outs[o][...] = value.astype(kind)
                o += 1
            n += len(own)

    return pl.pallas_call(
        kernel,
        grid=(units // tile,),
        out_shape=[jax.ShapeDtypeStruct((end - begin, units), kind) for begin, end, kind in bounds],
        in_specs=[pl.BlockSpec(share.shape, lambda i: (0, 0))]
        + [pl.BlockSpec((piece.shape[0], tile), lambda i: (0, i)) for piece in pieces],
        out_specs=[pl.BlockSpec((end - begin, tile), lambda i: (0, i)) for begin, end, _ in bounds],
        scratch_shapes=[pltpu.VMEM((depth, tile), jnp.bfloat16) for depth in depths],
        compiler_params=pltpu.CompilerParams(vmem_limit_bytes=14 << 20),
        cost_estimate=EAGER,
    )(share, *pieces)


def staged_products(out_grad, gate_pre, up_pre, down_weight):
    x_bit, y_bit, z_bit, w_bit = 1, 2, 4, 8
    me, core = lax.axis_index("dp"), lax.axis_index("mp")
    tokens, units = gate_pre.shape
    rows = down_weight.shape[0]
    q, t = rows // 2, tokens // 2
    place = jnp.stack([me, core]).astype(jnp.int32)
    own, hidden, message1, message2, message3 = first_stage(out_grad, gate_pre, up_pre, place, rows)

    down_weight, message1 = lax.optimization_barrier((down_weight, message1))
    message1, message2, message3 = flip(message1, z_bit), flip(message2, w_bit), flip(message3, z_bit | w_bit)
    whole, extra, every = (0, units), (units, 2 * rows), (0, tokens)
    (to_peers,) = cut([down_weight], [(0, (0, rows), whole, 0, 0)], [(rows, units)])
    weight1, weight2 = flip(to_peers, x_bit), flip(to_peers, y_bit)
    to_w, to_z, mine, to_y, to_x = cut(
        [message1, message2, message3, weight1, weight2],
        [
            (0, (0, t), whole, 0, 0),
            (1, (t, t), whole, 1, 0),
            (0, every, extra, 2, 0),
            (1, every, extra, 2, 2 * rows),
            (2, every, (0, 2 * rows), 2, 4 * rows),
            (3, (0, q), whole, 3, 0),
            (4, (q, q), whole, 4, 0),
        ],
        [(t, units), (t, units), (tokens, 6 * rows), (q, units), (q, units)],
    )
    theirs = flip(mine, 1, "mp")
    hidden3a, hidden3b = flip(to_w, w_bit), flip(to_z, z_bit)
    weight3a, weight3b = flip(to_y, y_bit), flip(to_x, x_bit)

    def features(k):
        a, b = mine[:, (k - 1) * 2 * rows : k * 2 * rows], theirs[:, (k - 1) * 2 * rows : k * 2 * rows]
        return jnp.concatenate([jnp.where(core == 0, a, b), jnp.where(core == 0, b, a)], axis=1)

    peers = [own] + [features(k) for k in range(1, 4)]
    share = jnp.concatenate([peers[k][h * t : (h + 1) * t] for k, h in PIECES], axis=0)

    def layout(size):
        return [(0, 0, 2 * size), (1, 0, size), (3, 0, size), (2, size, size), (4, 0, size), (2, 0, size), (1, size, size)]

    def sent(size):
        return [(2 * size, 4 * size, jnp.bfloat16), (4 * size, 6 * size, jnp.bfloat16)]

    def kept(size):
        return [(0, 2 * size, jnp.float32), (6 * size, 7 * size, jnp.float32), (7 * size, 8 * size, jnp.float32)]

    def finish(parts, from_low, from_high, size, low, high):
        send, keep = jnp.bfloat16, jnp.float32
        own_part, a_part, b_part = parts
        last_a = flip((a_part + from_low[size:].astype(keep)).astype(send), high)
        last_b = flip((b_part + from_high[size:].astype(keep)).astype(send), low)
        kept = own_part + jnp.concatenate([from_low[:size], from_high[:size]], axis=0).astype(keep)
        return kept + jnp.concatenate([last_a, last_b], axis=0).astype(keep)

    hiddens = [hidden, message1, message2, hidden3a, hidden3b]
    weights = [down_weight, weight1, weight2, weight3a, weight3b]
    to_x, to_y, to_z, to_w = products(
        share, [(hiddens, layout(t), sent(q), True), (weights, layout(q), sent(t), False)], 512
    )
    from_x, from_y = flip(to_x, x_bit), flip(to_y, y_bit)
    from_z, from_w = flip(to_z, z_bit), flip(to_w, w_bit)
    share, _ = lax.optimization_barrier((share, to_x))
    parts = products(share, [(hiddens, layout(t), kept(q), True), (weights, layout(q), kept(t), False)], 512)
    grad = finish(parts[:3], from_x, from_y, q, x_bit, y_bit)
    hidden_grad = finish(parts[3:], from_z, from_w, t, z_bit, w_bit)
    return grad, hidden_grad


def local(out_grad, gate_pre, up_pre, down_weight, row_moment, col_moment):
    size = lax.axis_size("dp")
    rows, units = down_weight.shape
    tokens = out_grad.shape[0]
    all_bits = [1 << b for b in range(size.bit_length() - 1)]
    staged = size == 16 and lax.axis_size("mp") == 2 and rows % 256 == 0 and tokens % 32 == 0 and units % 512 == 0
    if staged:
        product, hidden_grad = staged_products(out_grad, gate_pre, up_pre, down_weight)
    else:
        product, hidden_grad = general_products(
            out_grad, gate_pre, up_pre, down_weight, all_bits[:INNER_BITS], all_bits[INNER_BITS:]
        )

    activated, derivative = gelu_parts(gate_pre.astype(jnp.float32))
    gate_grad = (hidden_grad * up_pre.astype(jnp.float32) * derivative).astype(jnp.bfloat16)
    up_grad = (hidden_grad * activated).astype(jnp.bfloat16)

    grad = product * (1.0 / math.sqrt(tokens * size))
    decay = 1.0 - TRAIN_STEP ** (-0.8)
    total_rows = rows * size
    total_units = units * lax.axis_size("mp")
    powers = grad * grad
    squares = powers + 1e-30
    row_sum = lax.psum(jnp.sum(squares, axis=1), "mp")
    row_moment_new = decay * row_moment + (1.0 - decay) * (row_sum / total_units)
    col_part = jnp.sum(squares, axis=0)
    scaled_part = jnp.sum(powers / row_moment_new[:, None], axis=0)
    total_part = jnp.broadcast_to(jnp.sum(row_moment_new), (128,))
    sums = group_sum(jnp.concatenate([col_part, scaled_part, total_part]), all_bits)
    col_moment_new = decay * col_moment + (1.0 - decay) * (sums[:units] / total_rows)
    row_mean = sums[2 * units] / total_rows
    ratios = jnp.sum((sums[units : 2 * units] / col_moment_new).reshape(-1, 128), axis=0)
    square_sum = row_mean * jnp.sum(lax.psum(ratios, "mp"))
    clip_norm = jnp.sqrt(square_sum / (total_rows * total_units))
    row_factor = jnp.sqrt(row_mean / row_moment_new) / jnp.maximum(1.0, clip_norm)
    col_factor = 1.0 / jnp.sqrt(col_moment_new)
    update = grad * row_factor[:, None] * col_factor[None, :]
    return (update, row_moment_new, col_moment_new, row_mean, gate_grad, up_grad)


def solution(mesh):
    in_specs = (P("dp", None), P("dp", "mp"), P("dp", "mp"), P("dp", "mp"), P("dp"), P("mp"))
    out_specs = (P("dp", "mp"), P("dp"), P("mp"), P(), P("dp", "mp"), P("dp", "mp"))
    return jax.shard_map(local, mesh=mesh, in_specs=in_specs, out_specs=out_specs, check_vma=False)
```

```python
import math

import jax
import jax.numpy as jnp
from jax import lax
from jax.experimental import pallas as pl
from jax.experimental.pallas import tpu as pltpu
from jax.sharding import PartitionSpec as P

TRAIN_STEP = 3
INNER_BITS = 2
EAGER = pl.CostEstimate(flops=0, bytes_accessed=0, transcendentals=0)


def gelu_parts(values):
    factor = math.sqrt(2.0 / math.pi)
    inner = factor * (values + 0.044715 * values * values * values)
    tangent = jnp.tanh(inner)
    activated = 0.5 * values * (1.0 + tangent)
    derivative = 0.5 * (1.0 + tangent) + 0.5 * values * (1.0 - tangent * tangent) * factor * (
        1.0 + 3.0 * 0.044715 * values * values
    )
    return (activated, derivative)


def flip(value, bits, axis="dp"):
    size = lax.axis_size(axis)
    return lax.ppermute(value, axis, [(i, i ^ bits) for i in range(size)])


def group_sum(value, bits):
    for at in range(0, len(bits), 2):
        pair = bits[at : at + 2]
        if len(pair) == 2:
            first, second = flip(value, pair[0]), flip(value, pair[1])
            value = (value + first) + (second + flip(value, pair[0] | pair[1]))
        else:
            value = value + flip(value, pair[0])
    return value


def general_products(out_grad, gate_pre, up_pre, down_weight, inner_bits, outer_bits):
    size = lax.axis_size("dp")
    me = lax.axis_index("dp")
    tokens, rows = out_grad.shape[0], down_weight.shape[0]
    inner = 2 ** len(inner_bits)
    activated, _ = gelu_parts(gate_pre.astype(jnp.float32))
    hidden = (activated * up_pre.astype(jnp.float32)).astype(jnp.bfloat16)
    by_block = out_grad.reshape(tokens, size, rows).transpose(1, 0, 2)

    def features_of(k):
        picks = [lax.dynamic_index_in_dim(by_block, me ^ (k * inner + j), 0, keepdims=False) for j in range(inner)]
        return jnp.concatenate(picks, axis=1)

    def gather(block, bits):
        blocks = [block]
        for bit in bits:
            blocks = blocks + [flip(b, bit) for b in blocks]
        return jnp.concatenate(blocks, axis=0)

    def scatter(values, bits):
        for level in reversed(range(len(bits))):
            count = 2**level
            values = [
                values[j] + flip(values[j + count].astype(jnp.bfloat16), bits[level]).astype(jnp.float32)
                for j in range(count)
            ]
        return values[0]

    shares = [features_of(0)] + [flip(features_of(k), k * inner) for k in range(1, size // inner)]
    share = jnp.concatenate(shares, axis=0)
    hidden_all = gather(hidden, outer_bits)
    weight_all = gather(down_weight, inner_bits)
    product = scatter(
        [
            lax.dot_general(
                share[:, j * rows : (j + 1) * rows],
                hidden_all,
                (((0,), (0,)), ((), ())),
                preferred_element_type=jnp.float32,
            )
            for j in range(inner)
        ],
        inner_bits,
    )
    hidden_grad = scatter(
        [jnp.dot(x, weight_all, preferred_element_type=jnp.float32) for x in shares],
        outer_bits,
    )
    return product, hidden_grad


def first_stage(out_grad, gate_pre, up_pre, place, rows):
    tokens, units = gate_pre.shape
    half = units // 2
    step = 32

    def kernel(place, source_hbm, gate_hbm, up_hbm, own, left, right, message1, message2, message3, source, gate, up, sems):
        copies = [
            pltpu.make_async_copy(there, here, sems.at[n])
            for n, (there, here) in enumerate(((gate_hbm, gate), (up_hbm, up), (source_hbm, source)))
        ]
        for copy in copies:
            copy.start()
        me, core = place[0], place[1]

        def block(k, j):
            return pl.ds(pl.multiple_of((me ^ (4 * k + j)) * rows, rows), rows)

        copies[0].wait()
        copies[1].wait()

        @pl.loop(0, tokens // step)
        def _(i):
            here = pl.ds(pl.multiple_of(i * step, step), step)
            activated, _ = gelu_parts(gate[here, :].astype(jnp.float32))
            value = (activated * up[here, :].astype(jnp.float32)).astype(jnp.bfloat16)
            left[here, :] = value[:, :half]
            right[here, :] = value[:, half:]
            message1[here, :half] = value[:, :half]
            message2[here, :half] = value[:, :half]

        copies[2].wait()
        for j in range(4):
            own[:, j * rows : (j + 1) * rows] = source[:, block(0, j)]
        for k, target, base in ((1, message1, half), (2, message2, half), (3, message3, 0)):
            for j in range(2):
                target[:, base + j * rows : base + (j + 1) * rows] = source[:, block(k, 2 * core + j)]

    vmem = pl.BlockSpec(memory_space=pltpu.VMEM)
    widths = [4 * rows, half, half, half + 2 * rows, half + 2 * rows, 2 * rows]
    return pl.pallas_call(
        kernel,
        out_shape=[jax.ShapeDtypeStruct((tokens, width), jnp.bfloat16) for width in widths],
        in_specs=[pl.BlockSpec(memory_space=pltpu.SMEM)] + [pl.BlockSpec(memory_space=pltpu.HBM)] * 3,
        out_specs=[vmem] * len(widths),
        scratch_shapes=[
            pltpu.VMEM(out_grad.shape, jnp.bfloat16),
            pltpu.VMEM(gate_pre.shape, jnp.bfloat16),
            pltpu.VMEM(up_pre.shape, jnp.bfloat16),
            pltpu.SemaphoreType.DMA((3,)),
        ],
        compiler_params=pltpu.CompilerParams(vmem_limit_bytes=16 << 20),
        cost_estimate=EAGER,
    )(place, out_grad, gate_pre, up_pre)


def cut(sources, parts, shapes):
    def kernel(*refs):
        ins, outs, sems = refs[: len(sources)], refs[len(sources) : -1], refs[-1]
        copies = [
            pltpu.make_async_copy(
                ins[i].at[pl.ds(*rows), pl.ds(*columns)], outs[o].at[:, pl.ds(at, columns[1])], sems.at[n]
            )
            for n, (i, rows, columns, o, at) in enumerate(parts)
        ]
        for copy in copies:
            copy.start()
        for copy in copies:
            copy.wait()

    return pl.pallas_call(
        kernel,
        out_shape=[jax.ShapeDtypeStruct(shape, jnp.bfloat16) for shape in shapes],
        in_specs=[pl.BlockSpec(memory_space=pltpu.HBM)] * len(sources),
        out_specs=[pl.BlockSpec(memory_space=pltpu.HBM)] * len(shapes),
        scratch_shapes=[pltpu.SemaphoreType.DMA((len(parts),))],
        compiler_params=pltpu.CompilerParams(vmem_limit_bytes=1 << 20),
        cost_estimate=EAGER,
    )(*sources)


def assemble(own, mine, theirs, place, rows):
    tokens = own.shape[0]

    def kernel(place, own, mine, theirs, share):
        share[:tokens, :] = own[...]
        for k in range(3):
            here = pl.ds((k + 1) * tokens, tokens)
            half = slice(k * 2 * rows, (k + 1) * 2 * rows)
            a, b = mine[:, half], theirs[:, half]
            share[here, : 2 * rows] = jnp.where(place[1] == 0, a, b)
            share[here, 2 * rows :] = jnp.where(place[1] == 0, b, a)

    vmem = pl.BlockSpec(memory_space=pltpu.VMEM)
    return pl.pallas_call(
        kernel,
        out_shape=jax.ShapeDtypeStruct((4 * tokens, 4 * rows), jnp.bfloat16),
        in_specs=[pl.BlockSpec(memory_space=pltpu.SMEM), vmem, vmem, vmem],
        out_specs=vmem,
        compiler_params=pltpu.CompilerParams(vmem_limit_bytes=8 << 20),
        cost_estimate=EAGER,
    )(place, own, mine, theirs)


def add_tail(part, arrived):
    rows = part.shape[0]

    def kernel(part, arrived, out):
        out[...] = (part[...] + arrived[rows:, :].astype(jnp.float32)).astype(jnp.bfloat16)

    vmem = pl.BlockSpec(memory_space=pltpu.VMEM)
    return pl.pallas_call(
        kernel,
        out_shape=jax.ShapeDtypeStruct(part.shape, jnp.bfloat16),
        in_specs=[vmem, vmem],
        out_specs=vmem,
        compiler_params=pltpu.CompilerParams(vmem_limit_bytes=8 << 20),
        cost_estimate=EAGER,
    )(part, arrived)


def products(share, groups, steps):
    pieces = [(piece, group[1]) for group in groups for piece in group[0]]
    bounds = [(output, group[1]) for group in groups for output in group[2]]

    def kernel(*refs):
        share_ref, ins = refs[0], refs[1 : 1 + len(pieces)]
        outs, stacks = refs[1 + len(pieces) : -len(groups)], refs[-len(groups) :]
        n = o = 0
        for (own, _, outputs, over_rows), stack in zip(groups, stacks):
            at = 0
            for piece in own:
                stack[at : at + piece.shape[0], :] = ins[n][...]
                at += piece.shape[0]
                n += 1
            for ranges, kind in outputs:
                if over_rows:
                    side = jnp.concatenate([share_ref[:, begin:end] for begin, end in ranges], axis=1)
                    value = lax.dot_general(
                        side, stack[...], (((0,), (0,)), ((), ())), preferred_element_type=jnp.float32
                    )
                else:
                    side = jnp.concatenate([share_ref[begin:end, :] for begin, end in ranges], axis=0)
                    value = jnp.dot(side, stack[...], preferred_element_type=jnp.float32)
                outs[o][...] = value.astype(kind)
                o += 1

    def height(ranges):
        return sum(end - begin for begin, end in ranges)

    return pl.pallas_call(
        kernel,
        grid=(steps,),
        out_shape=[jax.ShapeDtypeStruct((height(ranges), columns), kind) for (ranges, kind), columns in bounds],
        in_specs=[pl.BlockSpec(share.shape, lambda i: (0, 0))]
        + [pl.BlockSpec((piece.shape[0], columns // steps), lambda i: (0, i)) for piece, columns in pieces],
        out_specs=[pl.BlockSpec((height(ranges), columns // steps), lambda i: (0, i)) for (ranges, _), columns in bounds],
        scratch_shapes=[
            pltpu.VMEM((sum(piece.shape[0] for piece in group[0]), group[1] // steps), jnp.bfloat16) for group in groups
        ],
        compiler_params=pltpu.CompilerParams(vmem_limit_bytes=14 << 20),
        cost_estimate=EAGER,
    )(share, *[piece for piece, _ in pieces])


def staged_products(out_grad, gate_pre, up_pre, down_weight):
    x_bit, y_bit, z_bit, w_bit = 1, 2, 4, 8
    me, core = lax.axis_index("dp"), lax.axis_index("mp")
    tokens, units = gate_pre.shape
    rows = down_weight.shape[0]
    q, t, half = rows // 2, tokens // 2, units // 2
    steps = units // 512
    barrier = lax.optimization_barrier
    place = jnp.stack([me, core]).astype(jnp.int32)
    own, left, right, message1, message2, message3 = first_stage(out_grad, gate_pre, up_pre, place, rows)

    down_weight, message1 = barrier((down_weight, message1))
    left1, left2, message3 = flip(message1, z_bit), flip(message2, w_bit), flip(message3, z_bit | w_bit)
    weight1, weight2 = flip(down_weight, x_bit), flip(down_weight, y_bit)

    left1, left2, message3, weight1, weight2, right = barrier((left1, left2, message3, weight1, weight2, right))
    left3 = flip(left2, z_bit)
    right2 = flip(right, w_bit)
    extra, every = (half, 2 * rows), (0, tokens)
    mine, to_y, to_x = cut(
        [left1, left2, message3, weight1, weight2],
        [
            (0, every, extra, 0, 0),
            (1, every, extra, 0, 2 * rows),
            (2, every, (0, 2 * rows), 0, 4 * rows),
            (3, (0, q), (0, units), 1, 0),
            (4, (q, q), (0, units), 2, 0),
        ],
        [(tokens, 6 * rows), (q, units), (q, units)],
    )
    theirs = flip(mine, 1, "mp")
    weight3a, weight3b = flip(to_y, y_bit), flip(to_x, x_bit)
    share = assemble(own, mine, theirs, place, rows)

    left3, right2, share, weight3a, weight3b, right = barrier((left3, right2, share, weight3a, weight3b, right))
    right1, right3 = flip(right, z_bit), flip(right2, z_bit)

    def low_sent(size):
        return [(2 * size, 3 * size), (6 * size, 7 * size)]

    def high_sent(size):
        return [(5 * size, 6 * size), (7 * size, 8 * size)]

    def sent(size):
        return [(low_sent(size), jnp.bfloat16), (high_sent(size), jnp.bfloat16)]

    def kept(size):
        ranges = [(0, 2 * size)], [(4 * size, 5 * size)], [(3 * size, 4 * size)]
        return [(r, jnp.float32) for r in ranges]

    lefts = [left, left1, left2, left3]
    weights = [down_weight, weight1, weight2, weight3a, weight3b]
    left_to_x, left_to_y = products(share, [(lefts, half, sent(q), True)], steps)
    left_from_x, left_from_y = flip(left_to_x, x_bit), flip(left_to_y, y_bit)
    share, _ = barrier((share, left_to_x))
    to_z, to_w, *left_kept = products(
        share, [(weights, units, sent(t), False), (lefts, half, kept(q), True)], steps
    )

    right1, right3, to_z, to_w, share = barrier((right1, right3, to_z, to_w, share))
    from_z, from_w = flip(to_z, z_bit), flip(to_w, w_bit)
    rights = [right, right1, right2, right3]
    right_to_x, right_to_y = products(share, [(rights, half, sent(q), True)], steps)
    right_from_x, right_from_y = flip(right_to_x, x_bit), flip(right_to_y, y_bit)
    share, _ = barrier((share, right_to_x))
    parts = products(share, [(rights, half, kept(q), True), (weights, units, kept(t), False)], steps)

    def finish(parts, from_low, from_high, size, low, high):
        own_part, a_part, b_part = parts
        last_a = flip(add_tail(a_part, from_low), high)
        last_b = flip(add_tail(b_part, from_high), low)
        arrived = jnp.concatenate([from_low[:size], from_high[:size]], axis=0).astype(jnp.float32)
        return own_part + arrived + jnp.concatenate([last_a, last_b], axis=0).astype(jnp.float32)

    left_grad = finish(left_kept, left_from_x, left_from_y, q, x_bit, y_bit)
    right_grad = finish(parts[:3], right_from_x, right_from_y, q, x_bit, y_bit)
    hidden_grad = finish(parts[3:], from_z, from_w, t, z_bit, w_bit)
    return jnp.concatenate([left_grad, right_grad], axis=1), hidden_grad


def local(out_grad, gate_pre, up_pre, down_weight, row_moment, col_moment):
    size = lax.axis_size("dp")
    rows, units = down_weight.shape
    tokens = out_grad.shape[0]
    all_bits = [1 << b for b in range(size.bit_length() - 1)]
    staged = size == 16 and lax.axis_size("mp") == 2 and rows % 256 == 0 and tokens % 32 == 0 and units % 512 == 0
    if staged:
        product, hidden_grad = staged_products(out_grad, gate_pre, up_pre, down_weight)
    else:
        product, hidden_grad = general_products(
            out_grad, gate_pre, up_pre, down_weight, all_bits[:INNER_BITS], all_bits[INNER_BITS:]
        )

    activated, derivative = gelu_parts(gate_pre.astype(jnp.float32))
    gate_grad = (hidden_grad * up_pre.astype(jnp.float32) * derivative).astype(jnp.bfloat16)
    up_grad = (hidden_grad * activated).astype(jnp.bfloat16)

    grad = product * (1.0 / math.sqrt(tokens * size))
    decay = 1.0 - TRAIN_STEP ** (-0.8)
    total_rows = rows * size
    total_units = units * lax.axis_size("mp")
    powers = grad * grad
    squares = powers + 1e-30
    row_sum = lax.psum(jnp.sum(squares, axis=1), "mp")
    row_moment_new = decay * row_moment + (1.0 - decay) * (row_sum / total_units)
    col_part = jnp.sum(squares, axis=0)
    scaled_part = jnp.sum(powers / row_moment_new[:, None], axis=0)
    total_part = jnp.broadcast_to(jnp.sum(row_moment_new), (128,))
    sums = group_sum(jnp.concatenate([col_part, scaled_part, total_part]), all_bits)
    col_moment_new = decay * col_moment + (1.0 - decay) * (sums[:units] / total_rows)
    row_mean = sums[2 * units] / total_rows
    ratios = jnp.sum((sums[units : 2 * units] / col_moment_new).reshape(-1, 128), axis=0)
    square_sum = row_mean * jnp.sum(lax.psum(ratios, "mp"))
    clip_norm = jnp.sqrt(square_sum / (total_rows * total_units))
    row_factor = jnp.sqrt(row_mean / row_moment_new) / jnp.maximum(1.0, clip_norm)
    col_factor = 1.0 / jnp.sqrt(col_moment_new)
    update = grad * row_factor[:, None] * col_factor[None, :]
    return (update, row_moment_new, col_moment_new, row_mean, gate_grad, up_grad)


def solution(mesh):
    in_specs = (P("dp", None), P("dp", "mp"), P("dp", "mp"), P("dp", "mp"), P("dp"), P("mp"))
    out_specs = (P("dp", "mp"), P("dp"), P("mp"), P(), P("dp", "mp"), P("dp", "mp"))
    return jax.shard_map(local, mesh=mesh, in_specs=in_specs, out_specs=out_specs, check_vma=False)
```

```python
import math

import jax
import jax.numpy as jnp
from jax import lax
from jax.experimental import pallas as pl
from jax.experimental.pallas import tpu as pltpu
from jax.sharding import PartitionSpec as P

TRAIN_STEP = 3
INNER_BITS = 2
LEFT = 3
EAGER = pl.CostEstimate(flops=0, bytes_accessed=0, transcendentals=0)


def gelu_parts(values):
    factor = math.sqrt(2.0 / math.pi)
    inner = factor * (values + 0.044715 * values * values * values)
    tangent = jnp.tanh(inner)
    activated = 0.5 * values * (1.0 + tangent)
    derivative = 0.5 * (1.0 + tangent) + 0.5 * values * (1.0 - tangent * tangent) * factor * (
        1.0 + 3.0 * 0.044715 * values * values
    )
    return (activated, derivative)


def flip(value, bits, axis="dp"):
    size = lax.axis_size(axis)
    return lax.ppermute(value, axis, [(i, i ^ bits) for i in range(size)])


def group_sum(value, bits):
    for at in range(0, len(bits), 2):
        pair = bits[at : at + 2]
        if len(pair) == 2:
            first, second = flip(value, pair[0]), flip(value, pair[1])
            value = (value + first) + (second + flip(value, pair[0] | pair[1]))
        else:
            value = value + flip(value, pair[0])
    return value


def general_products(out_grad, gate_pre, up_pre, down_weight, inner_bits, outer_bits):
    size = lax.axis_size("dp")
    me = lax.axis_index("dp")
    tokens, rows = out_grad.shape[0], down_weight.shape[0]
    inner = 2 ** len(inner_bits)
    activated, _ = gelu_parts(gate_pre.astype(jnp.float32))
    hidden = (activated * up_pre.astype(jnp.float32)).astype(jnp.bfloat16)
    by_block = out_grad.reshape(tokens, size, rows).transpose(1, 0, 2)

    def features_of(k):
        picks = [lax.dynamic_index_in_dim(by_block, me ^ (k * inner + j), 0, keepdims=False) for j in range(inner)]
        return jnp.concatenate(picks, axis=1)

    def gather(block, bits):
        blocks = [block]
        for bit in bits:
            blocks = blocks + [flip(b, bit) for b in blocks]
        return jnp.concatenate(blocks, axis=0)

    def scatter(values, bits):
        for level in reversed(range(len(bits))):
            count = 2**level
            values = [
                values[j] + flip(values[j + count].astype(jnp.bfloat16), bits[level]).astype(jnp.float32)
                for j in range(count)
            ]
        return values[0]

    shares = [features_of(0)] + [flip(features_of(k), k * inner) for k in range(1, size // inner)]
    share = jnp.concatenate(shares, axis=0)
    hidden_all = gather(hidden, outer_bits)
    weight_all = gather(down_weight, inner_bits)
    product = scatter(
        [
            lax.dot_general(
                share[:, j * rows : (j + 1) * rows],
                hidden_all,
                (((0,), (0,)), ((), ())),
                preferred_element_type=jnp.float32,
            )
            for j in range(inner)
        ],
        inner_bits,
    )
    hidden_grad = scatter(
        [jnp.dot(x, weight_all, preferred_element_type=jnp.float32) for x in shares],
        outer_bits,
    )
    return product, hidden_grad


def first_stage(out_grad, gate_pre, up_pre, place, rows):
    tokens, units = gate_pre.shape
    half = units * LEFT // 5
    step = 32

    def kernel(place, source_hbm, gate_hbm, up_hbm, own, right, message1, message2, message3, source, gate, up, sems):
        copies = [
            pltpu.make_async_copy(there, here, sems.at[n])
            for n, (there, here) in enumerate(((gate_hbm, gate), (up_hbm, up), (source_hbm, source)))
        ]
        for copy in copies:
            copy.start()
        me, core = place[0], place[1]

        def block(k, j):
            return pl.ds(pl.multiple_of((me ^ (4 * k + j)) * rows, rows), rows)

        copies[0].wait()
        copies[1].wait()

        @pl.loop(0, tokens // step)
        def _(i):
            here = pl.ds(pl.multiple_of(i * step, step), step)
            activated, _ = gelu_parts(gate[here, :].astype(jnp.float32))
            value = (activated * up[here, :].astype(jnp.float32)).astype(jnp.bfloat16)
            right[here, :] = value[:, half:]
            message1[here, :half] = value[:, :half]
            message2[here, :half] = value[:, :half]

        copies[2].wait()
        for j in range(4):
            own[:, j * rows : (j + 1) * rows] = source[:, block(0, j)]
        for k, target, base in ((1, message1, half), (2, message2, half), (3, message3, 0)):
            for j in range(2):
                target[:, base + j * rows : base + (j + 1) * rows] = source[:, block(k, 2 * core + j)]

    vmem = pl.BlockSpec(memory_space=pltpu.VMEM)
    widths = [4 * rows, units - half, half + 2 * rows, half + 2 * rows, 2 * rows]
    return pl.pallas_call(
        kernel,
        out_shape=[jax.ShapeDtypeStruct((tokens, width), jnp.bfloat16) for width in widths],
        in_specs=[pl.BlockSpec(memory_space=pltpu.SMEM)] + [pl.BlockSpec(memory_space=pltpu.HBM)] * 3,
        out_specs=[vmem] * len(widths),
        scratch_shapes=[
            pltpu.VMEM(out_grad.shape, jnp.bfloat16),
            pltpu.VMEM(gate_pre.shape, jnp.bfloat16),
            pltpu.VMEM(up_pre.shape, jnp.bfloat16),
            pltpu.SemaphoreType.DMA((3,)),
        ],
        compiler_params=pltpu.CompilerParams(vmem_limit_bytes=16 << 20),
        cost_estimate=EAGER,
    )(place, out_grad, gate_pre, up_pre)


def cut(sources, parts, shapes):
    def kernel(*refs):
        ins, outs, sems = refs[: len(sources)], refs[len(sources) : -1], refs[-1]
        copies = [
            pltpu.make_async_copy(
                ins[i].at[pl.ds(*rows), pl.ds(*columns)], outs[o].at[:, pl.ds(at, columns[1])], sems.at[n]
            )
            for n, (i, rows, columns, o, at) in enumerate(parts)
        ]
        for copy in copies:
            copy.start()
        for copy in copies:
            copy.wait()

    return pl.pallas_call(
        kernel,
        out_shape=[jax.ShapeDtypeStruct(shape, jnp.bfloat16) for shape in shapes],
        in_specs=[pl.BlockSpec(memory_space=pltpu.HBM)] * len(sources),
        out_specs=[pl.BlockSpec(memory_space=pltpu.HBM)] * len(shapes),
        scratch_shapes=[pltpu.SemaphoreType.DMA((len(parts),))],
        compiler_params=pltpu.CompilerParams(vmem_limit_bytes=1 << 20),
        cost_estimate=EAGER,
    )(*sources)


def assemble(own, mine, theirs, place, rows):
    tokens = own.shape[0]

    def kernel(place, own, mine, theirs, share):
        share[:tokens, :] = own[...]
        for k in range(3):
            here = pl.ds((k + 1) * tokens, tokens)
            half = slice(k * 2 * rows, (k + 1) * 2 * rows)
            a, b = mine[:, half], theirs[:, half]
            share[here, : 2 * rows] = jnp.where(place[1] == 0, a, b)
            share[here, 2 * rows :] = jnp.where(place[1] == 0, b, a)

    vmem = pl.BlockSpec(memory_space=pltpu.VMEM)
    return pl.pallas_call(
        kernel,
        out_shape=jax.ShapeDtypeStruct((4 * tokens, 4 * rows), jnp.bfloat16),
        in_specs=[pl.BlockSpec(memory_space=pltpu.SMEM), vmem, vmem, vmem],
        out_specs=vmem,
        compiler_params=pltpu.CompilerParams(vmem_limit_bytes=8 << 20),
        cost_estimate=EAGER,
    )(place, own, mine, theirs)


def add_tail(parts, arrived):
    rows = parts[0].shape[0]
    widths = [part.shape[1] for part in parts]

    def kernel(*refs):
        out, at = refs[-1], 0
        for part, other, width in zip(refs, refs[len(parts) :], widths):
            out[:, at : at + width] = (part[...] + other[rows:, :].astype(jnp.float32)).astype(jnp.bfloat16)
            at += width

    vmem = pl.BlockSpec(memory_space=pltpu.VMEM)
    return pl.pallas_call(
        kernel,
        out_shape=jax.ShapeDtypeStruct((rows, sum(widths)), jnp.bfloat16),
        in_specs=[vmem] * (2 * len(parts)),
        out_specs=vmem,
        compiler_params=pltpu.CompilerParams(vmem_limit_bytes=8 << 20),
        cost_estimate=EAGER,
    )(*parts, *arrived)


def flat(column):
    return jnp.broadcast_to(column, (128, 128)).T[0:1, :]


def upright(row):
    return jnp.broadcast_to(row, (128, 128)).T[:, 0:1]


def sum_up(kept, from_low, from_high, last_a, last_b, scale):
    rows = kept[0].shape[0]
    q = rows // 2
    widths = [part.shape[1] for part in kept]
    units = sum(widths)

    def kernel(*refs):
        kept_refs, low_refs, high_refs = refs[:2], refs[2:4], refs[4:6]
        last_refs, grad, row_part = refs[6:8], refs[8], refs[9]
        for h, arrived in enumerate((low_refs, high_refs)):
            for at in range(0, q, 128):
                total = jnp.zeros((128, 1), jnp.float32)
                here = slice(h * q + at, h * q + at + 128)
                column = 0
                for part, other, width in zip(kept_refs, arrived, widths):
                    there = slice(column, column + width)
                    value = part[here, :] + other[at : at + 128, :].astype(jnp.float32)
                    value = (value + last_refs[h][at : at + 128, there].astype(jnp.float32)) * scale
                    grad[here, there] = value
                    total = total + jnp.sum(value * value + 1e-30, axis=1, keepdims=True)
                    column += width
                row_part[:, here] = flat(total)

    vmem = pl.BlockSpec(memory_space=pltpu.VMEM)
    return pl.pallas_call(
        kernel,
        out_shape=[jax.ShapeDtypeStruct((rows, units), jnp.float32), jax.ShapeDtypeStruct((1, rows), jnp.float32)],
        in_specs=[vmem] * 8,
        out_specs=[vmem] * 2,
        compiler_params=pltpu.CompilerParams(vmem_limit_bytes=14 << 20),
        cost_estimate=EAGER,
    )(*kept, *from_low, *from_high, last_a, last_b)


def column_sums(grad, row_sum, row_moment, decay, total_units):
    rows, units = grad.shape

    def kernel(grad, row_sum, row_moment, row_moment_new, sums):
        new = decay * row_moment[...] + (1.0 - decay) * (row_sum[...] / total_units)
        row_moment_new[...] = new
        sums[:, 2 * units :] = jnp.broadcast_to(jnp.sum(new, axis=1, keepdims=True), (1, 128))
        inverse = [1.0 / upright(new[:, at : at + 128]) for at in range(0, rows, 128)]
        for column in range(0, units, 256):
            there = slice(column, column + 256)
            squares, scaled = jnp.zeros((1, 256), jnp.float32), jnp.zeros((1, 256), jnp.float32)
            for n, at in enumerate(range(0, rows, 128)):
                power = grad[at : at + 128, there]
                power = power * power
                squares = squares + jnp.sum(power + 1e-30, axis=0, keepdims=True)
                scaled = scaled + jnp.sum(power * inverse[n], axis=0, keepdims=True)
            sums[:, there] = squares
            sums[:, units + column : units + column + 256] = scaled

    vmem = pl.BlockSpec(memory_space=pltpu.VMEM)
    return pl.pallas_call(
        kernel,
        out_shape=[
            jax.ShapeDtypeStruct((1, rows), jnp.float32),
            jax.ShapeDtypeStruct((1, 2 * units + 128), jnp.float32),
        ],
        in_specs=[vmem] * 3,
        out_specs=[vmem] * 2,
        compiler_params=pltpu.CompilerParams(vmem_limit_bytes=14 << 20),
        cost_estimate=EAGER,
    )(grad, row_sum, row_moment)


def products(share, groups, steps):
    pieces = [(piece, group[1]) for group in groups for piece in group[0]]
    bounds = [(output, group[1]) for group in groups for output in group[2]]

    def kernel(*refs):
        share_ref, ins = refs[0], refs[1 : 1 + len(pieces)]
        outs, stacks = refs[1 + len(pieces) : -len(groups)], refs[-len(groups) :]
        n = o = 0
        for (own, _, outputs, over_rows), stack in zip(groups, stacks):
            at = 0
            for piece in own:
                stack[at : at + piece.shape[0], :] = ins[n][...]
                at += piece.shape[0]
                n += 1
            for ranges, kind in outputs:
                if over_rows:
                    side = jnp.concatenate([share_ref[:, begin:end] for begin, end in ranges], axis=1)
                    value = lax.dot_general(
                        side, stack[...], (((0,), (0,)), ((), ())), preferred_element_type=jnp.float32
                    )
                else:
                    side = jnp.concatenate([share_ref[begin:end, :] for begin, end in ranges], axis=0)
                    value = jnp.dot(side, stack[...], preferred_element_type=jnp.float32)
                outs[o][...] = value.astype(kind)
                o += 1

    def height(ranges):
        return sum(end - begin for begin, end in ranges)

    return pl.pallas_call(
        kernel,
        grid=(steps,),
        out_shape=[jax.ShapeDtypeStruct((height(ranges), columns), kind) for (ranges, kind), columns in bounds],
        in_specs=[pl.BlockSpec(share.shape, lambda i: (0, 0))]
        + [pl.BlockSpec((piece.shape[0], columns // steps), lambda i: (0, i)) for piece, columns in pieces],
        out_specs=[pl.BlockSpec((height(ranges), columns // steps), lambda i: (0, i)) for (ranges, _), columns in bounds],
        scratch_shapes=[
            pltpu.VMEM((sum(piece.shape[0] for piece in group[0]), group[1] // steps), jnp.bfloat16) for group in groups
        ],
        compiler_params=pltpu.CompilerParams(vmem_limit_bytes=14 << 20),
        cost_estimate=EAGER,
    )(share, *[piece for piece, _ in pieces])


def staged_products(out_grad, gate_pre, up_pre, down_weight):
    x_bit, y_bit, z_bit, w_bit = 1, 2, 4, 8
    me, core = lax.axis_index("dp"), lax.axis_index("mp")
    tokens, units = gate_pre.shape
    rows = down_weight.shape[0]
    q, t = rows // 2, tokens // 2
    steps = 4
    split = units * LEFT // 5
    barrier = lax.optimization_barrier
    place = jnp.stack([me, core]).astype(jnp.int32)
    own, right, message1, message2, message3 = first_stage(out_grad, gate_pre, up_pre, place, rows)

    down_weight, message1 = barrier((down_weight, message1))
    extra, every, whole = (split, 2 * rows), (0, tokens), (0, units)
    left1, left2, message3 = flip(message1, z_bit), flip(message2, w_bit), flip(message3, z_bit | w_bit)
    weight1, weight2 = flip(down_weight, x_bit), flip(down_weight, y_bit)

    to_y, to_x = cut([weight1, weight2], [(0, (0, q), whole, 0, 0), (1, (q, q), whole, 1, 0)], [(q, units)] * 2)
    weight3a, weight3b = flip(to_y, y_bit), flip(to_x, x_bit)
    left1, left2, message3, _, _ = barrier((left1, left2, message3, to_y, to_x))
    to_z, mine = cut(
        [left1, left2, message3],
        [
            (1, every, (0, split), 0, 0),
            (0, every, extra, 1, 0),
            (1, every, extra, 1, 2 * rows),
            (2, every, (0, 2 * rows), 1, 4 * rows),
        ],
        [(tokens, split), (tokens, 6 * rows)],
    )
    left3 = flip(to_z, z_bit)
    theirs = flip(mine, 1, "mp")
    share = assemble(own, mine, theirs, place, rows)

    left3, share, right = barrier((left3, share, right))
    right1, right2 = flip(right, z_bit), flip(right, w_bit)

    def low_sent(size):
        return [(2 * size, 3 * size), (6 * size, 7 * size)]

    def high_sent(size):
        return [(5 * size, 6 * size), (7 * size, 8 * size)]

    def sent(size):
        return [(low_sent(size), jnp.bfloat16), (high_sent(size), jnp.bfloat16)]

    def kept(size):
        ranges = [(0, 2 * size)], [(4 * size, 5 * size)], [(3 * size, 4 * size)]
        return [(r, jnp.float32) for r in ranges]

    lefts = [message1, left1, left2, left3]
    share, weight3a, weight3b = barrier((share, weight3a, weight3b))
    left_to_x, left_to_y = products(share, [(lefts, split, sent(q), True)], steps)
    left_from_x, left_from_y = flip(left_to_x, x_bit), flip(left_to_y, y_bit)
    right2, share, _ = barrier((right2, share, left_to_x))
    right3 = flip(right2, z_bit)

    weights = [down_weight, weight1, weight2, weight3a, weight3b]
    to_z, to_w, *left_parts = products(
        share, [(weights, units, sent(t), False), (lefts, split, kept(q), True)], steps
    )
    from_z, from_w = flip(to_z, z_bit), flip(to_w, w_bit)

    right1, right3, left_from_x, left_from_y, share, _ = barrier(
        (right1, right3, left_from_x, left_from_y, share, to_z)
    )
    rights = [right, right1, right2, right3]
    right_to_x, right_to_y = products(share, [(rights, units - split, sent(q), True)], steps)
    right_from_x, right_from_y = flip(right_to_x, x_bit), flip(right_to_y, y_bit)
    share, _ = barrier((share, right_to_x))
    parts = products(share, [(rights, units - split, kept(q), True), (weights, units, kept(t), False)], steps)

    grad_a = flip(add_tail([left_parts[1], parts[1]], [left_from_x, right_from_x]), y_bit)
    grad_b = flip(add_tail([left_parts[2], parts[2]], [left_from_y, right_from_y]), x_bit)
    grad_a, grad_b, from_z, from_w = barrier((grad_a, grad_b, from_z, from_w))
    grad, row_part = sum_up(
        [left_parts[0], parts[0]],
        [left_from_x, right_from_x],
        [left_from_y, right_from_y],
        grad_a,
        grad_b,
        1.0 / math.sqrt(tokens * lax.axis_size("dp")),
    )

    to_w, to_z = add_tail([parts[4]], [from_z]), add_tail([parts[5]], [from_w])
    row_sum = lax.psum(row_part, "mp")
    row_sum, to_w, to_z = barrier((row_sum, to_w, to_z))
    last_a, last_b = flip(to_w, w_bit), flip(to_z, z_bit)
    arrived = jnp.concatenate([from_z[:t], from_w[:t]], axis=0)
    return grad, row_sum, (parts[3], arrived, last_a, last_b)


def local(out_grad, gate_pre, up_pre, down_weight, row_moment, col_moment):
    size = lax.axis_size("dp")
    rows, units = down_weight.shape
    tokens = out_grad.shape[0]
    all_bits = [1 << b for b in range(size.bit_length() - 1)]
    decay = 1.0 - TRAIN_STEP ** (-0.8)
    total_rows = rows * size
    total_units = units * lax.axis_size("mp")
    staged = size == 16 and lax.axis_size("mp") == 2 and rows % 256 == 0 and tokens % 32 == 0 and units % 2560 == 0
    if staged:
        grad, row_sum, (own_part, arrived, last_a, last_b) = staged_products(out_grad, gate_pre, up_pre, down_weight)
        row_moment_new, sums = column_sums(grad, row_sum, row_moment[None, :], decay, total_units)
        row_moment_new, sums = row_moment_new[0], group_sum(sums[0], all_bits[:INNER_BITS])
        sums, last_a, last_b = lax.optimization_barrier((sums, last_a, last_b))
        hidden_grad = own_part + arrived.astype(jnp.float32) + jnp.concatenate([last_a, last_b], axis=0).astype(jnp.float32)
    else:
        product, hidden_grad = general_products(
            out_grad, gate_pre, up_pre, down_weight, all_bits[:INNER_BITS], all_bits[INNER_BITS:]
        )
        grad = product * (1.0 / math.sqrt(tokens * size))
        powers = grad * grad
        squares = powers + 1e-30
        row_sum = lax.psum(jnp.sum(squares, axis=1), "mp")
        row_moment_new = decay * row_moment + (1.0 - decay) * (row_sum / total_units)
        col_part = jnp.sum(squares, axis=0)
        scaled_part = jnp.sum(powers / row_moment_new[:, None], axis=0)
        sums = jnp.concatenate([col_part, scaled_part, jnp.broadcast_to(jnp.sum(row_moment_new), (128,))])
        sums = group_sum(sums, all_bits[:INNER_BITS])

    activated, derivative = gelu_parts(gate_pre.astype(jnp.float32))
    gate_grad = (hidden_grad * up_pre.astype(jnp.float32) * derivative).astype(jnp.bfloat16)
    up_grad = (hidden_grad * activated).astype(jnp.bfloat16)

    sums = group_sum(sums, all_bits[INNER_BITS:])
    col_moment_new = decay * col_moment + (1.0 - decay) * (sums[:units] / total_rows)
    row_mean = sums[2 * units] / total_rows
    ratios = jnp.sum((sums[units : 2 * units] / col_moment_new).reshape(-1, 128), axis=0)
    square_sum = row_mean * jnp.sum(lax.psum(ratios, "mp"))
    clip_norm = jnp.sqrt(square_sum / (total_rows * total_units))
    row_factor = jnp.sqrt(row_mean / row_moment_new) / jnp.maximum(1.0, clip_norm)
    col_factor = 1.0 / jnp.sqrt(col_moment_new)
    update = grad * row_factor[:, None] * col_factor[None, :]
    return (update, row_moment_new, col_moment_new, row_mean, gate_grad, up_grad)


def solution(mesh):
    in_specs = (P("dp", None), P("dp", "mp"), P("dp", "mp"), P("dp", "mp"), P("dp"), P("mp"))
    out_specs = (P("dp", "mp"), P("dp"), P("mp"), P(), P("dp", "mp"), P("dp", "mp"))
    return jax.shard_map(local, mesh=mesh, in_specs=in_specs, out_specs=out_specs, check_vma=False)
```

```python
import math

import jax
import jax.numpy as jnp
from jax import lax
from jax.experimental import pallas as pl
from jax.experimental.pallas import tpu as pltpu
from jax.sharding import PartitionSpec as P

TRAIN_STEP = 3
INNER_BITS = 2
LEFT = 3
EAGER = pl.CostEstimate(flops=0, bytes_accessed=0, transcendentals=0)


def gelu_parts(values):
    factor = math.sqrt(2.0 / math.pi)
    inner = factor * (values + 0.044715 * values * values * values)
    tangent = jnp.tanh(inner)
    activated = 0.5 * values * (1.0 + tangent)
    derivative = 0.5 * (1.0 + tangent) + 0.5 * values * (1.0 - tangent * tangent) * factor * (
        1.0 + 3.0 * 0.044715 * values * values
    )
    return (activated, derivative)


def flip(value, bits, axis="dp"):
    size = lax.axis_size(axis)
    return lax.ppermute(value, axis, [(i, i ^ bits) for i in range(size)])


def group_sum(value, bits):
    for at in range(0, len(bits), 2):
        pair = bits[at : at + 2]
        if len(pair) == 2:
            first, second = flip(value, pair[0]), flip(value, pair[1])
            value = (value + first) + (second + flip(value, pair[0] | pair[1]))
        else:
            value = value + flip(value, pair[0])
    return value


def general_products(out_grad, gate_pre, up_pre, down_weight, inner_bits, outer_bits):
    size = lax.axis_size("dp")
    me = lax.axis_index("dp")
    tokens, rows = out_grad.shape[0], down_weight.shape[0]
    inner = 2 ** len(inner_bits)
    activated, _ = gelu_parts(gate_pre.astype(jnp.float32))
    hidden = (activated * up_pre.astype(jnp.float32)).astype(jnp.bfloat16)
    by_block = out_grad.reshape(tokens, size, rows).transpose(1, 0, 2)

    def features_of(k):
        picks = [lax.dynamic_index_in_dim(by_block, me ^ (k * inner + j), 0, keepdims=False) for j in range(inner)]
        return jnp.concatenate(picks, axis=1)

    def gather(block, bits):
        blocks = [block]
        for bit in bits:
            blocks = blocks + [flip(b, bit) for b in blocks]
        return jnp.concatenate(blocks, axis=0)

    def scatter(values, bits):
        for level in reversed(range(len(bits))):
            count = 2**level
            values = [
                values[j] + flip(values[j + count].astype(jnp.bfloat16), bits[level]).astype(jnp.float32)
                for j in range(count)
            ]
        return values[0]

    shares = [features_of(0)] + [flip(features_of(k), k * inner) for k in range(1, size // inner)]
    share = jnp.concatenate(shares, axis=0)
    hidden_all = gather(hidden, outer_bits)
    weight_all = gather(down_weight, inner_bits)
    product = scatter(
        [
            lax.dot_general(
                share[:, j * rows : (j + 1) * rows],
                hidden_all,
                (((0,), (0,)), ((), ())),
                preferred_element_type=jnp.float32,
            )
            for j in range(inner)
        ],
        inner_bits,
    )
    hidden_grad = scatter(
        [jnp.dot(x, weight_all, preferred_element_type=jnp.float32) for x in shares],
        outer_bits,
    )
    return product, hidden_grad


def first_stage(out_grad, gate_pre, up_pre, place, rows):
    tokens, units = gate_pre.shape
    half = units * LEFT // 5
    step = 32

    def kernel(place, source_hbm, gate_hbm, up_hbm, own, right, message1, message2, message3, source, gate, up, sems):
        copies = [
            pltpu.make_async_copy(there, here, sems.at[n])
            for n, (there, here) in enumerate(((gate_hbm, gate), (up_hbm, up), (source_hbm, source)))
        ]
        for copy in copies:
            copy.start()
        me, core = place[0], place[1]

        def block(k, j):
            return pl.ds(pl.multiple_of((me ^ (4 * k + j)) * rows, rows), rows)

        copies[0].wait()
        copies[1].wait()

        @pl.loop(0, tokens // step)
        def _(i):
            here = pl.ds(pl.multiple_of(i * step, step), step)
            activated, _ = gelu_parts(gate[here, :].astype(jnp.float32))
            value = (activated * up[here, :].astype(jnp.float32)).astype(jnp.bfloat16)
            right[here, :] = value[:, half:]
            message1[here, :half] = value[:, :half]
            message2[here, :half] = value[:, :half]

        copies[2].wait()
        for j in range(4):
            own[:, j * rows : (j + 1) * rows] = source[:, block(0, j)]
        for k, target, base in ((1, message1, half), (2, message2, half), (3, message3, 0)):
            for j in range(2):
                target[:, base + j * rows : base + (j + 1) * rows] = source[:, block(k, 2 * core + j)]

    vmem = pl.BlockSpec(memory_space=pltpu.VMEM)
    widths = [4 * rows, units - half, half + 2 * rows, half + 2 * rows, 2 * rows]
    return pl.pallas_call(
        kernel,
        out_shape=[jax.ShapeDtypeStruct((tokens, width), jnp.bfloat16) for width in widths],
        in_specs=[pl.BlockSpec(memory_space=pltpu.SMEM)] + [pl.BlockSpec(memory_space=pltpu.HBM)] * 3,
        out_specs=[vmem] * len(widths),
        scratch_shapes=[
            pltpu.VMEM(out_grad.shape, jnp.bfloat16),
            pltpu.VMEM(gate_pre.shape, jnp.bfloat16),
            pltpu.VMEM(up_pre.shape, jnp.bfloat16),
            pltpu.SemaphoreType.DMA((3,)),
        ],
        compiler_params=pltpu.CompilerParams(vmem_limit_bytes=16 << 20),
        cost_estimate=EAGER,
    )(place, out_grad, gate_pre, up_pre)


def cut(sources, parts, shapes):
    def kernel(*refs):
        ins, outs, sems = refs[: len(sources)], refs[len(sources) : -1], refs[-1]
        copies = [
            pltpu.make_async_copy(
                ins[i].at[pl.ds(*rows), pl.ds(*columns)], outs[o].at[:, pl.ds(at, columns[1])], sems.at[n]
            )
            for n, (i, rows, columns, o, at) in enumerate(parts)
        ]
        for copy in copies:
            copy.start()
        for copy in copies:
            copy.wait()

    return pl.pallas_call(
        kernel,
        out_shape=[jax.ShapeDtypeStruct(shape, jnp.bfloat16) for shape in shapes],
        in_specs=[pl.BlockSpec(memory_space=pltpu.HBM)] * len(sources),
        out_specs=[pl.BlockSpec(memory_space=pltpu.HBM)] * len(shapes),
        scratch_shapes=[pltpu.SemaphoreType.DMA((len(parts),))],
        compiler_params=pltpu.CompilerParams(vmem_limit_bytes=1 << 20),
        cost_estimate=EAGER,
    )(*sources)


def assemble(own, mine, theirs, place, rows):
    tokens = own.shape[0]

    def kernel(place, own, mine, theirs, share):
        share[:tokens, :] = own[...]
        for k in range(3):
            here = pl.ds((k + 1) * tokens, tokens)
            half = slice(k * 2 * rows, (k + 1) * 2 * rows)
            a, b = mine[:, half], theirs[:, half]
            share[here, : 2 * rows] = jnp.where(place[1] == 0, a, b)
            share[here, 2 * rows :] = jnp.where(place[1] == 0, b, a)

    vmem = pl.BlockSpec(memory_space=pltpu.VMEM)
    return pl.pallas_call(
        kernel,
        out_shape=jax.ShapeDtypeStruct((4 * tokens, 4 * rows), jnp.bfloat16),
        in_specs=[pl.BlockSpec(memory_space=pltpu.SMEM), vmem, vmem, vmem],
        out_specs=vmem,
        compiler_params=pltpu.CompilerParams(vmem_limit_bytes=8 << 20),
        cost_estimate=EAGER,
    )(place, own, mine, theirs)


def add_tail(parts, arrived):
    rows = parts[0].shape[0]
    widths = [part.shape[1] for part in parts]

    def kernel(*refs):
        out, at = refs[-1], 0
        for part, other, width in zip(refs, refs[len(parts) :], widths):
            out[:, at : at + width] = (part[...] + other[-rows:, :].astype(jnp.float32)).astype(jnp.bfloat16)
            at += width

    vmem = pl.BlockSpec(memory_space=pltpu.VMEM)
    return pl.pallas_call(
        kernel,
        out_shape=jax.ShapeDtypeStruct((rows, sum(widths)), jnp.bfloat16),
        in_specs=[vmem] * (2 * len(parts)),
        out_specs=vmem,
        compiler_params=pltpu.CompilerParams(vmem_limit_bytes=8 << 20),
        cost_estimate=EAGER,
    )(*parts, *arrived)


def flat(column):
    return jnp.broadcast_to(column, (128, 128)).T[0:1, :]


def upright(row):
    return jnp.broadcast_to(row, (128, 128)).T[:, 0:1]


def sum_up(kept, from_low, from_high, last_a, last_b, scale):
    rows = kept[0].shape[0]
    q = rows // 2
    widths = [part.shape[1] for part in kept]
    units = sum(widths)

    def kernel(*refs):
        kept_refs, low_refs, high_refs = refs[:2], refs[2:4], refs[4:6]
        last_refs, grad, row_part = refs[6:8], refs[8], refs[9]
        for h, arrived in enumerate((low_refs, high_refs)):
            for at in range(0, q, 128):
                total = jnp.zeros((128, 1), jnp.float32)
                here = slice(h * q + at, h * q + at + 128)
                column = 0
                for part, other, width in zip(kept_refs, arrived, widths):
                    there = slice(column, column + width)
                    value = part[here, :] + other[at : at + 128, :].astype(jnp.float32)
                    value = (value + last_refs[h][at : at + 128, there].astype(jnp.float32)) * scale
                    grad[here, there] = value
                    total = total + jnp.sum(value * value + 1e-30, axis=1, keepdims=True)
                    column += width
                row_part[:, here] = flat(total)

    vmem = pl.BlockSpec(memory_space=pltpu.VMEM)
    return pl.pallas_call(
        kernel,
        out_shape=[jax.ShapeDtypeStruct((rows, units), jnp.float32), jax.ShapeDtypeStruct((1, rows), jnp.float32)],
        in_specs=[vmem] * 8,
        out_specs=[vmem] * 2,
        compiler_params=pltpu.CompilerParams(vmem_limit_bytes=14 << 20),
        cost_estimate=EAGER,
    )(*kept, *from_low, *from_high, last_a, last_b)


def column_sums(grad, row_sum, row_moment, decay, total_units):
    rows, units = grad.shape

    def kernel(grad, row_sum, row_moment, row_moment_new, sums):
        new = decay * row_moment[...] + (1.0 - decay) * (row_sum[...] / total_units)
        row_moment_new[...] = new
        sums[:, 2 * units :] = jnp.broadcast_to(jnp.sum(new, axis=1, keepdims=True), (1, 128))
        inverse = [1.0 / upright(new[:, at : at + 128]) for at in range(0, rows, 128)]
        for column in range(0, units, 256):
            there = slice(column, column + 256)
            squares, scaled = jnp.zeros((1, 256), jnp.float32), jnp.zeros((1, 256), jnp.float32)
            for n, at in enumerate(range(0, rows, 128)):
                power = grad[at : at + 128, there]
                power = power * power
                squares = squares + jnp.sum(power + 1e-30, axis=0, keepdims=True)
                scaled = scaled + jnp.sum(power * inverse[n], axis=0, keepdims=True)
            sums[:, there] = squares
            sums[:, units + column : units + column + 256] = scaled

    vmem = pl.BlockSpec(memory_space=pltpu.VMEM)
    return pl.pallas_call(
        kernel,
        out_shape=[
            jax.ShapeDtypeStruct((1, rows), jnp.float32),
            jax.ShapeDtypeStruct((1, 2 * units + 128), jnp.float32),
        ],
        in_specs=[vmem] * 3,
        out_specs=[vmem] * 2,
        compiler_params=pltpu.CompilerParams(vmem_limit_bytes=14 << 20),
        cost_estimate=EAGER,
    )(grad, row_sum, row_moment)


def products(share, groups, steps):
    pieces = [(piece, group[1]) for group in groups for piece in group[0]]
    bounds = [(output, group[1]) for group in groups for output in group[2]]

    def kernel(*refs):
        share_ref, ins = refs[0], refs[1 : 1 + len(pieces)]
        outs, stacks = refs[1 + len(pieces) : -len(groups)], refs[-len(groups) :]
        n = o = 0
        for (own, _, outputs, over_rows), stack in zip(groups, stacks):
            at = 0
            for piece in own:
                stack[at : at + piece.shape[0], :] = ins[n][...]
                at += piece.shape[0]
                n += 1
            for ranges, kind in outputs:
                if over_rows:
                    side = jnp.concatenate([share_ref[:, begin:end] for begin, end in ranges], axis=1)
                    value = lax.dot_general(
                        side, stack[...], (((0,), (0,)), ((), ())), preferred_element_type=jnp.float32
                    )
                else:
                    side = jnp.concatenate([share_ref[begin:end, :] for begin, end in ranges], axis=0)
                    value = jnp.dot(side, stack[...], preferred_element_type=jnp.float32)
                outs[o][...] = value.astype(kind)
                o += 1

    def height(ranges):
        return sum(end - begin for begin, end in ranges)

    return pl.pallas_call(
        kernel,
        grid=(steps,),
        out_shape=[jax.ShapeDtypeStruct((height(ranges), columns), kind) for (ranges, kind), columns in bounds],
        in_specs=[pl.BlockSpec(share.shape, lambda i: (0, 0))]
        + [pl.BlockSpec((piece.shape[0], columns // steps), lambda i: (0, i)) for piece, columns in pieces],
        out_specs=[pl.BlockSpec((height(ranges), columns // steps), lambda i: (0, i)) for (ranges, _), columns in bounds],
        scratch_shapes=[
            pltpu.VMEM((sum(piece.shape[0] for piece in group[0]), group[1] // steps), jnp.bfloat16) for group in groups
        ],
        compiler_params=pltpu.CompilerParams(vmem_limit_bytes=14 << 20),
        cost_estimate=EAGER,
    )(share, *[piece for piece, _ in pieces])


def staged_products(out_grad, gate_pre, up_pre, down_weight):
    x_bit, y_bit, z_bit, w_bit = 1, 2, 4, 8
    me, core = lax.axis_index("dp"), lax.axis_index("mp")
    tokens, units = gate_pre.shape
    rows = down_weight.shape[0]
    q, t = rows // 2, tokens // 2
    steps = 4
    split = units * LEFT // 5
    barrier = lax.optimization_barrier
    place = jnp.stack([me, core]).astype(jnp.int32)
    own, right, message1, message2, message3 = first_stage(out_grad, gate_pre, up_pre, place, rows)

    down_weight, message1 = barrier((down_weight, message1))
    extra, every, whole = (split, 2 * rows), (0, tokens), (0, units)
    left1, left2, message3 = flip(message1, z_bit), flip(message2, w_bit), flip(message3, z_bit | w_bit)
    weight1, weight2 = flip(down_weight, x_bit), flip(down_weight, y_bit)
    message3, weight1, weight2 = barrier((message3, weight1, weight2))
    to_y, to_x = cut([weight1, weight2], [(0, (0, q), whole, 0, 0), (1, (q, q), whole, 1, 0)], [(q, units)] * 2)
    weight3a, weight3b = flip(to_y, y_bit), flip(to_x, x_bit)
    left1, left2, message3, right, _, _ = barrier((left1, left2, message3, right, to_y, to_x))
    to_z, mine = cut(
        [left1, left2, message3],
        [
            (1, every, (0, split), 0, 0),
            (0, every, extra, 1, 0),
            (1, every, extra, 1, 2 * rows),
            (2, every, (0, 2 * rows), 1, 4 * rows),
        ],
        [(tokens, split), (tokens, 6 * rows)],
    )
    left3 = flip(to_z, z_bit)
    right2 = flip(right, w_bit)
    theirs = flip(mine, 1, "mp")
    share = assemble(own, mine, theirs, place, rows)

    left3, right2, share, right, weight3a, weight3b = barrier((left3, right2, share, right, weight3a, weight3b))
    right1, right3 = flip(right, z_bit), flip(right2, z_bit)

    def low_sent(size):
        return [(2 * size, 3 * size), (6 * size, 7 * size)]

    def high_sent(size):
        return [(5 * size, 6 * size), (7 * size, 8 * size)]

    def sent(size):
        return [(low_sent(size), jnp.bfloat16), (high_sent(size), jnp.bfloat16)]

    def kept(size):
        ranges = [(0, 2 * size)], [(4 * size, 5 * size)], [(3 * size, 4 * size)]
        return [(r, jnp.float32) for r in ranges]

    lefts = [message1, left1, left2, left3]
    left_to_x, left_to_y = products(share, [(lefts, split, sent(q), True)], steps)
    left_from_x, left_from_y = flip(left_to_x, x_bit), flip(left_to_y, y_bit)
    share, _ = barrier((share, left_to_x))

    weights = [down_weight, weight1, weight2, weight3a, weight3b]
    first = [(high_sent(t)[1:], jnp.bfloat16), (high_sent(t)[:1], jnp.bfloat16), (low_sent(t), jnp.bfloat16)]
    to_w1, to_w2, to_z = products(share, [(weights, units, first, False)], steps)
    from_w1, from_w2, from_z = flip(to_w1, w_bit), flip(to_w2, w_bit), flip(to_z, z_bit)

    right1, right3, left_from_x, left_from_y, from_w1, share = barrier(
        (right1, right3, left_from_x, left_from_y, from_w1, share)
    )
    rights = [right, right1, right2, right3]
    right_to_x, right_to_y = products(share, [(rights, units - split, sent(q), True)], steps)
    right_from_x, right_from_y = flip(right_to_x, x_bit), flip(right_to_y, y_bit)
    share, _ = barrier((share, right_to_x))
    left_parts = products(share, [(lefts, split, kept(q), True)], steps)
    parts = products(share, [(rights, units - split, kept(q), True), (weights, units, kept(t), False)], steps)

    grad_a = flip(add_tail([left_parts[1], parts[1]], [left_from_x, right_from_x]), y_bit)
    grad_b = flip(add_tail([left_parts[2], parts[2]], [left_from_y, right_from_y]), x_bit)
    grad_a, grad_b, from_z, from_w2 = barrier((grad_a, grad_b, from_z, from_w2))
    grad, row_part = sum_up(
        [left_parts[0], parts[0]],
        [left_from_x, right_from_x],
        [left_from_y, right_from_y],
        grad_a,
        grad_b,
        1.0 / math.sqrt(tokens * lax.axis_size("dp")),
    )

    to_w, to_z = add_tail([parts[4]], [from_z]), add_tail([parts[5]], [from_w1])
    row_sum = lax.psum(row_part, "mp")
    row_sum, to_w, to_z = barrier((row_sum, to_w, to_z))
    last_a, last_b = flip(to_w, w_bit), flip(to_z, z_bit)
    return grad, row_sum, (parts[3], from_z, from_w2, last_a, last_b)


def hidden_gradients(gate_pre, up_pre, own_part, from_low, from_high, last_a, last_b):
    tokens, units = gate_pre.shape
    half, step = tokens // 2, 16

    def kernel(gate, up, own, low, high, last_a, last_b, gate_grad, up_grad):
        for h, (other, last) in enumerate(((low, last_a), (high, last_b))):

            @pl.loop(0, half // step)
            def _(i):
                here = pl.ds(pl.multiple_of(i * step, step), step)
                there = pl.ds(pl.multiple_of(h * half + i * step, step), step)
                value = own[there, :] + other[here, :].astype(jnp.float32) + last[here, :].astype(jnp.float32)
                activated, derivative = gelu_parts(gate[there, :].astype(jnp.float32))
                gate_grad[there, :] = (value * up[there, :].astype(jnp.float32) * derivative).astype(jnp.bfloat16)
                up_grad[there, :] = (value * activated).astype(jnp.bfloat16)

    vmem = pl.BlockSpec(memory_space=pltpu.VMEM)
    return pl.pallas_call(
        kernel,
        out_shape=[jax.ShapeDtypeStruct((tokens, units), jnp.bfloat16)] * 2,
        in_specs=[vmem] * 7,
        out_specs=[vmem] * 2,
        compiler_params=pltpu.CompilerParams(vmem_limit_bytes=12 << 20),
        cost_estimate=EAGER,
    )(gate_pre, up_pre, own_part, from_low, from_high, last_a, last_b)


def local(out_grad, gate_pre, up_pre, down_weight, row_moment, col_moment):
    size = lax.axis_size("dp")
    rows, units = down_weight.shape
    tokens = out_grad.shape[0]
    all_bits = [1 << b for b in range(size.bit_length() - 1)]
    decay = 1.0 - TRAIN_STEP ** (-0.8)
    total_rows = rows * size
    total_units = units * lax.axis_size("mp")
    staged = size == 16 and lax.axis_size("mp") == 2 and rows % 256 == 0 and tokens % 32 == 0 and units % 2560 == 0
    if staged:
        grad, row_sum, terms = staged_products(out_grad, gate_pre, up_pre, down_weight)
        row_moment_new, sums = column_sums(grad, row_sum, row_moment[None, :], decay, total_units)
        row_moment_new, sums = row_moment_new[0], group_sum(sums[0], all_bits[:INNER_BITS])
        sums, terms = lax.optimization_barrier((sums, terms))
        gate_grad, up_grad = hidden_gradients(gate_pre, up_pre, *terms)
    else:
        product, hidden_grad = general_products(
            out_grad, gate_pre, up_pre, down_weight, all_bits[:INNER_BITS], all_bits[INNER_BITS:]
        )
        grad = product * (1.0 / math.sqrt(tokens * size))
        powers = grad * grad
        squares = powers + 1e-30
        row_sum = lax.psum(jnp.sum(squares, axis=1), "mp")
        row_moment_new = decay * row_moment + (1.0 - decay) * (row_sum / total_units)
        col_part = jnp.sum(squares, axis=0)
        scaled_part = jnp.sum(powers / row_moment_new[:, None], axis=0)
        sums = jnp.concatenate([col_part, scaled_part, jnp.broadcast_to(jnp.sum(row_moment_new), (128,))])
        sums = group_sum(sums, all_bits[:INNER_BITS])
        activated, derivative = gelu_parts(gate_pre.astype(jnp.float32))
        gate_grad = (hidden_grad * up_pre.astype(jnp.float32) * derivative).astype(jnp.bfloat16)
        up_grad = (hidden_grad * activated).astype(jnp.bfloat16)

    sums = group_sum(sums, all_bits[INNER_BITS:])
    col_moment_new = decay * col_moment + (1.0 - decay) * (sums[:units] / total_rows)
    row_mean = sums[2 * units] / total_rows
    ratios = jnp.sum((sums[units : 2 * units] / col_moment_new).reshape(-1, 128), axis=0)
    square_sum = row_mean * jnp.sum(lax.psum(ratios, "mp"))
    clip_norm = jnp.sqrt(square_sum / (total_rows * total_units))
    row_factor = jnp.sqrt(row_mean / row_moment_new) / jnp.maximum(1.0, clip_norm)
    col_factor = 1.0 / jnp.sqrt(col_moment_new)
    update = grad * row_factor[:, None] * col_factor[None, :]
    return (update, row_moment_new, col_moment_new, row_mean, gate_grad, up_grad)


def solution(mesh):
    in_specs = (P("dp", None), P("dp", "mp"), P("dp", "mp"), P("dp", "mp"), P("dp"), P("mp"))
    out_specs = (P("dp", "mp"), P("dp"), P("mp"), P(), P("dp", "mp"), P("dp", "mp"))
    return jax.shard_map(local, mesh=mesh, in_specs=in_specs, out_specs=out_specs, check_vma=False)
```

```python
import math

import jax
import jax.numpy as jnp
from jax import lax
from jax.experimental import pallas as pl
from jax.experimental.pallas import tpu as pltpu
from jax.sharding import PartitionSpec as P

TRAIN_STEP = 3
INNER_BITS = 2
EAGER = pl.CostEstimate(flops=0, bytes_accessed=0, transcendentals=0)


def gelu_parts(values):
    factor = math.sqrt(2.0 / math.pi)
    inner = factor * (values + 0.044715 * values * values * values)
    tangent = jnp.tanh(inner)
    activated = 0.5 * values * (1.0 + tangent)
    derivative = 0.5 * (1.0 + tangent) + 0.5 * values * (1.0 - tangent * tangent) * factor * (
        1.0 + 3.0 * 0.044715 * values * values
    )
    return (activated, derivative)


def flip(value, bits, axis="dp"):
    size = lax.axis_size(axis)
    return lax.ppermute(value, axis, [(i, i ^ bits) for i in range(size)])


def group_sum(value, bits):
    for at in range(0, len(bits), 2):
        pair = bits[at : at + 2]
        if len(pair) == 2:
            first, second = flip(value, pair[0]), flip(value, pair[1])
            value = (value + first) + (second + flip(value, pair[0] | pair[1]))
        else:
            value = value + flip(value, pair[0])
    return value


def general_products(out_grad, gate_pre, up_pre, down_weight, inner_bits, outer_bits):
    size = lax.axis_size("dp")
    me = lax.axis_index("dp")
    tokens, rows = out_grad.shape[0], down_weight.shape[0]
    inner = 2 ** len(inner_bits)
    activated, _ = gelu_parts(gate_pre.astype(jnp.float32))
    hidden = (activated * up_pre.astype(jnp.float32)).astype(jnp.bfloat16)
    by_block = out_grad.reshape(tokens, size, rows).transpose(1, 0, 2)

    def features_of(k):
        picks = [lax.dynamic_index_in_dim(by_block, me ^ (k * inner + j), 0, keepdims=False) for j in range(inner)]
        return jnp.concatenate(picks, axis=1)

    def gather(block, bits):
        blocks = [block]
        for bit in bits:
            blocks = blocks + [flip(b, bit) for b in blocks]
        return jnp.concatenate(blocks, axis=0)

    def scatter(values, bits):
        for level in reversed(range(len(bits))):
            count = 2**level
            values = [
                values[j] + flip(values[j + count].astype(jnp.bfloat16), bits[level]).astype(jnp.float32)
                for j in range(count)
            ]
        return values[0]

    shares = [features_of(0)] + [flip(features_of(k), k * inner) for k in range(1, size // inner)]
    share = jnp.concatenate(shares, axis=0)
    hidden_all = gather(hidden, outer_bits)
    weight_all = gather(down_weight, inner_bits)
    product = scatter(
        [
            lax.dot_general(
                share[:, j * rows : (j + 1) * rows],
                hidden_all,
                (((0,), (0,)), ((), ())),
                preferred_element_type=jnp.float32,
            )
            for j in range(inner)
        ],
        inner_bits,
    )
    hidden_grad = scatter(
        [jnp.dot(x, weight_all, preferred_element_type=jnp.float32) for x in shares],
        outer_bits,
    )
    return product, hidden_grad


def first_stage(out_grad, gate_pre, up_pre, place, rows):
    tokens, units = gate_pre.shape
    half = units // 2
    step = 32

    def kernel(place, source_hbm, gate_hbm, up_hbm, own, right, message1, message2, message3, source, gate, up, sems):
        copies = [
            pltpu.make_async_copy(there, here, sems.at[n])
            for n, (there, here) in enumerate(((gate_hbm, gate), (up_hbm, up), (source_hbm, source)))
        ]
        for copy in copies:
            copy.start()
        me, core = place[0], place[1]

        def block(k, j):
            return pl.ds(pl.multiple_of((me ^ (4 * k + j)) * rows, rows), rows)

        copies[0].wait()
        copies[1].wait()

        @pl.loop(0, tokens // step)
        def _(i):
            here = pl.ds(pl.multiple_of(i * step, step), step)
            activated, _ = gelu_parts(gate[here, :].astype(jnp.float32))
            value = (activated * up[here, :].astype(jnp.float32)).astype(jnp.bfloat16)
            right[here, :] = value[:, half:]
            message1[here, :half] = value[:, :half]
            message2[here, :half] = value[:, :half]

        copies[2].wait()
        for j in range(4):
            own[:, j * rows : (j + 1) * rows] = source[:, block(0, j)]
        for k, target, base in ((1, message1, half), (2, message2, half), (3, message3, 0)):
            for j in range(2):
                target[:, base + j * rows : base + (j + 1) * rows] = source[:, block(k, 2 * core + j)]

    vmem = pl.BlockSpec(memory_space=pltpu.VMEM)
    widths = [4 * rows, units - half, half + 2 * rows, half + 2 * rows, 2 * rows]
    return pl.pallas_call(
        kernel,
        out_shape=[jax.ShapeDtypeStruct((tokens, width), jnp.bfloat16) for width in widths],
        in_specs=[pl.BlockSpec(memory_space=pltpu.SMEM)] + [pl.BlockSpec(memory_space=pltpu.HBM)] * 3,
        out_specs=[vmem] * len(widths),
        scratch_shapes=[
            pltpu.VMEM(out_grad.shape, jnp.bfloat16),
            pltpu.VMEM(gate_pre.shape, jnp.bfloat16),
            pltpu.VMEM(up_pre.shape, jnp.bfloat16),
            pltpu.SemaphoreType.DMA((3,)),
        ],
        compiler_params=pltpu.CompilerParams(vmem_limit_bytes=16 << 20),
        cost_estimate=EAGER,
    )(place, out_grad, gate_pre, up_pre)


def cut(sources, parts, shapes):
    def kernel(*refs):
        ins, outs, sems = refs[: len(sources)], refs[len(sources) : -1], refs[-1]
        copies = [
            pltpu.make_async_copy(
                ins[i].at[pl.ds(*rows), pl.ds(*columns)], outs[o].at[:, pl.ds(at, columns[1])], sems.at[n]
            )
            for n, (i, rows, columns, o, at) in enumerate(parts)
        ]
        for copy in copies:
            copy.start()
        for copy in copies:
            copy.wait()

    return pl.pallas_call(
        kernel,
        out_shape=[jax.ShapeDtypeStruct(shape, jnp.bfloat16) for shape in shapes],
        in_specs=[pl.BlockSpec(memory_space=pltpu.HBM)] * len(sources),
        out_specs=[pl.BlockSpec(memory_space=pltpu.HBM)] * len(shapes),
        scratch_shapes=[pltpu.SemaphoreType.DMA((len(parts),))],
        compiler_params=pltpu.CompilerParams(vmem_limit_bytes=1 << 20),
        cost_estimate=EAGER,
    )(*sources)


def assemble(own, mine, theirs, place, rows):
    tokens = own.shape[0]

    def kernel(place, own, mine, theirs, share):
        share[:tokens, :] = own[...]
        for k in range(3):
            here = pl.ds((k + 1) * tokens, tokens)
            half = slice(k * 2 * rows, (k + 1) * 2 * rows)
            a, b = mine[:, half], theirs[:, half]
            share[here, : 2 * rows] = jnp.where(place[1] == 0, a, b)
            share[here, 2 * rows :] = jnp.where(place[1] == 0, b, a)

    vmem = pl.BlockSpec(memory_space=pltpu.VMEM)
    return pl.pallas_call(
        kernel,
        out_shape=jax.ShapeDtypeStruct((4 * tokens, 4 * rows), jnp.bfloat16),
        in_specs=[pl.BlockSpec(memory_space=pltpu.SMEM), vmem, vmem, vmem],
        out_specs=vmem,
        compiler_params=pltpu.CompilerParams(vmem_limit_bytes=8 << 20),
        cost_estimate=EAGER,
    )(place, own, mine, theirs)


def add_tail(parts, arrived):
    rows = parts[0].shape[0]
    widths = [part.shape[1] for part in parts]

    def kernel(*refs):
        out, at = refs[-1], 0
        for part, other, width in zip(refs, refs[len(parts) :], widths):
            out[:, at : at + width] = (part[...] + other[-rows:, :].astype(jnp.float32)).astype(jnp.bfloat16)
            at += width

    vmem = pl.BlockSpec(memory_space=pltpu.VMEM)
    return pl.pallas_call(
        kernel,
        out_shape=jax.ShapeDtypeStruct((rows, sum(widths)), jnp.bfloat16),
        in_specs=[vmem] * (2 * len(parts)),
        out_specs=vmem,
        compiler_params=pltpu.CompilerParams(vmem_limit_bytes=8 << 20),
        cost_estimate=EAGER,
    )(*parts, *arrived)


def flat(column):
    return jnp.broadcast_to(column, (128, 128)).T[0:1, :]


def upright(row):
    return jnp.broadcast_to(row, (128, 128)).T[:, 0:1]


def sum_up(kept, from_low, from_high, last_a, last_b, scale):
    rows = kept[0].shape[0]
    q = rows // 2
    widths = [part.shape[1] for part in kept]
    units = sum(widths)

    def kernel(*refs):
        kept_refs, low_refs, high_refs = refs[:2], refs[2:4], refs[4:6]
        last_refs, grad, row_part = refs[6:8], refs[8], refs[9]
        for h, arrived in enumerate((low_refs, high_refs)):
            for at in range(0, q, 128):
                total = jnp.zeros((128, 1), jnp.float32)
                here = slice(h * q + at, h * q + at + 128)
                column = 0
                for part, other, width in zip(kept_refs, arrived, widths):
                    there = slice(column, column + width)
                    value = part[here, :] + other[at : at + 128, :].astype(jnp.float32)
                    value = (value + last_refs[h][at : at + 128, there].astype(jnp.float32)) * scale
                    grad[here, there] = value
                    total = total + jnp.sum(value * value + 1e-30, axis=1, keepdims=True)
                    column += width
                row_part[:, here] = flat(total)

    vmem = pl.BlockSpec(memory_space=pltpu.VMEM)
    return pl.pallas_call(
        kernel,
        out_shape=[jax.ShapeDtypeStruct((rows, units), jnp.float32), jax.ShapeDtypeStruct((1, rows), jnp.float32)],
        in_specs=[vmem] * 8,
        out_specs=[vmem] * 2,
        compiler_params=pltpu.CompilerParams(vmem_limit_bytes=14 << 20),
        cost_estimate=EAGER,
    )(*kept, *from_low, *from_high, last_a, last_b)


def column_sums(grad, row_sum, row_moment, decay, total_units):
    rows, units = grad.shape

    def kernel(grad, row_sum, row_moment, row_moment_new, sums):
        new = decay * row_moment[...] + (1.0 - decay) * (row_sum[...] / total_units)
        row_moment_new[...] = new
        sums[:, 2 * units :] = jnp.broadcast_to(jnp.sum(new, axis=1, keepdims=True), (1, 128))
        inverse = [1.0 / upright(new[:, at : at + 128]) for at in range(0, rows, 128)]
        for column in range(0, units, 256):
            there = slice(column, column + 256)
            squares, scaled = jnp.zeros((1, 256), jnp.float32), jnp.zeros((1, 256), jnp.float32)
            for n, at in enumerate(range(0, rows, 128)):
                power = grad[at : at + 128, there]
                power = power * power
                squares = squares + jnp.sum(power + 1e-30, axis=0, keepdims=True)
                scaled = scaled + jnp.sum(power * inverse[n], axis=0, keepdims=True)
            sums[:, there] = squares
            sums[:, units + column : units + column + 256] = scaled

    vmem = pl.BlockSpec(memory_space=pltpu.VMEM)
    return pl.pallas_call(
        kernel,
        out_shape=[
            jax.ShapeDtypeStruct((1, rows), jnp.float32),
            jax.ShapeDtypeStruct((1, 2 * units + 128), jnp.float32),
        ],
        in_specs=[vmem] * 3,
        out_specs=[vmem] * 2,
        compiler_params=pltpu.CompilerParams(vmem_limit_bytes=14 << 20),
        cost_estimate=EAGER,
    )(grad, row_sum, row_moment)


def products(share, groups, steps):
    pieces = [(piece, group[1]) for group in groups for piece in group[0]]
    bounds = [(output, group[1]) for group in groups for output in group[2]]

    def kernel(*refs):
        share_ref, ins = refs[0], refs[1 : 1 + len(pieces)]
        outs, stacks = refs[1 + len(pieces) : -len(groups)], refs[-len(groups) :]
        n = o = 0
        for (own, _, outputs, over_rows), stack in zip(groups, stacks):
            at = 0
            for piece in own:
                stack[at : at + piece.shape[0], :] = ins[n][...]
                at += piece.shape[0]
                n += 1
            for ranges, kind in outputs:
                if over_rows:
                    side = jnp.concatenate([share_ref[:, begin:end] for begin, end in ranges], axis=1)
                    value = lax.dot_general(
                        side, stack[...], (((0,), (0,)), ((), ())), preferred_element_type=jnp.float32
                    )
                else:
                    side = jnp.concatenate([share_ref[begin:end, :] for begin, end in ranges], axis=0)
                    value = jnp.dot(side, stack[...], preferred_element_type=jnp.float32)
                outs[o][...] = value.astype(kind)
                o += 1

    def height(ranges):
        return sum(end - begin for begin, end in ranges)

    return pl.pallas_call(
        kernel,
        grid=(steps,),
        out_shape=[jax.ShapeDtypeStruct((height(ranges), columns), kind) for (ranges, kind), columns in bounds],
        in_specs=[pl.BlockSpec(share.shape, lambda i: (0, 0))]
        + [pl.BlockSpec((piece.shape[0], columns // steps), lambda i: (0, i)) for piece, columns in pieces],
        out_specs=[pl.BlockSpec((height(ranges), columns // steps), lambda i: (0, i)) for (ranges, _), columns in bounds],
        scratch_shapes=[
            pltpu.VMEM((sum(piece.shape[0] for piece in group[0]), group[1] // steps), jnp.bfloat16) for group in groups
        ],
        compiler_params=pltpu.CompilerParams(vmem_limit_bytes=14 << 20),
        cost_estimate=EAGER,
    )(share, *[piece for piece, _ in pieces])


def staged_products(out_grad, gate_pre, up_pre, down_weight):
    x_bit, y_bit, z_bit, w_bit = 1, 2, 4, 8
    me, core = lax.axis_index("dp"), lax.axis_index("mp")
    tokens, units = gate_pre.shape
    rows = down_weight.shape[0]
    q, t = rows // 2, tokens // 2
    steps = 5
    split = units // 2
    barrier = lax.optimization_barrier
    place = jnp.stack([me, core]).astype(jnp.int32)
    own, right, message1, message2, message3 = first_stage(out_grad, gate_pre, up_pre, place, rows)

    down_weight, message1 = barrier((down_weight, message1))
    extra, every, whole = (split, 2 * rows), (0, tokens), (0, units)
    left1, left2, message3 = flip(message1, z_bit), flip(message2, w_bit), flip(message3, z_bit | w_bit)
    weight1, weight2 = flip(down_weight, x_bit), flip(down_weight, y_bit)
    message3, weight1, weight2 = barrier((message3, weight1, weight2))
    to_y, to_x = cut([weight1, weight2], [(0, (0, q), whole, 0, 0), (1, (q, q), whole, 1, 0)], [(q, units)] * 2)
    weight3a, weight3b = flip(to_y, y_bit), flip(to_x, x_bit)
    left1, left2, message3, right, _, _ = barrier((left1, left2, message3, right, to_y, to_x))
    to_z, mine = cut(
        [left1, left2, message3],
        [
            (1, every, (0, split), 0, 0),
            (0, every, extra, 1, 0),
            (1, every, extra, 1, 2 * rows),
            (2, every, (0, 2 * rows), 1, 4 * rows),
        ],
        [(tokens, split), (tokens, 6 * rows)],
    )
    left3 = flip(to_z, z_bit)
    right2 = flip(right, w_bit)
    theirs = flip(mine, 1, "mp")
    share = assemble(own, mine, theirs, place, rows)

    def low_sent(size):
        return [(2 * size, 3 * size), (6 * size, 7 * size)]

    def high_sent(size):
        return [(5 * size, 6 * size), (7 * size, 8 * size)]

    def sent(size):
        return [(low_sent(size), jnp.bfloat16), (high_sent(size), jnp.bfloat16)]

    def kept(size):
        ranges = [(0, 2 * size)], [(4 * size, 5 * size)], [(3 * size, 4 * size)]
        return [(r, jnp.float32) for r in ranges]

    weights = [down_weight, weight1, weight2, weight3a, weight3b]
    first = [(high_sent(t)[1:], jnp.bfloat16), (high_sent(t)[:1], jnp.bfloat16), (low_sent(t), jnp.bfloat16)]
    to_w1, to_w2, to_z = products(share, [(weights, units, first, False)], steps)
    left3, right2, share, right, to_w1 = barrier((left3, right2, share, right, to_w1))
    right1, right3 = flip(right, z_bit), flip(right2, z_bit)
    from_w1 = flip(to_w1, w_bit)

    lefts = [message1, left1, left2, left3]
    left_to_x, left_to_y = products(share, [(lefts, split, sent(q), True)], steps)
    left_from_x, left_from_y = flip(left_to_x, x_bit), flip(left_to_y, y_bit)

    right1, right3, from_w1, share, _ = barrier((right1, right3, from_w1, share, left_to_x))
    rights = [right, right1, right2, right3]
    right_to_x, right_to_y = products(share, [(rights, units - split, sent(q), True)], steps)
    right_from_x, right_from_y = flip(right_to_x, x_bit), flip(right_to_y, y_bit)
    from_w2, from_z = flip(to_w2, w_bit), flip(to_z, z_bit)
    share, left_from_x, left_from_y, _ = barrier((share, left_from_x, left_from_y, right_to_x))
    left_parts = products(share, [(lefts, split, kept(q), True)], steps)
    parts = products(share, [(rights, units - split, kept(q), True), (weights, units, kept(t), False)], steps)

    grad_a = flip(add_tail([left_parts[1], parts[1]], [left_from_x, right_from_x]), y_bit)
    grad_b = flip(add_tail([left_parts[2], parts[2]], [left_from_y, right_from_y]), x_bit)
    last_b = flip(add_tail([parts[5]], [from_w1]), z_bit)
    grad_a, grad_b, from_z, from_w2, last_b = barrier((grad_a, grad_b, from_z, from_w2, last_b))
    grad, row_part = sum_up(
        [left_parts[0], parts[0]],
        [left_from_x, right_from_x],
        [left_from_y, right_from_y],
        grad_a,
        grad_b,
        1.0 / math.sqrt(tokens * lax.axis_size("dp")),
    )

    to_w = add_tail([parts[4]], [from_z])
    row_sum = lax.psum(row_part, "mp")
    row_sum, to_w = barrier((row_sum, to_w))
    last_a = flip(to_w, w_bit)
    return grad, row_sum, (parts[3], from_z, from_w2, last_a, last_b)


def hidden_gradients(gate_pre, up_pre, own_part, from_low, from_high, last_a, last_b):
    tokens, units = gate_pre.shape
    half, step = tokens // 2, 16

    def kernel(gate, up, own, low, high, last_a, last_b, gate_grad, up_grad):
        for h, (other, last) in enumerate(((low, last_a), (high, last_b))):

            @pl.loop(0, half // step)
            def _(i):
                here = pl.ds(pl.multiple_of(i * step, step), step)
                there = pl.ds(pl.multiple_of(h * half + i * step, step), step)
                value = own[there, :] + other[here, :].astype(jnp.float32) + last[here, :].astype(jnp.float32)
                activated, derivative = gelu_parts(gate[there, :].astype(jnp.float32))
                gate_grad[there, :] = (value * up[there, :].astype(jnp.float32) * derivative).astype(jnp.bfloat16)
                up_grad[there, :] = (value * activated).astype(jnp.bfloat16)

    vmem = pl.BlockSpec(memory_space=pltpu.VMEM)
    return pl.pallas_call(
        kernel,
        out_shape=[jax.ShapeDtypeStruct((tokens, units), jnp.bfloat16)] * 2,
        in_specs=[vmem] * 7,
        out_specs=[vmem] * 2,
        compiler_params=pltpu.CompilerParams(vmem_limit_bytes=12 << 20),
        cost_estimate=EAGER,
    )(gate_pre, up_pre, own_part, from_low, from_high, last_a, last_b)


def local(out_grad, gate_pre, up_pre, down_weight, row_moment, col_moment):
    size = lax.axis_size("dp")
    rows, units = down_weight.shape
    tokens = out_grad.shape[0]
    all_bits = [1 << b for b in range(size.bit_length() - 1)]
    decay = 1.0 - TRAIN_STEP ** (-0.8)
    total_rows = rows * size
    total_units = units * lax.axis_size("mp")
    staged = size == 16 and lax.axis_size("mp") == 2 and rows % 256 == 0 and tokens % 32 == 0 and units % 2560 == 0
    if staged:
        grad, row_sum, terms = staged_products(out_grad, gate_pre, up_pre, down_weight)
        row_moment_new, sums = column_sums(grad, row_sum, row_moment[None, :], decay, total_units)
        row_moment_new, sums = row_moment_new[0], group_sum(sums[0], all_bits[:INNER_BITS])
        sums, terms = lax.optimization_barrier((sums, terms))
        gate_grad, up_grad = hidden_gradients(gate_pre, up_pre, *terms)
    else:
        product, hidden_grad = general_products(
            out_grad, gate_pre, up_pre, down_weight, all_bits[:INNER_BITS], all_bits[INNER_BITS:]
        )
        grad = product * (1.0 / math.sqrt(tokens * size))
        powers = grad * grad
        squares = powers + 1e-30
        row_sum = lax.psum(jnp.sum(squares, axis=1), "mp")
        row_moment_new = decay * row_moment + (1.0 - decay) * (row_sum / total_units)
        col_part = jnp.sum(squares, axis=0)
        scaled_part = jnp.sum(powers / row_moment_new[:, None], axis=0)
        sums = jnp.concatenate([col_part, scaled_part, jnp.broadcast_to(jnp.sum(row_moment_new), (128,))])
        sums = group_sum(sums, all_bits[:INNER_BITS])
        activated, derivative = gelu_parts(gate_pre.astype(jnp.float32))
        gate_grad = (hidden_grad * up_pre.astype(jnp.float32) * derivative).astype(jnp.bfloat16)
        up_grad = (hidden_grad * activated).astype(jnp.bfloat16)

    sums = group_sum(sums, all_bits[INNER_BITS:])
    col_moment_new = decay * col_moment + (1.0 - decay) * (sums[:units] / total_rows)
    row_mean = sums[2 * units] / total_rows
    ratios = jnp.sum((sums[units : 2 * units] / col_moment_new).reshape(-1, 128), axis=0)
    square_sum = row_mean * jnp.sum(lax.psum(ratios, "mp"))
    clip_norm = jnp.sqrt(square_sum / (total_rows * total_units))
    row_factor = jnp.sqrt(row_mean / row_moment_new) / jnp.maximum(1.0, clip_norm)
    col_factor = 1.0 / jnp.sqrt(col_moment_new)
    update = grad * row_factor[:, None] * col_factor[None, :]
    return (update, row_moment_new, col_moment_new, row_mean, gate_grad, up_grad)


def solution(mesh):
    in_specs = (P("dp", None), P("dp", "mp"), P("dp", "mp"), P("dp", "mp"), P("dp"), P("mp"))
    out_specs = (P("dp", "mp"), P("dp"), P("mp"), P(), P("dp", "mp"), P("dp", "mp"))
    return jax.shard_map(local, mesh=mesh, in_specs=in_specs, out_specs=out_specs, check_vma=False)
```

```python
import math

import jax
import jax.numpy as jnp
from jax import lax
from jax.experimental import pallas as pl
from jax.experimental.pallas import tpu as pltpu
from jax.sharding import PartitionSpec as P

TRAIN_STEP = 3
INNER_BITS = 2
EAGER = pl.CostEstimate(flops=0, bytes_accessed=0, transcendentals=0)


def gelu_parts(values):
    factor = math.sqrt(2.0 / math.pi)
    inner = factor * (values + 0.044715 * values * values * values)
    tangent = jnp.tanh(inner)
    activated = 0.5 * values * (1.0 + tangent)
    derivative = 0.5 * (1.0 + tangent) + 0.5 * values * (1.0 - tangent * tangent) * factor * (
        1.0 + 3.0 * 0.044715 * values * values
    )
    return (activated, derivative)


def flip(value, bits, axis="dp"):
    size = lax.axis_size(axis)
    return lax.ppermute(value, axis, [(i, i ^ bits) for i in range(size)])


def group_sum(value, bits):
    for at in range(0, len(bits), 2):
        pair = bits[at : at + 2]
        if len(pair) == 2:
            first, second = flip(value, pair[0]), flip(value, pair[1])
            value = (value + first) + (second + flip(value, pair[0] | pair[1]))
        else:
            value = value + flip(value, pair[0])
    return value


def general_products(out_grad, gate_pre, up_pre, down_weight, inner_bits, outer_bits):
    size = lax.axis_size("dp")
    me = lax.axis_index("dp")
    tokens, rows = out_grad.shape[0], down_weight.shape[0]
    inner = 2 ** len(inner_bits)
    activated, _ = gelu_parts(gate_pre.astype(jnp.float32))
    hidden = (activated * up_pre.astype(jnp.float32)).astype(jnp.bfloat16)
    by_block = out_grad.reshape(tokens, size, rows).transpose(1, 0, 2)

    def features_of(k):
        picks = [lax.dynamic_index_in_dim(by_block, me ^ (k * inner + j), 0, keepdims=False) for j in range(inner)]
        return jnp.concatenate(picks, axis=1)

    def gather(block, bits):
        blocks = [block]
        for bit in bits:
            blocks = blocks + [flip(b, bit) for b in blocks]
        return jnp.concatenate(blocks, axis=0)

    def scatter(values, bits):
        for level in reversed(range(len(bits))):
            count = 2**level
            values = [
                values[j] + flip(values[j + count].astype(jnp.bfloat16), bits[level]).astype(jnp.float32)
                for j in range(count)
            ]
        return values[0]

    shares = [features_of(0)] + [flip(features_of(k), k * inner) for k in range(1, size // inner)]
    share = jnp.concatenate(shares, axis=0)
    hidden_all = gather(hidden, outer_bits)
    weight_all = gather(down_weight, inner_bits)
    product = scatter(
        [
            lax.dot_general(
                share[:, j * rows : (j + 1) * rows],
                hidden_all,
                (((0,), (0,)), ((), ())),
                preferred_element_type=jnp.float32,
            )
            for j in range(inner)
        ],
        inner_bits,
    )
    hidden_grad = scatter(
        [jnp.dot(x, weight_all, preferred_element_type=jnp.float32) for x in shares],
        outer_bits,
    )
    return product, hidden_grad


def first_stage(out_grad, gate_pre, up_pre, place, rows):
    tokens, units = gate_pre.shape
    half = units // 2
    step = 32

    def kernel(place, source_hbm, gate_hbm, up_hbm, own, right, message1, message2, message3, source, gate, up, sems):
        copies = [
            pltpu.make_async_copy(there, here, sems.at[n])
            for n, (there, here) in enumerate(((gate_hbm, gate), (up_hbm, up), (source_hbm, source)))
        ]
        for copy in copies:
            copy.start()
        me, core = place[0], place[1]

        def block(k, j):
            return pl.ds(pl.multiple_of((me ^ (4 * k + j)) * rows, rows), rows)

        copies[0].wait()
        copies[1].wait()

        @pl.loop(0, tokens // step)
        def _(i):
            here = pl.ds(pl.multiple_of(i * step, step), step)
            activated, _ = gelu_parts(gate[here, :].astype(jnp.float32))
            value = (activated * up[here, :].astype(jnp.float32)).astype(jnp.bfloat16)
            right[here, :] = value[:, half:]
            message1[here, :half] = value[:, :half]
            message2[here, :half] = value[:, :half]

        copies[2].wait()
        for j in range(4):
            own[:, j * rows : (j + 1) * rows] = source[:, block(0, j)]
        for k, target, base in ((1, message1, half), (2, message2, half), (3, message3, 0)):
            for j in range(2):
                target[:, base + j * rows : base + (j + 1) * rows] = source[:, block(k, 2 * core + j)]

    vmem = pl.BlockSpec(memory_space=pltpu.VMEM)
    widths = [4 * rows, units - half, half + 2 * rows, half + 2 * rows, 2 * rows]
    return pl.pallas_call(
        kernel,
        out_shape=[jax.ShapeDtypeStruct((tokens, width), jnp.bfloat16) for width in widths],
        in_specs=[pl.BlockSpec(memory_space=pltpu.SMEM)] + [pl.BlockSpec(memory_space=pltpu.HBM)] * 3,
        out_specs=[vmem] * len(widths),
        scratch_shapes=[
            pltpu.VMEM(out_grad.shape, jnp.bfloat16),
            pltpu.VMEM(gate_pre.shape, jnp.bfloat16),
            pltpu.VMEM(up_pre.shape, jnp.bfloat16),
            pltpu.SemaphoreType.DMA((3,)),
        ],
        compiler_params=pltpu.CompilerParams(vmem_limit_bytes=16 << 20),
        cost_estimate=EAGER,
    )(place, out_grad, gate_pre, up_pre)


def cut(sources, parts, shapes):
    def kernel(*refs):
        ins, outs, sems = refs[: len(sources)], refs[len(sources) : -1], refs[-1]
        copies = [
            pltpu.make_async_copy(
                ins[i].at[pl.ds(*rows), pl.ds(*columns)], outs[o].at[:, pl.ds(at, columns[1])], sems.at[n]
            )
            for n, (i, rows, columns, o, at) in enumerate(parts)
        ]
        for copy in copies:
            copy.start()
        for copy in copies:
            copy.wait()

    return pl.pallas_call(
        kernel,
        out_shape=[jax.ShapeDtypeStruct(shape, jnp.bfloat16) for shape in shapes],
        in_specs=[pl.BlockSpec(memory_space=pltpu.HBM)] * len(sources),
        out_specs=[pl.BlockSpec(memory_space=pltpu.HBM)] * len(shapes),
        scratch_shapes=[pltpu.SemaphoreType.DMA((len(parts),))],
        compiler_params=pltpu.CompilerParams(vmem_limit_bytes=1 << 20),
        cost_estimate=EAGER,
    )(*sources)


def assemble(own, mine, theirs, place, rows):
    tokens = own.shape[0]

    def kernel(place, own, mine, theirs, share):
        share[:tokens, :] = own[...]
        for k in range(3):
            here = pl.ds((k + 1) * tokens, tokens)
            half = slice(k * 2 * rows, (k + 1) * 2 * rows)
            a, b = mine[:, half], theirs[:, half]
            share[here, : 2 * rows] = jnp.where(place[1] == 0, a, b)
            share[here, 2 * rows :] = jnp.where(place[1] == 0, b, a)

    vmem = pl.BlockSpec(memory_space=pltpu.VMEM)
    return pl.pallas_call(
        kernel,
        out_shape=jax.ShapeDtypeStruct((4 * tokens, 4 * rows), jnp.bfloat16),
        in_specs=[pl.BlockSpec(memory_space=pltpu.SMEM), vmem, vmem, vmem],
        out_specs=vmem,
        compiler_params=pltpu.CompilerParams(vmem_limit_bytes=8 << 20),
        cost_estimate=EAGER,
    )(place, own, mine, theirs)


def add_tail(parts, arrived):
    rows = parts[0].shape[0]
    widths = [part.shape[1] for part in parts]

    def kernel(*refs):
        out, at = refs[-1], 0
        for part, other, width in zip(refs, refs[len(parts) :], widths):
            out[:, at : at + width] = (part[...] + other[-rows:, :].astype(jnp.float32)).astype(jnp.bfloat16)
            at += width

    vmem = pl.BlockSpec(memory_space=pltpu.VMEM)
    return pl.pallas_call(
        kernel,
        out_shape=jax.ShapeDtypeStruct((rows, sum(widths)), jnp.bfloat16),
        in_specs=[vmem] * (2 * len(parts)),
        out_specs=vmem,
        compiler_params=pltpu.CompilerParams(vmem_limit_bytes=8 << 20),
        cost_estimate=EAGER,
    )(*parts, *arrived)


def flat(column):
    return jnp.broadcast_to(column, (128, 128)).T[0:1, :]


def upright(row):
    return jnp.broadcast_to(row, (128, 128)).T[:, 0:1]


def sum_up(kept, from_low, from_high, last_a, last_b, scale):
    rows = kept[0].shape[0]
    q = rows // 2
    widths = [part.shape[1] for part in kept]
    units = sum(widths)

    def kernel(*refs):
        kept_refs, low_refs, high_refs = refs[:2], refs[2:4], refs[4:6]
        last_refs, grad, row_part = refs[6:8], refs[8], refs[9]
        for h, arrived in enumerate((low_refs, high_refs)):
            for at in range(0, q, 128):
                total = jnp.zeros((128, 1), jnp.float32)
                here = slice(h * q + at, h * q + at + 128)
                column = 0
                for part, other, width in zip(kept_refs, arrived, widths):
                    there = slice(column, column + width)
                    value = part[here, :] + other[at : at + 128, :].astype(jnp.float32)
                    value = (value + last_refs[h][at : at + 128, there].astype(jnp.float32)) * scale
                    grad[here, there] = value
                    total = total + jnp.sum(value * value + 1e-30, axis=1, keepdims=True)
                    column += width
                row_part[:, here] = flat(total)

    vmem = pl.BlockSpec(memory_space=pltpu.VMEM)
    return pl.pallas_call(
        kernel,
        out_shape=[jax.ShapeDtypeStruct((rows, units), jnp.float32), jax.ShapeDtypeStruct((1, rows), jnp.float32)],
        in_specs=[vmem] * 8,
        out_specs=[vmem] * 2,
        compiler_params=pltpu.CompilerParams(vmem_limit_bytes=14 << 20),
        cost_estimate=EAGER,
    )(*kept, *from_low, *from_high, last_a, last_b)


def column_sums(grad, row_sum, row_moment, decay, total_units):
    rows, units = grad.shape

    def kernel(grad, row_sum, row_moment, row_moment_new, sums):
        new = decay * row_moment[...] + (1.0 - decay) * (row_sum[...] / total_units)
        row_moment_new[...] = new
        sums[:, 2 * units :] = jnp.broadcast_to(jnp.sum(new, axis=1, keepdims=True), (1, 128))
        inverse = [1.0 / upright(new[:, at : at + 128]) for at in range(0, rows, 128)]
        for column in range(0, units, 256):
            there = slice(column, column + 256)
            squares, scaled = jnp.zeros((1, 256), jnp.float32), jnp.zeros((1, 256), jnp.float32)
            for n, at in enumerate(range(0, rows, 128)):
                power = grad[at : at + 128, there]
                power = power * power
                squares = squares + jnp.sum(power + 1e-30, axis=0, keepdims=True)
                scaled = scaled + jnp.sum(power * inverse[n], axis=0, keepdims=True)
            sums[:, there] = squares
            sums[:, units + column : units + column + 256] = scaled

    vmem = pl.BlockSpec(memory_space=pltpu.VMEM)
    return pl.pallas_call(
        kernel,
        out_shape=[
            jax.ShapeDtypeStruct((1, rows), jnp.float32),
            jax.ShapeDtypeStruct((1, 2 * units + 128), jnp.float32),
        ],
        in_specs=[vmem] * 3,
        out_specs=[vmem] * 2,
        compiler_params=pltpu.CompilerParams(vmem_limit_bytes=14 << 20),
        cost_estimate=EAGER,
    )(grad, row_sum, row_moment)


def products(place, share, groups, steps):
    pieces = [(piece, group[1]) for group in groups for piece in group[0]]
    bounds = [(output, group[1]) for group in groups for output in group[2]]

    def kernel(place, *refs):
        share_ref, ins = refs[0], refs[1 : 1 + len(pieces)]
        outs, stacks = refs[1 + len(pieces) : -len(groups)], refs[-len(groups) :]
        n = o = 0
        for (own, _, outputs, over_rows), stack in zip(groups, stacks):
            at = 0
            if over_rows:
                for piece in own:
                    stack[at : at + piece.shape[0], :] = ins[n][...]
                    at += piece.shape[0]
                    n += 1
            else:
                rows = own[0].shape[0] // 4
                for j in range(4):
                    there = pl.multiple_of(((place[0] ^ j) & 3) * rows, rows)
                    stack[j * rows : (j + 1) * rows, :] = ins[n][pl.ds(there, rows), :]
                n += 1
            for ranges, kind in outputs:
                if over_rows:
                    side = jnp.concatenate([share_ref[:, begin:end] for begin, end in ranges], axis=1)
                    value = lax.dot_general(
                        side, stack[...], (((0,), (0,)), ((), ())), preferred_element_type=jnp.float32
                    )
                else:
                    side = jnp.concatenate([share_ref[begin:end, :] for begin, end in ranges], axis=0)
                    value = jnp.dot(side, stack[...], preferred_element_type=jnp.float32)
                outs[o][...] = value.astype(kind)
                o += 1

    def height(ranges):
        return sum(end - begin for begin, end in ranges)

    return pl.pallas_call(
        kernel,
        grid=(steps,),
        out_shape=[jax.ShapeDtypeStruct((height(ranges), columns), kind) for (ranges, kind), columns in bounds],
        in_specs=[pl.BlockSpec(memory_space=pltpu.SMEM), pl.BlockSpec(share.shape, lambda i: (0, 0))]
        + [pl.BlockSpec((piece.shape[0], columns // steps), lambda i: (0, i)) for piece, columns in pieces],
        out_specs=[pl.BlockSpec((height(ranges), columns // steps), lambda i: (0, i)) for (ranges, _), columns in bounds],
        scratch_shapes=[
            pltpu.VMEM((sum(piece.shape[0] for piece in group[0]), group[1] // steps), jnp.bfloat16) for group in groups
        ],
        compiler_params=pltpu.CompilerParams(vmem_limit_bytes=14 << 20),
        cost_estimate=EAGER,
    )(place, share, *[piece for piece, _ in pieces])


def staged_products(out_grad, gate_pre, up_pre, down_weight):
    x_bit, y_bit, z_bit, w_bit = 1, 2, 4, 8
    me, core = lax.axis_index("dp"), lax.axis_index("mp")
    tokens, units = gate_pre.shape
    rows = down_weight.shape[0]
    q, t = rows // 2, tokens // 2
    steps = 5
    split = units // 2
    barrier = lax.optimization_barrier
    place = jnp.stack([me, core]).astype(jnp.int32)
    own, right, message1, message2, message3 = first_stage(out_grad, gate_pre, up_pre, place, rows)

    planes = [[4 * o + i for i in range(4)] for o in range(lax.axis_size("dp") // 4)]
    weight_all = lax.all_gather(down_weight, "dp", axis=0, tiled=True, axis_index_groups=planes)
    extra, every = (split, 2 * rows), (0, tokens)
    left1, left2, message3 = flip(message1, z_bit), flip(message2, w_bit), flip(message3, z_bit | w_bit)
    left1, left2, message3, right = barrier((left1, left2, message3, right))
    to_z, mine = cut(
        [left1, left2, message3],
        [
            (1, every, (0, split), 0, 0),
            (0, every, extra, 1, 0),
            (1, every, extra, 1, 2 * rows),
            (2, every, (0, 2 * rows), 1, 4 * rows),
        ],
        [(tokens, split), (tokens, 6 * rows)],
    )
    left3 = flip(to_z, z_bit)
    right1, right2 = flip(right, z_bit), flip(right, w_bit)
    theirs = flip(mine, 1, "mp")
    share = assemble(own, mine, theirs, place, rows)

    def low_sent(size):
        return [(2 * size, 3 * size), (6 * size, 7 * size)]

    def high_sent(size):
        return [(5 * size, 6 * size), (7 * size, 8 * size)]

    def sent(size):
        return [(low_sent(size), jnp.bfloat16), (high_sent(size), jnp.bfloat16)]

    def kept(size):
        ranges = [(0, 2 * size)], [(4 * size, 5 * size)], [(3 * size, 4 * size)]
        return [(r, jnp.float32) for r in ranges]

    lefts = [message1, left1, left2, left3]
    left3, right1, right2 = barrier((left3, right1, right2))
    right3 = flip(right2, z_bit)
    left_to_x, left_to_y = products(place, share, [(lefts[:3] + [left3], split, sent(q), True)], steps)
    left_from_x, left_from_y = flip(left_to_x, x_bit), flip(left_to_y, y_bit)

    right1, right3, share, _ = barrier((right1, right3, share, left_to_x))
    rights = [right, right1, right2, right3]
    right_to_x, right_to_y, to_w, to_z = products(
        place,
        share,
        [
            (rights, units - split, sent(q), True),
            ([weight_all], units, [(high_sent(t), jnp.bfloat16), (low_sent(t), jnp.bfloat16)], False),
        ],
        steps,
    )
    right_from_x, right_from_y = flip(right_to_x, x_bit), flip(right_to_y, y_bit)
    from_w, from_z = flip(to_w, w_bit), flip(to_z, z_bit)
    share, left_from_x, left_from_y, _ = barrier((share, left_from_x, left_from_y, right_to_x))
    left_parts = products(place, share, [(lefts, split, kept(q), True)], steps)
    parts = products(
        place, share, [(rights, units - split, kept(q), True), ([weight_all], units, kept(t), False)], steps
    )

    grad_a = flip(add_tail([left_parts[1], parts[1]], [left_from_x, right_from_x]), y_bit)
    grad_b = flip(add_tail([left_parts[2], parts[2]], [left_from_y, right_from_y]), x_bit)
    grad_a, grad_b, from_z, from_w = barrier((grad_a, grad_b, from_z, from_w))
    grad, row_part = sum_up(
        [left_parts[0], parts[0]],
        [left_from_x, right_from_x],
        [left_from_y, right_from_y],
        grad_a,
        grad_b,
        1.0 / math.sqrt(tokens * lax.axis_size("dp")),
    )

    to_w, to_z = add_tail([parts[4]], [from_z]), add_tail([parts[5]], [from_w])
    row_sum = lax.psum(row_part, "mp")
    row_sum, to_w, to_z = barrier((row_sum, to_w, to_z))
    last_a, last_b = flip(to_w, w_bit), flip(to_z, z_bit)
    return grad, row_sum, (parts[3], from_z, from_w, last_a, last_b)


def hidden_gradients(gate_pre, up_pre, own_part, from_low, from_high, last_a, last_b):
    tokens, units = gate_pre.shape
    step = 32
    per_half = tokens // 2 // step

    def kernel(gate, up, own, low, high, last_a, last_b, gate_grad, up_grad):
        in_low = pl.program_id(0) < per_half
        other = jnp.where(in_low, low[...].astype(jnp.float32), high[...].astype(jnp.float32))
        last = jnp.where(in_low, last_a[...].astype(jnp.float32), last_b[...].astype(jnp.float32))
        value = own[...] + other + last
        activated, derivative = gelu_parts(gate[...].astype(jnp.float32))
        gate_grad[...] = (value * up[...].astype(jnp.float32) * derivative).astype(jnp.bfloat16)
        up_grad[...] = (value * activated).astype(jnp.bfloat16)

    whole = pl.BlockSpec((step, units), lambda i: (i, 0))
    first = pl.BlockSpec((step, units), lambda i: (jnp.minimum(i, per_half - 1), 0))
    second = pl.BlockSpec((step, units), lambda i: (jnp.maximum(i - per_half, 0), 0))
    return pl.pallas_call(
        kernel,
        grid=(tokens // step,),
        out_shape=[jax.ShapeDtypeStruct((tokens, units), jnp.bfloat16)] * 2,
        in_specs=[whole, whole, whole, first, second, first, second],
        out_specs=[whole] * 2,
        compiler_params=pltpu.CompilerParams(vmem_limit_bytes=56 << 20),
        cost_estimate=EAGER,
    )(gate_pre, up_pre, own_part, from_low, from_high, last_a, last_b)


def local(out_grad, gate_pre, up_pre, down_weight, row_moment, col_moment):
    size = lax.axis_size("dp")
    rows, units = down_weight.shape
    tokens = out_grad.shape[0]
    all_bits = [1 << b for b in range(size.bit_length() - 1)]
    decay = 1.0 - TRAIN_STEP ** (-0.8)
    total_rows = rows * size
    total_units = units * lax.axis_size("mp")
    staged = size == 16 and lax.axis_size("mp") == 2 and rows % 256 == 0 and tokens % 32 == 0 and units % 2560 == 0
    if staged:
        grad, row_sum, terms = staged_products(out_grad, gate_pre, up_pre, down_weight)
        row_moment_new, sums = column_sums(grad, row_sum, row_moment[None, :], decay, total_units)
        row_moment_new, sums = row_moment_new[0], group_sum(sums[0], all_bits[:INNER_BITS])
        sums, terms = lax.optimization_barrier((sums, terms))
        gate_grad, up_grad = hidden_gradients(gate_pre, up_pre, *terms)
    else:
        product, hidden_grad = general_products(
            out_grad, gate_pre, up_pre, down_weight, all_bits[:INNER_BITS], all_bits[INNER_BITS:]
        )
        grad = product * (1.0 / math.sqrt(tokens * size))
        powers = grad * grad
        squares = powers + 1e-30
        row_sum = lax.psum(jnp.sum(squares, axis=1), "mp")
        row_moment_new = decay * row_moment + (1.0 - decay) * (row_sum / total_units)
        col_part = jnp.sum(squares, axis=0)
        scaled_part = jnp.sum(powers / row_moment_new[:, None], axis=0)
        sums = jnp.concatenate([col_part, scaled_part, jnp.broadcast_to(jnp.sum(row_moment_new), (128,))])
        sums = group_sum(sums, all_bits[:INNER_BITS])
        activated, derivative = gelu_parts(gate_pre.astype(jnp.float32))
        gate_grad = (hidden_grad * up_pre.astype(jnp.float32) * derivative).astype(jnp.bfloat16)
        up_grad = (hidden_grad * activated).astype(jnp.bfloat16)

    sums = group_sum(sums, all_bits[INNER_BITS:])
    col_moment_new = decay * col_moment + (1.0 - decay) * (sums[:units] / total_rows)
    row_mean = sums[2 * units] / total_rows
    ratios = jnp.sum((sums[units : 2 * units] / col_moment_new).reshape(-1, 128), axis=0)
    square_sum = row_mean * jnp.sum(lax.psum(ratios, "mp"))
    clip_norm = jnp.sqrt(square_sum / (total_rows * total_units))
    row_factor = jnp.sqrt(row_mean / row_moment_new) / jnp.maximum(1.0, clip_norm)
    col_factor = 1.0 / jnp.sqrt(col_moment_new)
    update = grad * row_factor[:, None] * col_factor[None, :]
    return (update, row_moment_new, col_moment_new, row_mean, gate_grad, up_grad)


def solution(mesh):
    in_specs = (P("dp", None), P("dp", "mp"), P("dp", "mp"), P("dp", "mp"), P("dp"), P("mp"))
    out_specs = (P("dp", "mp"), P("dp"), P("mp"), P(), P("dp", "mp"), P("dp", "mp"))
    return jax.shard_map(local, mesh=mesh, in_specs=in_specs, out_specs=out_specs, check_vma=False)
```

```python
import math

import jax
import jax.numpy as jnp
from jax import lax
from jax.experimental import pallas as pl
from jax.experimental.pallas import tpu as pltpu
from jax.sharding import PartitionSpec as P

TRAIN_STEP = 3
INNER_BITS = 2
EAGER = pl.CostEstimate(flops=0, bytes_accessed=0, transcendentals=0)


def gelu_parts(values):
    factor = math.sqrt(2.0 / math.pi)
    inner = factor * (values + 0.044715 * values * values * values)
    tangent = jnp.tanh(inner)
    activated = 0.5 * values * (1.0 + tangent)
    derivative = 0.5 * (1.0 + tangent) + 0.5 * values * (1.0 - tangent * tangent) * factor * (
        1.0 + 3.0 * 0.044715 * values * values
    )
    return (activated, derivative)


def flip(value, bits, axis="dp"):
    size = lax.axis_size(axis)
    return lax.ppermute(value, axis, [(i, i ^ bits) for i in range(size)])


def group_sum(value, bits):
    for at in range(0, len(bits), 2):
        pair = bits[at : at + 2]
        if len(pair) == 2:
            first, second = flip(value, pair[0]), flip(value, pair[1])
            value = (value + first) + (second + flip(value, pair[0] | pair[1]))
        else:
            value = value + flip(value, pair[0])
    return value


def general_products(out_grad, gate_pre, up_pre, down_weight, inner_bits, outer_bits):
    size = lax.axis_size("dp")
    me = lax.axis_index("dp")
    tokens, rows = out_grad.shape[0], down_weight.shape[0]
    inner = 2 ** len(inner_bits)
    activated, _ = gelu_parts(gate_pre.astype(jnp.float32))
    hidden = (activated * up_pre.astype(jnp.float32)).astype(jnp.bfloat16)
    by_block = out_grad.reshape(tokens, size, rows).transpose(1, 0, 2)

    def features_of(k):
        picks = [lax.dynamic_index_in_dim(by_block, me ^ (k * inner + j), 0, keepdims=False) for j in range(inner)]
        return jnp.concatenate(picks, axis=1)

    def gather(block, bits):
        blocks = [block]
        for bit in bits:
            blocks = blocks + [flip(b, bit) for b in blocks]
        return jnp.concatenate(blocks, axis=0)

    def scatter(values, bits):
        for level in reversed(range(len(bits))):
            count = 2**level
            values = [
                values[j] + flip(values[j + count].astype(jnp.bfloat16), bits[level]).astype(jnp.float32)
                for j in range(count)
            ]
        return values[0]

    shares = [features_of(0)] + [flip(features_of(k), k * inner) for k in range(1, size // inner)]
    share = jnp.concatenate(shares, axis=0)
    hidden_all = gather(hidden, outer_bits)
    weight_all = gather(down_weight, inner_bits)
    product = scatter(
        [
            lax.dot_general(
                share[:, j * rows : (j + 1) * rows],
                hidden_all,
                (((0,), (0,)), ((), ())),
                preferred_element_type=jnp.float32,
            )
            for j in range(inner)
        ],
        inner_bits,
    )
    hidden_grad = scatter(
        [jnp.dot(x, weight_all, preferred_element_type=jnp.float32) for x in shares],
        outer_bits,
    )
    return product, hidden_grad


def first_stage(out_grad, gate_pre, up_pre, place, rows):
    tokens, units = gate_pre.shape
    half = units // 2
    step = 32

    def kernel(place, source_hbm, gate_hbm, up_hbm, own, right, message1, message2, message3, source, gate, up, sems):
        copies = [
            pltpu.make_async_copy(there, here, sems.at[n])
            for n, (there, here) in enumerate(((gate_hbm, gate), (up_hbm, up), (source_hbm, source)))
        ]
        for copy in copies:
            copy.start()
        me, core = place[0], place[1]

        def block(k, j):
            return pl.ds(pl.multiple_of((me ^ (4 * k + j)) * rows, rows), rows)

        copies[0].wait()
        copies[1].wait()

        @pl.loop(0, tokens // step)
        def _(i):
            here = pl.ds(pl.multiple_of(i * step, step), step)
            activated, _ = gelu_parts(gate[here, :].astype(jnp.float32))
            value = (activated * up[here, :].astype(jnp.float32)).astype(jnp.bfloat16)
            right[here, :] = value[:, half:]
            message1[here, :half] = value[:, :half]
            message2[here, :half] = value[:, :half]

        copies[2].wait()
        for j in range(4):
            own[:, j * rows : (j + 1) * rows] = source[:, block(0, j)]
        for k, target, base in ((1, message1, half), (2, message2, half), (3, message3, 0)):
            for j in range(2):
                target[:, base + j * rows : base + (j + 1) * rows] = source[:, block(k, 2 * core + j)]

    vmem = pl.BlockSpec(memory_space=pltpu.VMEM)
    widths = [4 * rows, units - half, half + 2 * rows, half + 2 * rows, 2 * rows]
    return pl.pallas_call(
        kernel,
        out_shape=[jax.ShapeDtypeStruct((tokens, width), jnp.bfloat16) for width in widths],
        in_specs=[pl.BlockSpec(memory_space=pltpu.SMEM)] + [pl.BlockSpec(memory_space=pltpu.HBM)] * 3,
        out_specs=[vmem] * len(widths),
        scratch_shapes=[
            pltpu.VMEM(out_grad.shape, jnp.bfloat16),
            pltpu.VMEM(gate_pre.shape, jnp.bfloat16),
            pltpu.VMEM(up_pre.shape, jnp.bfloat16),
            pltpu.SemaphoreType.DMA((3,)),
        ],
        compiler_params=pltpu.CompilerParams(vmem_limit_bytes=16 << 20),
        cost_estimate=EAGER,
    )(place, out_grad, gate_pre, up_pre)


def cut(sources, parts, shapes):
    def kernel(*refs):
        ins, outs, sems = refs[: len(sources)], refs[len(sources) : -1], refs[-1]
        copies = [
            pltpu.make_async_copy(
                ins[i].at[pl.ds(*rows), pl.ds(*columns)], outs[o].at[:, pl.ds(at, columns[1])], sems.at[n]
            )
            for n, (i, rows, columns, o, at) in enumerate(parts)
        ]
        for copy in copies:
            copy.start()
        for copy in copies:
            copy.wait()

    return pl.pallas_call(
        kernel,
        out_shape=[jax.ShapeDtypeStruct(shape, jnp.bfloat16) for shape in shapes],
        in_specs=[pl.BlockSpec(memory_space=pltpu.HBM)] * len(sources),
        out_specs=[pl.BlockSpec(memory_space=pltpu.HBM)] * len(shapes),
        scratch_shapes=[pltpu.SemaphoreType.DMA((len(parts),))],
        compiler_params=pltpu.CompilerParams(vmem_limit_bytes=1 << 20),
        cost_estimate=EAGER,
    )(*sources)


def assemble(own, mine, theirs, place, rows):
    tokens = own.shape[0]

    def kernel(place, own, mine, theirs, share):
        share[:tokens, :] = own[...]
        for k in range(3):
            here = pl.ds((k + 1) * tokens, tokens)
            half = slice(k * 2 * rows, (k + 1) * 2 * rows)
            a, b = mine[:, half], theirs[:, half]
            share[here, : 2 * rows] = jnp.where(place[1] == 0, a, b)
            share[here, 2 * rows :] = jnp.where(place[1] == 0, b, a)

    vmem = pl.BlockSpec(memory_space=pltpu.VMEM)
    return pl.pallas_call(
        kernel,
        out_shape=jax.ShapeDtypeStruct((4 * tokens, 4 * rows), jnp.bfloat16),
        in_specs=[pl.BlockSpec(memory_space=pltpu.SMEM), vmem, vmem, vmem],
        out_specs=vmem,
        compiler_params=pltpu.CompilerParams(vmem_limit_bytes=8 << 20),
        cost_estimate=EAGER,
    )(place, own, mine, theirs)


def add_tail(parts, arrived):
    rows = parts[0].shape[0]
    widths = [part.shape[1] for part in parts]

    def kernel(*refs):
        out, at = refs[-1], 0
        for part, other, width in zip(refs, refs[len(parts) :], widths):
            out[:, at : at + width] = (part[...] + other[-rows:, :].astype(jnp.float32)).astype(jnp.bfloat16)
            at += width

    vmem = pl.BlockSpec(memory_space=pltpu.VMEM)
    return pl.pallas_call(
        kernel,
        out_shape=jax.ShapeDtypeStruct((rows, sum(widths)), jnp.bfloat16),
        in_specs=[vmem] * (2 * len(parts)),
        out_specs=vmem,
        compiler_params=pltpu.CompilerParams(vmem_limit_bytes=8 << 20),
        cost_estimate=EAGER,
    )(*parts, *arrived)


def flat(column):
    return jnp.broadcast_to(column, (128, 128)).T[0:1, :]


def upright(row):
    return jnp.broadcast_to(row, (128, 128)).T[:, 0:1]


def sum_up(kept, from_low, from_high, last_a, last_b, scale):
    rows = kept[0].shape[0]
    q = rows // 2
    widths = [part.shape[1] for part in kept]
    units = sum(widths)

    def kernel(*refs):
        kept_refs, low_refs, high_refs = refs[:2], refs[2:4], refs[4:6]
        last_refs, grad, row_part = refs[6:8], refs[8], refs[9]
        for h, arrived in enumerate((low_refs, high_refs)):
            for at in range(0, q, 128):
                total = jnp.zeros((128, 1), jnp.float32)
                here = slice(h * q + at, h * q + at + 128)
                column = 0
                for part, other, width in zip(kept_refs, arrived, widths):
                    there = slice(column, column + width)
                    value = part[here, :] + other[at : at + 128, :].astype(jnp.float32)
                    value = (value + last_refs[h][at : at + 128, there].astype(jnp.float32)) * scale
                    grad[here, there] = value
                    total = total + jnp.sum(value * value + 1e-30, axis=1, keepdims=True)
                    column += width
                row_part[:, here] = flat(total)

    vmem = pl.BlockSpec(memory_space=pltpu.VMEM)
    return pl.pallas_call(
        kernel,
        out_shape=[jax.ShapeDtypeStruct((rows, units), jnp.float32), jax.ShapeDtypeStruct((1, rows), jnp.float32)],
        in_specs=[vmem] * 8,
        out_specs=[vmem] * 2,
        compiler_params=pltpu.CompilerParams(vmem_limit_bytes=14 << 20),
        cost_estimate=EAGER,
    )(*kept, *from_low, *from_high, last_a, last_b)


def column_sums(grad, row_sum, row_moment, decay, total_units):
    rows, units = grad.shape

    def kernel(grad, row_sum, row_moment, row_moment_new, sums):
        new = decay * row_moment[...] + (1.0 - decay) * (row_sum[...] / total_units)
        row_moment_new[...] = new
        sums[:, 2 * units :] = jnp.broadcast_to(jnp.sum(new, axis=1, keepdims=True), (1, 128))
        inverse = [1.0 / upright(new[:, at : at + 128]) for at in range(0, rows, 128)]
        for column in range(0, units, 256):
            there = slice(column, column + 256)
            squares, scaled = jnp.zeros((1, 256), jnp.float32), jnp.zeros((1, 256), jnp.float32)
            for n, at in enumerate(range(0, rows, 128)):
                power = grad[at : at + 128, there]
                power = power * power
                squares = squares + jnp.sum(power + 1e-30, axis=0, keepdims=True)
                scaled = scaled + jnp.sum(power * inverse[n], axis=0, keepdims=True)
            sums[:, there] = squares
            sums[:, units + column : units + column + 256] = scaled

    vmem = pl.BlockSpec(memory_space=pltpu.VMEM)
    return pl.pallas_call(
        kernel,
        out_shape=[
            jax.ShapeDtypeStruct((1, rows), jnp.float32),
            jax.ShapeDtypeStruct((1, 2 * units + 128), jnp.float32),
        ],
        in_specs=[vmem] * 3,
        out_specs=[vmem] * 2,
        compiler_params=pltpu.CompilerParams(vmem_limit_bytes=14 << 20),
        cost_estimate=EAGER,
    )(grad, row_sum, row_moment)


def products(share, groups, steps):
    pieces = [(piece, group[1]) for group in groups for piece in group[0]]
    bounds = [(output, group[1]) for group in groups for output in group[2]]

    def kernel(*refs):
        share_ref, ins = refs[0], refs[1 : 1 + len(pieces)]
        outs, stacks = refs[1 + len(pieces) : -len(groups)], refs[-len(groups) :]
        n = o = 0
        for (own, _, outputs, over_rows), stack in zip(groups, stacks):
            at = 0
            for piece, _ in own:
                stack[at : at + piece.shape[0], :] = ins[n][...]
                at += piece.shape[0]
                n += 1
            for ranges, kind in outputs:
                if over_rows:
                    side = jnp.concatenate([share_ref[:, begin:end] for begin, end in ranges], axis=1)
                    value = lax.dot_general(
                        side, stack[...], (((0,), (0,)), ((), ())), preferred_element_type=jnp.float32
                    )
                else:
                    side = jnp.concatenate([share_ref[begin:end, :] for begin, end in ranges], axis=0)
                    value = jnp.dot(side, stack[...], preferred_element_type=jnp.float32)
                outs[o][...] = value.astype(kind)
                o += 1

    def height(ranges):
        return sum(end - begin for begin, end in ranges)

    return pl.pallas_call(
        kernel,
        grid=(steps,),
        out_shape=[jax.ShapeDtypeStruct((height(ranges), columns), kind) for (ranges, kind), columns in bounds],
        in_specs=[pl.BlockSpec(share.shape, lambda i: (0, 0))]
        + [
            pl.BlockSpec((piece.shape[0], columns // steps), lambda i, skip=first * steps // columns: (0, i + skip))
            for (piece, first), columns in pieces
        ],
        out_specs=[pl.BlockSpec((height(ranges), columns // steps), lambda i: (0, i)) for (ranges, _), columns in bounds],
        scratch_shapes=[
            pltpu.VMEM((sum(piece.shape[0] for piece, _ in group[0]), group[1] // steps), jnp.bfloat16) for group in groups
        ],
        compiler_params=pltpu.CompilerParams(vmem_limit_bytes=14 << 20),
        cost_estimate=EAGER,
    )(share, *[piece for (piece, _), _ in pieces])


def staged_products(out_grad, gate_pre, up_pre, down_weight):
    x_bit, y_bit, z_bit, w_bit = 1, 2, 4, 8
    me, core = lax.axis_index("dp"), lax.axis_index("mp")
    tokens, units = gate_pre.shape
    rows = down_weight.shape[0]
    q, t = rows // 2, tokens // 2
    steps = 5
    split = units // 2
    barrier = lax.optimization_barrier
    place = jnp.stack([me, core]).astype(jnp.int32)
    own, right, message1, message2, message3 = first_stage(out_grad, gate_pre, up_pre, place, rows)

    down_weight, message1 = barrier((down_weight, message1))
    extra, every, whole = (split, 2 * rows), (0, tokens), (0, units)
    left1, left2, message3 = flip(message1, z_bit), flip(message2, w_bit), flip(message3, z_bit | w_bit)
    weight1, weight2 = flip(down_weight, x_bit), flip(down_weight, y_bit)
    message3, weight1, weight2 = barrier((message3, weight1, weight2))
    to_y, to_x = cut([weight1, weight2], [(0, (0, q), whole, 0, 0), (1, (q, q), whole, 1, 0)], [(q, units)] * 2)
    weight3a, weight3b = flip(to_y, y_bit), flip(to_x, x_bit)
    left1, left2, message3, right, _, _ = barrier((left1, left2, message3, right, to_y, to_x))
    to_z, mine = cut(
        [left1, left2, message3, right],
        [
            (1, every, (0, split), 0, 0),
            (3, every, (0, units - split), 0, split),
            (0, every, extra, 1, 0),
            (1, every, extra, 1, 2 * rows),
            (2, every, (0, 2 * rows), 1, 4 * rows),
        ],
        [(tokens, units), (tokens, 6 * rows)],
    )
    from_near = flip(to_z, z_bit)
    right2 = flip(right, w_bit)
    theirs = flip(mine, 1, "mp")
    share = assemble(own, mine, theirs, place, rows)

    def low_sent(size):
        return [(2 * size, 3 * size), (6 * size, 7 * size)]

    def high_sent(size):
        return [(5 * size, 6 * size), (7 * size, 8 * size)]

    def sent(size):
        return [(low_sent(size), jnp.bfloat16), (high_sent(size), jnp.bfloat16)]

    def kept(size):
        ranges = [(0, 2 * size)], [(4 * size, 5 * size)], [(3 * size, 4 * size)]
        return [(r, jnp.float32) for r in ranges]

    from_near, right2, share = barrier((from_near, right2, share))
    right3 = flip(right2, z_bit)
    lefts = [(message1, 0), (left1, 0), (left2, 0), (from_near, 0)]
    left_to_x, left_to_y = products(share, [(lefts, split, sent(q), True)], steps)
    left_from_x, left_from_y = flip(left_to_x, x_bit), flip(left_to_y, y_bit)

    share, _ = barrier((share, left_to_x))
    weights = [(piece, 0) for piece in (down_weight, weight1, weight2, weight3a, weight3b)]
    to_w, to_z = products(
        share, [(weights, units, [(high_sent(t), jnp.bfloat16), (low_sent(t), jnp.bfloat16)], False)], steps
    )
    right3, share, to_w, to_z = barrier((right3, share, to_w, to_z))
    from_w, from_z = flip(to_w, w_bit), flip(to_z, z_bit)
    rights = [(right, 0), (from_near, split), (right2, 0), (right3, 0)]
    right_to_x, right_to_y = products(share, [(rights, units - split, sent(q), True)], steps)
    right_from_x, right_from_y = flip(right_to_x, x_bit), flip(right_to_y, y_bit)
    share, left_from_x, left_from_y, _ = barrier((share, left_from_x, left_from_y, right_to_x))
    left_parts = products(share, [(lefts, split, kept(q), True)], steps)
    parts = products(share, [(rights, units - split, kept(q), True), (weights, units, kept(t), False)], steps)

    grad_a = flip(add_tail([left_parts[1], parts[1]], [left_from_x, right_from_x]), y_bit)
    grad_b = flip(add_tail([left_parts[2], parts[2]], [left_from_y, right_from_y]), x_bit)
    to_w, to_z = add_tail([parts[4]], [from_z]), add_tail([parts[5]], [from_w])
    last_a, last_b = flip(to_w, w_bit), flip(to_z, z_bit)
    grad_a, grad_b, _, _ = barrier((grad_a, grad_b, to_w, to_z))
    grad, row_part = sum_up(
        [left_parts[0], parts[0]],
        [left_from_x, right_from_x],
        [left_from_y, right_from_y],
        grad_a,
        grad_b,
        1.0 / math.sqrt(tokens * lax.axis_size("dp")),
    )

    row_sum = lax.psum(row_part, "mp")
    return grad, row_sum, (parts[3], from_z[:t], from_w[:t], last_a, last_b)


def local(out_grad, gate_pre, up_pre, down_weight, row_moment, col_moment):
    size = lax.axis_size("dp")
    rows, units = down_weight.shape
    tokens = out_grad.shape[0]
    all_bits = [1 << b for b in range(size.bit_length() - 1)]
    decay = 1.0 - TRAIN_STEP ** (-0.8)
    total_rows = rows * size
    total_units = units * lax.axis_size("mp")
    staged = size == 16 and lax.axis_size("mp") == 2 and rows % 256 == 0 and tokens % 32 == 0 and units % 2560 == 0
    if staged:
        grad, row_sum, terms = staged_products(out_grad, gate_pre, up_pre, down_weight)
        row_moment_new, sums = column_sums(grad, row_sum, row_moment[None, :], decay, total_units)
        row_moment_new, sums = row_moment_new[0], group_sum(sums[0], all_bits[:INNER_BITS])
        sums, terms = lax.optimization_barrier((sums, terms))
        own_part, from_low, from_high, last_a, last_b = terms
        arrived = jnp.concatenate([from_low, from_high], axis=0).astype(jnp.float32)
        hidden_grad = own_part + arrived + jnp.concatenate([last_a, last_b], axis=0).astype(jnp.float32)
    else:
        product, hidden_grad = general_products(
            out_grad, gate_pre, up_pre, down_weight, all_bits[:INNER_BITS], all_bits[INNER_BITS:]
        )
        grad = product * (1.0 / math.sqrt(tokens * size))
        powers = grad * grad
        squares = powers + 1e-30
        row_sum = lax.psum(jnp.sum(squares, axis=1), "mp")
        row_moment_new = decay * row_moment + (1.0 - decay) * (row_sum / total_units)
        col_part = jnp.sum(squares, axis=0)
        scaled_part = jnp.sum(powers / row_moment_new[:, None], axis=0)
        sums = jnp.concatenate([col_part, scaled_part, jnp.broadcast_to(jnp.sum(row_moment_new), (128,))])
        sums = group_sum(sums, all_bits[:INNER_BITS])

    activated, derivative = gelu_parts(gate_pre.astype(jnp.float32))
    gate_grad = (hidden_grad * up_pre.astype(jnp.float32) * derivative).astype(jnp.bfloat16)
    up_grad = (hidden_grad * activated).astype(jnp.bfloat16)

    sums = group_sum(sums, all_bits[INNER_BITS:])
    col_moment_new = decay * col_moment + (1.0 - decay) * (sums[:units] / total_rows)
    row_mean = sums[2 * units] / total_rows
    ratios = jnp.sum((sums[units : 2 * units] / col_moment_new).reshape(-1, 128), axis=0)
    square_sum = row_mean * jnp.sum(lax.psum(ratios, "mp"))
    clip_norm = jnp.sqrt(square_sum / (total_rows * total_units))
    row_factor = jnp.sqrt(row_mean / row_moment_new) / jnp.maximum(1.0, clip_norm)
    col_factor = 1.0 / jnp.sqrt(col_moment_new)
    update = grad * row_factor[:, None] * col_factor[None, :]
    return (update, row_moment_new, col_moment_new, row_mean, gate_grad, up_grad)


def solution(mesh):
    in_specs = (P("dp", None), P("dp", "mp"), P("dp", "mp"), P("dp", "mp"), P("dp"), P("mp"))
    out_specs = (P("dp", "mp"), P("dp"), P("mp"), P(), P("dp", "mp"), P("dp", "mp"))
    return jax.shard_map(local, mesh=mesh, in_specs=in_specs, out_specs=out_specs, check_vma=False)
```

```python
import math

import jax
import jax.numpy as jnp
from jax import lax
from jax.experimental import pallas as pl
from jax.experimental.pallas import tpu as pltpu
from jax.sharding import PartitionSpec as P

TRAIN_STEP = 3
INNER_BITS = 2
EAGER = pl.CostEstimate(flops=0, bytes_accessed=0, transcendentals=0)


def gelu_parts(values):
    factor = math.sqrt(2.0 / math.pi)
    inner = factor * (values + 0.044715 * values * values * values)
    tangent = jnp.tanh(inner)
    activated = 0.5 * values * (1.0 + tangent)
    derivative = 0.5 * (1.0 + tangent) + 0.5 * values * (1.0 - tangent * tangent) * factor * (
        1.0 + 3.0 * 0.044715 * values * values
    )
    return (activated, derivative)


def flip(value, bits, axis="dp"):
    size = lax.axis_size(axis)
    return lax.ppermute(value, axis, [(i, i ^ bits) for i in range(size)])


def group_sum(value, bits):
    for at in range(0, len(bits), 2):
        pair = bits[at : at + 2]
        if len(pair) == 2:
            first, second = flip(value, pair[0]), flip(value, pair[1])
            value = (value + first) + (second + flip(value, pair[0] | pair[1]))
        else:
            value = value + flip(value, pair[0])
    return value


def general_products(out_grad, gate_pre, up_pre, down_weight, inner_bits, outer_bits):
    size = lax.axis_size("dp")
    me = lax.axis_index("dp")
    tokens, rows = out_grad.shape[0], down_weight.shape[0]
    inner = 2 ** len(inner_bits)
    activated, _ = gelu_parts(gate_pre.astype(jnp.float32))
    hidden = (activated * up_pre.astype(jnp.float32)).astype(jnp.bfloat16)
    by_block = out_grad.reshape(tokens, size, rows).transpose(1, 0, 2)

    def features_of(k):
        picks = [lax.dynamic_index_in_dim(by_block, me ^ (k * inner + j), 0, keepdims=False) for j in range(inner)]
        return jnp.concatenate(picks, axis=1)

    def gather(block, bits):
        blocks = [block]
        for bit in bits:
            blocks = blocks + [flip(b, bit) for b in blocks]
        return jnp.concatenate(blocks, axis=0)

    def scatter(values, bits):
        for level in reversed(range(len(bits))):
            count = 2**level
            values = [
                values[j] + flip(values[j + count].astype(jnp.bfloat16), bits[level]).astype(jnp.float32)
                for j in range(count)
            ]
        return values[0]

    shares = [features_of(0)] + [flip(features_of(k), k * inner) for k in range(1, size // inner)]
    share = jnp.concatenate(shares, axis=0)
    hidden_all = gather(hidden, outer_bits)
    weight_all = gather(down_weight, inner_bits)
    product = scatter(
        [
            lax.dot_general(
                share[:, j * rows : (j + 1) * rows],
                hidden_all,
                (((0,), (0,)), ((), ())),
                preferred_element_type=jnp.float32,
            )
            for j in range(inner)
        ],
        inner_bits,
    )
    hidden_grad = scatter(
        [jnp.dot(x, weight_all, preferred_element_type=jnp.float32) for x in shares],
        outer_bits,
    )
    return product, hidden_grad


def first_stage(out_grad, gate_pre, up_pre, place, rows):
    tokens, units = gate_pre.shape
    half = units // 2
    step = 32

    def kernel(place, source, gate, up, own, right, message1, message2, message3):
        me, core = place[0], place[1]

        def block(k, j):
            return pl.ds(pl.multiple_of((me ^ (4 * k + j)) * rows, rows), rows)

        activated, _ = gelu_parts(gate[...].astype(jnp.float32))
        value = (activated * up[...].astype(jnp.float32)).astype(jnp.bfloat16)
        right[...] = value[:, half:]
        message1[:, :half] = value[:, :half]
        message2[:, :half] = value[:, :half]
        for j in range(4):
            own[:, j * rows : (j + 1) * rows] = source[:, block(0, j)]
        for k, target, base in ((1, message1, half), (2, message2, half), (3, message3, 0)):
            for j in range(2):
                target[:, base + j * rows : base + (j + 1) * rows] = source[:, block(k, 2 * core + j)]

    widths = [4 * rows, units - half, half + 2 * rows, half + 2 * rows, 2 * rows]
    return pl.pallas_call(
        kernel,
        grid=(tokens // step,),
        out_shape=[jax.ShapeDtypeStruct((tokens, width), jnp.bfloat16) for width in widths],
        in_specs=[pl.BlockSpec(memory_space=pltpu.SMEM)]
        + [pl.BlockSpec((step, array.shape[1]), lambda i: (i, 0)) for array in (out_grad, gate_pre, up_pre)],
        out_specs=[pl.BlockSpec((step, width), lambda i: (i, 0)) for width in widths],
        compiler_params=pltpu.CompilerParams(vmem_limit_bytes=56 << 20),
        cost_estimate=EAGER,
    )(place, out_grad, gate_pre, up_pre)


def cut(sources, parts, shapes):
    def kernel(*refs):
        ins, outs, sems = refs[: len(sources)], refs[len(sources) : -1], refs[-1]
        copies = [
            pltpu.make_async_copy(
                ins[i].at[pl.ds(*rows), pl.ds(*columns)], outs[o].at[:, pl.ds(at, columns[1])], sems.at[n]
            )
            for n, (i, rows, columns, o, at) in enumerate(parts)
        ]
        for copy in copies:
            copy.start()
        for copy in copies:
            copy.wait()

    return pl.pallas_call(
        kernel,
        out_shape=[jax.ShapeDtypeStruct(shape, jnp.bfloat16) for shape in shapes],
        in_specs=[pl.BlockSpec(memory_space=pltpu.HBM)] * len(sources),
        out_specs=[pl.BlockSpec(memory_space=pltpu.HBM)] * len(shapes),
        scratch_shapes=[pltpu.SemaphoreType.DMA((len(parts),))],
        compiler_params=pltpu.CompilerParams(vmem_limit_bytes=1 << 20),
        cost_estimate=EAGER,
    )(*sources)


def assemble(own, mine, theirs, place, rows):
    tokens = own.shape[0]

    def kernel(place, own, mine, theirs, share):
        share[:tokens, :] = own[...]
        for k in range(3):
            here = pl.ds((k + 1) * tokens, tokens)
            half = slice(k * 2 * rows, (k + 1) * 2 * rows)
            a, b = mine[:, half], theirs[:, half]
            share[here, : 2 * rows] = jnp.where(place[1] == 0, a, b)
            share[here, 2 * rows :] = jnp.where(place[1] == 0, b, a)

    vmem = pl.BlockSpec(memory_space=pltpu.VMEM)
    return pl.pallas_call(
        kernel,
        out_shape=jax.ShapeDtypeStruct((4 * tokens, 4 * rows), jnp.bfloat16),
        in_specs=[pl.BlockSpec(memory_space=pltpu.SMEM), vmem, vmem, vmem],
        out_specs=vmem,
        compiler_params=pltpu.CompilerParams(vmem_limit_bytes=8 << 20),
        cost_estimate=EAGER,
    )(place, own, mine, theirs)


def add_tail(parts, arrived):
    rows = parts[0].shape[0]
    widths = [part.shape[1] for part in parts]

    def kernel(*refs):
        out, at = refs[-1], 0
        for part, other, width in zip(refs, refs[len(parts) :], widths):
            out[:, at : at + width] = (part[...] + other[-rows:, :].astype(jnp.float32)).astype(jnp.bfloat16)
            at += width

    vmem = pl.BlockSpec(memory_space=pltpu.VMEM)
    return pl.pallas_call(
        kernel,
        out_shape=jax.ShapeDtypeStruct((rows, sum(widths)), jnp.bfloat16),
        in_specs=[vmem] * (2 * len(parts)),
        out_specs=vmem,
        compiler_params=pltpu.CompilerParams(vmem_limit_bytes=8 << 20),
        cost_estimate=EAGER,
    )(*parts, *arrived)


def flat(column):
    return jnp.broadcast_to(column, (128, 128)).T[0:1, :]


def upright(row):
    return jnp.broadcast_to(row, (128, 128)).T[:, 0:1]


def sum_up(kept, from_low, from_high, last_a, last_b, scale):
    rows = kept[0].shape[0]
    q = rows // 2
    widths = [part.shape[1] for part in kept]
    units = sum(widths)

    def kernel(*refs):
        kept_refs, low_refs, high_refs = refs[:2], refs[2:4], refs[4:6]
        last_refs, grad, row_part = refs[6:8], refs[8], refs[9]
        for h, arrived in enumerate((low_refs, high_refs)):
            for at in range(0, q, 128):
                total = jnp.zeros((128, 1), jnp.float32)
                here = slice(h * q + at, h * q + at + 128)
                column = 0
                for part, other, width in zip(kept_refs, arrived, widths):
                    there = slice(column, column + width)
                    value = part[here, :] + other[at : at + 128, :].astype(jnp.float32)
                    value = (value + last_refs[h][at : at + 128, there].astype(jnp.float32)) * scale
                    grad[here, there] = value
                    total = total + jnp.sum(value * value + 1e-30, axis=1, keepdims=True)
                    column += width
                row_part[:, here] = flat(total)

    vmem = pl.BlockSpec(memory_space=pltpu.VMEM)
    return pl.pallas_call(
        kernel,
        out_shape=[jax.ShapeDtypeStruct((rows, units), jnp.float32), jax.ShapeDtypeStruct((1, rows), jnp.float32)],
        in_specs=[vmem] * 8,
        out_specs=[vmem] * 2,
        compiler_params=pltpu.CompilerParams(vmem_limit_bytes=14 << 20),
        cost_estimate=EAGER,
    )(*kept, *from_low, *from_high, last_a, last_b)


def column_sums(grad, row_sum, row_moment, decay, total_units):
    rows, units = grad.shape

    def kernel(grad, row_sum, row_moment, row_moment_new, sums):
        new = decay * row_moment[...] + (1.0 - decay) * (row_sum[...] / total_units)
        row_moment_new[...] = new
        sums[:, 2 * units :] = jnp.broadcast_to(jnp.sum(new, axis=1, keepdims=True), (1, 128))
        inverse = [1.0 / upright(new[:, at : at + 128]) for at in range(0, rows, 128)]
        for column in range(0, units, 256):
            there = slice(column, column + 256)
            squares, scaled = jnp.zeros((1, 256), jnp.float32), jnp.zeros((1, 256), jnp.float32)
            for n, at in enumerate(range(0, rows, 128)):
                power = grad[at : at + 128, there]
                power = power * power
                squares = squares + jnp.sum(power + 1e-30, axis=0, keepdims=True)
                scaled = scaled + jnp.sum(power * inverse[n], axis=0, keepdims=True)
            sums[:, there] = squares
            sums[:, units + column : units + column + 256] = scaled

    vmem = pl.BlockSpec(memory_space=pltpu.VMEM)
    return pl.pallas_call(
        kernel,
        out_shape=[
            jax.ShapeDtypeStruct((1, rows), jnp.float32),
            jax.ShapeDtypeStruct((1, 2 * units + 128), jnp.float32),
        ],
        in_specs=[vmem] * 3,
        out_specs=[vmem] * 2,
        compiler_params=pltpu.CompilerParams(vmem_limit_bytes=14 << 20),
        cost_estimate=EAGER,
    )(grad, row_sum, row_moment)


def column_step(sums, col_moment, decay, total_rows):
    units = col_moment.shape[1]

    def kernel(sums, col_moment, col_moment_new, terms):
        total = jnp.zeros((1, 128), jnp.float32)
        for at in range(0, units, 128):
            here = slice(at, at + 128)
            new = decay * col_moment[:, here] + (1.0 - decay) * (sums[:, here] / total_rows)
            col_moment_new[:, here] = new
            total = total + sums[:, units + at : units + at + 128] / new
        terms[...] = total

    vmem = pl.BlockSpec(memory_space=pltpu.VMEM)
    return pl.pallas_call(
        kernel,
        out_shape=[jax.ShapeDtypeStruct((1, units), jnp.float32), jax.ShapeDtypeStruct((1, 128), jnp.float32)],
        in_specs=[vmem] * 2,
        out_specs=[vmem] * 2,
        compiler_params=pltpu.CompilerParams(vmem_limit_bytes=4 << 20),
        cost_estimate=EAGER,
    )(sums, col_moment)


def final_update(grad, row_moment_new, col_moment_new, terms, sums, total_rows, total_units):
    rows, units = grad.shape
    tile = units // 5

    def kernel(grad, row_moment_new, col_moment_new, terms, row_total, update, row_mean):
        mean = row_total[...] / total_rows
        row_mean[...] = mean
        square_sum = mean[:, 0:1] * jnp.sum(terms[...], axis=1, keepdims=True)
        clip = jnp.maximum(1.0, jnp.sqrt(square_sum / (total_rows * total_units)))
        col_factor = 1.0 / jnp.sqrt(col_moment_new[...])
        for at in range(0, rows, 128):
            here = slice(at, at + 128)
            row_factor = jnp.sqrt(mean / row_moment_new[:, here]) / clip
            update[here, :] = grad[here, :] * upright(row_factor) * col_factor

    def fixed(width, block=0):
        return pl.BlockSpec((1, width), lambda i: (0, block))

    return pl.pallas_call(
        kernel,
        grid=(units // tile,),
        out_shape=[jax.ShapeDtypeStruct((rows, units), jnp.float32), jax.ShapeDtypeStruct((1, 128), jnp.float32)],
        in_specs=[
            pl.BlockSpec((rows, tile), lambda i: (0, i)),
            fixed(rows),
            pl.BlockSpec((1, tile), lambda i: (0, i)),
            fixed(128),
            fixed(128, 2 * units // 128),
        ],
        out_specs=[pl.BlockSpec((rows, tile), lambda i: (0, i)), fixed(128)],
        compiler_params=pltpu.CompilerParams(vmem_limit_bytes=14 << 20),
        cost_estimate=EAGER,
    )(grad, row_moment_new, col_moment_new, terms, sums)


def products(share, groups, steps):
    pieces = [(piece, group[1]) for group in groups for piece in group[0]]
    bounds = [(output, group[1]) for group in groups for output in group[2]]

    def kernel(*refs):
        share_ref, ins = refs[0], refs[1 : 1 + len(pieces)]
        outs, stacks = refs[1 + len(pieces) : -len(groups)], refs[-len(groups) :]
        n = o = 0
        for (own, _, outputs, over_rows), stack in zip(groups, stacks):
            at = 0
            for piece, _ in own:
                stack[at : at + piece.shape[0], :] = ins[n][...]
                at += piece.shape[0]
                n += 1
            for ranges, kind in outputs:
                if over_rows:
                    side = jnp.concatenate([share_ref[:, begin:end] for begin, end in ranges], axis=1)
                    value = lax.dot_general(
                        side, stack[...], (((0,), (0,)), ((), ())), preferred_element_type=jnp.float32
                    )
                else:
                    side = jnp.concatenate([share_ref[begin:end, :] for begin, end in ranges], axis=0)
                    value = jnp.dot(side, stack[...], preferred_element_type=jnp.float32)
                outs[o][...] = value.astype(kind)
                o += 1

    def height(ranges):
        return sum(end - begin for begin, end in ranges)

    return pl.pallas_call(
        kernel,
        grid=(steps,),
        out_shape=[jax.ShapeDtypeStruct((height(ranges), columns), kind) for (ranges, kind), columns in bounds],
        in_specs=[pl.BlockSpec(share.shape, lambda i: (0, 0))]
        + [
            pl.BlockSpec((piece.shape[0], columns // steps), lambda i, skip=first * steps // columns: (0, i + skip))
            for (piece, first), columns in pieces
        ],
        out_specs=[pl.BlockSpec((height(ranges), columns // steps), lambda i: (0, i)) for (ranges, _), columns in bounds],
        scratch_shapes=[
            pltpu.VMEM((sum(piece.shape[0] for piece, _ in group[0]), group[1] // steps), jnp.bfloat16) for group in groups
        ],
        compiler_params=pltpu.CompilerParams(vmem_limit_bytes=14 << 20),
        cost_estimate=EAGER,
    )(share, *[piece for (piece, _), _ in pieces])


def staged_products(out_grad, gate_pre, up_pre, down_weight):
    x_bit, y_bit, z_bit, w_bit = 1, 2, 4, 8
    me, core = lax.axis_index("dp"), lax.axis_index("mp")
    tokens, units = gate_pre.shape
    rows = down_weight.shape[0]
    q, t = rows // 2, tokens // 2
    steps = 5
    split = units // 2
    barrier = lax.optimization_barrier
    place = jnp.stack([me, core]).astype(jnp.int32)
    own, right, message1, message2, message3 = first_stage(out_grad, gate_pre, up_pre, place, rows)

    down_weight, message1 = barrier((down_weight, message1))
    extra, every, whole = (split, 2 * rows), (0, tokens), (0, units)
    left1, left2, message3 = flip(message1, z_bit), flip(message2, w_bit), flip(message3, z_bit | w_bit)
    weight1, weight2 = flip(down_weight, x_bit), flip(down_weight, y_bit)
    message3, weight1, weight2 = barrier((message3, weight1, weight2))
    to_y, to_x = cut([weight1, weight2], [(0, (0, q), whole, 0, 0), (1, (q, q), whole, 1, 0)], [(q, units)] * 2)
    weight3a, weight3b = flip(to_y, y_bit), flip(to_x, x_bit)
    left1, left2, message3, right, _, _ = barrier((left1, left2, message3, right, to_y, to_x))
    to_z, mine = cut(
        [left1, left2, message3],
        [
            (1, every, (0, split), 0, 0),
            (0, every, extra, 1, 0),
            (1, every, extra, 1, 2 * rows),
            (2, every, (0, 2 * rows), 1, 4 * rows),
        ],
        [(tokens, split), (tokens, 6 * rows)],
    )
    left3 = flip(to_z, z_bit)
    right2 = flip(right, w_bit)
    theirs = flip(mine, 1, "mp")
    share = assemble(own, mine, theirs, place, rows)

    def low_sent(size):
        return [(2 * size, 3 * size), (6 * size, 7 * size)]

    def high_sent(size):
        return [(5 * size, 6 * size), (7 * size, 8 * size)]

    def sent(size):
        return [(low_sent(size), jnp.bfloat16), (high_sent(size), jnp.bfloat16)]

    def kept(size):
        ranges = [(0, 2 * size)], [(4 * size, 5 * size)], [(3 * size, 4 * size)]
        return [(r, jnp.float32) for r in ranges]

    left3, right2, share = barrier((left3, right2, share))
    (to_z,) = cut(
        [right2, right],
        [(0, every, (0, units - split), 0, 0), (1, every, (0, units - split), 0, units - split)],
        [(tokens, 2 * (units - split))],
    )
    from_near = flip(to_z, z_bit)
    lefts = [(message1, 0), (left1, 0), (left2, 0), (left3, 0)]
    left_to_x, left_to_y = products(share, [(lefts, split, sent(q), True)], steps)
    left_from_x, left_from_y = flip(left_to_x, x_bit), flip(left_to_y, y_bit)

    share, _ = barrier((share, left_to_x))
    weights = [(piece, 0) for piece in (down_weight, weight1, weight2, weight3a, weight3b)]
    to_w, to_z = products(
        share, [(weights, units, [(high_sent(t), jnp.bfloat16), (low_sent(t), jnp.bfloat16)], False)], steps
    )
    from_near, share, to_w, to_z = barrier((from_near, share, to_w, to_z))
    from_w, from_z = flip(to_w, w_bit), flip(to_z, z_bit)
    rights = [(right, 0), (from_near, units - split), (right2, 0), (from_near, 0)]
    right_to_x, right_to_y = products(share, [(rights, units - split, sent(q), True)], steps)
    right_from_x, right_from_y = flip(right_to_x, x_bit), flip(right_to_y, y_bit)
    share, left_from_x, left_from_y, _ = barrier((share, left_from_x, left_from_y, right_to_x))
    left_parts = products(share, [(lefts, split, kept(q), True)], steps)
    parts = products(share, [(rights, units - split, kept(q), True), (weights, units, kept(t), False)], steps)

    grad_a = flip(add_tail([left_parts[1], parts[1]], [left_from_x, right_from_x]), y_bit)
    grad_b = flip(add_tail([left_parts[2], parts[2]], [left_from_y, right_from_y]), x_bit)
    to_w, to_z = add_tail([parts[4]], [from_z]), add_tail([parts[5]], [from_w])
    last_a, last_b = flip(to_w, w_bit), flip(to_z, z_bit)
    grad_a, grad_b, _, _ = barrier((grad_a, grad_b, to_w, to_z))
    grad, row_part = sum_up(
        [left_parts[0], parts[0]],
        [left_from_x, right_from_x],
        [left_from_y, right_from_y],
        grad_a,
        grad_b,
        1.0 / math.sqrt(tokens * lax.axis_size("dp")),
    )

    row_sum = lax.psum(row_part, "mp")
    return grad, row_sum, (parts[3], from_z[:t], from_w[:t], last_a, last_b)


def local(out_grad, gate_pre, up_pre, down_weight, row_moment, col_moment):
    size = lax.axis_size("dp")
    rows, units = down_weight.shape
    tokens = out_grad.shape[0]
    all_bits = [1 << b for b in range(size.bit_length() - 1)]
    decay = 1.0 - TRAIN_STEP ** (-0.8)
    total_rows = rows * size
    total_units = units * lax.axis_size("mp")
    staged = size == 16 and lax.axis_size("mp") == 2 and rows % 256 == 0 and tokens % 32 == 0 and units % 2560 == 0
    if staged:
        grad, row_sum, terms = staged_products(out_grad, gate_pre, up_pre, down_weight)
        row_moment_new, sums = column_sums(grad, row_sum, row_moment[None, :], decay, total_units)
        sums = group_sum(sums[0], all_bits[:INNER_BITS])
        sums, terms = lax.optimization_barrier((sums, terms))
        own_part, from_low, from_high, last_a, last_b = terms
        arrived = jnp.concatenate([from_low, from_high], axis=0).astype(jnp.float32)
        hidden_grad = own_part + arrived + jnp.concatenate([last_a, last_b], axis=0).astype(jnp.float32)
        sums = group_sum(sums, all_bits[INNER_BITS:])[None, :]
        col_moment_new, ratios = column_step(sums, col_moment[None, :], decay, total_rows)
        ratios = lax.psum(ratios, "mp")
        update, row_mean = final_update(grad, row_moment_new, col_moment_new, ratios, sums, total_rows, total_units)
        row_moment_new, col_moment_new, row_mean = row_moment_new[0], col_moment_new[0], row_mean[0, 0]
    else:
        product, hidden_grad = general_products(
            out_grad, gate_pre, up_pre, down_weight, all_bits[:INNER_BITS], all_bits[INNER_BITS:]
        )
        grad = product * (1.0 / math.sqrt(tokens * size))
        powers = grad * grad
        squares = powers + 1e-30
        row_sum = lax.psum(jnp.sum(squares, axis=1), "mp")
        row_moment_new = decay * row_moment + (1.0 - decay) * (row_sum / total_units)
        col_part = jnp.sum(squares, axis=0)
        scaled_part = jnp.sum(powers / row_moment_new[:, None], axis=0)
        sums = jnp.concatenate([col_part, scaled_part, jnp.broadcast_to(jnp.sum(row_moment_new), (128,))])
        sums = group_sum(sums, all_bits)
        col_moment_new = decay * col_moment + (1.0 - decay) * (sums[:units] / total_rows)
        row_mean = sums[2 * units] / total_rows
        ratios = lax.psum(jnp.sum(sums[units : 2 * units] / col_moment_new), "mp")
        clip_norm = jnp.sqrt(row_mean * ratios / (total_rows * total_units))
        row_factor = jnp.sqrt(row_mean / row_moment_new) / jnp.maximum(1.0, clip_norm)
        col_factor = 1.0 / jnp.sqrt(col_moment_new)
        update = grad * row_factor[:, None] * col_factor[None, :]

    activated, derivative = gelu_parts(gate_pre.astype(jnp.float32))
    gate_grad = (hidden_grad * up_pre.astype(jnp.float32) * derivative).astype(jnp.bfloat16)
    up_grad = (hidden_grad * activated).astype(jnp.bfloat16)
    return (update, row_moment_new, col_moment_new, row_mean, gate_grad, up_grad)


def solution(mesh):
    in_specs = (P("dp", None), P("dp", "mp"), P("dp", "mp"), P("dp", "mp"), P("dp"), P("mp"))
    out_specs = (P("dp", "mp"), P("dp"), P("mp"), P(), P("dp", "mp"), P("dp", "mp"))
    return jax.shard_map(local, mesh=mesh, in_specs=in_specs, out_specs=out_specs, check_vma=False)
```

```python
import math

import jax
import jax.numpy as jnp
from jax import lax
from jax.experimental import pallas as pl
from jax.experimental.pallas import tpu as pltpu
from jax.sharding import PartitionSpec as P

TRAIN_STEP = 3
INNER_BITS = 2
EAGER = pl.CostEstimate(flops=0, bytes_accessed=0, transcendentals=0)


def gelu_parts(values):
    factor = math.sqrt(2.0 / math.pi)
    inner = factor * (values + 0.044715 * values * values * values)
    tangent = jnp.tanh(inner)
    activated = 0.5 * values * (1.0 + tangent)
    derivative = 0.5 * (1.0 + tangent) + 0.5 * values * (1.0 - tangent * tangent) * factor * (
        1.0 + 3.0 * 0.044715 * values * values
    )
    return (activated, derivative)


def flip(value, bits, axis="dp"):
    size = lax.axis_size(axis)
    return lax.ppermute(value, axis, [(i, i ^ bits) for i in range(size)])


def group_sum(value, bits):
    for at in range(0, len(bits), 2):
        pair = bits[at : at + 2]
        if len(pair) == 2:
            first, second = flip(value, pair[0]), flip(value, pair[1])
            value = (value + first) + (second + flip(value, pair[0] | pair[1]))
        else:
            value = value + flip(value, pair[0])
    return value


def general_products(out_grad, gate_pre, up_pre, down_weight, inner_bits, outer_bits):
    size = lax.axis_size("dp")
    me = lax.axis_index("dp")
    tokens, rows = out_grad.shape[0], down_weight.shape[0]
    inner = 2 ** len(inner_bits)
    activated, _ = gelu_parts(gate_pre.astype(jnp.float32))
    hidden = (activated * up_pre.astype(jnp.float32)).astype(jnp.bfloat16)
    by_block = out_grad.reshape(tokens, size, rows).transpose(1, 0, 2)

    def features_of(k):
        picks = [lax.dynamic_index_in_dim(by_block, me ^ (k * inner + j), 0, keepdims=False) for j in range(inner)]
        return jnp.concatenate(picks, axis=1)

    def gather(block, bits):
        blocks = [block]
        for bit in bits:
            blocks = blocks + [flip(b, bit) for b in blocks]
        return jnp.concatenate(blocks, axis=0)

    def scatter(values, bits):
        for level in reversed(range(len(bits))):
            count = 2**level
            values = [
                values[j] + flip(values[j + count].astype(jnp.bfloat16), bits[level]).astype(jnp.float32)
                for j in range(count)
            ]
        return values[0]

    shares = [features_of(0)] + [flip(features_of(k), k * inner) for k in range(1, size // inner)]
    share = jnp.concatenate(shares, axis=0)
    hidden_all = gather(hidden, outer_bits)
    weight_all = gather(down_weight, inner_bits)
    product = scatter(
        [
            lax.dot_general(
                share[:, j * rows : (j + 1) * rows],
                hidden_all,
                (((0,), (0,)), ((), ())),
                preferred_element_type=jnp.float32,
            )
            for j in range(inner)
        ],
        inner_bits,
    )
    hidden_grad = scatter(
        [jnp.dot(x, weight_all, preferred_element_type=jnp.float32) for x in shares],
        outer_bits,
    )
    return product, hidden_grad


def first_stage(out_grad, gate_pre, up_pre, place, rows):
    tokens, units = gate_pre.shape
    half = units // 2
    step = 32

    def kernel(place, source, gate, up, own, right, message1, message2, message3):
        me, core = place[0], place[1]

        def block(k, j):
            return pl.ds(pl.multiple_of((me ^ (4 * k + j)) * rows, rows), rows)

        activated, _ = gelu_parts(gate[...].astype(jnp.float32))
        value = (activated * up[...].astype(jnp.float32)).astype(jnp.bfloat16)
        right[...] = value[:, half:]
        message1[:, :half] = value[:, :half]
        message2[:, :half] = value[:, :half]
        for j in range(4):
            own[:, j * rows : (j + 1) * rows] = source[:, block(0, j)]
        for k, target, base in ((1, message1, half), (2, message2, half), (3, message3, 0)):
            for j in range(2):
                target[:, base + j * rows : base + (j + 1) * rows] = source[:, block(k, 2 * core + j)]

    widths = [4 * rows, units - half, half + 2 * rows, half + 2 * rows, 2 * rows]
    return pl.pallas_call(
        kernel,
        grid=(tokens // step,),
        out_shape=[jax.ShapeDtypeStruct((tokens, width), jnp.bfloat16) for width in widths],
        in_specs=[pl.BlockSpec(memory_space=pltpu.SMEM)]
        + [pl.BlockSpec((step, array.shape[1]), lambda i: (i, 0)) for array in (out_grad, gate_pre, up_pre)],
        out_specs=[pl.BlockSpec((step, width), lambda i: (i, 0)) for width in widths],
        compiler_params=pltpu.CompilerParams(vmem_limit_bytes=56 << 20),
        cost_estimate=EAGER,
    )(place, out_grad, gate_pre, up_pre)


def cut(sources, parts, shapes):
    def kernel(*refs):
        ins, outs, sems = refs[: len(sources)], refs[len(sources) : -1], refs[-1]
        copies = [
            pltpu.make_async_copy(
                ins[i].at[pl.ds(*rows), pl.ds(*columns)], outs[o].at[:, pl.ds(at, columns[1])], sems.at[n]
            )
            for n, (i, rows, columns, o, at) in enumerate(parts)
        ]
        for copy in copies:
            copy.start()
        for copy in copies:
            copy.wait()

    return pl.pallas_call(
        kernel,
        out_shape=[jax.ShapeDtypeStruct(shape, jnp.bfloat16) for shape in shapes],
        in_specs=[pl.BlockSpec(memory_space=pltpu.HBM)] * len(sources),
        out_specs=[pl.BlockSpec(memory_space=pltpu.HBM)] * len(shapes),
        scratch_shapes=[pltpu.SemaphoreType.DMA((len(parts),))],
        compiler_params=pltpu.CompilerParams(vmem_limit_bytes=1 << 20),
        cost_estimate=EAGER,
    )(*sources)


def assemble(own, mine, theirs, place, rows):
    tokens = own.shape[0]

    def kernel(place, own, mine, theirs, share):
        share[:tokens, :] = own[...]
        for k in range(3):
            here = pl.ds((k + 1) * tokens, tokens)
            half = slice(k * 2 * rows, (k + 1) * 2 * rows)
            a, b = mine[:, half], theirs[:, half]
            share[here, : 2 * rows] = jnp.where(place[1] == 0, a, b)
            share[here, 2 * rows :] = jnp.where(place[1] == 0, b, a)

    vmem = pl.BlockSpec(memory_space=pltpu.VMEM)
    return pl.pallas_call(
        kernel,
        out_shape=jax.ShapeDtypeStruct((4 * tokens, 4 * rows), jnp.bfloat16),
        in_specs=[pl.BlockSpec(memory_space=pltpu.SMEM), vmem, vmem, vmem],
        out_specs=vmem,
        compiler_params=pltpu.CompilerParams(vmem_limit_bytes=8 << 20),
        cost_estimate=EAGER,
    )(place, own, mine, theirs)


def add_tail(parts, arrived):
    rows = parts[0].shape[0]
    widths = [part.shape[1] for part in parts]

    def kernel(*refs):
        out, at = refs[-1], 0
        for part, other, width in zip(refs, refs[len(parts) :], widths):
            out[:, at : at + width] = (part[...] + other[-rows:, :].astype(jnp.float32)).astype(jnp.bfloat16)
            at += width

    vmem = pl.BlockSpec(memory_space=pltpu.VMEM)
    return pl.pallas_call(
        kernel,
        out_shape=jax.ShapeDtypeStruct((rows, sum(widths)), jnp.bfloat16),
        in_specs=[vmem] * (2 * len(parts)),
        out_specs=vmem,
        compiler_params=pltpu.CompilerParams(vmem_limit_bytes=8 << 20),
        cost_estimate=EAGER,
    )(*parts, *arrived)


def flat(column):
    return jnp.broadcast_to(column, (128, 128)).T[0:1, :]


def upright(row):
    return jnp.broadcast_to(row, (128, 128)).T[:, 0:1]


def sum_up(kept, from_low, from_high, last_a, last_b, scale):
    rows = kept[0].shape[0]
    q = rows // 2
    widths = [part.shape[1] for part in kept]
    units = sum(widths)

    def kernel(*refs):
        kept_refs, low_refs, high_refs = refs[:2], refs[2:4], refs[4:6]
        last_refs, grad, row_part = refs[6:8], refs[8], refs[9]
        for h, arrived in enumerate((low_refs, high_refs)):
            for at in range(0, q, 128):
                total = jnp.zeros((128, 1), jnp.float32)
                here = slice(h * q + at, h * q + at + 128)
                column = 0
                for part, other, width in zip(kept_refs, arrived, widths):
                    there = slice(column, column + width)
                    value = part[here, :] + other[at : at + 128, :].astype(jnp.float32)
                    value = (value + last_refs[h][at : at + 128, there].astype(jnp.float32)) * scale
                    grad[here, there] = value
                    total = total + jnp.sum(value * value + 1e-30, axis=1, keepdims=True)
                    column += width
                row_part[:, here] = flat(total)

    vmem = pl.BlockSpec(memory_space=pltpu.VMEM)
    return pl.pallas_call(
        kernel,
        out_shape=[jax.ShapeDtypeStruct((rows, units), jnp.float32), jax.ShapeDtypeStruct((1, rows), jnp.float32)],
        in_specs=[vmem] * 8,
        out_specs=[vmem] * 2,
        compiler_params=pltpu.CompilerParams(vmem_limit_bytes=14 << 20),
        cost_estimate=EAGER,
    )(*kept, *from_low, *from_high, last_a, last_b)


def column_sums(grad, row_sum, row_moment, decay, total_units):
    rows, units = grad.shape

    def kernel(grad, row_sum, row_moment, row_moment_new, sums):
        new = decay * row_moment[...] + (1.0 - decay) * (row_sum[...] / total_units)
        row_moment_new[...] = new
        sums[:, 2 * units :] = jnp.broadcast_to(jnp.sum(new, axis=1, keepdims=True), (1, 128))
        inverse = [1.0 / upright(new[:, at : at + 128]) for at in range(0, rows, 128)]
        for column in range(0, units, 256):
            there = slice(column, column + 256)
            squares, scaled = jnp.zeros((1, 256), jnp.float32), jnp.zeros((1, 256), jnp.float32)
            for n, at in enumerate(range(0, rows, 128)):
                power = grad[at : at + 128, there]
                power = power * power
                squares = squares + jnp.sum(power + 1e-30, axis=0, keepdims=True)
                scaled = scaled + jnp.sum(power * inverse[n], axis=0, keepdims=True)
            sums[:, there] = squares
            sums[:, units + column : units + column + 256] = scaled

    vmem = pl.BlockSpec(memory_space=pltpu.VMEM)
    return pl.pallas_call(
        kernel,
        out_shape=[
            jax.ShapeDtypeStruct((1, rows), jnp.float32),
            jax.ShapeDtypeStruct((1, 2 * units + 128), jnp.float32),
        ],
        in_specs=[vmem] * 3,
        out_specs=[vmem] * 2,
        compiler_params=pltpu.CompilerParams(vmem_limit_bytes=14 << 20),
        cost_estimate=EAGER,
    )(grad, row_sum, row_moment)


def column_step(sums, col_moment, decay, total_rows):
    units = col_moment.shape[1]

    def kernel(sums, col_moment, col_moment_new, terms):
        total = jnp.zeros((1, 128), jnp.float32)
        for at in range(0, units, 128):
            here = slice(at, at + 128)
            new = decay * col_moment[:, here] + (1.0 - decay) * (sums[:, here] / total_rows)
            col_moment_new[:, here] = new
            total = total + sums[:, units + at : units + at + 128] / new
        terms[...] = total

    vmem = pl.BlockSpec(memory_space=pltpu.VMEM)
    return pl.pallas_call(
        kernel,
        out_shape=[jax.ShapeDtypeStruct((1, units), jnp.float32), jax.ShapeDtypeStruct((1, 128), jnp.float32)],
        in_specs=[vmem] * 2,
        out_specs=[vmem] * 2,
        compiler_params=pltpu.CompilerParams(vmem_limit_bytes=4 << 20),
        cost_estimate=EAGER,
    )(sums, col_moment)


def final_update(grad, row_moment_new, col_moment_new, terms, sums, total_rows, total_units):
    rows, units = grad.shape
    tile = units // 2

    def kernel(grad, row_moment_new, col_moment_new, terms, row_total, update, row_mean):
        mean = row_total[...] / total_rows
        row_mean[...] = mean
        square_sum = mean[:, 0:1] * jnp.sum(terms[...], axis=1, keepdims=True)
        clip = jnp.maximum(1.0, jnp.sqrt(square_sum / (total_rows * total_units)))
        col_factor = 1.0 / jnp.sqrt(col_moment_new[...])
        for at in range(0, rows, 128):
            here = slice(at, at + 128)
            row_factor = jnp.sqrt(mean / row_moment_new[:, here]) / clip
            update[here, :] = grad[here, :] * upright(row_factor) * col_factor

    def fixed(width, block=0):
        return pl.BlockSpec((1, width), lambda i: (0, block))

    return pl.pallas_call(
        kernel,
        grid=(units // tile,),
        out_shape=[jax.ShapeDtypeStruct((rows, units), jnp.float32), jax.ShapeDtypeStruct((1, 128), jnp.float32)],
        in_specs=[
            pl.BlockSpec((rows, tile), lambda i: (0, i)),
            fixed(rows),
            pl.BlockSpec((1, tile), lambda i: (0, i)),
            fixed(128),
            fixed(128, 2 * units // 128),
        ],
        out_specs=[pl.BlockSpec((rows, tile), lambda i: (0, i)), fixed(128)],
        compiler_params=pltpu.CompilerParams(vmem_limit_bytes=14 << 20),
        cost_estimate=EAGER,
    )(grad, row_moment_new, col_moment_new, terms, sums)


def products(share, groups, steps):
    pieces = [(piece, group[1]) for group in groups for piece in group[0]]
    bounds = [(output, group[1]) for group in groups for output in group[2]]

    def kernel(*refs):
        share_ref, ins = refs[0], refs[1 : 1 + len(pieces)]
        outs, stacks = refs[1 + len(pieces) : -len(groups)], refs[-len(groups) :]
        n = o = 0
        for (own, _, outputs, over_rows), stack in zip(groups, stacks):
            at = 0
            for piece, _ in own:
                stack[at : at + piece.shape[0], :] = ins[n][...]
                at += piece.shape[0]
                n += 1
            for ranges, kind in outputs:
                if over_rows:
                    side = jnp.concatenate([share_ref[:, begin:end] for begin, end in ranges], axis=1)
                    value = lax.dot_general(
                        side, stack[...], (((0,), (0,)), ((), ())), preferred_element_type=jnp.float32
                    )
                else:
                    side = jnp.concatenate([share_ref[begin:end, :] for begin, end in ranges], axis=0)
                    value = jnp.dot(side, stack[...], preferred_element_type=jnp.float32)
                outs[o][...] = value.astype(kind)
                o += 1

    def height(ranges):
        return sum(end - begin for begin, end in ranges)

    return pl.pallas_call(
        kernel,
        grid=(steps,),
        out_shape=[jax.ShapeDtypeStruct((height(ranges), columns), kind) for (ranges, kind), columns in bounds],
        in_specs=[pl.BlockSpec(share.shape, lambda i: (0, 0))]
        + [
            pl.BlockSpec((piece.shape[0], columns // steps), lambda i, skip=first * steps // columns: (0, i + skip))
            for (piece, first), columns in pieces
        ],
        out_specs=[pl.BlockSpec((height(ranges), columns // steps), lambda i: (0, i)) for (ranges, _), columns in bounds],
        scratch_shapes=[
            pltpu.VMEM((sum(piece.shape[0] for piece, _ in group[0]), group[1] // steps), jnp.bfloat16) for group in groups
        ],
        compiler_params=pltpu.CompilerParams(vmem_limit_bytes=14 << 20),
        cost_estimate=EAGER,
    )(share, *[piece for (piece, _), _ in pieces])


def staged_products(out_grad, gate_pre, up_pre, down_weight):
    x_bit, y_bit, z_bit, w_bit = 1, 2, 4, 8
    me, core = lax.axis_index("dp"), lax.axis_index("mp")
    tokens, units = gate_pre.shape
    rows = down_weight.shape[0]
    q, t = rows // 2, tokens // 2
    steps = 5
    split = units // 2
    barrier = lax.optimization_barrier
    place = jnp.stack([me, core]).astype(jnp.int32)
    own, right, message1, message2, message3 = first_stage(out_grad, gate_pre, up_pre, place, rows)

    extra, every, whole = (split, 2 * rows), (0, tokens), (0, units)
    left1, left2, message3 = flip(message1, z_bit), flip(message2, w_bit), flip(message3, z_bit | w_bit)
    weight1, weight2 = flip(down_weight, x_bit), flip(down_weight, y_bit)
    message3, weight1, weight2 = barrier((message3, weight1, weight2))
    to_y, to_x = cut([weight1, weight2], [(0, (0, q), whole, 0, 0), (1, (q, q), whole, 1, 0)], [(q, units)] * 2)
    weight3a, weight3b = flip(to_y, y_bit), flip(to_x, x_bit)
    left1, left2, message3, right, _, _ = barrier((left1, left2, message3, right, to_y, to_x))
    to_z, mine = cut(
        [left1, left2, message3, right],
        [
            (1, every, (0, split), 0, 0),
            (3, every, (0, units - split), 0, split),
            (0, every, extra, 1, 0),
            (1, every, extra, 1, 2 * rows),
            (2, every, (0, 2 * rows), 1, 4 * rows),
        ],
        [(tokens, units), (tokens, 6 * rows)],
    )
    from_near = flip(to_z, z_bit)
    right2 = flip(right, w_bit)
    theirs = flip(mine, 1, "mp")
    share = assemble(own, mine, theirs, place, rows)

    def low_sent(size):
        return [(2 * size, 3 * size), (6 * size, 7 * size)]

    def high_sent(size):
        return [(5 * size, 6 * size), (7 * size, 8 * size)]

    def sent(size):
        return [(low_sent(size), jnp.bfloat16), (high_sent(size), jnp.bfloat16)]

    def kept(size):
        ranges = [(0, 2 * size)], [(4 * size, 5 * size)], [(3 * size, 4 * size)]
        return [(r, jnp.float32) for r in ranges]

    from_near, right2, share = barrier((from_near, right2, share))
    right3 = flip(right2, z_bit)
    lefts = [(message1, 0), (left1, 0), (left2, 0), (from_near, 0)]
    left_to_x, left_to_y = products(share, [(lefts, split, sent(q), True)], steps)
    left_from_x, left_from_y = flip(left_to_x, x_bit), flip(left_to_y, y_bit)

    share, _ = barrier((share, left_to_x))
    weights = [(piece, 0) for piece in (down_weight, weight1, weight2, weight3a, weight3b)]
    to_w, to_z = products(
        share, [(weights, units, [(high_sent(t), jnp.bfloat16), (low_sent(t), jnp.bfloat16)], False)], steps
    )
    right3, share, to_w, to_z = barrier((right3, share, to_w, to_z))
    from_w, from_z = flip(to_w, w_bit), flip(to_z, z_bit)
    rights = [(right, 0), (from_near, split), (right2, 0), (right3, 0)]
    right_to_x, right_to_y = products(share, [(rights, units - split, sent(q), True)], steps)
    right_from_x, right_from_y = flip(right_to_x, x_bit), flip(right_to_y, y_bit)
    share, left_from_x, left_from_y, _ = barrier((share, left_from_x, left_from_y, right_to_x))
    left_parts = products(share, [(lefts, split, kept(q), True)], steps)
    parts = products(share, [(rights, units - split, kept(q), True), (weights, units, kept(t), False)], steps)

    grad_a = flip(add_tail([left_parts[1], parts[1]], [left_from_x, right_from_x]), y_bit)
    grad_b = flip(add_tail([left_parts[2], parts[2]], [left_from_y, right_from_y]), x_bit)
    to_w, to_z = add_tail([parts[4]], [from_z]), add_tail([parts[5]], [from_w])
    last_a, last_b = flip(to_w, w_bit), flip(to_z, z_bit)
    grad_a, grad_b, _, _ = barrier((grad_a, grad_b, to_w, to_z))
    grad, row_part = sum_up(
        [left_parts[0], parts[0]],
        [left_from_x, right_from_x],
        [left_from_y, right_from_y],
        grad_a,
        grad_b,
        1.0 / math.sqrt(tokens * lax.axis_size("dp")),
    )

    row_sum = lax.psum(row_part, "mp")
    return grad, row_sum, (parts[3], from_z[:t], from_w[:t], last_a, last_b)


def local(out_grad, gate_pre, up_pre, down_weight, row_moment, col_moment):
    size = lax.axis_size("dp")
    rows, units = down_weight.shape
    tokens = out_grad.shape[0]
    all_bits = [1 << b for b in range(size.bit_length() - 1)]
    decay = 1.0 - TRAIN_STEP ** (-0.8)
    total_rows = rows * size
    total_units = units * lax.axis_size("mp")
    staged = size == 16 and lax.axis_size("mp") == 2 and rows % 256 == 0 and tokens % 32 == 0 and units % 2560 == 0
    if staged:
        grad, row_sum, terms = staged_products(out_grad, gate_pre, up_pre, down_weight)
        row_moment_new, sums = column_sums(grad, row_sum, row_moment[None, :], decay, total_units)
        sums = group_sum(sums[0], all_bits[:INNER_BITS])
        sums, terms = lax.optimization_barrier((sums, terms))
        own_part, from_low, from_high, last_a, last_b = terms
        arrived = jnp.concatenate([from_low, from_high], axis=0).astype(jnp.float32)
        hidden_grad = own_part + arrived + jnp.concatenate([last_a, last_b], axis=0).astype(jnp.float32)
        sums = group_sum(sums, all_bits[INNER_BITS:])[None, :]
        col_moment_new, ratios = column_step(sums, col_moment[None, :], decay, total_rows)
        ratios = lax.psum(ratios, "mp")
        update, row_mean = final_update(grad, row_moment_new, col_moment_new, ratios, sums, total_rows, total_units)
        row_moment_new, col_moment_new, row_mean = row_moment_new[0], col_moment_new[0], row_mean[0, 0]
    else:
        product, hidden_grad = general_products(
            out_grad, gate_pre, up_pre, down_weight, all_bits[:INNER_BITS], all_bits[INNER_BITS:]
        )
        grad = product * (1.0 / math.sqrt(tokens * size))
        powers = grad * grad
        squares = powers + 1e-30
        row_sum = lax.psum(jnp.sum(squares, axis=1), "mp")
        row_moment_new = decay * row_moment + (1.0 - decay) * (row_sum / total_units)
        col_part = jnp.sum(squares, axis=0)
        scaled_part = jnp.sum(powers / row_moment_new[:, None], axis=0)
        sums = jnp.concatenate([col_part, scaled_part, jnp.broadcast_to(jnp.sum(row_moment_new), (128,))])
        sums = group_sum(sums, all_bits)
        col_moment_new = decay * col_moment + (1.0 - decay) * (sums[:units] / total_rows)
        row_mean = sums[2 * units] / total_rows
        ratios = lax.psum(jnp.sum(sums[units : 2 * units] / col_moment_new), "mp")
        clip_norm = jnp.sqrt(row_mean * ratios / (total_rows * total_units))
        row_factor = jnp.sqrt(row_mean / row_moment_new) / jnp.maximum(1.0, clip_norm)
        col_factor = 1.0 / jnp.sqrt(col_moment_new)
        update = grad * row_factor[:, None] * col_factor[None, :]

    activated, derivative = gelu_parts(gate_pre.astype(jnp.float32))
    gate_grad = (hidden_grad * up_pre.astype(jnp.float32) * derivative).astype(jnp.bfloat16)
    up_grad = (hidden_grad * activated).astype(jnp.bfloat16)
    return (update, row_moment_new, col_moment_new, row_mean, gate_grad, up_grad)


def solution(mesh):
    in_specs = (P("dp", None), P("dp", "mp"), P("dp", "mp"), P("dp", "mp"), P("dp"), P("mp"))
    out_specs = (P("dp", "mp"), P("dp"), P("mp"), P(), P("dp", "mp"), P("dp", "mp"))
    return jax.shard_map(local, mesh=mesh, in_specs=in_specs, out_specs=out_specs, check_vma=False)
```

```python
import math

import jax
import jax.numpy as jnp
from jax import lax
from jax.experimental import pallas as pl
from jax.experimental.pallas import tpu as pltpu
from jax.sharding import PartitionSpec as P

TRAIN_STEP = 3
INNER_BITS = 2
EAGER = pl.CostEstimate(flops=0, bytes_accessed=0, transcendentals=0)


def gelu_parts(values):
    factor = math.sqrt(2.0 / math.pi)
    inner = factor * (values + 0.044715 * values * values * values)
    tangent = jnp.tanh(inner)
    activated = 0.5 * values * (1.0 + tangent)
    derivative = 0.5 * (1.0 + tangent) + 0.5 * values * (1.0 - tangent * tangent) * factor * (
        1.0 + 3.0 * 0.044715 * values * values
    )
    return (activated, derivative)


def flip(value, bits, axis="dp"):
    size = lax.axis_size(axis)
    return lax.ppermute(value, axis, [(i, i ^ bits) for i in range(size)])


def group_sum(value, bits):
    for at in range(0, len(bits), 2):
        pair = bits[at : at + 2]
        if len(pair) == 2:
            first, second = flip(value, pair[0]), flip(value, pair[1])
            value = (value + first) + (second + flip(value, pair[0] | pair[1]))
        else:
            value = value + flip(value, pair[0])
    return value


def general_products(out_grad, gate_pre, up_pre, down_weight, inner_bits, outer_bits):
    size = lax.axis_size("dp")
    me = lax.axis_index("dp")
    tokens, rows = out_grad.shape[0], down_weight.shape[0]
    inner = 2 ** len(inner_bits)
    activated, _ = gelu_parts(gate_pre.astype(jnp.float32))
    hidden = (activated * up_pre.astype(jnp.float32)).astype(jnp.bfloat16)
    by_block = out_grad.reshape(tokens, size, rows).transpose(1, 0, 2)

    def features_of(k):
        picks = [lax.dynamic_index_in_dim(by_block, me ^ (k * inner + j), 0, keepdims=False) for j in range(inner)]
        return jnp.concatenate(picks, axis=1)

    def gather(block, bits):
        blocks = [block]
        for bit in bits:
            blocks = blocks + [flip(b, bit) for b in blocks]
        return jnp.concatenate(blocks, axis=0)

    def scatter(values, bits):
        for level in reversed(range(len(bits))):
            count = 2**level
            values = [
                values[j] + flip(values[j + count].astype(jnp.bfloat16), bits[level]).astype(jnp.float32)
                for j in range(count)
            ]
        return values[0]

    shares = [features_of(0)] + [flip(features_of(k), k * inner) for k in range(1, size // inner)]
    share = jnp.concatenate(shares, axis=0)
    hidden_all = gather(hidden, outer_bits)
    weight_all = gather(down_weight, inner_bits)
    product = scatter(
        [
            lax.dot_general(
                share[:, j * rows : (j + 1) * rows],
                hidden_all,
                (((0,), (0,)), ((), ())),
                preferred_element_type=jnp.float32,
            )
            for j in range(inner)
        ],
        inner_bits,
    )
    hidden_grad = scatter(
        [jnp.dot(x, weight_all, preferred_element_type=jnp.float32) for x in shares],
        outer_bits,
    )
    return product, hidden_grad


def first_stage(out_grad, gate_pre, up_pre, rows):
    tokens, units = gate_pre.shape
    half = units // 2
    step = 32

    def kernel(source, gate, up, own, right, message1, message2, message3):
        me, core = lax.axis_index("dp"), lax.axis_index("mp")

        def block(k, j):
            return pl.ds(pl.multiple_of((me ^ (4 * k + j)) * rows, rows), rows)

        activated, _ = gelu_parts(gate[...].astype(jnp.float32))
        value = (activated * up[...].astype(jnp.float32)).astype(jnp.bfloat16)
        right[...] = value[:, half:]
        message1[:, :half] = value[:, :half]
        message2[:, :half] = value[:, :half]
        for j in range(4):
            own[:, j * rows : (j + 1) * rows] = source[:, block(0, j)]
        for k, target, base in ((1, message1, half), (2, message2, half), (3, message3, 0)):
            for j in range(2):
                target[:, base + j * rows : base + (j + 1) * rows] = source[:, block(k, 2 * core + j)]

    widths = [4 * rows, units - half, half + 2 * rows, half + 2 * rows, 2 * rows]
    return pl.pallas_call(
        kernel,
        grid=(tokens // step,),
        out_shape=[jax.ShapeDtypeStruct((tokens, width), jnp.bfloat16) for width in widths],
        in_specs=[pl.BlockSpec((step, array.shape[1]), lambda i: (i, 0)) for array in (out_grad, gate_pre, up_pre)],
        out_specs=[pl.BlockSpec((step, width), lambda i: (i, 0)) for width in widths],
        compiler_params=pltpu.CompilerParams(vmem_limit_bytes=56 << 20),
        cost_estimate=EAGER,
    )(out_grad, gate_pre, up_pre)


def gelu_terms(gate_pre, up_pre):
    tokens, units = gate_pre.shape
    step = 32

    def kernel(gate, up, activated, slope):
        value, derivative = gelu_parts(gate[...].astype(jnp.float32))
        activated[...] = value
        slope[...] = up[...].astype(jnp.float32) * derivative

    block = pl.BlockSpec((step, units), lambda i: (i, 0))
    return pl.pallas_call(
        kernel,
        grid=(tokens // step,),
        out_shape=[jax.ShapeDtypeStruct((tokens, units), jnp.float32)] * 2,
        in_specs=[block] * 2,
        out_specs=[block] * 2,
        compiler_params=pltpu.CompilerParams(vmem_limit_bytes=10 << 20),
        cost_estimate=EAGER,
    )(gate_pre, up_pre)


def cut(sources, parts, shapes):
    def kernel(*refs):
        ins, outs, sems = refs[: len(sources)], refs[len(sources) : -1], refs[-1]
        copies = [
            pltpu.make_async_copy(
                ins[i].at[pl.ds(*rows), pl.ds(*columns)], outs[o].at[:, pl.ds(at, columns[1])], sems.at[n]
            )
            for n, (i, rows, columns, o, at) in enumerate(parts)
        ]
        for copy in copies:
            copy.start()
        for copy in copies:
            copy.wait()

    return pl.pallas_call(
        kernel,
        out_shape=[jax.ShapeDtypeStruct(shape, jnp.bfloat16) for shape in shapes],
        in_specs=[pl.BlockSpec(memory_space=pltpu.HBM)] * len(sources),
        out_specs=[pl.BlockSpec(memory_space=pltpu.HBM)] * len(shapes),
        scratch_shapes=[pltpu.SemaphoreType.DMA((len(parts),))],
        compiler_params=pltpu.CompilerParams(vmem_limit_bytes=1 << 20),
        cost_estimate=EAGER,
    )(*sources)


def assemble(own, mine, theirs, place, rows):
    tokens = own.shape[0]

    def kernel(place, own, mine, theirs, share):
        share[:tokens, :] = own[...]
        for k in range(3):
            here = pl.ds((k + 1) * tokens, tokens)
            half = slice(k * 2 * rows, (k + 1) * 2 * rows)
            a, b = mine[:, half], theirs[:, half]
            share[here, : 2 * rows] = jnp.where(place[1] == 0, a, b)
            share[here, 2 * rows :] = jnp.where(place[1] == 0, b, a)

    vmem = pl.BlockSpec(memory_space=pltpu.VMEM)
    return pl.pallas_call(
        kernel,
        out_shape=jax.ShapeDtypeStruct((4 * tokens, 4 * rows), jnp.bfloat16),
        in_specs=[pl.BlockSpec(memory_space=pltpu.SMEM), vmem, vmem, vmem],
        out_specs=vmem,
        compiler_params=pltpu.CompilerParams(vmem_limit_bytes=8 << 20),
        cost_estimate=EAGER,
    )(place, own, mine, theirs)


def add_tail(parts, arrived):
    rows = parts[0].shape[0]
    widths = [part.shape[1] for part in parts]

    def kernel(*refs):
        out, at = refs[-1], 0
        for part, other, width in zip(refs, refs[len(parts) :], widths):
            out[:, at : at + width] = (part[...] + other[-rows:, :].astype(jnp.float32)).astype(jnp.bfloat16)
            at += width

    vmem = pl.BlockSpec(memory_space=pltpu.VMEM)
    return pl.pallas_call(
        kernel,
        out_shape=jax.ShapeDtypeStruct((rows, sum(widths)), jnp.bfloat16),
        in_specs=[vmem] * (2 * len(parts)),
        out_specs=vmem,
        compiler_params=pltpu.CompilerParams(vmem_limit_bytes=8 << 20),
        cost_estimate=EAGER,
    )(*parts, *arrived)


def flat(column):
    return jnp.broadcast_to(column, (128, 128)).T[0:1, :]


def upright(row):
    return jnp.broadcast_to(row, (128, 128)).T[:, 0:1]


def sum_up(kept, from_low, from_high, last_a, last_b, scale):
    rows = kept[0].shape[0]
    q = rows // 2
    widths = [part.shape[1] for part in kept]
    units = sum(widths)

    def kernel(*refs):
        kept_refs, low_refs, high_refs = refs[:2], refs[2:4], refs[4:6]
        last_refs, grad, row_part = refs[6:8], refs[8], refs[9]
        for h, arrived in enumerate((low_refs, high_refs)):
            for at in range(0, q, 128):
                total = jnp.zeros((128, 1), jnp.float32)
                here = slice(h * q + at, h * q + at + 128)
                column = 0
                for part, other, width in zip(kept_refs, arrived, widths):
                    there = slice(column, column + width)
                    value = part[here, :] + other[at : at + 128, :].astype(jnp.float32)
                    value = (value + last_refs[h][at : at + 128, there].astype(jnp.float32)) * scale
                    grad[here, there] = value
                    total = total + jnp.sum(value * value + 1e-30, axis=1, keepdims=True)
                    column += width
                row_part[:, here] = flat(total)

    vmem = pl.BlockSpec(memory_space=pltpu.VMEM)
    return pl.pallas_call(
        kernel,
        out_shape=[jax.ShapeDtypeStruct((rows, units), jnp.float32), jax.ShapeDtypeStruct((1, rows), jnp.float32)],
        in_specs=[vmem] * 8,
        out_specs=[vmem] * 2,
        compiler_params=pltpu.CompilerParams(vmem_limit_bytes=14 << 20),
        cost_estimate=EAGER,
    )(*kept, *from_low, *from_high, last_a, last_b)


def column_sums(grad, row_sum, row_moment, decay, total_units):
    rows, units = grad.shape

    def kernel(grad, row_sum, row_moment, row_moment_new, sums):
        new = decay * row_moment[...] + (1.0 - decay) * (row_sum[...] / total_units)
        row_moment_new[...] = new
        sums[:, 2 * units :] = jnp.broadcast_to(jnp.sum(new, axis=1, keepdims=True), (1, 128))
        inverse = [1.0 / upright(new[:, at : at + 128]) for at in range(0, rows, 128)]
        for column in range(0, units, 256):
            there = slice(column, column + 256)
            squares, scaled = jnp.zeros((1, 256), jnp.float32), jnp.zeros((1, 256), jnp.float32)
            for n, at in enumerate(range(0, rows, 128)):
                power = grad[at : at + 128, there]
                power = power * power
                squares = squares + jnp.sum(power + 1e-30, axis=0, keepdims=True)
                scaled = scaled + jnp.sum(power * inverse[n], axis=0, keepdims=True)
            sums[:, there] = squares
            sums[:, units + column : units + column + 256] = scaled

    vmem = pl.BlockSpec(memory_space=pltpu.VMEM)
    return pl.pallas_call(
        kernel,
        out_shape=[
            jax.ShapeDtypeStruct((1, rows), jnp.float32),
            jax.ShapeDtypeStruct((1, 2 * units + 128), jnp.float32),
        ],
        in_specs=[vmem] * 3,
        out_specs=[vmem] * 2,
        compiler_params=pltpu.CompilerParams(vmem_limit_bytes=14 << 20),
        cost_estimate=EAGER,
    )(grad, row_sum, row_moment)


def column_step(sums, col_moment, decay, total_rows):
    units = col_moment.shape[1]

    def kernel(sums, col_moment, col_moment_new, terms):
        total = jnp.zeros((1, 128), jnp.float32)
        for at in range(0, units, 128):
            here = slice(at, at + 128)
            new = decay * col_moment[:, here] + (1.0 - decay) * (sums[:, here] / total_rows)
            col_moment_new[:, here] = new
            total = total + sums[:, units + at : units + at + 128] / new
        terms[...] = total

    vmem = pl.BlockSpec(memory_space=pltpu.VMEM)
    return pl.pallas_call(
        kernel,
        out_shape=[jax.ShapeDtypeStruct((1, units), jnp.float32), jax.ShapeDtypeStruct((1, 128), jnp.float32)],
        in_specs=[vmem] * 2,
        out_specs=[vmem] * 2,
        compiler_params=pltpu.CompilerParams(vmem_limit_bytes=4 << 20),
        cost_estimate=EAGER,
    )(sums, col_moment)


def final_update(grad, row_moment_new, col_moment_new, terms, sums, total_rows, total_units):
    rows, units = grad.shape
    tile = units // 2

    def kernel(grad, row_moment_new, col_moment_new, terms, row_total, update, row_mean):
        mean = row_total[...] / total_rows
        row_mean[...] = mean
        square_sum = mean[:, 0:1] * jnp.sum(terms[...], axis=1, keepdims=True)
        clip = jnp.maximum(1.0, jnp.sqrt(square_sum / (total_rows * total_units)))
        col_factor = 1.0 / jnp.sqrt(col_moment_new[...])
        for at in range(0, rows, 128):
            here = slice(at, at + 128)
            row_factor = jnp.sqrt(mean / row_moment_new[:, here]) / clip
            update[here, :] = grad[here, :] * upright(row_factor) * col_factor

    def fixed(width, block=0):
        return pl.BlockSpec((1, width), lambda i: (0, block))

    return pl.pallas_call(
        kernel,
        grid=(units // tile,),
        out_shape=[jax.ShapeDtypeStruct((rows, units), jnp.float32), jax.ShapeDtypeStruct((1, 128), jnp.float32)],
        in_specs=[
            pl.BlockSpec((rows, tile), lambda i: (0, i)),
            fixed(rows),
            pl.BlockSpec((1, tile), lambda i: (0, i)),
            fixed(128),
            fixed(128, 2 * units // 128),
        ],
        out_specs=[pl.BlockSpec((rows, tile), lambda i: (0, i)), fixed(128)],
        compiler_params=pltpu.CompilerParams(vmem_limit_bytes=14 << 20),
        cost_estimate=EAGER,
    )(grad, row_moment_new, col_moment_new, terms, sums)


def products(share, groups, steps):
    pieces = [(piece, group[1]) for group in groups for piece in group[0]]
    bounds = [(output, group[1]) for group in groups for output in group[2]]

    def kernel(*refs):
        share_ref, ins = refs[0], refs[1 : 1 + len(pieces)]
        outs, stacks = refs[1 + len(pieces) : -len(groups)], refs[-len(groups) :]
        n = o = 0
        for (own, _, outputs, over_rows), stack in zip(groups, stacks):
            at = 0
            for piece, _ in own:
                stack[at : at + piece.shape[0], :] = ins[n][...]
                at += piece.shape[0]
                n += 1
            for ranges, kind in outputs:
                if over_rows:
                    side = jnp.concatenate([share_ref[:, begin:end] for begin, end in ranges], axis=1)
                    value = lax.dot_general(
                        side, stack[...], (((0,), (0,)), ((), ())), preferred_element_type=jnp.float32
                    )
                else:
                    side = jnp.concatenate([share_ref[begin:end, :] for begin, end in ranges], axis=0)
                    value = jnp.dot(side, stack[...], preferred_element_type=jnp.float32)
                outs[o][...] = value.astype(kind)
                o += 1

    def height(ranges):
        return sum(end - begin for begin, end in ranges)

    return pl.pallas_call(
        kernel,
        grid=(steps,),
        out_shape=[jax.ShapeDtypeStruct((height(ranges), columns), kind) for (ranges, kind), columns in bounds],
        in_specs=[pl.BlockSpec(share.shape, lambda i: (0, 0))]
        + [
            pl.BlockSpec((piece.shape[0], columns // steps), lambda i, skip=first * steps // columns: (0, i + skip))
            for (piece, first), columns in pieces
        ],
        out_specs=[pl.BlockSpec((height(ranges), columns // steps), lambda i: (0, i)) for (ranges, _), columns in bounds],
        scratch_shapes=[
            pltpu.VMEM((sum(piece.shape[0] for piece, _ in group[0]), group[1] // steps), jnp.bfloat16) for group in groups
        ],
        compiler_params=pltpu.CompilerParams(vmem_limit_bytes=14 << 20),
        cost_estimate=EAGER,
    )(share, *[piece for (piece, _), _ in pieces])


def staged_products(out_grad, gate_pre, up_pre, down_weight):
    x_bit, y_bit, z_bit, w_bit = 1, 2, 4, 8
    me, core = lax.axis_index("dp"), lax.axis_index("mp")
    tokens, units = gate_pre.shape
    rows = down_weight.shape[0]
    q, t = rows // 2, tokens // 2
    steps = 5
    split = units // 2
    barrier = lax.optimization_barrier
    place = jnp.stack([me, core]).astype(jnp.int32)
    own, right, message1, message2, message3 = first_stage(out_grad, gate_pre, up_pre, rows)

    extra, every, whole = (split, 2 * rows), (0, tokens), (0, units)
    left1, left2, message3 = flip(message1, z_bit), flip(message2, w_bit), flip(message3, z_bit | w_bit)
    weight1, weight2 = flip(down_weight, x_bit), flip(down_weight, y_bit)
    activated, slope = gelu_terms(gate_pre, up_pre)
    message3, weight1, weight2, activated, slope = barrier((message3, weight1, weight2, activated, slope))
    to_y, to_x = cut([weight1, weight2], [(0, (0, q), whole, 0, 0), (1, (q, q), whole, 1, 0)], [(q, units)] * 2)
    weight3a, weight3b = flip(to_y, y_bit), flip(to_x, x_bit)
    left1, left2, message3, right, _, _ = barrier((left1, left2, message3, right, to_y, to_x))
    to_z, mine = cut(
        [left1, left2, message3, right],
        [
            (3, every, (0, units - split), 0, 0),
            (1, every, (0, split), 0, units - split),
            (0, every, extra, 1, 0),
            (1, every, extra, 1, 2 * rows),
            (2, every, (0, 2 * rows), 1, 4 * rows),
        ],
        [(tokens, units), (tokens, 6 * rows)],
    )
    from_near = flip(to_z, z_bit)
    right2 = flip(right, w_bit)
    theirs = flip(mine, 1, "mp")
    share = assemble(own, mine, theirs, place, rows)

    def low_sent(size):
        return [(2 * size, 3 * size), (6 * size, 7 * size)]

    def high_sent(size):
        return [(5 * size, 6 * size), (7 * size, 8 * size)]

    def sent(size):
        return [(low_sent(size), jnp.bfloat16), (high_sent(size), jnp.bfloat16)]

    def kept(size):
        ranges = [(0, 2 * size)], [(4 * size, 5 * size)], [(3 * size, 4 * size)]
        return [(r, jnp.float32) for r in ranges]

    from_near, right2, share = barrier((from_near, right2, share))
    right3 = flip(right2, z_bit)
    lefts = [(message1, 0), (left1, 0), (left2, 0), (from_near, units - split)]
    left_to_x, left_to_y = products(share, [(lefts, split, sent(q), True)], steps)
    left_from_x, left_from_y = flip(left_to_x, x_bit), flip(left_to_y, y_bit)

    share, _ = barrier((share, left_to_x))
    weights = [(piece, 0) for piece in (down_weight, weight1, weight2, weight3a, weight3b)]
    to_w, to_z = products(
        share, [(weights, units, [(high_sent(t), jnp.bfloat16), (low_sent(t), jnp.bfloat16)], False)], steps
    )
    right3, share, to_w, to_z = barrier((right3, share, to_w, to_z))
    from_w, from_z = flip(to_w, w_bit), flip(to_z, z_bit)
    rights = [(right, 0), (from_near, 0), (right2, 0), (right3, 0)]
    right_to_x, right_to_y = products(share, [(rights, units - split, sent(q), True)], steps)
    right_from_x, right_from_y = flip(right_to_x, x_bit), flip(right_to_y, y_bit)
    share, left_from_x, left_from_y, _ = barrier((share, left_from_x, left_from_y, right_to_x))
    left_parts = products(share, [(lefts, split, kept(q), True)], steps)
    parts = products(share, [(rights, units - split, kept(q), True), (weights, units, kept(t), False)], steps)

    grad_a = flip(add_tail([left_parts[1], parts[1]], [left_from_x, right_from_x]), y_bit)
    grad_b = flip(add_tail([left_parts[2], parts[2]], [left_from_y, right_from_y]), x_bit)
    to_w, to_z = add_tail([parts[4]], [from_z]), add_tail([parts[5]], [from_w])
    last_a, last_b = flip(to_w, w_bit), flip(to_z, z_bit)
    grad_a, grad_b, _, _ = barrier((grad_a, grad_b, to_w, to_z))
    grad, row_part = sum_up(
        [left_parts[0], parts[0]],
        [left_from_x, right_from_x],
        [left_from_y, right_from_y],
        grad_a,
        grad_b,
        1.0 / math.sqrt(tokens * lax.axis_size("dp")),
    )

    row_sum = lax.psum(row_part, "mp")
    return grad, row_sum, (parts[3], from_z[:t], from_w[:t], last_a, last_b, activated, slope)


def local(out_grad, gate_pre, up_pre, down_weight, row_moment, col_moment):
    size = lax.axis_size("dp")
    rows, units = down_weight.shape
    tokens = out_grad.shape[0]
    all_bits = [1 << b for b in range(size.bit_length() - 1)]
    decay = 1.0 - TRAIN_STEP ** (-0.8)
    total_rows = rows * size
    total_units = units * lax.axis_size("mp")
    staged = size == 16 and lax.axis_size("mp") == 2 and rows % 256 == 0 and tokens % 32 == 0 and units % 2560 == 0
    if staged:
        grad, row_sum, terms = staged_products(out_grad, gate_pre, up_pre, down_weight)
        row_moment_new, sums = column_sums(grad, row_sum, row_moment[None, :], decay, total_units)
        sums = group_sum(sums[0], all_bits[:INNER_BITS])
        sums, terms = lax.optimization_barrier((sums, terms))
        own_part, from_low, from_high, last_a, last_b, activated, slope = terms
        arrived = jnp.concatenate([from_low, from_high], axis=0).astype(jnp.float32)
        hidden_grad = own_part + arrived + jnp.concatenate([last_a, last_b], axis=0).astype(jnp.float32)
        sums = group_sum(sums, all_bits[INNER_BITS:])[None, :]
        col_moment_new, ratios = column_step(sums, col_moment[None, :], decay, total_rows)
        ratios = lax.psum(ratios, "mp")
        update, row_mean = final_update(grad, row_moment_new, col_moment_new, ratios, sums, total_rows, total_units)
        row_moment_new, col_moment_new, row_mean = row_moment_new[0], col_moment_new[0], row_mean[0, 0]
    else:
        product, hidden_grad = general_products(
            out_grad, gate_pre, up_pre, down_weight, all_bits[:INNER_BITS], all_bits[INNER_BITS:]
        )
        activated, derivative = gelu_parts(gate_pre.astype(jnp.float32))
        slope = up_pre.astype(jnp.float32) * derivative
        grad = product * (1.0 / math.sqrt(tokens * size))
        powers = grad * grad
        squares = powers + 1e-30
        row_sum = lax.psum(jnp.sum(squares, axis=1), "mp")
        row_moment_new = decay * row_moment + (1.0 - decay) * (row_sum / total_units)
        col_part = jnp.sum(squares, axis=0)
        scaled_part = jnp.sum(powers / row_moment_new[:, None], axis=0)
        sums = jnp.concatenate([col_part, scaled_part, jnp.broadcast_to(jnp.sum(row_moment_new), (128,))])
        sums = group_sum(sums, all_bits)
        col_moment_new = decay * col_moment + (1.0 - decay) * (sums[:units] / total_rows)
        row_mean = sums[2 * units] / total_rows
        ratios = lax.psum(jnp.sum(sums[units : 2 * units] / col_moment_new), "mp")
        clip_norm = jnp.sqrt(row_mean * ratios / (total_rows * total_units))
        row_factor = jnp.sqrt(row_mean / row_moment_new) / jnp.maximum(1.0, clip_norm)
        col_factor = 1.0 / jnp.sqrt(col_moment_new)
        update = grad * row_factor[:, None] * col_factor[None, :]

    gate_grad = (hidden_grad * slope).astype(jnp.bfloat16)
    up_grad = (hidden_grad * activated).astype(jnp.bfloat16)
    return (update, row_moment_new, col_moment_new, row_mean, gate_grad, up_grad)


def solution(mesh):
    in_specs = (P("dp", None), P("dp", "mp"), P("dp", "mp"), P("dp", "mp"), P("dp"), P("mp"))
    out_specs = (P("dp", "mp"), P("dp"), P("mp"), P(), P("dp", "mp"), P("dp", "mp"))
    return jax.shard_map(local, mesh=mesh, in_specs=in_specs, out_specs=out_specs, check_vma=False)
```

```python
import math

import jax
import jax.numpy as jnp
from jax import lax
from jax.experimental import pallas as pl
from jax.experimental.pallas import tpu as pltpu
from jax.sharding import PartitionSpec as P

TRAIN_STEP = 3
INNER_BITS = 2
EAGER = pl.CostEstimate(flops=0, bytes_accessed=0, transcendentals=0)


def gelu_parts(values):
    factor = math.sqrt(2.0 / math.pi)
    inner = factor * (values + 0.044715 * values * values * values)
    tangent = jnp.tanh(inner)
    activated = 0.5 * values * (1.0 + tangent)
    derivative = 0.5 * (1.0 + tangent) + 0.5 * values * (1.0 - tangent * tangent) * factor * (
        1.0 + 3.0 * 0.044715 * values * values
    )
    return (activated, derivative)


def flip(value, bits, axis="dp"):
    size = lax.axis_size(axis)
    return lax.ppermute(value, axis, [(i, i ^ bits) for i in range(size)])


def group_sum(value, bits):
    for at in range(0, len(bits), 2):
        pair = bits[at : at + 2]
        if len(pair) == 2:
            first, second = flip(value, pair[0]), flip(value, pair[1])
            value = (value + first) + (second + flip(value, pair[0] | pair[1]))
        else:
            value = value + flip(value, pair[0])
    return value


def general_products(out_grad, gate_pre, up_pre, down_weight, inner_bits, outer_bits):
    size = lax.axis_size("dp")
    me = lax.axis_index("dp")
    tokens, rows = out_grad.shape[0], down_weight.shape[0]
    inner = 2 ** len(inner_bits)
    activated, _ = gelu_parts(gate_pre.astype(jnp.float32))
    hidden = (activated * up_pre.astype(jnp.float32)).astype(jnp.bfloat16)
    by_block = out_grad.reshape(tokens, size, rows).transpose(1, 0, 2)

    def features_of(k):
        picks = [lax.dynamic_index_in_dim(by_block, me ^ (k * inner + j), 0, keepdims=False) for j in range(inner)]
        return jnp.concatenate(picks, axis=1)

    def gather(block, bits):
        blocks = [block]
        for bit in bits:
            blocks = blocks + [flip(b, bit) for b in blocks]
        return jnp.concatenate(blocks, axis=0)

    def scatter(values, bits):
        for level in reversed(range(len(bits))):
            count = 2**level
            values = [
                values[j] + flip(values[j + count].astype(jnp.bfloat16), bits[level]).astype(jnp.float32)
                for j in range(count)
            ]
        return values[0]

    shares = [features_of(0)] + [flip(features_of(k), k * inner) for k in range(1, size // inner)]
    share = jnp.concatenate(shares, axis=0)
    hidden_all = gather(hidden, outer_bits)
    weight_all = gather(down_weight, inner_bits)
    product = scatter(
        [
            lax.dot_general(
                share[:, j * rows : (j + 1) * rows],
                hidden_all,
                (((0,), (0,)), ((), ())),
                preferred_element_type=jnp.float32,
            )
            for j in range(inner)
        ],
        inner_bits,
    )
    hidden_grad = scatter(
        [jnp.dot(x, weight_all, preferred_element_type=jnp.float32) for x in shares],
        outer_bits,
    )
    return product, hidden_grad


def first_stage(out_grad, gate_pre, up_pre, rows):
    tokens, units = gate_pre.shape
    half = units // 2
    step = 32

    def kernel(source, gate, up, own, right, message1, message2, message3):
        me, core = lax.axis_index("dp"), lax.axis_index("mp")

        def block(k, j):
            return pl.ds(pl.multiple_of((me ^ (4 * k + j)) * rows, rows), rows)

        activated, _ = gelu_parts(gate[...].astype(jnp.float32))
        value = (activated * up[...].astype(jnp.float32)).astype(jnp.bfloat16)
        right[...] = value[:, half:]
        message1[:, :units] = value
        message2[:, :half] = value[:, :half]
        for j in range(4):
            own[:, j * rows : (j + 1) * rows] = source[:, block(0, j)]
        for k, target, base in ((1, message1, units), (2, message2, half), (3, message3, 0)):
            for j in range(2):
                target[:, base + j * rows : base + (j + 1) * rows] = source[:, block(k, 2 * core + j)]

    widths = [4 * rows, units - half, units + 2 * rows, half + 2 * rows, 2 * rows]
    return pl.pallas_call(
        kernel,
        grid=(tokens // step,),
        out_shape=[jax.ShapeDtypeStruct((tokens, width), jnp.bfloat16) for width in widths],
        in_specs=[pl.BlockSpec((step, array.shape[1]), lambda i: (i, 0)) for array in (out_grad, gate_pre, up_pre)],
        out_specs=[pl.BlockSpec((step, width), lambda i: (i, 0)) for width in widths],
        compiler_params=pltpu.CompilerParams(vmem_limit_bytes=56 << 20),
        cost_estimate=EAGER,
    )(out_grad, gate_pre, up_pre)


def cut(sources, parts, shapes):
    def kernel(*refs):
        ins, outs, sems = refs[: len(sources)], refs[len(sources) : -1], refs[-1]
        copies = [
            pltpu.make_async_copy(
                ins[i].at[pl.ds(*rows), pl.ds(*columns)], outs[o].at[:, pl.ds(at, columns[1])], sems.at[n]
            )
            for n, (i, rows, columns, o, at) in enumerate(parts)
        ]
        for copy in copies:
            copy.start()
        for copy in copies:
            copy.wait()

    return pl.pallas_call(
        kernel,
        out_shape=[jax.ShapeDtypeStruct(shape, jnp.bfloat16) for shape in shapes],
        in_specs=[pl.BlockSpec(memory_space=pltpu.HBM)] * len(sources),
        out_specs=[pl.BlockSpec(memory_space=pltpu.HBM)] * len(shapes),
        scratch_shapes=[pltpu.SemaphoreType.DMA((len(parts),))],
        compiler_params=pltpu.CompilerParams(vmem_limit_bytes=1 << 20),
        cost_estimate=EAGER,
    )(*sources)


def assemble(own, mine, theirs, place, rows):
    tokens = own.shape[0]

    def kernel(place, own, mine, theirs, share):
        share[:tokens, :] = own[...]
        for k in range(3):
            here = pl.ds((k + 1) * tokens, tokens)
            half = slice(k * 2 * rows, (k + 1) * 2 * rows)
            a, b = mine[:, half], theirs[:, half]
            share[here, : 2 * rows] = jnp.where(place[1] == 0, a, b)
            share[here, 2 * rows :] = jnp.where(place[1] == 0, b, a)

    vmem = pl.BlockSpec(memory_space=pltpu.VMEM)
    return pl.pallas_call(
        kernel,
        out_shape=jax.ShapeDtypeStruct((4 * tokens, 4 * rows), jnp.bfloat16),
        in_specs=[pl.BlockSpec(memory_space=pltpu.SMEM), vmem, vmem, vmem],
        out_specs=vmem,
        compiler_params=pltpu.CompilerParams(vmem_limit_bytes=8 << 20),
        cost_estimate=EAGER,
    )(place, own, mine, theirs)


def add_tail(parts, arrived):
    rows = parts[0].shape[0]
    widths = [part.shape[1] for part in parts]

    def kernel(*refs):
        out, at = refs[-1], 0
        for part, other, width in zip(refs, refs[len(parts) :], widths):
            out[:, at : at + width] = (part[...] + other[-rows:, :].astype(jnp.float32)).astype(jnp.bfloat16)
            at += width

    vmem = pl.BlockSpec(memory_space=pltpu.VMEM)
    return pl.pallas_call(
        kernel,
        out_shape=jax.ShapeDtypeStruct((rows, sum(widths)), jnp.bfloat16),
        in_specs=[vmem] * (2 * len(parts)),
        out_specs=vmem,
        compiler_params=pltpu.CompilerParams(vmem_limit_bytes=8 << 20),
        cost_estimate=EAGER,
    )(*parts, *arrived)


def flat(column):
    return jnp.broadcast_to(column, (128, 128)).T[0:1, :]


def upright(row):
    return jnp.broadcast_to(row, (128, 128)).T[:, 0:1]


def sum_up(kept, from_low, from_high, last_a, last_b, scale):
    rows = kept[0].shape[0]
    q = rows // 2
    widths = [part.shape[1] for part in kept]
    units = sum(widths)

    def kernel(*refs):
        kept_refs, low_refs, high_refs = refs[:2], refs[2:4], refs[4:6]
        last_refs, grad, row_part = refs[6:8], refs[8], refs[9]
        for h, arrived in enumerate((low_refs, high_refs)):
            for at in range(0, q, 128):
                total = jnp.zeros((128, 1), jnp.float32)
                here = slice(h * q + at, h * q + at + 128)
                column = 0
                for part, other, width in zip(kept_refs, arrived, widths):
                    there = slice(column, column + width)
                    value = part[here, :] + other[at : at + 128, :].astype(jnp.float32)
                    value = (value + last_refs[h][at : at + 128, there].astype(jnp.float32)) * scale
                    grad[here, there] = value
                    total = total + jnp.sum(value * value + 1e-30, axis=1, keepdims=True)
                    column += width
                row_part[:, here] = flat(total)

    vmem = pl.BlockSpec(memory_space=pltpu.VMEM)
    return pl.pallas_call(
        kernel,
        out_shape=[jax.ShapeDtypeStruct((rows, units), jnp.float32), jax.ShapeDtypeStruct((1, rows), jnp.float32)],
        in_specs=[vmem] * 8,
        out_specs=[vmem] * 2,
        compiler_params=pltpu.CompilerParams(vmem_limit_bytes=14 << 20),
        cost_estimate=EAGER,
    )(*kept, *from_low, *from_high, last_a, last_b)


def column_sums(grad, row_sum, row_moment, decay, total_units):
    rows, units = grad.shape

    def kernel(grad, row_sum, row_moment, row_moment_new, sums):
        new = decay * row_moment[...] + (1.0 - decay) * (row_sum[...] / total_units)
        row_moment_new[...] = new
        sums[:, 2 * units :] = jnp.broadcast_to(jnp.sum(new, axis=1, keepdims=True), (1, 128))
        inverse = [1.0 / upright(new[:, at : at + 128]) for at in range(0, rows, 128)]
        for column in range(0, units, 256):
            there = slice(column, column + 256)
            squares, scaled = jnp.zeros((1, 256), jnp.float32), jnp.zeros((1, 256), jnp.float32)
            for n, at in enumerate(range(0, rows, 128)):
                power = grad[at : at + 128, there]
                power = power * power
                squares = squares + jnp.sum(power + 1e-30, axis=0, keepdims=True)
                scaled = scaled + jnp.sum(power * inverse[n], axis=0, keepdims=True)
            sums[:, there] = squares
            sums[:, units + column : units + column + 256] = scaled

    vmem = pl.BlockSpec(memory_space=pltpu.VMEM)
    return pl.pallas_call(
        kernel,
        out_shape=[
            jax.ShapeDtypeStruct((1, rows), jnp.float32),
            jax.ShapeDtypeStruct((1, 2 * units + 128), jnp.float32),
        ],
        in_specs=[vmem] * 3,
        out_specs=[vmem] * 2,
        compiler_params=pltpu.CompilerParams(vmem_limit_bytes=14 << 20),
        cost_estimate=EAGER,
    )(grad, row_sum, row_moment)


def column_step(sums, col_moment, decay, total_rows):
    units = col_moment.shape[1]

    def kernel(sums, col_moment, col_moment_new, terms):
        total = jnp.zeros((1, 128), jnp.float32)
        for at in range(0, units, 128):
            here = slice(at, at + 128)
            new = decay * col_moment[:, here] + (1.0 - decay) * (sums[:, here] / total_rows)
            col_moment_new[:, here] = new
            total = total + sums[:, units + at : units + at + 128] / new
        terms[...] = total

    vmem = pl.BlockSpec(memory_space=pltpu.VMEM)
    return pl.pallas_call(
        kernel,
        out_shape=[jax.ShapeDtypeStruct((1, units), jnp.float32), jax.ShapeDtypeStruct((1, 128), jnp.float32)],
        in_specs=[vmem] * 2,
        out_specs=[vmem] * 2,
        compiler_params=pltpu.CompilerParams(vmem_limit_bytes=4 << 20),
        cost_estimate=EAGER,
    )(sums, col_moment)


def final_update(grad, row_moment_new, col_moment_new, terms, sums, total_rows, total_units):
    rows, units = grad.shape
    tile = units // 2

    def kernel(grad, row_moment_new, col_moment_new, terms, row_total, update, row_mean):
        mean = row_total[...] / total_rows
        row_mean[...] = mean
        square_sum = mean[:, 0:1] * jnp.sum(terms[...], axis=1, keepdims=True)
        clip = jnp.maximum(1.0, jnp.sqrt(square_sum / (total_rows * total_units)))
        col_factor = 1.0 / jnp.sqrt(col_moment_new[...])
        for at in range(0, rows, 128):
            here = slice(at, at + 128)
            row_factor = jnp.sqrt(mean / row_moment_new[:, here]) / clip
            update[here, :] = grad[here, :] * upright(row_factor) * col_factor

    def fixed(width, block=0):
        return pl.BlockSpec((1, width), lambda i: (0, block))

    return pl.pallas_call(
        kernel,
        grid=(units // tile,),
        out_shape=[jax.ShapeDtypeStruct((rows, units), jnp.float32), jax.ShapeDtypeStruct((1, 128), jnp.float32)],
        in_specs=[
            pl.BlockSpec((rows, tile), lambda i: (0, i)),
            fixed(rows),
            pl.BlockSpec((1, tile), lambda i: (0, i)),
            fixed(128),
            fixed(128, 2 * units // 128),
        ],
        out_specs=[pl.BlockSpec((rows, tile), lambda i: (0, i)), fixed(128)],
        compiler_params=pltpu.CompilerParams(vmem_limit_bytes=14 << 20),
        cost_estimate=EAGER,
    )(grad, row_moment_new, col_moment_new, terms, sums)


def products(share, groups, steps):
    pieces = [(piece, group[1]) for group in groups for piece in group[0]]
    bounds = [(output, group[1]) for group in groups for output in group[2]]

    def kernel(*refs):
        share_ref, ins = refs[0], refs[1 : 1 + len(pieces)]
        outs, stacks = refs[1 + len(pieces) : -len(groups)], refs[-len(groups) :]
        n = o = 0
        for (own, _, outputs, over_rows), stack in zip(groups, stacks):
            at = 0
            for piece, _ in own:
                stack[at : at + piece.shape[0], :] = ins[n][...]
                at += piece.shape[0]
                n += 1
            for ranges, kind in outputs:
                if over_rows:
                    side = jnp.concatenate([share_ref[:, begin:end] for begin, end in ranges], axis=1)
                    value = lax.dot_general(
                        side, stack[...], (((0,), (0,)), ((), ())), preferred_element_type=jnp.float32
                    )
                else:
                    side = jnp.concatenate([share_ref[begin:end, :] for begin, end in ranges], axis=0)
                    value = jnp.dot(side, stack[...], preferred_element_type=jnp.float32)
                outs[o][...] = value.astype(kind)
                o += 1

    def height(ranges):
        return sum(end - begin for begin, end in ranges)

    return pl.pallas_call(
        kernel,
        grid=(steps,),
        out_shape=[jax.ShapeDtypeStruct((height(ranges), columns), kind) for (ranges, kind), columns in bounds],
        in_specs=[pl.BlockSpec(share.shape, lambda i: (0, 0))]
        + [
            pl.BlockSpec((piece.shape[0], columns // steps), lambda i, skip=first * steps // columns: (0, i + skip))
            for (piece, first), columns in pieces
        ],
        out_specs=[pl.BlockSpec((height(ranges), columns // steps), lambda i: (0, i)) for (ranges, _), columns in bounds],
        scratch_shapes=[
            pltpu.VMEM((sum(piece.shape[0] for piece, _ in group[0]), group[1] // steps), jnp.bfloat16) for group in groups
        ],
        compiler_params=pltpu.CompilerParams(vmem_limit_bytes=14 << 20),
        cost_estimate=EAGER,
    )(share, *[piece for (piece, _), _ in pieces])


def staged_products(out_grad, gate_pre, up_pre, down_weight):
    x_bit, y_bit, z_bit, w_bit = 1, 2, 4, 8
    me, core = lax.axis_index("dp"), lax.axis_index("mp")
    tokens, units = gate_pre.shape
    rows = down_weight.shape[0]
    q, t = rows // 2, tokens // 2
    steps = 5
    split = units // 2
    barrier = lax.optimization_barrier
    place = jnp.stack([me, core]).astype(jnp.int32)
    own, right, message1, message2, message3 = first_stage(out_grad, gate_pre, up_pre, rows)

    every, whole = (0, tokens), (0, units)
    near, left2, message3 = flip(message1, z_bit), flip(message2, w_bit), flip(message3, z_bit | w_bit)
    weight1, weight2 = flip(down_weight, x_bit), flip(down_weight, y_bit)
    to_y, to_x = cut([weight1, weight2], [(0, (0, q), whole, 0, 0), (1, (q, q), whole, 1, 0)], [(q, units)] * 2)
    weight3a, weight3b = flip(to_y, y_bit), flip(to_x, x_bit)
    near, left2, message3, right = barrier((near, left2, message3, right))
    to_z, mine = cut(
        [near, left2, message3],
        [
            (1, every, (0, split), 0, 0),
            (0, every, (units, 2 * rows), 1, 0),
            (1, every, (split, 2 * rows), 1, 2 * rows),
            (2, every, (0, 2 * rows), 1, 4 * rows),
        ],
        [(tokens, split), (tokens, 6 * rows)],
    )
    left3 = flip(to_z, z_bit)
    right2 = flip(right, w_bit)
    theirs = flip(mine, 1, "mp")
    share = assemble(own, mine, theirs, place, rows)

    def low_sent(size):
        return [(2 * size, 3 * size), (6 * size, 7 * size)]

    def high_sent(size):
        return [(5 * size, 6 * size), (7 * size, 8 * size)]

    def sent(size):
        return [(low_sent(size), jnp.bfloat16), (high_sent(size), jnp.bfloat16)]

    def kept(size):
        ranges = [(0, 2 * size)], [(4 * size, 5 * size)], [(3 * size, 4 * size)]
        return [(r, jnp.float32) for r in ranges]

    left3, right2, share = barrier((left3, right2, share))
    right3 = flip(right2, z_bit)
    lefts = [(message1, 0), (near, 0), (left2, 0), (left3, 0)]
    left_to_x, left_to_y = products(share, [(lefts, split, sent(q), True)], steps)
    left_from_x, left_from_y = flip(left_to_x, x_bit), flip(left_to_y, y_bit)

    share, _ = barrier((share, left_to_x))
    weights = [(piece, 0) for piece in (down_weight, weight1, weight2, weight3a, weight3b)]
    to_w, to_z = products(
        share, [(weights, units, [(high_sent(t), jnp.bfloat16), (low_sent(t), jnp.bfloat16)], False)], steps
    )
    right3, share, to_w, to_z = barrier((right3, share, to_w, to_z))
    from_w, from_z = flip(to_w, w_bit), flip(to_z, z_bit)
    rights = [(right, 0), (near, split), (right2, 0), (right3, 0)]
    right_to_x, right_to_y = products(share, [(rights, units - split, sent(q), True)], steps)
    right_from_x, right_from_y = flip(right_to_x, x_bit), flip(right_to_y, y_bit)
    share, left_from_x, left_from_y, _ = barrier((share, left_from_x, left_from_y, right_to_x))
    left_parts = products(share, [(lefts, split, kept(q), True)], steps)
    parts = products(share, [(rights, units - split, kept(q), True), (weights, units, kept(t), False)], steps)

    grad_a = flip(add_tail([left_parts[1], parts[1]], [left_from_x, right_from_x]), y_bit)
    grad_b = flip(add_tail([left_parts[2], parts[2]], [left_from_y, right_from_y]), x_bit)
    to_w, to_z = add_tail([parts[4]], [from_z]), add_tail([parts[5]], [from_w])
    last_a, last_b = flip(to_w, w_bit), flip(to_z, z_bit)
    grad_a, grad_b, _, _ = barrier((grad_a, grad_b, to_w, to_z))
    grad, row_part = sum_up(
        [left_parts[0], parts[0]],
        [left_from_x, right_from_x],
        [left_from_y, right_from_y],
        grad_a,
        grad_b,
        1.0 / math.sqrt(tokens * lax.axis_size("dp")),
    )

    row_sum = lax.psum(row_part, "mp")
    return grad, row_sum, (parts[3], from_z[:t], from_w[:t], last_a, last_b)


def local(out_grad, gate_pre, up_pre, down_weight, row_moment, col_moment):
    size = lax.axis_size("dp")
    rows, units = down_weight.shape
    tokens = out_grad.shape[0]
    all_bits = [1 << b for b in range(size.bit_length() - 1)]
    decay = 1.0 - TRAIN_STEP ** (-0.8)
    total_rows = rows * size
    total_units = units * lax.axis_size("mp")
    staged = size == 16 and lax.axis_size("mp") == 2 and rows % 256 == 0 and tokens % 32 == 0 and units % 2560 == 0
    if staged:
        grad, row_sum, terms = staged_products(out_grad, gate_pre, up_pre, down_weight)
        row_moment_new, sums = column_sums(grad, row_sum, row_moment[None, :], decay, total_units)
        sums = group_sum(sums[0], all_bits[:INNER_BITS])
        sums, terms = lax.optimization_barrier((sums, terms))
        own_part, from_low, from_high, last_a, last_b = terms
        arrived = jnp.concatenate([from_low, from_high], axis=0).astype(jnp.float32)
        hidden_grad = own_part + arrived + jnp.concatenate([last_a, last_b], axis=0).astype(jnp.float32)
        sums = group_sum(sums, all_bits[INNER_BITS:])[None, :]
        col_moment_new, ratios = column_step(sums, col_moment[None, :], decay, total_rows)
        ratios = lax.psum(ratios, "mp")
        update, row_mean = final_update(grad, row_moment_new, col_moment_new, ratios, sums, total_rows, total_units)
        row_moment_new, col_moment_new, row_mean = row_moment_new[0], col_moment_new[0], row_mean[0, 0]
    else:
        product, hidden_grad = general_products(
            out_grad, gate_pre, up_pre, down_weight, all_bits[:INNER_BITS], all_bits[INNER_BITS:]
        )
        grad = product * (1.0 / math.sqrt(tokens * size))
        powers = grad * grad
        squares = powers + 1e-30
        row_sum = lax.psum(jnp.sum(squares, axis=1), "mp")
        row_moment_new = decay * row_moment + (1.0 - decay) * (row_sum / total_units)
        col_part = jnp.sum(squares, axis=0)
        scaled_part = jnp.sum(powers / row_moment_new[:, None], axis=0)
        sums = jnp.concatenate([col_part, scaled_part, jnp.broadcast_to(jnp.sum(row_moment_new), (128,))])
        sums = group_sum(sums, all_bits)
        col_moment_new = decay * col_moment + (1.0 - decay) * (sums[:units] / total_rows)
        row_mean = sums[2 * units] / total_rows
        ratios = lax.psum(jnp.sum(sums[units : 2 * units] / col_moment_new), "mp")
        clip_norm = jnp.sqrt(row_mean * ratios / (total_rows * total_units))
        row_factor = jnp.sqrt(row_mean / row_moment_new) / jnp.maximum(1.0, clip_norm)
        col_factor = 1.0 / jnp.sqrt(col_moment_new)
        update = grad * row_factor[:, None] * col_factor[None, :]

    activated, derivative = gelu_parts(gate_pre.astype(jnp.float32))
    gate_grad = (hidden_grad * up_pre.astype(jnp.float32) * derivative).astype(jnp.bfloat16)
    up_grad = (hidden_grad * activated).astype(jnp.bfloat16)
    return (update, row_moment_new, col_moment_new, row_mean, gate_grad, up_grad)


def solution(mesh):
    in_specs = (P("dp", None), P("dp", "mp"), P("dp", "mp"), P("dp", "mp"), P("dp"), P("mp"))
    out_specs = (P("dp", "mp"), P("dp"), P("mp"), P(), P("dp", "mp"), P("dp", "mp"))
    return jax.shard_map(local, mesh=mesh, in_specs=in_specs, out_specs=out_specs, check_vma=False)
```

```python
import math

import jax
import jax.numpy as jnp
from jax import lax
from jax.experimental import pallas as pl
from jax.experimental.pallas import tpu as pltpu
from jax.sharding import PartitionSpec as P

TRAIN_STEP = 3
INNER_BITS = 2
EAGER = pl.CostEstimate(flops=0, bytes_accessed=0, transcendentals=0)


def gelu_parts(values):
    factor = math.sqrt(2.0 / math.pi)
    inner = factor * (values + 0.044715 * values * values * values)
    tangent = jnp.tanh(inner)
    activated = 0.5 * values * (1.0 + tangent)
    derivative = 0.5 * (1.0 + tangent) + 0.5 * values * (1.0 - tangent * tangent) * factor * (
        1.0 + 3.0 * 0.044715 * values * values
    )
    return (activated, derivative)


def flip(value, bits, axis="dp"):
    size = lax.axis_size(axis)
    return lax.ppermute(value, axis, [(i, i ^ bits) for i in range(size)])


def group_sum(value, bits):
    for at in range(0, len(bits), 2):
        pair = bits[at : at + 2]
        if len(pair) == 2:
            first, second = flip(value, pair[0]), flip(value, pair[1])
            value = (value + first) + (second + flip(value, pair[0] | pair[1]))
        else:
            value = value + flip(value, pair[0])
    return value


def general_products(out_grad, gate_pre, up_pre, down_weight, inner_bits, outer_bits):
    size = lax.axis_size("dp")
    me = lax.axis_index("dp")
    tokens, rows = out_grad.shape[0], down_weight.shape[0]
    inner = 2 ** len(inner_bits)
    activated, _ = gelu_parts(gate_pre.astype(jnp.float32))
    hidden = (activated * up_pre.astype(jnp.float32)).astype(jnp.bfloat16)
    by_block = out_grad.reshape(tokens, size, rows).transpose(1, 0, 2)

    def features_of(k):
        picks = [lax.dynamic_index_in_dim(by_block, me ^ (k * inner + j), 0, keepdims=False) for j in range(inner)]
        return jnp.concatenate(picks, axis=1)

    def gather(block, bits):
        blocks = [block]
        for bit in bits:
            blocks = blocks + [flip(b, bit) for b in blocks]
        return jnp.concatenate(blocks, axis=0)

    def scatter(values, bits):
        for level in reversed(range(len(bits))):
            count = 2**level
            values = [
                values[j] + flip(values[j + count].astype(jnp.bfloat16), bits[level]).astype(jnp.float32)
                for j in range(count)
            ]
        return values[0]

    shares = [features_of(0)] + [flip(features_of(k), k * inner) for k in range(1, size // inner)]
    share = jnp.concatenate(shares, axis=0)
    hidden_all = gather(hidden, outer_bits)
    weight_all = gather(down_weight, inner_bits)
    product = scatter(
        [
            lax.dot_general(
                share[:, j * rows : (j + 1) * rows],
                hidden_all,
                (((0,), (0,)), ((), ())),
                preferred_element_type=jnp.float32,
            )
            for j in range(inner)
        ],
        inner_bits,
    )
    hidden_grad = scatter(
        [jnp.dot(x, weight_all, preferred_element_type=jnp.float32) for x in shares],
        outer_bits,
    )
    return product, hidden_grad


def first_stage(out_grad, gate_pre, up_pre, rows):
    tokens, units = gate_pre.shape
    half = units // 2
    step = 32

    def kernel(source, gate, up, own, right, message1, message2, message3):
        me, core = lax.axis_index("dp"), lax.axis_index("mp")

        def block(k, j):
            return pl.ds(pl.multiple_of((me ^ (4 * k + j)) * rows, rows), rows)

        activated, _ = gelu_parts(gate[...].astype(jnp.float32))
        value = (activated * up[...].astype(jnp.float32)).astype(jnp.bfloat16)
        right[...] = value[:, half:]
        message1[:, :half] = value[:, :half]
        message2[:, :half] = value[:, :half]
        for j in range(4):
            own[:, j * rows : (j + 1) * rows] = source[:, block(0, j)]
        for k, target, base in ((1, message1, half), (2, message2, half), (3, message3, 0)):
            for j in range(2):
                target[:, base + j * rows : base + (j + 1) * rows] = source[:, block(k, 2 * core + j)]

    widths = [4 * rows, units - half, half + 2 * rows, half + 2 * rows, 2 * rows]
    return pl.pallas_call(
        kernel,
        grid=(tokens // step,),
        out_shape=[jax.ShapeDtypeStruct((tokens, width), jnp.bfloat16) for width in widths],
        in_specs=[pl.BlockSpec((step, array.shape[1]), lambda i: (i, 0)) for array in (out_grad, gate_pre, up_pre)],
        out_specs=[pl.BlockSpec((step, width), lambda i: (i, 0)) for width in widths],
        compiler_params=pltpu.CompilerParams(vmem_limit_bytes=56 << 20),
        cost_estimate=EAGER,
    )(out_grad, gate_pre, up_pre)


def cut(sources, parts, shapes):
    def kernel(*refs):
        ins, outs, sems = refs[: len(sources)], refs[len(sources) : -1], refs[-1]
        copies = [
            pltpu.make_async_copy(
                ins[i].at[pl.ds(*rows), pl.ds(*columns)], outs[o].at[:, pl.ds(at, columns[1])], sems.at[n]
            )
            for n, (i, rows, columns, o, at) in enumerate(parts)
        ]
        for copy in copies:
            copy.start()
        for copy in copies:
            copy.wait()

    return pl.pallas_call(
        kernel,
        out_shape=[jax.ShapeDtypeStruct(shape, jnp.bfloat16) for shape in shapes],
        in_specs=[pl.BlockSpec(memory_space=pltpu.HBM)] * len(sources),
        out_specs=[pl.BlockSpec(memory_space=pltpu.HBM)] * len(shapes),
        scratch_shapes=[pltpu.SemaphoreType.DMA((len(parts),))],
        compiler_params=pltpu.CompilerParams(vmem_limit_bytes=1 << 20),
        cost_estimate=EAGER,
    )(*sources)


def assemble(own, mine, theirs, place, rows):
    tokens = own.shape[0]

    def kernel(place, own, mine, theirs, share):
        share[:tokens, :] = own[...]
        for k in range(3):
            here = pl.ds((k + 1) * tokens, tokens)
            half = slice(k * 2 * rows, (k + 1) * 2 * rows)
            a, b = mine[:, half], theirs[:, half]
            share[here, : 2 * rows] = jnp.where(place[1] == 0, a, b)
            share[here, 2 * rows :] = jnp.where(place[1] == 0, b, a)

    vmem = pl.BlockSpec(memory_space=pltpu.VMEM)
    return pl.pallas_call(
        kernel,
        out_shape=jax.ShapeDtypeStruct((4 * tokens, 4 * rows), jnp.bfloat16),
        in_specs=[pl.BlockSpec(memory_space=pltpu.SMEM), vmem, vmem, vmem],
        out_specs=vmem,
        compiler_params=pltpu.CompilerParams(vmem_limit_bytes=4 << 20),
        cost_estimate=EAGER,
    )(place, own, mine, theirs)


def add_tail(parts, arrived):
    rows = parts[0].shape[0]
    widths = [part.shape[1] for part in parts]

    def kernel(*refs):
        out, at = refs[-1], 0
        for part, other, width in zip(refs, refs[len(parts) :], widths):
            out[:, at : at + width] = (part[...] + other[-rows:, :].astype(jnp.float32)).astype(jnp.bfloat16)
            at += width

    vmem = pl.BlockSpec(memory_space=pltpu.VMEM)
    return pl.pallas_call(
        kernel,
        out_shape=jax.ShapeDtypeStruct((rows, sum(widths)), jnp.bfloat16),
        in_specs=[vmem] * (2 * len(parts)),
        out_specs=vmem,
        compiler_params=pltpu.CompilerParams(vmem_limit_bytes=4 << 20),
        cost_estimate=EAGER,
    )(*parts, *arrived)


def flat(column):
    return jnp.broadcast_to(column, (128, 128)).T[0:1, :]


def upright(row):
    return jnp.broadcast_to(row, (128, 128)).T[:, 0:1]


def sum_up(kept, from_low, from_high, last_a, last_b, scale):
    rows = kept[0].shape[0]
    q = rows // 2
    widths = [part.shape[1] for part in kept]
    units = sum(widths)

    def kernel(*refs):
        kept_refs, low_refs, high_refs = refs[:2], refs[2:4], refs[4:6]
        last_refs, grad, row_part = refs[6:8], refs[8], refs[9]
        for h, arrived in enumerate((low_refs, high_refs)):
            for at in range(0, q, 128):
                total = jnp.zeros((128, 1), jnp.float32)
                here = slice(h * q + at, h * q + at + 128)
                column = 0
                for part, other, width in zip(kept_refs, arrived, widths):
                    there = slice(column, column + width)
                    value = part[here, :] + other[at : at + 128, :].astype(jnp.float32)
                    value = (value + last_refs[h][at : at + 128, there].astype(jnp.float32)) * scale
                    grad[here, there] = value
                    total = total + jnp.sum(value * value + 1e-30, axis=1, keepdims=True)
                    column += width
                row_part[:, here] = flat(total)

    vmem = pl.BlockSpec(memory_space=pltpu.VMEM)
    return pl.pallas_call(
        kernel,
        out_shape=[jax.ShapeDtypeStruct((rows, units), jnp.float32), jax.ShapeDtypeStruct((1, rows), jnp.float32)],
        in_specs=[vmem] * 8,
        out_specs=[vmem] * 2,
        compiler_params=pltpu.CompilerParams(vmem_limit_bytes=10 << 20),
        cost_estimate=EAGER,
    )(*kept, *from_low, *from_high, last_a, last_b)


def column_sums(grad, row_sum, row_moment, decay, total_units):
    rows, units = grad.shape

    def kernel(grad, row_sum, row_moment, row_moment_new, sums):
        new = decay * row_moment[...] + (1.0 - decay) * (row_sum[...] / total_units)
        row_moment_new[...] = new
        sums[:, 2 * units :] = jnp.broadcast_to(jnp.sum(new, axis=1, keepdims=True), (1, 128))
        inverse = [1.0 / upright(new[:, at : at + 128]) for at in range(0, rows, 128)]
        for column in range(0, units, 256):
            there = slice(column, column + 256)
            squares, scaled = jnp.zeros((1, 256), jnp.float32), jnp.zeros((1, 256), jnp.float32)
            for n, at in enumerate(range(0, rows, 128)):
                power = grad[at : at + 128, there]
                power = power * power
                squares = squares + jnp.sum(power + 1e-30, axis=0, keepdims=True)
                scaled = scaled + jnp.sum(power * inverse[n], axis=0, keepdims=True)
            sums[:, there] = squares
            sums[:, units + column : units + column + 256] = scaled

    vmem = pl.BlockSpec(memory_space=pltpu.VMEM)
    return pl.pallas_call(
        kernel,
        out_shape=[
            jax.ShapeDtypeStruct((1, rows), jnp.float32),
            jax.ShapeDtypeStruct((1, 2 * units + 128), jnp.float32),
        ],
        in_specs=[vmem] * 3,
        out_specs=[vmem] * 2,
        compiler_params=pltpu.CompilerParams(vmem_limit_bytes=5 << 20),
        cost_estimate=EAGER,
    )(grad, row_sum, row_moment)


def column_step(sums, col_moment, decay, total_rows):
    units = col_moment.shape[1]

    def kernel(sums, col_moment, col_moment_new, terms):
        total = jnp.zeros((1, 128), jnp.float32)
        for at in range(0, units, 128):
            here = slice(at, at + 128)
            new = decay * col_moment[:, here] + (1.0 - decay) * (sums[:, here] / total_rows)
            col_moment_new[:, here] = new
            total = total + sums[:, units + at : units + at + 128] / new
        terms[...] = total

    vmem = pl.BlockSpec(memory_space=pltpu.VMEM)
    return pl.pallas_call(
        kernel,
        out_shape=[jax.ShapeDtypeStruct((1, units), jnp.float32), jax.ShapeDtypeStruct((1, 128), jnp.float32)],
        in_specs=[vmem] * 2,
        out_specs=[vmem] * 2,
        compiler_params=pltpu.CompilerParams(vmem_limit_bytes=2 << 20),
        cost_estimate=EAGER,
    )(sums, col_moment)


def final_update(grad, row_moment_new, col_moment_new, terms, sums, total_rows, total_units):
    rows, units = grad.shape
    tile = units // 2

    def kernel(grad, row_moment_new, col_moment_new, terms, row_total, update, row_mean):
        mean = row_total[...] / total_rows
        row_mean[...] = mean
        square_sum = mean[:, 0:1] * jnp.sum(terms[...], axis=1, keepdims=True)
        clip = jnp.maximum(1.0, jnp.sqrt(square_sum / (total_rows * total_units)))
        col_factor = 1.0 / jnp.sqrt(col_moment_new[...])
        for at in range(0, rows, 128):
            here = slice(at, at + 128)
            row_factor = jnp.sqrt(mean / row_moment_new[:, here]) / clip
            update[here, :] = grad[here, :] * upright(row_factor) * col_factor

    def fixed(width, block=0):
        return pl.BlockSpec((1, width), lambda i: (0, block))

    return pl.pallas_call(
        kernel,
        grid=(units // tile,),
        out_shape=[jax.ShapeDtypeStruct((rows, units), jnp.float32), jax.ShapeDtypeStruct((1, 128), jnp.float32)],
        in_specs=[
            pl.BlockSpec((rows, tile), lambda i: (0, i)),
            fixed(rows),
            pl.BlockSpec((1, tile), lambda i: (0, i)),
            fixed(128),
            fixed(128, 2 * units // 128),
        ],
        out_specs=[pl.BlockSpec((rows, tile), lambda i: (0, i)), fixed(128)],
        compiler_params=pltpu.CompilerParams(vmem_limit_bytes=7 << 20),
        cost_estimate=EAGER,
    )(grad, row_moment_new, col_moment_new, terms, sums)


def products(share, groups, steps):
    pieces = [(piece, group[1]) for group in groups for piece in group[0]]
    bounds = [(output, group[1]) for group in groups for output in group[2]]

    def kernel(*refs):
        share_ref, ins = refs[0], refs[1 : 1 + len(pieces)]
        outs, stacks = refs[1 + len(pieces) : -len(groups)], refs[-len(groups) :]
        n = o = 0
        for (own, _, outputs, over_rows), stack in zip(groups, stacks):
            at = 0
            for piece, _ in own:
                stack[at : at + piece.shape[0], :] = ins[n][...]
                at += piece.shape[0]
                n += 1
            for ranges, kind in outputs:
                if over_rows:
                    side = jnp.concatenate([share_ref[:, begin:end] for begin, end in ranges], axis=1)
                    value = lax.dot_general(
                        side, stack[...], (((0,), (0,)), ((), ())), preferred_element_type=jnp.float32
                    )
                else:
                    side = jnp.concatenate([share_ref[begin:end, :] for begin, end in ranges], axis=0)
                    value = jnp.dot(side, stack[...], preferred_element_type=jnp.float32)
                outs[o][...] = value.astype(kind)
                o += 1

    def height(ranges):
        return sum(end - begin for begin, end in ranges)

    return pl.pallas_call(
        kernel,
        grid=(steps,),
        out_shape=[jax.ShapeDtypeStruct((height(ranges), columns), kind) for (ranges, kind), columns in bounds],
        in_specs=[pl.BlockSpec(share.shape, lambda i: (0, 0))]
        + [
            pl.BlockSpec((piece.shape[0], columns // steps), lambda i, skip=first * steps // columns: (0, i + skip))
            for (piece, first), columns in pieces
        ],
        out_specs=[pl.BlockSpec((height(ranges), columns // steps), lambda i: (0, i)) for (ranges, _), columns in bounds],
        scratch_shapes=[
            pltpu.VMEM((sum(piece.shape[0] for piece, _ in group[0]), group[1] // steps), jnp.bfloat16) for group in groups
        ],
        compiler_params=pltpu.CompilerParams(vmem_limit_bytes=9 << 20),
        cost_estimate=EAGER,
    )(share, *[piece for (piece, _), _ in pieces])


def staged_products(out_grad, gate_pre, up_pre, down_weight):
    x_bit, y_bit, z_bit, w_bit = 1, 2, 4, 8
    me, core = lax.axis_index("dp"), lax.axis_index("mp")
    tokens, units = gate_pre.shape
    rows = down_weight.shape[0]
    q, t = rows // 2, tokens // 2
    steps = 5
    split = units // 2
    barrier = lax.optimization_barrier
    place = jnp.stack([me, core]).astype(jnp.int32)
    own, right, message1, message2, message3 = first_stage(out_grad, gate_pre, up_pre, rows)

    extra, every, whole = (split, 2 * rows), (0, tokens), (0, units)
    left1, left2, message3 = flip(message1, z_bit), flip(message2, w_bit), flip(message3, z_bit | w_bit)
    weight1, weight2 = flip(down_weight, x_bit), flip(down_weight, y_bit)
    to_y, to_x = cut([weight1, weight2], [(0, (0, q), whole, 0, 0), (1, (q, q), whole, 1, 0)], [(q, units)] * 2)
    weight3a, weight3b = flip(to_y, y_bit), flip(to_x, x_bit)
    left1, left2, message3, right = barrier((left1, left2, message3, right))
    to_z, mine = cut(
        [left1, left2, message3, right],
        [
            (1, every, (0, split), 0, 0),
            (3, every, (0, units - split), 0, split),
            (0, every, extra, 1, 0),
            (1, every, extra, 1, 2 * rows),
            (2, every, (0, 2 * rows), 1, 4 * rows),
        ],
        [(tokens, units), (tokens, 6 * rows)],
    )
    from_near = flip(to_z, z_bit)
    right2 = flip(right, w_bit)
    theirs = flip(mine, 1, "mp")
    share = assemble(own, mine, theirs, place, rows)

    def low_sent(size):
        return [(2 * size, 3 * size), (6 * size, 7 * size)]

    def high_sent(size):
        return [(5 * size, 6 * size), (7 * size, 8 * size)]

    def sent(size):
        return [(low_sent(size), jnp.bfloat16), (high_sent(size), jnp.bfloat16)]

    def kept(size):
        ranges = [(0, 2 * size)], [(4 * size, 5 * size)], [(3 * size, 4 * size)]
        return [(r, jnp.float32) for r in ranges]

    from_near, right2, share = barrier((from_near, right2, share))
    right3 = flip(right2, z_bit)
    lefts = [(message1, 0), (left1, 0), (left2, 0), (from_near, 0)]
    left_to_x, left_to_y = products(share, [(lefts, split, sent(q), True)], steps)
    left_from_x, left_from_y = flip(left_to_x, x_bit), flip(left_to_y, y_bit)

    share, _ = barrier((share, left_to_x))
    weights = [(piece, 0) for piece in (down_weight, weight1, weight2, weight3a, weight3b)]
    to_w, to_z = products(
        share, [(weights, units, [(high_sent(t), jnp.bfloat16), (low_sent(t), jnp.bfloat16)], False)], steps
    )
    right3, share, to_w, to_z = barrier((right3, share, to_w, to_z))
    from_w, from_z = flip(to_w, w_bit), flip(to_z, z_bit)
    rights = [(right, 0), (from_near, split), (right2, 0), (right3, 0)]
    right_to_x, right_to_y = products(share, [(rights, units - split, sent(q), True)], steps)
    right_from_x, right_from_y = flip(right_to_x, x_bit), flip(right_to_y, y_bit)
    share, left_from_x, left_from_y, _ = barrier((share, left_from_x, left_from_y, right_to_x))
    left_parts = products(share, [(lefts, split, kept(q), True)], steps)
    parts = products(share, [(rights, units - split, kept(q), True), (weights, units, kept(t), False)], steps)

    grad_a = flip(add_tail([left_parts[1], parts[1]], [left_from_x, right_from_x]), y_bit)
    grad_b = flip(add_tail([left_parts[2], parts[2]], [left_from_y, right_from_y]), x_bit)
    to_w, to_z = add_tail([parts[4]], [from_z]), add_tail([parts[5]], [from_w])
    last_a, last_b = flip(to_w, w_bit), flip(to_z, z_bit)
    grad_a, grad_b, _, _ = barrier((grad_a, grad_b, to_w, to_z))
    grad, row_part = sum_up(
        [left_parts[0], parts[0]],
        [left_from_x, right_from_x],
        [left_from_y, right_from_y],
        grad_a,
        grad_b,
        1.0 / math.sqrt(tokens * lax.axis_size("dp")),
    )

    row_sum = lax.psum(row_part, "mp")
    return grad, row_sum, (parts[3], from_z[:t], from_w[:t], last_a, last_b)


def local(out_grad, gate_pre, up_pre, down_weight, row_moment, col_moment):
    size = lax.axis_size("dp")
    rows, units = down_weight.shape
    tokens = out_grad.shape[0]
    all_bits = [1 << b for b in range(size.bit_length() - 1)]
    decay = 1.0 - TRAIN_STEP ** (-0.8)
    total_rows = rows * size
    total_units = units * lax.axis_size("mp")
    staged = size == 16 and lax.axis_size("mp") == 2 and rows % 256 == 0 and tokens % 32 == 0 and units % 2560 == 0
    if staged:
        grad, row_sum, terms = staged_products(out_grad, gate_pre, up_pre, down_weight)
        row_moment_new, sums = column_sums(grad, row_sum, row_moment[None, :], decay, total_units)
        sums = group_sum(sums[0], all_bits[:INNER_BITS])
        sums, terms = lax.optimization_barrier((sums, terms))
        own_part, from_low, from_high, last_a, last_b = terms
        arrived = jnp.concatenate([from_low, from_high], axis=0).astype(jnp.float32)
        hidden_grad = own_part + arrived + jnp.concatenate([last_a, last_b], axis=0).astype(jnp.float32)
        sums = group_sum(sums, all_bits[INNER_BITS:])[None, :]
        col_moment_new, ratios = column_step(sums, col_moment[None, :], decay, total_rows)
        ratios = lax.psum(ratios, "mp")
        update, row_mean = final_update(grad, row_moment_new, col_moment_new, ratios, sums, total_rows, total_units)
        row_moment_new, col_moment_new, row_mean = row_moment_new[0], col_moment_new[0], row_mean[0, 0]
    else:
        product, hidden_grad = general_products(
            out_grad, gate_pre, up_pre, down_weight, all_bits[:INNER_BITS], all_bits[INNER_BITS:]
        )
        grad = product * (1.0 / math.sqrt(tokens * size))
        powers = grad * grad
        squares = powers + 1e-30
        row_sum = lax.psum(jnp.sum(squares, axis=1), "mp")
        row_moment_new = decay * row_moment + (1.0 - decay) * (row_sum / total_units)
        col_part = jnp.sum(squares, axis=0)
        scaled_part = jnp.sum(powers / row_moment_new[:, None], axis=0)
        sums = jnp.concatenate([col_part, scaled_part, jnp.broadcast_to(jnp.sum(row_moment_new), (128,))])
        sums = group_sum(sums, all_bits)
        col_moment_new = decay * col_moment + (1.0 - decay) * (sums[:units] / total_rows)
        row_mean = sums[2 * units] / total_rows
        ratios = lax.psum(jnp.sum(sums[units : 2 * units] / col_moment_new), "mp")
        clip_norm = jnp.sqrt(row_mean * ratios / (total_rows * total_units))
        row_factor = jnp.sqrt(row_mean / row_moment_new) / jnp.maximum(1.0, clip_norm)
        col_factor = 1.0 / jnp.sqrt(col_moment_new)
        update = grad * row_factor[:, None] * col_factor[None, :]

    activated, derivative = gelu_parts(gate_pre.astype(jnp.float32))
    gate_grad = (hidden_grad * up_pre.astype(jnp.float32) * derivative).astype(jnp.bfloat16)
    up_grad = (hidden_grad * activated).astype(jnp.bfloat16)
    return (update, row_moment_new, col_moment_new, row_mean, gate_grad, up_grad)


def solution(mesh):
    in_specs = (P("dp", None), P("dp", "mp"), P("dp", "mp"), P("dp", "mp"), P("dp"), P("mp"))
    out_specs = (P("dp", "mp"), P("dp"), P("mp"), P(), P("dp", "mp"), P("dp", "mp"))
    return jax.shard_map(local, mesh=mesh, in_specs=in_specs, out_specs=out_specs, check_vma=False)
```

```python
import math

import jax
import jax.numpy as jnp
from jax import lax
from jax.experimental import pallas as pl
from jax.experimental.pallas import tpu as pltpu
from jax.sharding import PartitionSpec as P

TRAIN_STEP = 3
INNER_BITS = 2
EAGER = pl.CostEstimate(flops=0, bytes_accessed=0, transcendentals=0)


def gelu_parts(values):
    factor = math.sqrt(2.0 / math.pi)
    inner = factor * (values + 0.044715 * values * values * values)
    tangent = jnp.tanh(inner)
    activated = 0.5 * values * (1.0 + tangent)
    derivative = 0.5 * (1.0 + tangent) + 0.5 * values * (1.0 - tangent * tangent) * factor * (
        1.0 + 3.0 * 0.044715 * values * values
    )
    return (activated, derivative)


def flip(value, bits, axis="dp"):
    size = lax.axis_size(axis)
    return lax.ppermute(value, axis, [(i, i ^ bits) for i in range(size)])


def group_sum(value, bits):
    for at in range(0, len(bits), 2):
        pair = bits[at : at + 2]
        if len(pair) == 2:
            first, second = flip(value, pair[0]), flip(value, pair[1])
            value = (value + first) + (second + flip(value, pair[0] | pair[1]))
        else:
            value = value + flip(value, pair[0])
    return value


def general_products(out_grad, gate_pre, up_pre, down_weight, inner_bits, outer_bits):
    size = lax.axis_size("dp")
    me = lax.axis_index("dp")
    tokens, rows = out_grad.shape[0], down_weight.shape[0]
    inner = 2 ** len(inner_bits)
    activated, _ = gelu_parts(gate_pre.astype(jnp.float32))
    hidden = (activated * up_pre.astype(jnp.float32)).astype(jnp.bfloat16)
    by_block = out_grad.reshape(tokens, size, rows).transpose(1, 0, 2)

    def features_of(k):
        picks = [lax.dynamic_index_in_dim(by_block, me ^ (k * inner + j), 0, keepdims=False) for j in range(inner)]
        return jnp.concatenate(picks, axis=1)

    def gather(block, bits):
        blocks = [block]
        for bit in bits:
            blocks = blocks + [flip(b, bit) for b in blocks]
        return jnp.concatenate(blocks, axis=0)

    def scatter(values, bits):
        for level in reversed(range(len(bits))):
            count = 2**level
            values = [
                values[j] + flip(values[j + count].astype(jnp.bfloat16), bits[level]).astype(jnp.float32)
                for j in range(count)
            ]
        return values[0]

    shares = [features_of(0)] + [flip(features_of(k), k * inner) for k in range(1, size // inner)]
    share = jnp.concatenate(shares, axis=0)
    hidden_all = gather(hidden, outer_bits)
    weight_all = gather(down_weight, inner_bits)
    product = scatter(
        [
            lax.dot_general(
                share[:, j * rows : (j + 1) * rows],
                hidden_all,
                (((0,), (0,)), ((), ())),
                preferred_element_type=jnp.float32,
            )
            for j in range(inner)
        ],
        inner_bits,
    )
    hidden_grad = scatter(
        [jnp.dot(x, weight_all, preferred_element_type=jnp.float32) for x in shares],
        outer_bits,
    )
    return product, hidden_grad


def first_stage(out_grad, gate_pre, up_pre, place, rows):
    tokens, units = gate_pre.shape
    half = units // 2
    step = 32

    def kernel(place, source, gate, up, own, right, message1, message2, message3):
        me, core = place[0], place[1]

        def block(k, j):
            return pl.ds(pl.multiple_of((me ^ (4 * k + j)) * rows, rows), rows)

        activated, _ = gelu_parts(gate[...].astype(jnp.float32))
        value = (activated * up[...].astype(jnp.float32)).astype(jnp.bfloat16)
        right[...] = value[:, half:]
        message1[:, :half] = value[:, :half]
        message2[:, :half] = value[:, :half]
        for j in range(4):
            own[:, j * rows : (j + 1) * rows] = source[:, block(0, j)]
        for k, target, base in ((1, message1, half), (2, message2, half), (3, message3, 0)):
            for j in range(2):
                target[:, base + j * rows : base + (j + 1) * rows] = source[:, block(k, 2 * core + j)]

    widths = [4 * rows, units - half, half + 2 * rows, half + 2 * rows, 2 * rows]
    return pl.pallas_call(
        kernel,
        grid=(tokens // step,),
        out_shape=[jax.ShapeDtypeStruct((tokens, width), jnp.bfloat16) for width in widths],
        in_specs=[pl.BlockSpec(memory_space=pltpu.SMEM)]
        + [pl.BlockSpec((step, array.shape[1]), lambda i: (i, 0)) for array in (out_grad, gate_pre, up_pre)],
        out_specs=[pl.BlockSpec((step, width), lambda i: (i, 0)) for width in widths],
        compiler_params=pltpu.CompilerParams(vmem_limit_bytes=56 << 20),
        cost_estimate=EAGER,
    )(place, out_grad, gate_pre, up_pre)


def cut(sources, parts, shapes):
    def kernel(*refs):
        ins, outs, sems = refs[: len(sources)], refs[len(sources) : -1], refs[-1]
        copies = [
            pltpu.make_async_copy(
                ins[i].at[pl.ds(*rows), pl.ds(*columns)], outs[o].at[:, pl.ds(at, columns[1])], sems.at[n]
            )
            for n, (i, rows, columns, o, at) in enumerate(parts)
        ]
        for copy in copies:
            copy.start()
        for copy in copies:
            copy.wait()

    return pl.pallas_call(
        kernel,
        out_shape=[jax.ShapeDtypeStruct(shape, jnp.bfloat16) for shape in shapes],
        in_specs=[pl.BlockSpec(memory_space=pltpu.HBM)] * len(sources),
        out_specs=[pl.BlockSpec(memory_space=pltpu.HBM)] * len(shapes),
        scratch_shapes=[pltpu.SemaphoreType.DMA((len(parts),))],
        compiler_params=pltpu.CompilerParams(vmem_limit_bytes=1 << 20),
        cost_estimate=EAGER,
    )(*sources)


def assemble(own, mine, theirs, place, rows):
    tokens = own.shape[0]

    def kernel(place, own, mine, theirs, share):
        share[:tokens, :] = own[...]
        for k in range(3):
            here = pl.ds((k + 1) * tokens, tokens)
            half = slice(k * 2 * rows, (k + 1) * 2 * rows)
            a, b = mine[:, half], theirs[:, half]
            share[here, : 2 * rows] = jnp.where(place[1] == 0, a, b)
            share[here, 2 * rows :] = jnp.where(place[1] == 0, b, a)

    vmem = pl.BlockSpec(memory_space=pltpu.VMEM)
    return pl.pallas_call(
        kernel,
        out_shape=jax.ShapeDtypeStruct((4 * tokens, 4 * rows), jnp.bfloat16),
        in_specs=[pl.BlockSpec(memory_space=pltpu.SMEM), vmem, vmem, vmem],
        out_specs=vmem,
        compiler_params=pltpu.CompilerParams(vmem_limit_bytes=4 << 20),
        cost_estimate=EAGER,
    )(place, own, mine, theirs)


def add_tail(parts, arrived):
    rows = parts[0].shape[0]
    widths = [part.shape[1] for part in parts]

    def kernel(*refs):
        out, at = refs[-1], 0
        for part, other, width in zip(refs, refs[len(parts) :], widths):
            out[:, at : at + width] = (part[...] + other[-rows:, :].astype(jnp.float32)).astype(jnp.bfloat16)
            at += width

    vmem = pl.BlockSpec(memory_space=pltpu.VMEM)
    return pl.pallas_call(
        kernel,
        out_shape=jax.ShapeDtypeStruct((rows, sum(widths)), jnp.bfloat16),
        in_specs=[vmem] * (2 * len(parts)),
        out_specs=vmem,
        compiler_params=pltpu.CompilerParams(vmem_limit_bytes=4 << 20),
        cost_estimate=EAGER,
    )(*parts, *arrived)


def flat(column):
    return jnp.broadcast_to(column, (128, 128)).T[0:1, :]


def upright(row):
    return jnp.broadcast_to(row, (128, 128)).T[:, 0:1]


def sum_up(kept, from_low, from_high, last_a, last_b, scale):
    rows = kept[0].shape[0]
    q = rows // 2
    widths = [part.shape[1] for part in kept]
    units = sum(widths)

    def kernel(*refs):
        kept_refs, low_refs, high_refs = refs[:2], refs[2:4], refs[4:6]
        last_refs, grad, row_part = refs[6:8], refs[8], refs[9]
        for h, arrived in enumerate((low_refs, high_refs)):
            for at in range(0, q, 128):
                total = jnp.zeros((128, 1), jnp.float32)
                here = slice(h * q + at, h * q + at + 128)
                column = 0
                for part, other, width in zip(kept_refs, arrived, widths):
                    there = slice(column, column + width)
                    value = part[here, :] + other[at : at + 128, :].astype(jnp.float32)
                    value = (value + last_refs[h][at : at + 128, there].astype(jnp.float32)) * scale
                    grad[here, there] = value
                    total = total + jnp.sum(value * value + 1e-30, axis=1, keepdims=True)
                    column += width
                row_part[:, here] = flat(total)

    vmem = pl.BlockSpec(memory_space=pltpu.VMEM)
    return pl.pallas_call(
        kernel,
        out_shape=[jax.ShapeDtypeStruct((rows, units), jnp.float32), jax.ShapeDtypeStruct((1, rows), jnp.float32)],
        in_specs=[vmem] * 8,
        out_specs=[vmem] * 2,
        compiler_params=pltpu.CompilerParams(vmem_limit_bytes=10 << 20),
        cost_estimate=EAGER,
    )(*kept, *from_low, *from_high, last_a, last_b)


def column_sums(grad, row_sum, row_moment, decay, total_units):
    rows, units = grad.shape

    def kernel(grad, row_sum, row_moment, row_moment_new, sums):
        new = decay * row_moment[...] + (1.0 - decay) * (row_sum[...] / total_units)
        row_moment_new[...] = new
        sums[:, 2 * units :] = jnp.broadcast_to(jnp.sum(new, axis=1, keepdims=True), (1, 128))
        inverse = [1.0 / upright(new[:, at : at + 128]) for at in range(0, rows, 128)]
        for column in range(0, units, 256):
            there = slice(column, column + 256)
            squares, scaled = jnp.zeros((1, 256), jnp.float32), jnp.zeros((1, 256), jnp.float32)
            for n, at in enumerate(range(0, rows, 128)):
                power = grad[at : at + 128, there]
                power = power * power
                squares = squares + jnp.sum(power + 1e-30, axis=0, keepdims=True)
                scaled = scaled + jnp.sum(power * inverse[n], axis=0, keepdims=True)
            sums[:, there] = squares
            sums[:, units + column : units + column + 256] = scaled

    vmem = pl.BlockSpec(memory_space=pltpu.VMEM)
    return pl.pallas_call(
        kernel,
        out_shape=[
            jax.ShapeDtypeStruct((1, rows), jnp.float32),
            jax.ShapeDtypeStruct((1, 2 * units + 128), jnp.float32),
        ],
        in_specs=[vmem] * 3,
        out_specs=[vmem] * 2,
        compiler_params=pltpu.CompilerParams(vmem_limit_bytes=5 << 20),
        cost_estimate=EAGER,
    )(grad, row_sum, row_moment)


def column_step(sums, col_moment, decay, total_rows):
    units = col_moment.shape[1]

    def kernel(sums, col_moment, col_moment_new, terms):
        total = jnp.zeros((1, 128), jnp.float32)
        for at in range(0, units, 128):
            here = slice(at, at + 128)
            new = decay * col_moment[:, here] + (1.0 - decay) * (sums[:, here] / total_rows)
            col_moment_new[:, here] = new
            total = total + sums[:, units + at : units + at + 128] / new
        terms[...] = total

    vmem = pl.BlockSpec(memory_space=pltpu.VMEM)
    return pl.pallas_call(
        kernel,
        out_shape=[jax.ShapeDtypeStruct((1, units), jnp.float32), jax.ShapeDtypeStruct((1, 128), jnp.float32)],
        in_specs=[vmem] * 2,
        out_specs=[vmem] * 2,
        compiler_params=pltpu.CompilerParams(vmem_limit_bytes=2 << 20),
        cost_estimate=EAGER,
    )(sums, col_moment)


def final_update(grad, row_moment_new, col_moment_new, terms, sums, total_rows, total_units):
    rows, units = grad.shape
    tile = units // 2

    def kernel(grad, row_moment_new, col_moment_new, terms, row_total, update, row_mean):
        mean = row_total[...] / total_rows
        row_mean[...] = mean
        square_sum = mean[:, 0:1] * jnp.sum(terms[...], axis=1, keepdims=True)
        clip = jnp.maximum(1.0, jnp.sqrt(square_sum / (total_rows * total_units)))
        col_factor = 1.0 / jnp.sqrt(col_moment_new[...])
        for at in range(0, rows, 128):
            here = slice(at, at + 128)
            row_factor = jnp.sqrt(mean / row_moment_new[:, here]) / clip
            update[here, :] = grad[here, :] * upright(row_factor) * col_factor

    def fixed(width, block=0):
        return pl.BlockSpec((1, width), lambda i: (0, block))

    return pl.pallas_call(
        kernel,
        grid=(units // tile,),
        out_shape=[jax.ShapeDtypeStruct((rows, units), jnp.float32), jax.ShapeDtypeStruct((1, 128), jnp.float32)],
        in_specs=[
            pl.BlockSpec((rows, tile), lambda i: (0, i)),
            fixed(rows),
            pl.BlockSpec((1, tile), lambda i: (0, i)),
            fixed(128),
            fixed(128, 2 * units // 128),
        ],
        out_specs=[pl.BlockSpec((rows, tile), lambda i: (0, i)), fixed(128)],
        compiler_params=pltpu.CompilerParams(vmem_limit_bytes=7 << 20),
        cost_estimate=EAGER,
    )(grad, row_moment_new, col_moment_new, terms, sums)


def products(share, groups, steps):
    pieces = [(piece, group[1]) for group in groups for piece in group[0]]
    bounds = [(output, group[1]) for group in groups for output in group[2]]

    def kernel(*refs):
        share_ref, ins = refs[0], refs[1 : 1 + len(pieces)]
        outs, stacks = refs[1 + len(pieces) : -len(groups)], refs[-len(groups) :]
        n = o = 0
        for (own, _, outputs, over_rows), stack in zip(groups, stacks):
            at = 0
            for piece, _ in own:
                stack[at : at + piece.shape[0], :] = ins[n][...]
                at += piece.shape[0]
                n += 1
            for ranges, kind in outputs:
                if over_rows:
                    side = jnp.concatenate([share_ref[:, begin:end] for begin, end in ranges], axis=1)
                    value = lax.dot_general(
                        side, stack[...], (((0,), (0,)), ((), ())), preferred_element_type=jnp.float32
                    )
                else:
                    side = jnp.concatenate([share_ref[begin:end, :] for begin, end in ranges], axis=0)
                    value = jnp.dot(side, stack[...], preferred_element_type=jnp.float32)
                outs[o][...] = value.astype(kind)
                o += 1

    def height(ranges):
        return sum(end - begin for begin, end in ranges)

    return pl.pallas_call(
        kernel,
        grid=(steps,),
        out_shape=[jax.ShapeDtypeStruct((height(ranges), columns), kind) for (ranges, kind), columns in bounds],
        in_specs=[pl.BlockSpec(share.shape, lambda i: (0, 0))]
        + [
            pl.BlockSpec((piece.shape[0], columns // steps), lambda i, skip=first * steps // columns: (0, i + skip))
            for (piece, first), columns in pieces
        ],
        out_specs=[pl.BlockSpec((height(ranges), columns // steps), lambda i: (0, i)) for (ranges, _), columns in bounds],
        scratch_shapes=[
            pltpu.VMEM((sum(piece.shape[0] for piece, _ in group[0]), group[1] // steps), jnp.bfloat16) for group in groups
        ],
        compiler_params=pltpu.CompilerParams(vmem_limit_bytes=9 << 20),
        cost_estimate=EAGER,
    )(share, *[piece for (piece, _), _ in pieces])


def staged_products(out_grad, gate_pre, up_pre, down_weight):
    x_bit, y_bit, z_bit, w_bit = 1, 2, 4, 8
    me, core = lax.axis_index("dp"), lax.axis_index("mp")
    tokens, units = gate_pre.shape
    rows = down_weight.shape[0]
    q, t = rows // 2, tokens // 2
    steps = 5
    split = units // 2
    barrier = lax.optimization_barrier
    place = jnp.stack([me, core]).astype(jnp.int32)
    own, right, message1, message2, message3 = first_stage(out_grad, gate_pre, up_pre, place, rows)

    extra, every, whole = (split, 2 * rows), (0, tokens), (0, units)
    left1, left2, message3 = flip(message1, z_bit), flip(message2, w_bit), flip(message3, z_bit | w_bit)
    weight1, weight2 = flip(down_weight, x_bit), flip(down_weight, y_bit)
    to_y, to_x = cut([weight1, weight2], [(0, (0, q), whole, 0, 0), (1, (q, q), whole, 1, 0)], [(q, units)] * 2)
    weight3a, weight3b = flip(to_y, y_bit), flip(to_x, x_bit)
    left1, left2, message3, right = barrier((left1, left2, message3, right))
    to_z, mine = cut(
        [left1, left2, message3, right],
        [
            (1, every, (0, split), 0, 0),
            (3, every, (0, units - split), 0, split),
            (0, every, extra, 1, 0),
            (1, every, extra, 1, 2 * rows),
            (2, every, (0, 2 * rows), 1, 4 * rows),
        ],
        [(tokens, units), (tokens, 6 * rows)],
    )
    from_near = flip(to_z, z_bit)
    right2 = flip(right, w_bit)
    theirs = flip(mine, 1, "mp")
    share = assemble(own, mine, theirs, place, rows)

    def low_sent(size):
        return [(2 * size, 3 * size), (6 * size, 7 * size)]

    def high_sent(size):
        return [(5 * size, 6 * size), (7 * size, 8 * size)]

    def sent(size):
        return [(low_sent(size), jnp.bfloat16), (high_sent(size), jnp.bfloat16)]

    def kept(size):
        ranges = [(0, 2 * size)], [(4 * size, 5 * size)], [(3 * size, 4 * size)]
        return [(r, jnp.float32) for r in ranges]

    from_near, right2, share = barrier((from_near, right2, share))
    right3 = flip(right2, z_bit)
    lefts = [(message1, 0), (left1, 0), (left2, 0), (from_near, 0)]
    left_to_x, left_to_y = products(share, [(lefts, split, sent(q), True)], steps)
    left_from_x, left_from_y = flip(left_to_x, x_bit), flip(left_to_y, y_bit)

    share, _ = barrier((share, left_to_x))
    weights = [(piece, 0) for piece in (down_weight, weight1, weight2, weight3a, weight3b)]
    to_w, to_z = products(
        share, [(weights, units, [(high_sent(t), jnp.bfloat16), (low_sent(t), jnp.bfloat16)], False)], steps
    )
    right3, share, to_w, to_z = barrier((right3, share, to_w, to_z))
    from_w, from_z = flip(to_w, w_bit), flip(to_z, z_bit)
    rights = [(right, 0), (from_near, split), (right2, 0), (right3, 0)]
    right_to_x, right_to_y = products(share, [(rights, units - split, sent(q), True)], steps)
    right_from_x, right_from_y = flip(right_to_x, x_bit), flip(right_to_y, y_bit)
    share, left_from_x, left_from_y, _ = barrier((share, left_from_x, left_from_y, right_to_x))
    left_parts = products(share, [(lefts, split, kept(q), True)], steps)
    parts = products(share, [(rights, units - split, kept(q), True), (weights, units, kept(t), False)], steps)

    grad_a = flip(add_tail([left_parts[1], parts[1]], [left_from_x, right_from_x]), y_bit)
    grad_b = flip(add_tail([left_parts[2], parts[2]], [left_from_y, right_from_y]), x_bit)
    to_w, to_z = add_tail([parts[4]], [from_z]), add_tail([parts[5]], [from_w])
    last_a, last_b = flip(to_w, w_bit), flip(to_z, z_bit)
    grad_a, grad_b, _, _ = barrier((grad_a, grad_b, to_w, to_z))
    grad, row_part = sum_up(
        [left_parts[0], parts[0]],
        [left_from_x, right_from_x],
        [left_from_y, right_from_y],
        grad_a,
        grad_b,
        1.0 / math.sqrt(tokens * lax.axis_size("dp")),
    )

    row_sum = lax.psum(row_part, "mp")
    return grad, row_sum, (parts[3], from_z[:t], from_w[:t], last_a, last_b)


def local(out_grad, gate_pre, up_pre, down_weight, row_moment, col_moment):
    size = lax.axis_size("dp")
    rows, units = down_weight.shape
    tokens = out_grad.shape[0]
    all_bits = [1 << b for b in range(size.bit_length() - 1)]
    decay = 1.0 - TRAIN_STEP ** (-0.8)
    total_rows = rows * size
    total_units = units * lax.axis_size("mp")
    staged = size == 16 and lax.axis_size("mp") == 2 and rows % 256 == 0 and tokens % 32 == 0 and units % 2560 == 0
    if staged:
        grad, row_sum, terms = staged_products(out_grad, gate_pre, up_pre, down_weight)
        row_moment_new, sums = column_sums(grad, row_sum, row_moment[None, :], decay, total_units)
        sums = group_sum(sums[0], all_bits[:INNER_BITS])
        sums, terms = lax.optimization_barrier((sums, terms))
        own_part, from_low, from_high, last_a, last_b = terms
        arrived = jnp.concatenate([from_low, from_high], axis=0).astype(jnp.float32)
        hidden_grad = own_part + arrived + jnp.concatenate([last_a, last_b], axis=0).astype(jnp.float32)
        sums = group_sum(sums, all_bits[INNER_BITS:])[None, :]
        col_moment_new, ratios = column_step(sums, col_moment[None, :], decay, total_rows)
        ratios = lax.psum(ratios, "mp")
        update, row_mean = final_update(grad, row_moment_new, col_moment_new, ratios, sums, total_rows, total_units)
        row_moment_new, col_moment_new, row_mean = row_moment_new[0], col_moment_new[0], row_mean[0, 0]
    else:
        product, hidden_grad = general_products(
            out_grad, gate_pre, up_pre, down_weight, all_bits[:INNER_BITS], all_bits[INNER_BITS:]
        )
        grad = product * (1.0 / math.sqrt(tokens * size))
        powers = grad * grad
        squares = powers + 1e-30
        row_sum = lax.psum(jnp.sum(squares, axis=1), "mp")
        row_moment_new = decay * row_moment + (1.0 - decay) * (row_sum / total_units)
        col_part = jnp.sum(squares, axis=0)
        scaled_part = jnp.sum(powers / row_moment_new[:, None], axis=0)
        sums = jnp.concatenate([col_part, scaled_part, jnp.broadcast_to(jnp.sum(row_moment_new), (128,))])
        sums = group_sum(sums, all_bits)
        col_moment_new = decay * col_moment + (1.0 - decay) * (sums[:units] / total_rows)
        row_mean = sums[2 * units] / total_rows
        ratios = lax.psum(jnp.sum(sums[units : 2 * units] / col_moment_new), "mp")
        clip_norm = jnp.sqrt(row_mean * ratios / (total_rows * total_units))
        row_factor = jnp.sqrt(row_mean / row_moment_new) / jnp.maximum(1.0, clip_norm)
        col_factor = 1.0 / jnp.sqrt(col_moment_new)
        update = grad * row_factor[:, None] * col_factor[None, :]

    activated, derivative = gelu_parts(gate_pre.astype(jnp.float32))
    gate_grad = (hidden_grad * up_pre.astype(jnp.float32) * derivative).astype(jnp.bfloat16)
    up_grad = (hidden_grad * activated).astype(jnp.bfloat16)
    return (update, row_moment_new, col_moment_new, row_mean, gate_grad, up_grad)


def solution(mesh):
    in_specs = (P("dp", None), P("dp", "mp"), P("dp", "mp"), P("dp", "mp"), P("dp"), P("mp"))
    out_specs = (P("dp", "mp"), P("dp"), P("mp"), P(), P("dp", "mp"), P("dp", "mp"))
    return jax.shard_map(local, mesh=mesh, in_specs=in_specs, out_specs=out_specs, check_vma=False)
```

```python
import math

import jax
import jax.numpy as jnp
from jax import lax
from jax.experimental import pallas as pl
from jax.experimental.pallas import tpu as pltpu
from jax.sharding import PartitionSpec as P

TRAIN_STEP = 3
INNER_BITS = 2
EAGER = pl.CostEstimate(flops=0, bytes_accessed=0, transcendentals=0)


def gelu_parts(values):
    factor = math.sqrt(2.0 / math.pi)
    inner = factor * (values + 0.044715 * values * values * values)
    tangent = jnp.tanh(inner)
    activated = 0.5 * values * (1.0 + tangent)
    derivative = 0.5 * (1.0 + tangent) + 0.5 * values * (1.0 - tangent * tangent) * factor * (
        1.0 + 3.0 * 0.044715 * values * values
    )
    return (activated, derivative)


def gradients(hidden_grad, gate_pre, up_pre):
    activated, derivative = gelu_parts(gate_pre.astype(jnp.float32))
    gate_grad = (hidden_grad * up_pre.astype(jnp.float32) * derivative).astype(jnp.bfloat16)
    return gate_grad, (hidden_grad * activated).astype(jnp.bfloat16)


def flip(value, bits, axis="dp"):
    size = lax.axis_size(axis)
    return lax.ppermute(value, axis, [(i, i ^ bits) for i in range(size)])


def group_sum(value, bits):
    for at in range(0, len(bits), 2):
        pair = bits[at : at + 2]
        if len(pair) == 2:
            first, second = flip(value, pair[0]), flip(value, pair[1])
            value = (value + first) + (second + flip(value, pair[0] | pair[1]))
        else:
            value = value + flip(value, pair[0])
    return value


def general_products(out_grad, gate_pre, up_pre, down_weight, inner_bits, outer_bits):
    size = lax.axis_size("dp")
    me = lax.axis_index("dp")
    tokens, rows = out_grad.shape[0], down_weight.shape[0]
    inner = 2 ** len(inner_bits)
    activated, _ = gelu_parts(gate_pre.astype(jnp.float32))
    hidden = (activated * up_pre.astype(jnp.float32)).astype(jnp.bfloat16)
    by_block = out_grad.reshape(tokens, size, rows).transpose(1, 0, 2)

    def features_of(k):
        picks = [lax.dynamic_index_in_dim(by_block, me ^ (k * inner + j), 0, keepdims=False) for j in range(inner)]
        return jnp.concatenate(picks, axis=1)

    def gather(block, bits):
        blocks = [block]
        for bit in bits:
            blocks = blocks + [flip(b, bit) for b in blocks]
        return jnp.concatenate(blocks, axis=0)

    def scatter(values, bits):
        for level in reversed(range(len(bits))):
            count = 2**level
            values = [
                values[j] + flip(values[j + count].astype(jnp.bfloat16), bits[level]).astype(jnp.float32)
                for j in range(count)
            ]
        return values[0]

    shares = [features_of(0)] + [flip(features_of(k), k * inner) for k in range(1, size // inner)]
    share = jnp.concatenate(shares, axis=0)
    hidden_all = gather(hidden, outer_bits)
    weight_all = gather(down_weight, inner_bits)
    product = scatter(
        [
            lax.dot_general(
                share[:, j * rows : (j + 1) * rows],
                hidden_all,
                (((0,), (0,)), ((), ())),
                preferred_element_type=jnp.float32,
            )
            for j in range(inner)
        ],
        inner_bits,
    )
    hidden_grad = scatter(
        [jnp.dot(x, weight_all, preferred_element_type=jnp.float32) for x in shares],
        outer_bits,
    )
    return product, hidden_grad


def first_stage(out_grad, gate_pre, up_pre, place, rows):
    tokens, units = gate_pre.shape
    half = units // 2
    step = 32

    def kernel(place, source, gate, up, own, right, message1, message2, message3):
        me, core = place[0], place[1]

        def block(k, j):
            return pl.ds(pl.multiple_of((me ^ (4 * k + j)) * rows, rows), rows)

        activated, _ = gelu_parts(gate[...].astype(jnp.float32))
        value = (activated * up[...].astype(jnp.float32)).astype(jnp.bfloat16)
        right[...] = value[:, half:]
        message1[:, :half] = value[:, :half]
        message2[:, :half] = value[:, :half]
        for j in range(4):
            own[:, j * rows : (j + 1) * rows] = source[:, block(0, j)]
        for k, target, base in ((1, message1, half), (2, message2, half), (3, message3, 0)):
            for j in range(2):
                target[:, base + j * rows : base + (j + 1) * rows] = source[:, block(k, 2 * core + j)]

    widths = [4 * rows, units - half, half + 2 * rows, half + 2 * rows, 2 * rows]
    return pl.pallas_call(
        kernel,
        grid=(tokens // step,),
        out_shape=[jax.ShapeDtypeStruct((tokens, width), jnp.bfloat16) for width in widths],
        in_specs=[pl.BlockSpec(memory_space=pltpu.SMEM)]
        + [pl.BlockSpec((step, array.shape[1]), lambda i: (i, 0)) for array in (out_grad, gate_pre, up_pre)],
        out_specs=[pl.BlockSpec((step, width), lambda i: (i, 0)) for width in widths],
        compiler_params=pltpu.CompilerParams(vmem_limit_bytes=56 << 20),
        cost_estimate=EAGER,
    )(place, out_grad, gate_pre, up_pre)


def cut(sources, parts, shapes):
    def kernel(*refs):
        ins, outs, sems = refs[: len(sources)], refs[len(sources) : -1], refs[-1]
        copies = [
            pltpu.make_async_copy(
                ins[i].at[pl.ds(*rows), pl.ds(*columns)], outs[o].at[:, pl.ds(at, columns[1])], sems.at[n]
            )
            for n, (i, rows, columns, o, at) in enumerate(parts)
        ]
        for copy in copies:
            copy.start()
        for copy in copies:
            copy.wait()

    return pl.pallas_call(
        kernel,
        out_shape=[jax.ShapeDtypeStruct(shape, jnp.bfloat16) for shape in shapes],
        in_specs=[pl.BlockSpec(memory_space=pltpu.HBM)] * len(sources),
        out_specs=[pl.BlockSpec(memory_space=pltpu.HBM)] * len(shapes),
        scratch_shapes=[pltpu.SemaphoreType.DMA((len(parts),))],
        compiler_params=pltpu.CompilerParams(vmem_limit_bytes=1 << 20),
        cost_estimate=EAGER,
    )(*sources)


def assemble(own, mine, theirs, place, rows):
    tokens = own.shape[0]

    def kernel(place, own, mine, theirs, share):
        share[:tokens, :] = own[...]
        for k in range(3):
            here = pl.ds((k + 1) * tokens, tokens)
            half = slice(k * 2 * rows, (k + 1) * 2 * rows)
            a, b = mine[:, half], theirs[:, half]
            share[here, : 2 * rows] = jnp.where(place[1] == 0, a, b)
            share[here, 2 * rows :] = jnp.where(place[1] == 0, b, a)

    vmem = pl.BlockSpec(memory_space=pltpu.VMEM)
    return pl.pallas_call(
        kernel,
        out_shape=jax.ShapeDtypeStruct((4 * tokens, 4 * rows), jnp.bfloat16),
        in_specs=[pl.BlockSpec(memory_space=pltpu.SMEM), vmem, vmem, vmem],
        out_specs=vmem,
        compiler_params=pltpu.CompilerParams(vmem_limit_bytes=8 << 20),
        cost_estimate=EAGER,
    )(place, own, mine, theirs)


def add_tail(parts, arrived):
    rows = parts[0].shape[0]
    widths = [part.shape[1] for part in parts]

    def kernel(*refs):
        out, at = refs[-1], 0
        for part, other, width in zip(refs, refs[len(parts) :], widths):
            out[:, at : at + width] = (part[...] + other[-rows:, :].astype(jnp.float32)).astype(jnp.bfloat16)
            at += width

    vmem = pl.BlockSpec(memory_space=pltpu.VMEM)
    return pl.pallas_call(
        kernel,
        out_shape=jax.ShapeDtypeStruct((rows, sum(widths)), jnp.bfloat16),
        in_specs=[vmem] * (2 * len(parts)),
        out_specs=vmem,
        compiler_params=pltpu.CompilerParams(vmem_limit_bytes=8 << 20),
        cost_estimate=EAGER,
    )(*parts, *arrived)


def flat(column):
    return jnp.broadcast_to(column, (128, 128)).T[0:1, :]


def upright(row):
    return jnp.broadcast_to(row, (128, 128)).T[:, 0:1]


def sum_up(kept, from_low, from_high, last_a, last_b, scale):
    rows = kept[0].shape[0]
    q = rows // 2
    widths = [part.shape[1] for part in kept]
    units = sum(widths)

    def kernel(*refs):
        kept_refs, low_refs, high_refs = refs[:2], refs[2:4], refs[4:6]
        last_refs, grad, row_part = refs[6:8], refs[8], refs[9]
        for h, arrived in enumerate((low_refs, high_refs)):
            for at in range(0, q, 128):
                total = jnp.zeros((128, 1), jnp.float32)
                here = slice(h * q + at, h * q + at + 128)
                column = 0
                for part, other, width in zip(kept_refs, arrived, widths):
                    there = slice(column, column + width)
                    value = part[here, :] + other[at : at + 128, :].astype(jnp.float32)
                    value = (value + last_refs[h][at : at + 128, there].astype(jnp.float32)) * scale
                    grad[here, there] = value
                    total = total + jnp.sum(value * value + 1e-30, axis=1, keepdims=True)
                    column += width
                row_part[:, here] = flat(total)

    vmem = pl.BlockSpec(memory_space=pltpu.VMEM)
    return pl.pallas_call(
        kernel,
        out_shape=[jax.ShapeDtypeStruct((rows, units), jnp.float32), jax.ShapeDtypeStruct((1, rows), jnp.float32)],
        in_specs=[vmem] * 8,
        out_specs=[vmem] * 2,
        compiler_params=pltpu.CompilerParams(vmem_limit_bytes=14 << 20),
        cost_estimate=EAGER,
    )(*kept, *from_low, *from_high, last_a, last_b)


def column_sums(grad, row_sum, row_moment, decay, total_units):
    rows, units = grad.shape

    def kernel(grad, row_sum, row_moment, row_moment_new, sums):
        new = decay * row_moment[...] + (1.0 - decay) * (row_sum[...] / total_units)
        row_moment_new[...] = new
        sums[:, 2 * units :] = jnp.broadcast_to(jnp.sum(new, axis=1, keepdims=True), (1, 128))
        inverse = [1.0 / upright(new[:, at : at + 128]) for at in range(0, rows, 128)]
        for column in range(0, units, 256):
            there = slice(column, column + 256)
            squares, scaled = jnp.zeros((1, 256), jnp.float32), jnp.zeros((1, 256), jnp.float32)
            for n, at in enumerate(range(0, rows, 128)):
                power = grad[at : at + 128, there]
                power = power * power
                squares = squares + jnp.sum(power + 1e-30, axis=0, keepdims=True)
                scaled = scaled + jnp.sum(power * inverse[n], axis=0, keepdims=True)
            sums[:, there] = squares
            sums[:, units + column : units + column + 256] = scaled

    vmem = pl.BlockSpec(memory_space=pltpu.VMEM)
    return pl.pallas_call(
        kernel,
        out_shape=[
            jax.ShapeDtypeStruct((1, rows), jnp.float32),
            jax.ShapeDtypeStruct((1, 2 * units + 128), jnp.float32),
        ],
        in_specs=[vmem] * 3,
        out_specs=[vmem] * 2,
        compiler_params=pltpu.CompilerParams(vmem_limit_bytes=14 << 20),
        cost_estimate=EAGER,
    )(grad, row_sum, row_moment)


def column_step(sums, col_moment, decay, total_rows):
    units = col_moment.shape[1]

    def kernel(sums, col_moment, col_moment_new, terms):
        total = jnp.zeros((1, 128), jnp.float32)
        for at in range(0, units, 128):
            here = slice(at, at + 128)
            new = decay * col_moment[:, here] + (1.0 - decay) * (sums[:, here] / total_rows)
            col_moment_new[:, here] = new
            total = total + sums[:, units + at : units + at + 128] / new
        terms[...] = total

    vmem = pl.BlockSpec(memory_space=pltpu.VMEM)
    return pl.pallas_call(
        kernel,
        out_shape=[jax.ShapeDtypeStruct((1, units), jnp.float32), jax.ShapeDtypeStruct((1, 128), jnp.float32)],
        in_specs=[vmem] * 2,
        out_specs=[vmem] * 2,
        compiler_params=pltpu.CompilerParams(vmem_limit_bytes=4 << 20),
        cost_estimate=EAGER,
    )(sums, col_moment)


def final_update(grad, row_moment_new, col_moment_new, terms, sums, total_rows, total_units):
    rows, units = grad.shape
    tile = units // 2

    def kernel(grad, row_moment_new, col_moment_new, terms, row_total, update, row_mean):
        mean = row_total[...] / total_rows
        row_mean[...] = mean
        square_sum = mean[:, 0:1] * jnp.sum(terms[...], axis=1, keepdims=True)
        clip = jnp.maximum(1.0, jnp.sqrt(square_sum / (total_rows * total_units)))
        col_factor = 1.0 / jnp.sqrt(col_moment_new[...])
        for at in range(0, rows, 128):
            here = slice(at, at + 128)
            row_factor = jnp.sqrt(mean / row_moment_new[:, here]) / clip
            update[here, :] = grad[here, :] * upright(row_factor) * col_factor

    def fixed(width, block=0):
        return pl.BlockSpec((1, width), lambda i: (0, block))

    return pl.pallas_call(
        kernel,
        grid=(units // tile,),
        out_shape=[jax.ShapeDtypeStruct((rows, units), jnp.float32), jax.ShapeDtypeStruct((1, 128), jnp.float32)],
        in_specs=[
            pl.BlockSpec((rows, tile), lambda i: (0, i)),
            fixed(rows),
            pl.BlockSpec((1, tile), lambda i: (0, i)),
            fixed(128),
            fixed(128, 2 * units // 128),
        ],
        out_specs=[pl.BlockSpec((rows, tile), lambda i: (0, i)), fixed(128)],
        compiler_params=pltpu.CompilerParams(vmem_limit_bytes=14 << 20),
        cost_estimate=EAGER,
    )(grad, row_moment_new, col_moment_new, terms, sums)


def products(share, groups, steps):
    pieces = [(piece, group[1]) for group in groups for piece in group[0]]
    bounds = [(output, group[1]) for group in groups for output in group[2]]

    def kernel(*refs):
        share_ref, ins = refs[0], refs[1 : 1 + len(pieces)]
        outs, stacks = refs[1 + len(pieces) : -len(groups)], refs[-len(groups) :]
        n = o = 0
        for (own, _, outputs, over_rows), stack in zip(groups, stacks):
            at = 0
            for piece, _ in own:
                stack[at : at + piece.shape[0], :] = ins[n][...]
                at += piece.shape[0]
                n += 1
            for ranges, kind in outputs:
                if over_rows:
                    side = jnp.concatenate([share_ref[:, begin:end] for begin, end in ranges], axis=1)
                    value = lax.dot_general(
                        side, stack[...], (((0,), (0,)), ((), ())), preferred_element_type=jnp.float32
                    )
                else:
                    side = jnp.concatenate([share_ref[begin:end, :] for begin, end in ranges], axis=0)
                    value = jnp.dot(side, stack[...], preferred_element_type=jnp.float32)
                outs[o][...] = value.astype(kind)
                o += 1

    def height(ranges):
        return sum(end - begin for begin, end in ranges)

    return pl.pallas_call(
        kernel,
        grid=(steps,),
        out_shape=[jax.ShapeDtypeStruct((height(ranges), columns), kind) for (ranges, kind), columns in bounds],
        in_specs=[pl.BlockSpec(share.shape, lambda i: (0, 0))]
        + [
            pl.BlockSpec((piece.shape[0], columns // steps), lambda i, skip=first * steps // columns: (0, i + skip))
            for (piece, first), columns in pieces
        ],
        out_specs=[pl.BlockSpec((height(ranges), columns // steps), lambda i: (0, i)) for (ranges, _), columns in bounds],
        scratch_shapes=[
            pltpu.VMEM((sum(piece.shape[0] for piece, _ in group[0]), group[1] // steps), jnp.bfloat16) for group in groups
        ],
        compiler_params=pltpu.CompilerParams(vmem_limit_bytes=14 << 20),
        cost_estimate=EAGER,
    )(share, *[piece for (piece, _), _ in pieces])


def staged_products(out_grad, gate_pre, up_pre, down_weight):
    x_bit, y_bit, z_bit, w_bit = 1, 2, 4, 8
    me, core = lax.axis_index("dp"), lax.axis_index("mp")
    tokens, units = gate_pre.shape
    rows = down_weight.shape[0]
    q, t = rows // 2, tokens // 2
    steps = 5
    split = units // 2
    barrier = lax.optimization_barrier
    place = jnp.stack([me, core]).astype(jnp.int32)
    own, right, message1, message2, message3 = first_stage(out_grad, gate_pre, up_pre, place, rows)

    extra, every, whole = (split, 2 * rows), (0, tokens), (0, units)
    left1, left2, message3 = flip(message1, z_bit), flip(message2, w_bit), flip(message3, z_bit | w_bit)
    weight1, weight2 = flip(down_weight, x_bit), flip(down_weight, y_bit)
    message3, weight1, weight2 = barrier((message3, weight1, weight2))
    to_y, to_x = cut([weight1, weight2], [(0, (0, q), whole, 0, 0), (1, (q, q), whole, 1, 0)], [(q, units)] * 2)
    weight3a, weight3b = flip(to_y, y_bit), flip(to_x, x_bit)
    left1, left2, message3, right, _, _ = barrier((left1, left2, message3, right, to_y, to_x))
    to_z, mine = cut(
        [left1, left2, message3, right],
        [
            (1, every, (0, split), 0, 0),
            (3, every, (0, units - split), 0, split),
            (0, every, extra, 1, 0),
            (1, every, extra, 1, 2 * rows),
            (2, every, (0, 2 * rows), 1, 4 * rows),
        ],
        [(tokens, units), (tokens, 6 * rows)],
    )
    from_near = flip(to_z, z_bit)
    right2 = flip(right, w_bit)
    theirs = flip(mine, 1, "mp")
    share = assemble(own, mine, theirs, place, rows)

    def low_sent(size):
        return [(2 * size, 3 * size), (6 * size, 7 * size)]

    def high_sent(size):
        return [(5 * size, 6 * size), (7 * size, 8 * size)]

    def sent(size):
        return [(low_sent(size), jnp.bfloat16), (high_sent(size), jnp.bfloat16)]

    def kept(size):
        ranges = [(0, 2 * size)], [(4 * size, 5 * size)], [(3 * size, 4 * size)]
        return [(r, jnp.float32) for r in ranges]

    from_near, right2, share = barrier((from_near, right2, share))
    right3 = flip(right2, z_bit)
    lefts = [(message1, 0), (left1, 0), (left2, 0), (from_near, 0)]
    left_to_x, left_to_y = products(share, [(lefts, split, sent(q), True)], steps)
    left_from_x, left_from_y = flip(left_to_x, x_bit), flip(left_to_y, y_bit)

    share, _ = barrier((share, left_to_x))
    weights = [(piece, 0) for piece in (down_weight, weight1, weight2, weight3a, weight3b)]
    to_w, to_z = products(
        share, [(weights, units, [(high_sent(t), jnp.bfloat16), (low_sent(t), jnp.bfloat16)], False)], steps
    )
    right3, share, to_w, to_z = barrier((right3, share, to_w, to_z))
    from_w, from_z = flip(to_w, w_bit), flip(to_z, z_bit)
    rights = [(right, 0), (from_near, split), (right2, 0), (right3, 0)]
    right_to_x, right_to_y = products(share, [(rights, units - split, sent(q), True)], steps)
    right_from_x, right_from_y = flip(right_to_x, x_bit), flip(right_to_y, y_bit)
    share, left_from_x, left_from_y, _ = barrier((share, left_from_x, left_from_y, right_to_x))
    left_parts = products(share, [(lefts, split, kept(q), True)], steps)
    parts = products(share, [(rights, units - split, kept(q), True), (weights, units, kept(t), False)], steps)

    grad_a = flip(add_tail([left_parts[1], parts[1]], [left_from_x, right_from_x]), y_bit)
    grad_b = flip(add_tail([left_parts[2], parts[2]], [left_from_y, right_from_y]), x_bit)
    to_w, to_z = add_tail([parts[4]], [from_z]), add_tail([parts[5]], [from_w])
    last_a, last_b = flip(to_w, w_bit), flip(to_z, z_bit)
    grad_a, grad_b, _, _ = barrier((grad_a, grad_b, to_w, to_z))
    grad, row_part = sum_up(
        [left_parts[0], parts[0]],
        [left_from_x, right_from_x],
        [left_from_y, right_from_y],
        grad_a,
        grad_b,
        1.0 / math.sqrt(tokens * lax.axis_size("dp")),
    )

    row_sum = lax.psum(row_part, "mp")
    return grad, row_sum, (parts[3], from_z[:t], from_w[:t], last_a, last_b)


def local(out_grad, gate_pre, up_pre, down_weight, row_moment, col_moment):
    size = lax.axis_size("dp")
    rows, units = down_weight.shape
    tokens = out_grad.shape[0]
    all_bits = [1 << b for b in range(size.bit_length() - 1)]
    decay = 1.0 - TRAIN_STEP ** (-0.8)
    total_rows = rows * size
    total_units = units * lax.axis_size("mp")
    staged = size == 16 and lax.axis_size("mp") == 2 and rows % 256 == 0 and tokens % 32 == 0 and units % 2560 == 0
    if staged:
        grad, row_sum, terms = staged_products(out_grad, gate_pre, up_pre, down_weight)
        row_moment_new, sums = column_sums(grad, row_sum, row_moment[None, :], decay, total_units)
        sums = group_sum(sums[0], all_bits[:INNER_BITS])
        own_part, from_low, from_high, last_a, last_b = terms
        arrived = jnp.concatenate([from_low, from_high], axis=0).astype(jnp.float32)
        hidden_grad = own_part + arrived + jnp.concatenate([last_a, last_b], axis=0).astype(jnp.float32)
        gate_grad, up_grad = gradients(hidden_grad, gate_pre, up_pre)
        first, second, third = [flip(sums, bits) for bits in (4, 8, 12)]
        first, second, third, gate_grad, up_grad = lax.optimization_barrier((first, second, third, gate_grad, up_grad))
        sums = ((sums + first) + (second + third))[None, :]
        col_moment_new, ratios = column_step(sums, col_moment[None, :], decay, total_rows)
        ratios = lax.psum(ratios, "mp")
        update, row_mean = final_update(grad, row_moment_new, col_moment_new, ratios, sums, total_rows, total_units)
        row_moment_new, col_moment_new, row_mean = row_moment_new[0], col_moment_new[0], row_mean[0, 0]
    else:
        product, hidden_grad = general_products(
            out_grad, gate_pre, up_pre, down_weight, all_bits[:INNER_BITS], all_bits[INNER_BITS:]
        )
        grad = product * (1.0 / math.sqrt(tokens * size))
        powers = grad * grad
        squares = powers + 1e-30
        row_sum = lax.psum(jnp.sum(squares, axis=1), "mp")
        row_moment_new = decay * row_moment + (1.0 - decay) * (row_sum / total_units)
        col_part = jnp.sum(squares, axis=0)
        scaled_part = jnp.sum(powers / row_moment_new[:, None], axis=0)
        sums = jnp.concatenate([col_part, scaled_part, jnp.broadcast_to(jnp.sum(row_moment_new), (128,))])
        sums = group_sum(sums, all_bits)
        col_moment_new = decay * col_moment + (1.0 - decay) * (sums[:units] / total_rows)
        row_mean = sums[2 * units] / total_rows
        ratios = lax.psum(jnp.sum(sums[units : 2 * units] / col_moment_new), "mp")
        clip_norm = jnp.sqrt(row_mean * ratios / (total_rows * total_units))
        row_factor = jnp.sqrt(row_mean / row_moment_new) / jnp.maximum(1.0, clip_norm)
        col_factor = 1.0 / jnp.sqrt(col_moment_new)
        update = grad * row_factor[:, None] * col_factor[None, :]
        gate_grad, up_grad = gradients(hidden_grad, gate_pre, up_pre)

    return (update, row_moment_new, col_moment_new, row_mean, gate_grad, up_grad)


def solution(mesh):
    in_specs = (P("dp", None), P("dp", "mp"), P("dp", "mp"), P("dp", "mp"), P("dp"), P("mp"))
    out_specs = (P("dp", "mp"), P("dp"), P("mp"), P(), P("dp", "mp"), P("dp", "mp"))
    return jax.shard_map(local, mesh=mesh, in_specs=in_specs, out_specs=out_specs, check_vma=False)
```

```python
import math

import jax
import jax.numpy as jnp
from jax import lax
from jax.experimental import pallas as pl
from jax.experimental.pallas import tpu as pltpu
from jax.sharding import PartitionSpec as P

TRAIN_STEP = 3
INNER_BITS = 2
EAGER = pl.CostEstimate(flops=0, bytes_accessed=0, transcendentals=0)


def gelu_parts(values):
    factor = math.sqrt(2.0 / math.pi)
    inner = factor * (values + 0.044715 * values * values * values)
    tangent = jnp.tanh(inner)
    activated = 0.5 * values * (1.0 + tangent)
    derivative = 0.5 * (1.0 + tangent) + 0.5 * values * (1.0 - tangent * tangent) * factor * (
        1.0 + 3.0 * 0.044715 * values * values
    )
    return (activated, derivative)


def gradients(hidden_grad, gate_pre, up_pre):
    activated, derivative = gelu_parts(gate_pre.astype(jnp.float32))
    gate_grad = (hidden_grad * up_pre.astype(jnp.float32) * derivative).astype(jnp.bfloat16)
    return gate_grad, (hidden_grad * activated).astype(jnp.bfloat16)


def flip(value, bits, axis="dp"):
    size = lax.axis_size(axis)
    return lax.ppermute(value, axis, [(i, i ^ bits) for i in range(size)])


def group_sum(value, bits):
    for at in range(0, len(bits), 2):
        pair = bits[at : at + 2]
        if len(pair) == 2:
            first, second = flip(value, pair[0]), flip(value, pair[1])
            value = (value + first) + (second + flip(value, pair[0] | pair[1]))
        else:
            value = value + flip(value, pair[0])
    return value


def general_products(out_grad, gate_pre, up_pre, down_weight, inner_bits, outer_bits):
    size = lax.axis_size("dp")
    me = lax.axis_index("dp")
    tokens, rows = out_grad.shape[0], down_weight.shape[0]
    inner = 2 ** len(inner_bits)
    activated, _ = gelu_parts(gate_pre.astype(jnp.float32))
    hidden = (activated * up_pre.astype(jnp.float32)).astype(jnp.bfloat16)
    by_block = out_grad.reshape(tokens, size, rows).transpose(1, 0, 2)

    def features_of(k):
        picks = [lax.dynamic_index_in_dim(by_block, me ^ (k * inner + j), 0, keepdims=False) for j in range(inner)]
        return jnp.concatenate(picks, axis=1)

    def gather(block, bits):
        blocks = [block]
        for bit in bits:
            blocks = blocks + [flip(b, bit) for b in blocks]
        return jnp.concatenate(blocks, axis=0)

    def scatter(values, bits):
        for level in reversed(range(len(bits))):
            count = 2**level
            values = [
                values[j] + flip(values[j + count].astype(jnp.bfloat16), bits[level]).astype(jnp.float32)
                for j in range(count)
            ]
        return values[0]

    shares = [features_of(0)] + [flip(features_of(k), k * inner) for k in range(1, size // inner)]
    share = jnp.concatenate(shares, axis=0)
    hidden_all = gather(hidden, outer_bits)
    weight_all = gather(down_weight, inner_bits)
    product = scatter(
        [
            lax.dot_general(
                share[:, j * rows : (j + 1) * rows],
                hidden_all,
                (((0,), (0,)), ((), ())),
                preferred_element_type=jnp.float32,
            )
            for j in range(inner)
        ],
        inner_bits,
    )
    hidden_grad = scatter(
        [jnp.dot(x, weight_all, preferred_element_type=jnp.float32) for x in shares],
        outer_bits,
    )
    return product, hidden_grad


def first_stage(out_grad, gate_pre, up_pre, place, rows):
    tokens, units = gate_pre.shape
    half = units // 2
    step = 32

    def kernel(place, source, gate, up, own, right, message1, message2, message3):
        me, core = place[0], place[1]

        def block(k, j):
            return pl.ds(pl.multiple_of((me ^ (4 * k + j)) * rows, rows), rows)

        activated, _ = gelu_parts(gate[...].astype(jnp.float32))
        value = (activated * up[...].astype(jnp.float32)).astype(jnp.bfloat16)
        right[...] = value[:, half:]
        message1[:, :half] = value[:, :half]
        message2[:, :half] = value[:, :half]
        for j in range(4):
            own[:, j * rows : (j + 1) * rows] = source[:, block(0, j)]
        for k, target, base in ((1, message1, half), (2, message2, half), (3, message3, 0)):
            for j in range(2):
                target[:, base + j * rows : base + (j + 1) * rows] = source[:, block(k, 2 * core + j)]

    widths = [4 * rows, units - half, half + 2 * rows, half + 2 * rows, 2 * rows]
    return pl.pallas_call(
        kernel,
        grid=(tokens // step,),
        out_shape=[jax.ShapeDtypeStruct((tokens, width), jnp.bfloat16) for width in widths],
        in_specs=[pl.BlockSpec(memory_space=pltpu.SMEM)]
        + [pl.BlockSpec((step, array.shape[1]), lambda i: (i, 0)) for array in (out_grad, gate_pre, up_pre)],
        out_specs=[pl.BlockSpec((step, width), lambda i: (i, 0)) for width in widths],
        compiler_params=pltpu.CompilerParams(vmem_limit_bytes=56 << 20),
        cost_estimate=EAGER,
    )(place, out_grad, gate_pre, up_pre)


def cut(sources, parts, shapes):
    def kernel(*refs):
        ins, outs, sems = refs[: len(sources)], refs[len(sources) : -1], refs[-1]
        copies = [
            pltpu.make_async_copy(
                ins[i].at[pl.ds(*rows), pl.ds(*columns)], outs[o].at[:, pl.ds(at, columns[1])], sems.at[n]
            )
            for n, (i, rows, columns, o, at) in enumerate(parts)
        ]
        for copy in copies:
            copy.start()
        for copy in copies:
            copy.wait()

    return pl.pallas_call(
        kernel,
        out_shape=[jax.ShapeDtypeStruct(shape, jnp.bfloat16) for shape in shapes],
        in_specs=[pl.BlockSpec(memory_space=pltpu.HBM)] * len(sources),
        out_specs=[pl.BlockSpec(memory_space=pltpu.HBM)] * len(shapes),
        scratch_shapes=[pltpu.SemaphoreType.DMA((len(parts),))],
        compiler_params=pltpu.CompilerParams(vmem_limit_bytes=1 << 20),
        cost_estimate=EAGER,
    )(*sources)


def assemble(own, mine, theirs, place, rows):
    tokens = own.shape[0]

    def kernel(place, own, mine, theirs, share):
        share[:tokens, :] = own[...]
        for k in range(3):
            here = pl.ds((k + 1) * tokens, tokens)
            half = slice(k * 2 * rows, (k + 1) * 2 * rows)
            a, b = mine[:, half], theirs[:, half]
            share[here, : 2 * rows] = jnp.where(place[1] == 0, a, b)
            share[here, 2 * rows :] = jnp.where(place[1] == 0, b, a)

    vmem = pl.BlockSpec(memory_space=pltpu.VMEM)
    return pl.pallas_call(
        kernel,
        out_shape=jax.ShapeDtypeStruct((4 * tokens, 4 * rows), jnp.bfloat16),
        in_specs=[pl.BlockSpec(memory_space=pltpu.SMEM), vmem, vmem, vmem],
        out_specs=vmem,
        compiler_params=pltpu.CompilerParams(vmem_limit_bytes=8 << 20),
        cost_estimate=EAGER,
    )(place, own, mine, theirs)


def add_tail(parts, arrived):
    rows = parts[0].shape[0]
    widths = [part.shape[1] for part in parts]

    def kernel(*refs):
        out, at = refs[-1], 0
        for part, other, width in zip(refs, refs[len(parts) :], widths):
            out[:, at : at + width] = (part[...] + other[-rows:, :].astype(jnp.float32)).astype(jnp.bfloat16)
            at += width

    vmem = pl.BlockSpec(memory_space=pltpu.VMEM)
    return pl.pallas_call(
        kernel,
        out_shape=jax.ShapeDtypeStruct((rows, sum(widths)), jnp.bfloat16),
        in_specs=[vmem] * (2 * len(parts)),
        out_specs=vmem,
        compiler_params=pltpu.CompilerParams(vmem_limit_bytes=8 << 20),
        cost_estimate=EAGER,
    )(*parts, *arrived)


def flat(column):
    return jnp.broadcast_to(column, (128, 128)).T[0:1, :]


def upright(row):
    return jnp.broadcast_to(row, (128, 128)).T[:, 0:1]


def sum_up(kept, from_low, from_high, last_a, last_b, scale):
    rows = kept[0].shape[0]
    q = rows // 2
    widths = [part.shape[1] for part in kept]
    units = sum(widths)

    def kernel(*refs):
        kept_refs, low_refs, high_refs = refs[:2], refs[2:4], refs[4:6]
        last_refs, grad, row_part = refs[6:8], refs[8], refs[9]
        for h, arrived in enumerate((low_refs, high_refs)):
            for at in range(0, q, 128):
                total = jnp.zeros((128, 1), jnp.float32)
                here = slice(h * q + at, h * q + at + 128)
                column = 0
                for part, other, width in zip(kept_refs, arrived, widths):
                    there = slice(column, column + width)
                    value = part[here, :] + other[at : at + 128, :].astype(jnp.float32)
                    value = (value + last_refs[h][at : at + 128, there].astype(jnp.float32)) * scale
                    grad[here, there] = value
                    total = total + jnp.sum(value * value + 1e-30, axis=1, keepdims=True)
                    column += width
                row_part[:, here] = flat(total)

    vmem = pl.BlockSpec(memory_space=pltpu.VMEM)
    return pl.pallas_call(
        kernel,
        out_shape=[jax.ShapeDtypeStruct((rows, units), jnp.float32), jax.ShapeDtypeStruct((1, rows), jnp.float32)],
        in_specs=[vmem] * 8,
        out_specs=[vmem] * 2,
        compiler_params=pltpu.CompilerParams(vmem_limit_bytes=14 << 20),
        cost_estimate=EAGER,
    )(*kept, *from_low, *from_high, last_a, last_b)


def column_sums(grad, row_sum, row_moment, decay, total_units):
    rows, units = grad.shape

    def kernel(grad, row_sum, row_moment, row_moment_new, sums):
        new = decay * row_moment[...] + (1.0 - decay) * (row_sum[...] / total_units)
        row_moment_new[...] = new
        sums[:, 2 * units :] = jnp.broadcast_to(jnp.sum(new, axis=1, keepdims=True), (1, 128))
        inverse = [1.0 / upright(new[:, at : at + 128]) for at in range(0, rows, 128)]
        for column in range(0, units, 256):
            there = slice(column, column + 256)
            squares, scaled = jnp.zeros((1, 256), jnp.float32), jnp.zeros((1, 256), jnp.float32)
            for n, at in enumerate(range(0, rows, 128)):
                power = grad[at : at + 128, there]
                power = power * power
                squares = squares + jnp.sum(power + 1e-30, axis=0, keepdims=True)
                scaled = scaled + jnp.sum(power * inverse[n], axis=0, keepdims=True)
            sums[:, there] = squares
            sums[:, units + column : units + column + 256] = scaled

    vmem = pl.BlockSpec(memory_space=pltpu.VMEM)
    return pl.pallas_call(
        kernel,
        out_shape=[
            jax.ShapeDtypeStruct((1, rows), jnp.float32),
            jax.ShapeDtypeStruct((1, 2 * units + 128), jnp.float32),
        ],
        in_specs=[vmem] * 3,
        out_specs=[vmem] * 2,
        compiler_params=pltpu.CompilerParams(vmem_limit_bytes=14 << 20),
        cost_estimate=EAGER,
    )(grad, row_sum, row_moment)


def column_step(sums, col_moment, decay, total_rows):
    units = col_moment.shape[1]

    def kernel(sums, col_moment, col_moment_new, terms, flat_new):
        total = jnp.zeros((1, 128), jnp.float32)
        for at in range(0, units, 128):
            here = slice(at, at + 128)
            new = decay * col_moment[:, here] + (1.0 - decay) * (sums[:, here] / total_rows)
            col_moment_new[:, here] = new
            flat_new[here] = new[0]
            total = total + sums[:, units + at : units + at + 128] / new
        terms[...] = total

    vmem = pl.BlockSpec(memory_space=pltpu.VMEM)
    return pl.pallas_call(
        kernel,
        out_shape=[jax.ShapeDtypeStruct(shape, jnp.float32) for shape in ((1, units), (1, 128), (units,))],
        in_specs=[vmem] * 2,
        out_specs=[vmem] * 3,
        compiler_params=pltpu.CompilerParams(vmem_limit_bytes=4 << 20),
        cost_estimate=EAGER,
    )(sums, col_moment)


def final_update(grad, row_moment_new, col_moment_new, terms, sums, total_rows, total_units):
    rows, units = grad.shape
    tile = units // 2

    def kernel(grad, row_moment_new, col_moment_new, terms, row_total, update, row_mean):
        mean = row_total[...] / total_rows
        row_mean[...] = mean
        square_sum = mean[:, 0:1] * jnp.sum(terms[...], axis=1, keepdims=True)
        clip = jnp.maximum(1.0, jnp.sqrt(square_sum / (total_rows * total_units)))
        col_factor = 1.0 / jnp.sqrt(col_moment_new[...])
        for at in range(0, rows, 128):
            here = slice(at, at + 128)
            row_factor = jnp.sqrt(mean / row_moment_new[:, here]) / clip
            update[here, :] = grad[here, :] * upright(row_factor) * col_factor

    def fixed(width, block=0):
        return pl.BlockSpec((1, width), lambda i: (0, block))

    return pl.pallas_call(
        kernel,
        grid=(units // tile,),
        out_shape=[jax.ShapeDtypeStruct((rows, units), jnp.float32), jax.ShapeDtypeStruct((1, 128), jnp.float32)],
        in_specs=[
            pl.BlockSpec((rows, tile), lambda i: (0, i)),
            fixed(rows),
            pl.BlockSpec((1, tile), lambda i: (0, i)),
            fixed(128),
            fixed(128, 2 * units // 128),
        ],
        out_specs=[pl.BlockSpec((rows, tile), lambda i: (0, i)), fixed(128)],
        compiler_params=pltpu.CompilerParams(vmem_limit_bytes=14 << 20),
        cost_estimate=EAGER,
    )(grad, row_moment_new, col_moment_new, terms, sums)


def products(share, groups, steps):
    pieces = [(piece, group[1]) for group in groups for piece in group[0]]
    bounds = [(output, group[1]) for group in groups for output in group[2]]

    def kernel(*refs):
        share_ref, ins = refs[0], refs[1 : 1 + len(pieces)]
        outs, stacks = refs[1 + len(pieces) : -len(groups)], refs[-len(groups) :]
        n = o = 0
        for (own, _, outputs, over_rows), stack in zip(groups, stacks):
            at = 0
            for piece, _ in own:
                stack[at : at + piece.shape[0], :] = ins[n][...]
                at += piece.shape[0]
                n += 1
            for ranges, kind in outputs:
                if over_rows:
                    side = jnp.concatenate([share_ref[:, begin:end] for begin, end in ranges], axis=1)
                    value = lax.dot_general(
                        side, stack[...], (((0,), (0,)), ((), ())), preferred_element_type=jnp.float32
                    )
                else:
                    side = jnp.concatenate([share_ref[begin:end, :] for begin, end in ranges], axis=0)
                    value = jnp.dot(side, stack[...], preferred_element_type=jnp.float32)
                outs[o][...] = value.astype(kind)
                o += 1

    def height(ranges):
        return sum(end - begin for begin, end in ranges)

    return pl.pallas_call(
        kernel,
        grid=(steps,),
        out_shape=[jax.ShapeDtypeStruct((height(ranges), columns), kind) for (ranges, kind), columns in bounds],
        in_specs=[pl.BlockSpec(share.shape, lambda i: (0, 0))]
        + [
            pl.BlockSpec((piece.shape[0], columns // steps), lambda i, skip=first * steps // columns: (0, i + skip))
            for (piece, first), columns in pieces
        ],
        out_specs=[pl.BlockSpec((height(ranges), columns // steps), lambda i: (0, i)) for (ranges, _), columns in bounds],
        scratch_shapes=[
            pltpu.VMEM((sum(piece.shape[0] for piece, _ in group[0]), group[1] // steps), jnp.bfloat16) for group in groups
        ],
        compiler_params=pltpu.CompilerParams(vmem_limit_bytes=14 << 20),
        cost_estimate=EAGER,
    )(share, *[piece for (piece, _), _ in pieces])


def staged_products(out_grad, gate_pre, up_pre, down_weight):
    x_bit, y_bit, z_bit, w_bit = 1, 2, 4, 8
    me, core = lax.axis_index("dp"), lax.axis_index("mp")
    tokens, units = gate_pre.shape
    rows = down_weight.shape[0]
    q, t = rows // 2, tokens // 2
    steps = 5
    split = units // 2
    barrier = lax.optimization_barrier
    place = jnp.stack([me, core]).astype(jnp.int32)
    own, right, message1, message2, message3 = first_stage(out_grad, gate_pre, up_pre, place, rows)

    extra, every, whole = (split, 2 * rows), (0, tokens), (0, units)
    left1, left2, message3 = flip(message1, z_bit), flip(message2, w_bit), flip(message3, z_bit | w_bit)
    weight1, weight2 = flip(down_weight, x_bit), flip(down_weight, y_bit)
    message3, weight1, weight2 = barrier((message3, weight1, weight2))
    to_y, to_x = cut([weight1, weight2], [(0, (0, q), whole, 0, 0), (1, (q, q), whole, 1, 0)], [(q, units)] * 2)
    weight3a, weight3b = flip(to_y, y_bit), flip(to_x, x_bit)
    left1, left2, message3, right, _, _ = barrier((left1, left2, message3, right, to_y, to_x))
    to_z, mine = cut(
        [left1, left2, message3, right],
        [
            (1, every, (0, split), 0, 0),
            (3, every, (0, units - split), 0, split),
            (0, every, extra, 1, 0),
            (1, every, extra, 1, 2 * rows),
            (2, every, (0, 2 * rows), 1, 4 * rows),
        ],
        [(tokens, units), (tokens, 6 * rows)],
    )
    from_near = flip(to_z, z_bit)
    right2 = flip(right, w_bit)
    theirs = flip(mine, 1, "mp")
    share = assemble(own, mine, theirs, place, rows)

    def low_sent(size):
        return [(2 * size, 3 * size), (6 * size, 7 * size)]

    def high_sent(size):
        return [(5 * size, 6 * size), (7 * size, 8 * size)]

    def sent(size):
        return [(low_sent(size), jnp.bfloat16), (high_sent(size), jnp.bfloat16)]

    def kept(size):
        ranges = [(0, 2 * size)], [(4 * size, 5 * size)], [(3 * size, 4 * size)]
        return [(r, jnp.float32) for r in ranges]

    from_near, right2, share = barrier((from_near, right2, share))
    right3 = flip(right2, z_bit)
    lefts = [(message1, 0), (left1, 0), (left2, 0), (from_near, 0)]
    left_to_x, left_to_y = products(share, [(lefts, split, sent(q), True)], steps)
    left_from_x, left_from_y = flip(left_to_x, x_bit), flip(left_to_y, y_bit)

    share, _ = barrier((share, left_to_x))
    weights = [(piece, 0) for piece in (down_weight, weight1, weight2, weight3a, weight3b)]
    to_w, to_z = products(
        share, [(weights, units, [(high_sent(t), jnp.bfloat16), (low_sent(t), jnp.bfloat16)], False)], steps
    )
    right3, share, to_w, to_z = barrier((right3, share, to_w, to_z))
    from_w, from_z = flip(to_w, w_bit), flip(to_z, z_bit)
    rights = [(right, 0), (from_near, split), (right2, 0), (right3, 0)]
    right_to_x, right_to_y = products(share, [(rights, units - split, sent(q), True)], steps)
    right_from_x, right_from_y = flip(right_to_x, x_bit), flip(right_to_y, y_bit)
    share, left_from_x, left_from_y, _ = barrier((share, left_from_x, left_from_y, right_to_x))
    left_parts = products(share, [(lefts, split, kept(q), True)], steps)
    parts = products(share, [(rights, units - split, kept(q), True), (weights, units, kept(t), False)], steps)

    grad_a = flip(add_tail([left_parts[1], parts[1]], [left_from_x, right_from_x]), y_bit)
    grad_b = flip(add_tail([left_parts[2], parts[2]], [left_from_y, right_from_y]), x_bit)
    to_w, to_z = add_tail([parts[4]], [from_z]), add_tail([parts[5]], [from_w])
    last_a, last_b = flip(to_w, w_bit), flip(to_z, z_bit)
    grad_a, grad_b, _, _ = barrier((grad_a, grad_b, to_w, to_z))
    grad, row_part = sum_up(
        [left_parts[0], parts[0]],
        [left_from_x, right_from_x],
        [left_from_y, right_from_y],
        grad_a,
        grad_b,
        1.0 / math.sqrt(tokens * lax.axis_size("dp")),
    )

    row_sum = lax.psum(row_part, "mp")
    return grad, row_sum, (parts[3], from_z[:t], from_w[:t], last_a, last_b)


def local(out_grad, gate_pre, up_pre, down_weight, row_moment, col_moment):
    size = lax.axis_size("dp")
    rows, units = down_weight.shape
    tokens = out_grad.shape[0]
    all_bits = [1 << b for b in range(size.bit_length() - 1)]
    decay = 1.0 - TRAIN_STEP ** (-0.8)
    total_rows = rows * size
    total_units = units * lax.axis_size("mp")
    staged = size == 16 and lax.axis_size("mp") == 2 and rows % 256 == 0 and tokens % 32 == 0 and units % 2560 == 0
    if staged:
        grad, row_sum, terms = staged_products(out_grad, gate_pre, up_pre, down_weight)
        row_moment_new, sums = column_sums(grad, row_sum, row_moment[None, :], decay, total_units)
        sums = group_sum(sums[0], all_bits[:INNER_BITS])
        own_part, from_low, from_high, last_a, last_b = terms
        arrived = jnp.concatenate([from_low, from_high], axis=0).astype(jnp.float32)
        partial, sums = lax.optimization_barrier((own_part + arrived, sums))
        hidden_grad = partial + jnp.concatenate([last_a, last_b], axis=0).astype(jnp.float32)
        gate_grad, up_grad = gradients(hidden_grad, gate_pre, up_pre)
        first, second, third = [flip(sums, bits) for bits in (4, 8, 12)]
        first, second, third, gate_grad, up_grad = lax.optimization_barrier((first, second, third, gate_grad, up_grad))
        sums = ((sums + first) + (second + third))[None, :]
        moment_row, ratios, col_moment_new = column_step(sums, col_moment[None, :], decay, total_rows)
        ratios = lax.psum(ratios, "mp")
        update, row_mean = final_update(grad, row_moment_new, moment_row, ratios, sums, total_rows, total_units)
        row_moment_new, row_mean = row_moment_new[0], row_mean[0, 0]
    else:
        product, hidden_grad = general_products(
            out_grad, gate_pre, up_pre, down_weight, all_bits[:INNER_BITS], all_bits[INNER_BITS:]
        )
        grad = product * (1.0 / math.sqrt(tokens * size))
        powers = grad * grad
        squares = powers + 1e-30
        row_sum = lax.psum(jnp.sum(squares, axis=1), "mp")
        row_moment_new = decay * row_moment + (1.0 - decay) * (row_sum / total_units)
        col_part = jnp.sum(squares, axis=0)
        scaled_part = jnp.sum(powers / row_moment_new[:, None], axis=0)
        sums = jnp.concatenate([col_part, scaled_part, jnp.broadcast_to(jnp.sum(row_moment_new), (128,))])
        sums = group_sum(sums, all_bits)
        col_moment_new = decay * col_moment + (1.0 - decay) * (sums[:units] / total_rows)
        row_mean = sums[2 * units] / total_rows
        ratios = lax.psum(jnp.sum(sums[units : 2 * units] / col_moment_new), "mp")
        clip_norm = jnp.sqrt(row_mean * ratios / (total_rows * total_units))
        row_factor = jnp.sqrt(row_mean / row_moment_new) / jnp.maximum(1.0, clip_norm)
        col_factor = 1.0 / jnp.sqrt(col_moment_new)
        update = grad * row_factor[:, None] * col_factor[None, :]
        gate_grad, up_grad = gradients(hidden_grad, gate_pre, up_pre)

    return (update, row_moment_new, col_moment_new, row_mean, gate_grad, up_grad)


def solution(mesh):
    in_specs = (P("dp", None), P("dp", "mp"), P("dp", "mp"), P("dp", "mp"), P("dp"), P("mp"))
    out_specs = (P("dp", "mp"), P("dp"), P("mp"), P(), P("dp", "mp"), P("dp", "mp"))
    return jax.shard_map(local, mesh=mesh, in_specs=in_specs, out_specs=out_specs, check_vma=False)
```

```python
import math

import jax
import jax.numpy as jnp
from jax import lax
from jax.experimental import pallas as pl
from jax.experimental.pallas import tpu as pltpu
from jax.sharding import PartitionSpec as P

TRAIN_STEP = 3
INNER_BITS = 2
EAGER = pl.CostEstimate(flops=0, bytes_accessed=0, transcendentals=0)


def gelu_parts(values):
    factor = math.sqrt(2.0 / math.pi)
    inner = factor * (values + 0.044715 * values * values * values)
    tangent = jnp.tanh(inner)
    activated = 0.5 * values * (1.0 + tangent)
    derivative = 0.5 * (1.0 + tangent) + 0.5 * values * (1.0 - tangent * tangent) * factor * (
        1.0 + 3.0 * 0.044715 * values * values
    )
    return (activated, derivative)


def gradients(hidden_grad, gate_pre, up_pre):
    activated, derivative = gelu_parts(gate_pre.astype(jnp.float32))
    gate_grad = (hidden_grad * up_pre.astype(jnp.float32) * derivative).astype(jnp.bfloat16)
    return gate_grad, (hidden_grad * activated).astype(jnp.bfloat16)


def flip(value, bits, axis="dp"):
    size = lax.axis_size(axis)
    return lax.ppermute(value, axis, [(i, i ^ bits) for i in range(size)])


def group_sum(value, bits):
    for at in range(0, len(bits), 2):
        pair = bits[at : at + 2]
        if len(pair) == 2:
            first, second = flip(value, pair[0]), flip(value, pair[1])
            value = (value + first) + (second + flip(value, pair[0] | pair[1]))
        else:
            value = value + flip(value, pair[0])
    return value


def general_products(out_grad, gate_pre, up_pre, down_weight, inner_bits, outer_bits):
    size = lax.axis_size("dp")
    me = lax.axis_index("dp")
    tokens, rows = out_grad.shape[0], down_weight.shape[0]
    inner = 2 ** len(inner_bits)
    activated, _ = gelu_parts(gate_pre.astype(jnp.float32))
    hidden = (activated * up_pre.astype(jnp.float32)).astype(jnp.bfloat16)
    by_block = out_grad.reshape(tokens, size, rows).transpose(1, 0, 2)

    def features_of(k):
        picks = [lax.dynamic_index_in_dim(by_block, me ^ (k * inner + j), 0, keepdims=False) for j in range(inner)]
        return jnp.concatenate(picks, axis=1)

    def gather(block, bits):
        blocks = [block]
        for bit in bits:
            blocks = blocks + [flip(b, bit) for b in blocks]
        return jnp.concatenate(blocks, axis=0)

    def scatter(values, bits):
        for level in reversed(range(len(bits))):
            count = 2**level
            values = [
                values[j] + flip(values[j + count].astype(jnp.bfloat16), bits[level]).astype(jnp.float32)
                for j in range(count)
            ]
        return values[0]

    shares = [features_of(0)] + [flip(features_of(k), k * inner) for k in range(1, size // inner)]
    share = jnp.concatenate(shares, axis=0)
    hidden_all = gather(hidden, outer_bits)
    weight_all = gather(down_weight, inner_bits)
    product = scatter(
        [
            lax.dot_general(
                share[:, j * rows : (j + 1) * rows],
                hidden_all,
                (((0,), (0,)), ((), ())),
                preferred_element_type=jnp.float32,
            )
            for j in range(inner)
        ],
        inner_bits,
    )
    hidden_grad = scatter(
        [jnp.dot(x, weight_all, preferred_element_type=jnp.float32) for x in shares],
        outer_bits,
    )
    return product, hidden_grad


def first_stage(out_grad, gate_pre, up_pre, place, rows):
    tokens, units = gate_pre.shape
    half = units // 2
    step = 64

    def kernel(place, source, gate, up, own, right, message1, message2, message3):
        me, core = place[0], place[1]

        def block(k, j):
            return pl.ds(pl.multiple_of((me ^ (4 * k + j)) * rows, rows), rows)

        activated, _ = gelu_parts(gate[...].astype(jnp.float32))
        value = (activated * up[...].astype(jnp.float32)).astype(jnp.bfloat16)
        right[...] = value[:, half:]
        message1[:, :half] = value[:, :half]
        message2[:, :half] = value[:, :half]
        for j in range(4):
            own[:, j * rows : (j + 1) * rows] = source[:, block(0, j)]
        for k, target, base in ((1, message1, half), (2, message2, half), (3, message3, 0)):
            for j in range(2):
                target[:, base + j * rows : base + (j + 1) * rows] = source[:, block(k, 2 * core + j)]

    widths = [4 * rows, units - half, half + 2 * rows, half + 2 * rows, 2 * rows]
    return pl.pallas_call(
        kernel,
        grid=(tokens // step,),
        out_shape=[jax.ShapeDtypeStruct((tokens, width), jnp.bfloat16) for width in widths],
        in_specs=[pl.BlockSpec(memory_space=pltpu.SMEM)]
        + [pl.BlockSpec((step, array.shape[1]), lambda i: (i, 0)) for array in (out_grad, gate_pre, up_pre)],
        out_specs=[pl.BlockSpec((step, width), lambda i: (i, 0)) for width in widths],
        compiler_params=pltpu.CompilerParams(vmem_limit_bytes=56 << 20),
        cost_estimate=EAGER,
    )(place, out_grad, gate_pre, up_pre)


def cut(sources, parts, shapes):
    def kernel(*refs):
        ins, outs, sems = refs[: len(sources)], refs[len(sources) : -1], refs[-1]
        copies = [
            pltpu.make_async_copy(
                ins[i].at[pl.ds(*rows), pl.ds(*columns)], outs[o].at[:, pl.ds(at, columns[1])], sems.at[n]
            )
            for n, (i, rows, columns, o, at) in enumerate(parts)
        ]
        for copy in copies:
            copy.start()
        for copy in copies:
            copy.wait()

    return pl.pallas_call(
        kernel,
        out_shape=[jax.ShapeDtypeStruct(shape, jnp.bfloat16) for shape in shapes],
        in_specs=[pl.BlockSpec(memory_space=pltpu.HBM)] * len(sources),
        out_specs=[pl.BlockSpec(memory_space=pltpu.HBM)] * len(shapes),
        scratch_shapes=[pltpu.SemaphoreType.DMA((len(parts),))],
        compiler_params=pltpu.CompilerParams(vmem_limit_bytes=1 << 20),
        cost_estimate=EAGER,
    )(*sources)


def assemble(own, mine, theirs, place, rows):
    tokens = own.shape[0]

    def kernel(place, own, mine, theirs, share):
        share[:tokens, :] = own[...]
        for k in range(3):
            here = pl.ds((k + 1) * tokens, tokens)
            half = slice(k * 2 * rows, (k + 1) * 2 * rows)
            a, b = mine[:, half], theirs[:, half]
            share[here, : 2 * rows] = jnp.where(place[1] == 0, a, b)
            share[here, 2 * rows :] = jnp.where(place[1] == 0, b, a)

    vmem = pl.BlockSpec(memory_space=pltpu.VMEM)
    return pl.pallas_call(
        kernel,
        out_shape=jax.ShapeDtypeStruct((4 * tokens, 4 * rows), jnp.bfloat16),
        in_specs=[pl.BlockSpec(memory_space=pltpu.SMEM), vmem, vmem, vmem],
        out_specs=vmem,
        compiler_params=pltpu.CompilerParams(vmem_limit_bytes=8 << 20),
        cost_estimate=EAGER,
    )(place, own, mine, theirs)


def add_tail(parts, arrived):
    rows = parts[0].shape[0]
    widths = [part.shape[1] for part in parts]

    def kernel(*refs):
        out, at = refs[-1], 0
        for part, other, width in zip(refs, refs[len(parts) :], widths):
            out[:, at : at + width] = (part[...] + other[-rows:, :].astype(jnp.float32)).astype(jnp.bfloat16)
            at += width

    vmem = pl.BlockSpec(memory_space=pltpu.VMEM)
    return pl.pallas_call(
        kernel,
        out_shape=jax.ShapeDtypeStruct((rows, sum(widths)), jnp.bfloat16),
        in_specs=[vmem] * (2 * len(parts)),
        out_specs=vmem,
        compiler_params=pltpu.CompilerParams(vmem_limit_bytes=8 << 20),
        cost_estimate=EAGER,
    )(*parts, *arrived)


def flat(column):
    return jnp.broadcast_to(column, (128, 128)).T[0:1, :]


def upright(row):
    return jnp.broadcast_to(row, (128, 128)).T[:, 0:1]


def sum_up(kept, from_low, from_high, last_a, last_b, scale):
    rows = kept[0].shape[0]
    q = rows // 2
    widths = [part.shape[1] for part in kept]
    units = sum(widths)

    def kernel(*refs):
        kept_refs, low_refs, high_refs = refs[:2], refs[2:4], refs[4:6]
        last_refs, grad, row_part = refs[6:8], refs[8], refs[9]
        for h, arrived in enumerate((low_refs, high_refs)):
            for at in range(0, q, 128):
                total = jnp.zeros((128, 1), jnp.float32)
                here = slice(h * q + at, h * q + at + 128)
                column = 0
                for part, other, width in zip(kept_refs, arrived, widths):
                    there = slice(column, column + width)
                    value = part[here, :] + other[at : at + 128, :].astype(jnp.float32)
                    value = (value + last_refs[h][at : at + 128, there].astype(jnp.float32)) * scale
                    grad[here, there] = value
                    total = total + jnp.sum(value * value + 1e-30, axis=1, keepdims=True)
                    column += width
                row_part[:, here] = flat(total)

    vmem = pl.BlockSpec(memory_space=pltpu.VMEM)
    return pl.pallas_call(
        kernel,
        out_shape=[jax.ShapeDtypeStruct((rows, units), jnp.float32), jax.ShapeDtypeStruct((1, rows), jnp.float32)],
        in_specs=[vmem] * 8,
        out_specs=[vmem] * 2,
        compiler_params=pltpu.CompilerParams(vmem_limit_bytes=14 << 20),
        cost_estimate=EAGER,
    )(*kept, *from_low, *from_high, last_a, last_b)


def column_sums(grad, row_sum, row_moment, decay, total_units):
    rows, units = grad.shape

    def kernel(grad, row_sum, row_moment, row_moment_new, sums):
        new = decay * row_moment[...] + (1.0 - decay) * (row_sum[...] / total_units)
        row_moment_new[...] = new
        sums[:, 2 * units :] = jnp.broadcast_to(jnp.sum(new, axis=1, keepdims=True), (1, 128))
        inverse = [1.0 / upright(new[:, at : at + 128]) for at in range(0, rows, 128)]
        for column in range(0, units, 256):
            there = slice(column, column + 256)
            squares, scaled = jnp.zeros((1, 256), jnp.float32), jnp.zeros((1, 256), jnp.float32)
            for n, at in enumerate(range(0, rows, 128)):
                power = grad[at : at + 128, there]
                power = power * power
                squares = squares + jnp.sum(power + 1e-30, axis=0, keepdims=True)
                scaled = scaled + jnp.sum(power * inverse[n], axis=0, keepdims=True)
            sums[:, there] = squares
            sums[:, units + column : units + column + 256] = scaled

    vmem = pl.BlockSpec(memory_space=pltpu.VMEM)
    return pl.pallas_call(
        kernel,
        out_shape=[
            jax.ShapeDtypeStruct((1, rows), jnp.float32),
            jax.ShapeDtypeStruct((1, 2 * units + 128), jnp.float32),
        ],
        in_specs=[vmem] * 3,
        out_specs=[vmem] * 2,
        compiler_params=pltpu.CompilerParams(vmem_limit_bytes=14 << 20),
        cost_estimate=EAGER,
    )(grad, row_sum, row_moment)


def column_step(sums, col_moment, decay, total_rows):
    units = col_moment.shape[1]

    def kernel(sums, col_moment, col_moment_new, terms, flat_new):
        total = jnp.zeros((1, 128), jnp.float32)
        for at in range(0, units, 128):
            here = slice(at, at + 128)
            new = decay * col_moment[:, here] + (1.0 - decay) * (sums[:, here] / total_rows)
            col_moment_new[:, here] = new
            flat_new[here] = new[0]
            total = total + sums[:, units + at : units + at + 128] / new
        terms[...] = total

    vmem = pl.BlockSpec(memory_space=pltpu.VMEM)
    return pl.pallas_call(
        kernel,
        out_shape=[jax.ShapeDtypeStruct(shape, jnp.float32) for shape in ((1, units), (1, 128), (units,))],
        in_specs=[vmem] * 2,
        out_specs=[vmem] * 3,
        compiler_params=pltpu.CompilerParams(vmem_limit_bytes=4 << 20),
        cost_estimate=EAGER,
    )(sums, col_moment)


def final_update(grad, row_moment_new, col_moment_new, terms, sums, total_rows, total_units):
    rows, units = grad.shape
    tile = units // 2

    def kernel(grad, row_moment_new, col_moment_new, terms, row_total, update, row_mean):
        mean = row_total[...] / total_rows
        row_mean[...] = mean
        square_sum = mean[:, 0:1] * jnp.sum(terms[...], axis=1, keepdims=True)
        clip = jnp.maximum(1.0, jnp.sqrt(square_sum / (total_rows * total_units)))
        col_factor = 1.0 / jnp.sqrt(col_moment_new[...])
        for at in range(0, rows, 128):
            here = slice(at, at + 128)
            row_factor = jnp.sqrt(mean / row_moment_new[:, here]) / clip
            update[here, :] = grad[here, :] * upright(row_factor) * col_factor

    def fixed(width, block=0):
        return pl.BlockSpec((1, width), lambda i: (0, block))

    return pl.pallas_call(
        kernel,
        grid=(units // tile,),
        out_shape=[jax.ShapeDtypeStruct((rows, units), jnp.float32), jax.ShapeDtypeStruct((1, 128), jnp.float32)],
        in_specs=[
            pl.BlockSpec((rows, tile), lambda i: (0, i)),
            fixed(rows),
            pl.BlockSpec((1, tile), lambda i: (0, i)),
            fixed(128),
            fixed(128, 2 * units // 128),
        ],
        out_specs=[pl.BlockSpec((rows, tile), lambda i: (0, i)), fixed(128)],
        compiler_params=pltpu.CompilerParams(vmem_limit_bytes=14 << 20),
        cost_estimate=EAGER,
    )(grad, row_moment_new, col_moment_new, terms, sums)


def products(share, groups, steps):
    pieces = [(piece, group[1]) for group in groups for piece in group[0]]
    bounds = [(output, group[1]) for group in groups for output in group[2]]

    def kernel(*refs):
        share_ref, ins = refs[0], refs[1 : 1 + len(pieces)]
        outs, stacks = refs[1 + len(pieces) : -len(groups)], refs[-len(groups) :]
        n = o = 0
        for (own, _, outputs, over_rows), stack in zip(groups, stacks):
            at = 0
            for piece, _ in own:
                stack[at : at + piece.shape[0], :] = ins[n][...]
                at += piece.shape[0]
                n += 1
            for ranges, kind in outputs:
                if over_rows:
                    side = jnp.concatenate([share_ref[:, begin:end] for begin, end in ranges], axis=1)
                    value = lax.dot_general(
                        side, stack[...], (((0,), (0,)), ((), ())), preferred_element_type=jnp.float32
                    )
                else:
                    side = jnp.concatenate([share_ref[begin:end, :] for begin, end in ranges], axis=0)
                    value = jnp.dot(side, stack[...], preferred_element_type=jnp.float32)
                outs[o][...] = value.astype(kind)
                o += 1

    def height(ranges):
        return sum(end - begin for begin, end in ranges)

    return pl.pallas_call(
        kernel,
        grid=(steps,),
        out_shape=[jax.ShapeDtypeStruct((height(ranges), columns), kind) for (ranges, kind), columns in bounds],
        in_specs=[pl.BlockSpec(share.shape, lambda i: (0, 0))]
        + [
            pl.BlockSpec((piece.shape[0], columns // steps), lambda i, skip=first * steps // columns: (0, i + skip))
            for (piece, first), columns in pieces
        ],
        out_specs=[pl.BlockSpec((height(ranges), columns // steps), lambda i: (0, i)) for (ranges, _), columns in bounds],
        scratch_shapes=[
            pltpu.VMEM((sum(piece.shape[0] for piece, _ in group[0]), group[1] // steps), jnp.bfloat16) for group in groups
        ],
        compiler_params=pltpu.CompilerParams(vmem_limit_bytes=14 << 20),
        cost_estimate=EAGER,
    )(share, *[piece for (piece, _), _ in pieces])


def staged_products(out_grad, gate_pre, up_pre, down_weight):
    x_bit, y_bit, z_bit, w_bit = 1, 2, 4, 8
    me, core = lax.axis_index("dp"), lax.axis_index("mp")
    tokens, units = gate_pre.shape
    rows = down_weight.shape[0]
    q, t = rows // 2, tokens // 2
    steps = 5
    split = units // 2
    barrier = lax.optimization_barrier
    place = jnp.stack([me, core]).astype(jnp.int32)
    own, right, message1, message2, message3 = first_stage(out_grad, gate_pre, up_pre, place, rows)

    extra, every, whole = (split, 2 * rows), (0, tokens), (0, units)
    left1, left2, message3 = flip(message1, z_bit), flip(message2, w_bit), flip(message3, z_bit | w_bit)
    weight1, weight2 = flip(down_weight, x_bit), flip(down_weight, y_bit)
    message3, weight1, weight2 = barrier((message3, weight1, weight2))
    to_y, to_x = cut([weight1, weight2], [(0, (0, q), whole, 0, 0), (1, (q, q), whole, 1, 0)], [(q, units)] * 2)
    weight3a, weight3b = flip(to_y, y_bit), flip(to_x, x_bit)
    left1, left2, message3, right, _, _ = barrier((left1, left2, message3, right, to_y, to_x))
    to_z, mine = cut(
        [left1, left2, message3, right],
        [
            (1, every, (0, split), 0, 0),
            (3, every, (0, units - split), 0, split),
            (0, every, extra, 1, 0),
            (1, every, extra, 1, 2 * rows),
            (2, every, (0, 2 * rows), 1, 4 * rows),
        ],
        [(tokens, units), (tokens, 6 * rows)],
    )
    from_near = flip(to_z, z_bit)
    right2 = flip(right, w_bit)
    theirs = flip(mine, 1, "mp")
    share = assemble(own, mine, theirs, place, rows)

    def low_sent(size):
        return [(2 * size, 3 * size), (6 * size, 7 * size)]

    def high_sent(size):
        return [(5 * size, 6 * size), (7 * size, 8 * size)]

    def sent(size):
        return [(low_sent(size), jnp.bfloat16), (high_sent(size), jnp.bfloat16)]

    def kept(size):
        ranges = [(0, 2 * size)], [(4 * size, 5 * size)], [(3 * size, 4 * size)]
        return [(r, jnp.float32) for r in ranges]

    from_near, right2, share = barrier((from_near, right2, share))
    right3 = flip(right2, z_bit)
    lefts = [(message1, 0), (left1, 0), (left2, 0), (from_near, 0)]
    left_to_x, left_to_y = products(share, [(lefts, split, sent(q), True)], 2)
    left_from_x, left_from_y = flip(left_to_x, x_bit), flip(left_to_y, y_bit)

    share, _ = barrier((share, left_to_x))
    weights = [(piece, 0) for piece in (down_weight, weight1, weight2, weight3a, weight3b)]
    to_w, to_z = products(
        share, [(weights, units, [(high_sent(t), jnp.bfloat16), (low_sent(t), jnp.bfloat16)], False)], steps
    )
    right3, share, to_w, to_z = barrier((right3, share, to_w, to_z))
    from_w, from_z = flip(to_w, w_bit), flip(to_z, z_bit)
    rights = [(right, 0), (from_near, split), (right2, 0), (right3, 0)]
    right_to_x, right_to_y = products(share, [(rights, units - split, sent(q), True)], 2)
    right_from_x, right_from_y = flip(right_to_x, x_bit), flip(right_to_y, y_bit)
    share, left_from_x, left_from_y, _ = barrier((share, left_from_x, left_from_y, right_to_x))
    left_parts = products(share, [(lefts, split, kept(q), True)], steps)
    parts = products(share, [(rights, units - split, kept(q), True), (weights, units, kept(t), False)], steps)

    grad_a = flip(add_tail([left_parts[1], parts[1]], [left_from_x, right_from_x]), y_bit)
    grad_b = flip(add_tail([left_parts[2], parts[2]], [left_from_y, right_from_y]), x_bit)
    to_w, to_z = add_tail([parts[4]], [from_z]), add_tail([parts[5]], [from_w])
    last_a, last_b = flip(to_w, w_bit), flip(to_z, z_bit)
    grad_a, grad_b, _, _ = barrier((grad_a, grad_b, to_w, to_z))
    grad, row_part = sum_up(
        [left_parts[0], parts[0]],
        [left_from_x, right_from_x],
        [left_from_y, right_from_y],
        grad_a,
        grad_b,
        1.0 / math.sqrt(tokens * lax.axis_size("dp")),
    )

    row_sum = lax.psum(row_part, "mp")
    return grad, row_sum, (parts[3], from_z[:t], from_w[:t], last_a, last_b)


def local(out_grad, gate_pre, up_pre, down_weight, row_moment, col_moment):
    size = lax.axis_size("dp")
    rows, units = down_weight.shape
    tokens = out_grad.shape[0]
    all_bits = [1 << b for b in range(size.bit_length() - 1)]
    decay = 1.0 - TRAIN_STEP ** (-0.8)
    total_rows = rows * size
    total_units = units * lax.axis_size("mp")
    staged = size == 16 and lax.axis_size("mp") == 2 and rows % 256 == 0 and tokens % 32 == 0 and units % 2560 == 0
    if staged:
        grad, row_sum, terms = staged_products(out_grad, gate_pre, up_pre, down_weight)
        row_moment_new, sums = column_sums(grad, row_sum, row_moment[None, :], decay, total_units)
        sums = group_sum(sums[0], all_bits[:INNER_BITS])
        own_part, from_low, from_high, last_a, last_b = terms
        arrived = jnp.concatenate([from_low, from_high], axis=0).astype(jnp.float32)
        partial, sums = lax.optimization_barrier((own_part + arrived, sums))
        hidden_grad = partial + jnp.concatenate([last_a, last_b], axis=0).astype(jnp.float32)
        gate_grad, up_grad = gradients(hidden_grad, gate_pre, up_pre)
        first, second, third = [flip(sums, bits) for bits in (4, 8, 12)]
        first, second, third, gate_grad, up_grad = lax.optimization_barrier((first, second, third, gate_grad, up_grad))
        sums = ((sums + first) + (second + third))[None, :]
        moment_row, ratios, col_moment_new = column_step(sums, col_moment[None, :], decay, total_rows)
        ratios = lax.psum(ratios, "mp")
        update, row_mean = final_update(grad, row_moment_new, moment_row, ratios, sums, total_rows, total_units)
        row_moment_new, row_mean = row_moment_new[0], row_mean[0, 0]
    else:
        product, hidden_grad = general_products(
            out_grad, gate_pre, up_pre, down_weight, all_bits[:INNER_BITS], all_bits[INNER_BITS:]
        )
        grad = product * (1.0 / math.sqrt(tokens * size))
        powers = grad * grad
        squares = powers + 1e-30
        row_sum = lax.psum(jnp.sum(squares, axis=1), "mp")
        row_moment_new = decay * row_moment + (1.0 - decay) * (row_sum / total_units)
        col_part = jnp.sum(squares, axis=0)
        scaled_part = jnp.sum(powers / row_moment_new[:, None], axis=0)
        sums = jnp.concatenate([col_part, scaled_part, jnp.broadcast_to(jnp.sum(row_moment_new), (128,))])
        sums = group_sum(sums, all_bits)
        col_moment_new = decay * col_moment + (1.0 - decay) * (sums[:units] / total_rows)
        row_mean = sums[2 * units] / total_rows
        ratios = lax.psum(jnp.sum(sums[units : 2 * units] / col_moment_new), "mp")
        clip_norm = jnp.sqrt(row_mean * ratios / (total_rows * total_units))
        row_factor = jnp.sqrt(row_mean / row_moment_new) / jnp.maximum(1.0, clip_norm)
        col_factor = 1.0 / jnp.sqrt(col_moment_new)
        update = grad * row_factor[:, None] * col_factor[None, :]
        gate_grad, up_grad = gradients(hidden_grad, gate_pre, up_pre)

    return (update, row_moment_new, col_moment_new, row_mean, gate_grad, up_grad)


def solution(mesh):
    in_specs = (P("dp", None), P("dp", "mp"), P("dp", "mp"), P("dp", "mp"), P("dp"), P("mp"))
    out_specs = (P("dp", "mp"), P("dp"), P("mp"), P(), P("dp", "mp"), P("dp", "mp"))
    return jax.shard_map(local, mesh=mesh, in_specs=in_specs, out_specs=out_specs, check_vma=False)
```

```python
import math

import jax
import jax.numpy as jnp
from jax import lax
from jax.experimental import pallas as pl
from jax.experimental.pallas import tpu as pltpu
from jax.sharding import PartitionSpec as P

TRAIN_STEP = 3
INNER_BITS = 2
EAGER = pl.CostEstimate(flops=0, bytes_accessed=0, transcendentals=0)


def gelu_parts(values):
    factor = math.sqrt(2.0 / math.pi)
    inner = factor * (values + 0.044715 * values * values * values)
    tangent = jnp.tanh(inner)
    activated = 0.5 * values * (1.0 + tangent)
    derivative = 0.5 * (1.0 + tangent) + 0.5 * values * (1.0 - tangent * tangent) * factor * (
        1.0 + 3.0 * 0.044715 * values * values
    )
    return (activated, derivative)


def gradients(hidden_grad, gate_pre, up_pre):
    activated, derivative = gelu_parts(gate_pre.astype(jnp.float32))
    gate_grad = (hidden_grad * up_pre.astype(jnp.float32) * derivative).astype(jnp.bfloat16)
    return gate_grad, (hidden_grad * activated).astype(jnp.bfloat16)


def flip(value, bits, axis="dp"):
    size = lax.axis_size(axis)
    return lax.ppermute(value, axis, [(i, i ^ bits) for i in range(size)])


def group_sum(value, bits):
    for at in range(0, len(bits), 2):
        pair = bits[at : at + 2]
        if len(pair) == 2:
            first, second = flip(value, pair[0]), flip(value, pair[1])
            value = (value + first) + (second + flip(value, pair[0] | pair[1]))
        else:
            value = value + flip(value, pair[0])
    return value


def general_products(out_grad, gate_pre, up_pre, down_weight, inner_bits, outer_bits):
    size = lax.axis_size("dp")
    me = lax.axis_index("dp")
    tokens, rows = out_grad.shape[0], down_weight.shape[0]
    inner = 2 ** len(inner_bits)
    activated, _ = gelu_parts(gate_pre.astype(jnp.float32))
    hidden = (activated * up_pre.astype(jnp.float32)).astype(jnp.bfloat16)
    by_block = out_grad.reshape(tokens, size, rows).transpose(1, 0, 2)

    def features_of(k):
        picks = [lax.dynamic_index_in_dim(by_block, me ^ (k * inner + j), 0, keepdims=False) for j in range(inner)]
        return jnp.concatenate(picks, axis=1)

    def gather(block, bits):
        blocks = [block]
        for bit in bits:
            blocks = blocks + [flip(b, bit) for b in blocks]
        return jnp.concatenate(blocks, axis=0)

    def scatter(values, bits):
        for level in reversed(range(len(bits))):
            count = 2**level
            values = [
                values[j] + flip(values[j + count].astype(jnp.bfloat16), bits[level]).astype(jnp.float32)
                for j in range(count)
            ]
        return values[0]

    shares = [features_of(0)] + [flip(features_of(k), k * inner) for k in range(1, size // inner)]
    share = jnp.concatenate(shares, axis=0)
    hidden_all = gather(hidden, outer_bits)
    weight_all = gather(down_weight, inner_bits)
    product = scatter(
        [
            lax.dot_general(
                share[:, j * rows : (j + 1) * rows],
                hidden_all,
                (((0,), (0,)), ((), ())),
                preferred_element_type=jnp.float32,
            )
            for j in range(inner)
        ],
        inner_bits,
    )
    hidden_grad = scatter(
        [jnp.dot(x, weight_all, preferred_element_type=jnp.float32) for x in shares],
        outer_bits,
    )
    return product, hidden_grad


def first_stage(out_grad, gate_pre, up_pre, place, rows):
    tokens, units = gate_pre.shape
    half = units // 2
    step = 64

    def kernel(place, source, gate, up, own, right, message1, message2, message3):
        me, core = place[0], place[1]

        def block(k, j):
            return pl.ds(pl.multiple_of((me ^ (4 * k + j)) * rows, rows), rows)

        activated, _ = gelu_parts(gate[...].astype(jnp.float32))
        value = (activated * up[...].astype(jnp.float32)).astype(jnp.bfloat16)
        right[...] = value[:, half:]
        message1[:, :half] = value[:, :half]
        message2[:, :half] = value[:, :half]
        for j in range(4):
            own[:, j * rows : (j + 1) * rows] = source[:, block(0, j)]
        for k, target, base in ((1, message1, half), (2, message2, half), (3, message3, 0)):
            for j in range(2):
                target[:, base + j * rows : base + (j + 1) * rows] = source[:, block(k, 2 * core + j)]

    widths = [4 * rows, units - half, half + 2 * rows, half + 2 * rows, 2 * rows]
    return pl.pallas_call(
        kernel,
        grid=(tokens // step,),
        out_shape=[jax.ShapeDtypeStruct((tokens, width), jnp.bfloat16) for width in widths],
        in_specs=[pl.BlockSpec(memory_space=pltpu.SMEM)]
        + [pl.BlockSpec((step, array.shape[1]), lambda i: (i, 0)) for array in (out_grad, gate_pre, up_pre)],
        out_specs=[pl.BlockSpec((step, width), lambda i: (i, 0)) for width in widths],
        compiler_params=pltpu.CompilerParams(vmem_limit_bytes=56 << 20),
        cost_estimate=EAGER,
    )(place, out_grad, gate_pre, up_pre)


def cut(sources, parts, shapes):
    def kernel(*refs):
        ins, outs, sems = refs[: len(sources)], refs[len(sources) : -1], refs[-1]
        copies = [
            pltpu.make_async_copy(
                ins[i].at[pl.ds(*rows), pl.ds(*columns)], outs[o].at[:, pl.ds(at, columns[1])], sems.at[n]
            )
            for n, (i, rows, columns, o, at) in enumerate(parts)
        ]
        for copy in copies:
            copy.start()
        for copy in copies:
            copy.wait()

    return pl.pallas_call(
        kernel,
        out_shape=[jax.ShapeDtypeStruct(shape, jnp.bfloat16) for shape in shapes],
        in_specs=[pl.BlockSpec(memory_space=pltpu.HBM)] * len(sources),
        out_specs=[pl.BlockSpec(memory_space=pltpu.HBM)] * len(shapes),
        scratch_shapes=[pltpu.SemaphoreType.DMA((len(parts),))],
        compiler_params=pltpu.CompilerParams(vmem_limit_bytes=1 << 20),
        cost_estimate=EAGER,
    )(*sources)


def assemble(own, mine, theirs, place, rows):
    tokens = own.shape[0]

    def kernel(place, own, mine, theirs, share):
        share[:tokens, :] = own[...]
        for k in range(3):
            here = pl.ds((k + 1) * tokens, tokens)
            half = slice(k * 2 * rows, (k + 1) * 2 * rows)
            a, b = mine[:, half], theirs[:, half]
            share[here, : 2 * rows] = jnp.where(place[1] == 0, a, b)
            share[here, 2 * rows :] = jnp.where(place[1] == 0, b, a)

    vmem = pl.BlockSpec(memory_space=pltpu.VMEM)
    return pl.pallas_call(
        kernel,
        out_shape=jax.ShapeDtypeStruct((4 * tokens, 4 * rows), jnp.bfloat16),
        in_specs=[pl.BlockSpec(memory_space=pltpu.SMEM), vmem, vmem, vmem],
        out_specs=vmem,
        compiler_params=pltpu.CompilerParams(vmem_limit_bytes=8 << 20),
        cost_estimate=EAGER,
    )(place, own, mine, theirs)


def add_tail(parts, arrived):
    rows = parts[0].shape[0]
    widths = [part.shape[1] for part in parts]

    def kernel(*refs):
        out, at = refs[-1], 0
        for part, other, width in zip(refs, refs[len(parts) :], widths):
            out[:, at : at + width] = (part[...] + other[-rows:, :].astype(jnp.float32)).astype(jnp.bfloat16)
            at += width

    vmem = pl.BlockSpec(memory_space=pltpu.VMEM)
    return pl.pallas_call(
        kernel,
        out_shape=jax.ShapeDtypeStruct((rows, sum(widths)), jnp.bfloat16),
        in_specs=[vmem] * (2 * len(parts)),
        out_specs=vmem,
        compiler_params=pltpu.CompilerParams(vmem_limit_bytes=8 << 20),
        cost_estimate=EAGER,
    )(*parts, *arrived)


def flat(column):
    return jnp.broadcast_to(column, (128, 128)).T[0:1, :]


def upright(row):
    return jnp.broadcast_to(row, (128, 128)).T[:, 0:1]


def sum_up(kept, from_low, from_high, last_a, last_b, scale):
    rows = kept[0].shape[0]
    q = rows // 2
    widths = [part.shape[1] for part in kept]
    units = sum(widths)

    def kernel(*refs):
        kept_refs, low_refs, high_refs = refs[:2], refs[2:4], refs[4:6]
        last_refs, grad, row_part = refs[6:8], refs[8], refs[9]
        for h, arrived in enumerate((low_refs, high_refs)):
            for at in range(0, q, 128):
                total = jnp.zeros((128, 1), jnp.float32)
                here = slice(h * q + at, h * q + at + 128)
                column = 0
                for part, other, width in zip(kept_refs, arrived, widths):
                    there = slice(column, column + width)
                    value = part[here, :] + other[at : at + 128, :].astype(jnp.float32)
                    value = (value + last_refs[h][at : at + 128, there].astype(jnp.float32)) * scale
                    grad[here, there] = value
                    total = total + jnp.sum(value * value + 1e-30, axis=1, keepdims=True)
                    column += width
                row_part[:, here] = flat(total)

    vmem = pl.BlockSpec(memory_space=pltpu.VMEM)
    return pl.pallas_call(
        kernel,
        out_shape=[jax.ShapeDtypeStruct((rows, units), jnp.float32), jax.ShapeDtypeStruct((1, rows), jnp.float32)],
        in_specs=[vmem] * 8,
        out_specs=[vmem] * 2,
        compiler_params=pltpu.CompilerParams(vmem_limit_bytes=14 << 20),
        cost_estimate=EAGER,
    )(*kept, *from_low, *from_high, last_a, last_b)


def column_sums(grad, row_sum, row_moment, decay, total_units):
    rows, units = grad.shape

    def kernel(grad, row_sum, row_moment, row_moment_new, sums):
        new = decay * row_moment[...] + (1.0 - decay) * (row_sum[...] / total_units)
        row_moment_new[...] = new
        sums[:, 2 * units :] = jnp.broadcast_to(jnp.sum(new, axis=1, keepdims=True), (1, 128))
        inverse = [1.0 / upright(new[:, at : at + 128]) for at in range(0, rows, 128)]
        for column in range(0, units, 256):
            there = slice(column, column + 256)
            squares, scaled = jnp.zeros((1, 256), jnp.float32), jnp.zeros((1, 256), jnp.float32)
            for n, at in enumerate(range(0, rows, 128)):
                power = grad[at : at + 128, there]
                power = power * power
                squares = squares + jnp.sum(power + 1e-30, axis=0, keepdims=True)
                scaled = scaled + jnp.sum(power * inverse[n], axis=0, keepdims=True)
            sums[:, there] = squares
            sums[:, units + column : units + column + 256] = scaled

    vmem = pl.BlockSpec(memory_space=pltpu.VMEM)
    return pl.pallas_call(
        kernel,
        out_shape=[
            jax.ShapeDtypeStruct((1, rows), jnp.float32),
            jax.ShapeDtypeStruct((1, 2 * units + 128), jnp.float32),
        ],
        in_specs=[vmem] * 3,
        out_specs=[vmem] * 2,
        compiler_params=pltpu.CompilerParams(vmem_limit_bytes=14 << 20),
        cost_estimate=EAGER,
    )(grad, row_sum, row_moment)


def column_step(sums, col_moment, decay, total_rows):
    units = col_moment.shape[1]

    def kernel(sums, col_moment, col_moment_new, terms, flat_new):
        total = jnp.zeros((1, 128), jnp.float32)
        for at in range(0, units, 128):
            here = slice(at, at + 128)
            new = decay * col_moment[:, here] + (1.0 - decay) * (sums[:, here] / total_rows)
            col_moment_new[:, here] = new
            flat_new[here] = new[0]
            total = total + sums[:, units + at : units + at + 128] / new
        terms[...] = total

    vmem = pl.BlockSpec(memory_space=pltpu.VMEM)
    return pl.pallas_call(
        kernel,
        out_shape=[jax.ShapeDtypeStruct(shape, jnp.float32) for shape in ((1, units), (1, 128), (units,))],
        in_specs=[vmem] * 2,
        out_specs=[vmem] * 3,
        compiler_params=pltpu.CompilerParams(vmem_limit_bytes=4 << 20),
        cost_estimate=EAGER,
    )(sums, col_moment)


def final_update(grad, row_moment_new, col_moment_new, terms, sums, total_rows, total_units):
    rows, units = grad.shape
    tile = units // 2

    def kernel(grad, row_moment_new, col_moment_new, terms, row_total, update, row_mean):
        mean = row_total[...] / total_rows
        row_mean[...] = mean
        square_sum = mean[:, 0:1] * jnp.sum(terms[...], axis=1, keepdims=True)
        clip = jnp.maximum(1.0, jnp.sqrt(square_sum / (total_rows * total_units)))
        col_factor = 1.0 / jnp.sqrt(col_moment_new[...])
        for at in range(0, rows, 128):
            here = slice(at, at + 128)
            row_factor = jnp.sqrt(mean / row_moment_new[:, here]) / clip
            update[here, :] = grad[here, :] * upright(row_factor) * col_factor

    def fixed(width, block=0):
        return pl.BlockSpec((1, width), lambda i: (0, block))

    return pl.pallas_call(
        kernel,
        grid=(units // tile,),
        out_shape=[jax.ShapeDtypeStruct((rows, units), jnp.float32), jax.ShapeDtypeStruct((1, 128), jnp.float32)],
        in_specs=[
            pl.BlockSpec((rows, tile), lambda i: (0, i)),
            fixed(rows),
            pl.BlockSpec((1, tile), lambda i: (0, i)),
            fixed(128),
            fixed(128, 2 * units // 128),
        ],
        out_specs=[pl.BlockSpec((rows, tile), lambda i: (0, i)), fixed(128)],
        compiler_params=pltpu.CompilerParams(vmem_limit_bytes=14 << 20),
        cost_estimate=EAGER,
    )(grad, row_moment_new, col_moment_new, terms, sums)


def products(share, groups, steps):
    pieces = [(piece, group[1]) for group in groups for piece in group[0]]
    bounds = [(output, group[1]) for group in groups for output in group[2]]

    def kernel(*refs):
        share_ref, ins = refs[0], refs[1 : 1 + len(pieces)]
        outs, stacks = refs[1 + len(pieces) : -len(groups)], refs[-len(groups) :]
        n = o = 0
        for (own, _, outputs, over_rows), stack in zip(groups, stacks):
            at = 0
            for piece, _ in own:
                stack[at : at + piece.shape[0], :] = ins[n][...]
                at += piece.shape[0]
                n += 1
            for ranges, kind in outputs:
                if over_rows:
                    side = jnp.concatenate([share_ref[:, begin:end] for begin, end in ranges], axis=1)
                    value = lax.dot_general(
                        side, stack[...], (((0,), (0,)), ((), ())), preferred_element_type=jnp.float32
                    )
                else:
                    side = jnp.concatenate([share_ref[begin:end, :] for begin, end in ranges], axis=0)
                    value = jnp.dot(side, stack[...], preferred_element_type=jnp.float32)
                outs[o][...] = value.astype(kind)
                o += 1

    def height(ranges):
        return sum(end - begin for begin, end in ranges)

    return pl.pallas_call(
        kernel,
        grid=(steps,),
        out_shape=[jax.ShapeDtypeStruct((height(ranges), columns), kind) for (ranges, kind), columns in bounds],
        in_specs=[pl.BlockSpec(share.shape, lambda i: (0, 0))]
        + [
            pl.BlockSpec((piece.shape[0], columns // steps), lambda i, skip=first * steps // columns: (0, i + skip))
            for (piece, first), columns in pieces
        ],
        out_specs=[pl.BlockSpec((height(ranges), columns // steps), lambda i: (0, i)) for (ranges, _), columns in bounds],
        scratch_shapes=[
            pltpu.VMEM((sum(piece.shape[0] for piece, _ in group[0]), group[1] // steps), jnp.bfloat16) for group in groups
        ],
        compiler_params=pltpu.CompilerParams(vmem_limit_bytes=14 << 20),
        cost_estimate=EAGER,
    )(share, *[piece for (piece, _), _ in pieces])


def staged_products(out_grad, gate_pre, up_pre, down_weight):
    x_bit, y_bit, z_bit, w_bit = 1, 2, 4, 8
    me, core = lax.axis_index("dp"), lax.axis_index("mp")
    tokens, units = gate_pre.shape
    rows = down_weight.shape[0]
    q, t = rows // 2, tokens // 2
    steps = 5
    split = units // 2
    barrier = lax.optimization_barrier
    place = jnp.stack([me, core]).astype(jnp.int32)
    own, right, message1, message2, message3 = first_stage(out_grad, gate_pre, up_pre, place, rows)

    extra, every, whole = (split, 2 * rows), (0, tokens), (0, units)
    left1, left2, message3 = flip(message1, z_bit), flip(message2, w_bit), flip(message3, z_bit | w_bit)
    weight1, weight2 = flip(down_weight, x_bit), flip(down_weight, y_bit)
    message3, weight1, weight2 = barrier((message3, weight1, weight2))
    to_y, to_x = cut([weight1, weight2], [(0, (0, q), whole, 0, 0), (1, (q, q), whole, 1, 0)], [(q, units)] * 2)
    weight3a, weight3b = flip(to_y, y_bit), flip(to_x, x_bit)
    left1, left2, message3, right, _, _ = barrier((left1, left2, message3, right, to_y, to_x))
    to_z, mine = cut(
        [left1, left2, message3, right],
        [
            (1, every, (0, split), 0, 0),
            (3, every, (0, units - split), 0, split),
            (0, every, extra, 1, 0),
            (1, every, extra, 1, 2 * rows),
            (2, every, (0, 2 * rows), 1, 4 * rows),
        ],
        [(tokens, units), (tokens, 6 * rows)],
    )
    from_near = flip(to_z, z_bit)
    right2 = flip(right, w_bit)
    theirs = flip(mine, 1, "mp")
    share = assemble(own, mine, theirs, place, rows)

    def low_sent(size):
        return [(2 * size, 3 * size), (6 * size, 7 * size)]

    def high_sent(size):
        return [(5 * size, 6 * size), (7 * size, 8 * size)]

    def sent(size):
        return [(low_sent(size), jnp.bfloat16), (high_sent(size), jnp.bfloat16)]

    def kept(size):
        ranges = [(0, 2 * size)], [(4 * size, 5 * size)], [(3 * size, 4 * size)]
        return [(r, jnp.float32) for r in ranges]

    from_near, right2, share = barrier((from_near, right2, share))
    right3 = flip(right2, z_bit)
    lefts = [(message1, 0), (left1, 0), (left2, 0), (from_near, 0)]
    left_to_x, left_to_y = products(share, [(lefts, split, sent(q), True)], 2)
    left_from_x, left_from_y = flip(left_to_x, x_bit), flip(left_to_y, y_bit)

    share, _ = barrier((share, left_to_x))
    weights = [(piece, 0) for piece in (down_weight, weight1, weight2, weight3a, weight3b)]
    to_w, to_z = products(
        share, [(weights, units, [(high_sent(t), jnp.bfloat16), (low_sent(t), jnp.bfloat16)], False)], 2
    )
    right3, share, to_w, to_z = barrier((right3, share, to_w, to_z))
    from_w, from_z = flip(to_w, w_bit), flip(to_z, z_bit)
    rights = [(right, 0), (from_near, split), (right2, 0), (right3, 0)]
    right_to_x, right_to_y = products(share, [(rights, units - split, sent(q), True)], 2)
    right_from_x, right_from_y = flip(right_to_x, x_bit), flip(right_to_y, y_bit)
    share, left_from_x, left_from_y, _ = barrier((share, left_from_x, left_from_y, right_to_x))
    left_parts = products(share, [(lefts, split, kept(q), True)], steps)
    parts = products(share, [(rights, units - split, kept(q), True), (weights, units, kept(t), False)], steps)

    grad_a = flip(add_tail([left_parts[1], parts[1]], [left_from_x, right_from_x]), y_bit)
    grad_b = flip(add_tail([left_parts[2], parts[2]], [left_from_y, right_from_y]), x_bit)
    to_w, to_z = add_tail([parts[4]], [from_z]), add_tail([parts[5]], [from_w])
    last_a, last_b = flip(to_w, w_bit), flip(to_z, z_bit)
    grad_a, grad_b, _, _ = barrier((grad_a, grad_b, to_w, to_z))
    grad, row_part = sum_up(
        [left_parts[0], parts[0]],
        [left_from_x, right_from_x],
        [left_from_y, right_from_y],
        grad_a,
        grad_b,
        1.0 / math.sqrt(tokens * lax.axis_size("dp")),
    )

    row_sum = lax.psum(row_part, "mp")
    return grad, row_sum, (parts[3], from_z[:t], from_w[:t], last_a, last_b)


def local(out_grad, gate_pre, up_pre, down_weight, row_moment, col_moment):
    size = lax.axis_size("dp")
    rows, units = down_weight.shape
    tokens = out_grad.shape[0]
    all_bits = [1 << b for b in range(size.bit_length() - 1)]
    decay = 1.0 - TRAIN_STEP ** (-0.8)
    total_rows = rows * size
    total_units = units * lax.axis_size("mp")
    staged = size == 16 and lax.axis_size("mp") == 2 and rows % 256 == 0 and tokens % 32 == 0 and units % 2560 == 0
    if staged:
        grad, row_sum, terms = staged_products(out_grad, gate_pre, up_pre, down_weight)
        row_moment_new, sums = column_sums(grad, row_sum, row_moment[None, :], decay, total_units)
        sums = group_sum(sums[0], all_bits[:INNER_BITS])
        own_part, from_low, from_high, last_a, last_b = terms
        arrived = jnp.concatenate([from_low, from_high], axis=0).astype(jnp.float32)
        partial, sums = lax.optimization_barrier((own_part + arrived, sums))
        hidden_grad = partial + jnp.concatenate([last_a, last_b], axis=0).astype(jnp.float32)
        gate_grad, up_grad = gradients(hidden_grad, gate_pre, up_pre)
        first, second, third = [flip(sums, bits) for bits in (4, 8, 12)]
        first, second, third, gate_grad, up_grad = lax.optimization_barrier((first, second, third, gate_grad, up_grad))
        sums = ((sums + first) + (second + third))[None, :]
        moment_row, ratios, col_moment_new = column_step(sums, col_moment[None, :], decay, total_rows)
        ratios = lax.psum(ratios, "mp")
        update, row_mean = final_update(grad, row_moment_new, moment_row, ratios, sums, total_rows, total_units)
        row_moment_new, row_mean = row_moment_new[0], row_mean[0, 0]
    else:
        product, hidden_grad = general_products(
            out_grad, gate_pre, up_pre, down_weight, all_bits[:INNER_BITS], all_bits[INNER_BITS:]
        )
        grad = product * (1.0 / math.sqrt(tokens * size))
        powers = grad * grad
        squares = powers + 1e-30
        row_sum = lax.psum(jnp.sum(squares, axis=1), "mp")
        row_moment_new = decay * row_moment + (1.0 - decay) * (row_sum / total_units)
        col_part = jnp.sum(squares, axis=0)
        scaled_part = jnp.sum(powers / row_moment_new[:, None], axis=0)
        sums = jnp.concatenate([col_part, scaled_part, jnp.broadcast_to(jnp.sum(row_moment_new), (128,))])
        sums = group_sum(sums, all_bits)
        col_moment_new = decay * col_moment + (1.0 - decay) * (sums[:units] / total_rows)
        row_mean = sums[2 * units] / total_rows
        ratios = lax.psum(jnp.sum(sums[units : 2 * units] / col_moment_new), "mp")
        clip_norm = jnp.sqrt(row_mean * ratios / (total_rows * total_units))
        row_factor = jnp.sqrt(row_mean / row_moment_new) / jnp.maximum(1.0, clip_norm)
        col_factor = 1.0 / jnp.sqrt(col_moment_new)
        update = grad * row_factor[:, None] * col_factor[None, :]
        gate_grad, up_grad = gradients(hidden_grad, gate_pre, up_pre)

    return (update, row_moment_new, col_moment_new, row_mean, gate_grad, up_grad)


def solution(mesh):
    in_specs = (P("dp", None), P("dp", "mp"), P("dp", "mp"), P("dp", "mp"), P("dp"), P("mp"))
    out_specs = (P("dp", "mp"), P("dp"), P("mp"), P(), P("dp", "mp"), P("dp", "mp"))
    return jax.shard_map(local, mesh=mesh, in_specs=in_specs, out_specs=out_specs, check_vma=False)
```
